32 devices in a mesh: gx: 8 (over z, y), gz: 4 (over x, core).
Axes of the slice: x: 2, y: 2, z: 4, core: 2. Of those that a mesh axis runs over, the one named last changes fastest.
Arguments:
- temp: float32 [64, 512, 256], P('gz', 'gx'), may hold values from -6 to 6
- u_vel: float32 [64, 512, 256], P('gz', 'gx'), may hold values from -1.8 to 1.8
- v_vel: float32 [64, 512, 256], P('gz', 'gx'), may hold values from -1.8 to 1.8
- w_vel: float32 [64, 512, 256], P('gz', 'gx'), may hold values from -1.8 to 1.8
- temp_prev_tend: float32 [64, 512, 256], P('gz', 'gx'), may hold values from -6 to 6
- w_prev_tend: float32 [64, 512, 256], P('gz', 'gx'), may hold values from -6 to 6
- lower_coupling: float32 [64], P('gz'), may hold values from 256 to 4096
- upper_coupling: float32 [64], P('gz'), may hold values from 256 to 4096, as said below
- vertical_metric: float32 [64], P('gz'), may hold values from 0.25 to 2
Outputs:
- temp_next: float32 [64, 512, 256], P('gz', 'gx')
- w_next: float32 [64, 512, 256], P('gz', 'gx')
- temp_tend: float32 [64, 512, 256], P('gz', 'gx')
- w_tend: float32 [64, 512, 256], P('gz', 'gx')
The draws below stay inside these ranges and needn't reach their ends.
Inputs may be any that keep to these rules, and one draw needn't show every extreme that they name: upper_coupling[k] equals lower_coupling[k + 1] for k < 63: the face shared by two levels.
All inputs are finite; a program needn't handle non-finite values.
Results may differ from the reference program's by a relative error of at most 0.0003.
Values sent between devices are 32-bit elements; how exact they have to be, the bound alone decides.
No kernel may reach another device: no remote copies, remote signals or barrier semaphores. Data moves between devices by JAX's collectives and lax.ppermute only.
A program may use at most 128 MiB of HBM per device.

```python
import math
import jax
import jax.numpy as jnp
from jax import lax

CZ = 16
NY = 256
NZ = 64
NX = 512


def coupling_faces(key):
    spread = jax.random.uniform(jax.random.fold_in(key, 11), (NZ + 1,), jnp.float32)
    return CZ * CZ * jnp.exp(spread * math.log(16.0))


def draw_lower_coupling(key, part):
    return coupling_faces(key)[:NZ]


def draw_upper_coupling(key, part):
    return coupling_faces(key)[1:]


def draw_temp(key, part):
    noise_key = jax.random.fold_in(key, 5)
    return jnp.clip(jax.random.normal(noise_key, (NZ, NX, NY), jnp.float32), -6.0, 6.0)


def block_scale(stream_key, dims, pieces, low, largest):
    loudness, own = 1.0, jax.random.fold_in(stream_key, 6)
    for axis_at, parts in pieces:
        draws = jnp.exp(jax.random.uniform(jax.random.fold_in(own, axis_at), (parts,), jnp.float32, low / len(pieces), largest / len(pieces)))
        loudness = loudness * jnp.repeat(draws, dims[axis_at] // parts).reshape([-1 if axis == axis_at else 1 for axis in range(len(dims))])
    return loudness


def gaussian(key, dims, deviation, most, split=(), held_as=jnp.bfloat16):
    entries = deviation * jax.random.normal(key, dims, jnp.float32)
    if split:
        entries = entries * block_scale(key, dims, split, -0.22, 0.18)
    return jnp.clip(entries, -most, most).astype(held_as)


def setup_inputs(seed: int = 0) -> dict:
    arg_keys = jax.random.split(jax.random.key(seed), 10)
    return {
        "temp": draw_temp(jax.random.fold_in(arg_keys[9], 71), 0),
        "u_vel": gaussian(arg_keys[1], (NZ, NX, NY), 0.3, 1.8, ((0, 4), (1, 8)), jnp.float32),
        "v_vel": gaussian(arg_keys[2], (NZ, NX, NY), 0.3, 1.8, ((0, 4), (1, 8)), jnp.float32),
        "w_vel": gaussian(arg_keys[3], (NZ, NX, NY), 0.3, 1.8, ((0, 4), (1, 8)), jnp.float32),
        "temp_prev_tend": gaussian(arg_keys[4], (NZ, NX, NY), 1.0, 6.0, ((0, 4), (1, 8)), jnp.float32),
        "w_prev_tend": gaussian(arg_keys[5], (NZ, NX, NY), 1.0, 6.0, ((0, 4), (1, 8)), jnp.float32),
        "lower_coupling": draw_lower_coupling(jax.random.fold_in(arg_keys[9], 71), 0),
        "upper_coupling": draw_upper_coupling(jax.random.fold_in(arg_keys[9], 71), 0),
        "vertical_metric": jnp.clip(jnp.exp(math.log(2.0) - 2.0794415 * jax.random.uniform(arg_keys[8], (NZ,), jnp.float32) ** block_scale(arg_keys[8], (NZ,), ((0, 4),), -0.2, 0.2)), 0.25, 2.0),
    }


NEW_WEIGHT = 5.0 / 12.0
OLD_WEIGHT = -17.0 / 60.0
HORIZ_DIFF = 0.1


def tendency(field, u_vel, v_vel, w_vel, vertical_metric, source):
    flux_x = u_vel * field
    advect = 0.5 * (jnp.roll(flux_x, -1, 1) - jnp.roll(flux_x, 1, 1))
    flux_y = v_vel * field
    advect = advect + 0.5 * (jnp.roll(flux_y, -1, 2) - jnp.roll(flux_y, 1, 2))
    flux_z = jnp.pad(w_vel * field, ((1, 1), (0, 0), (0, 0)))
    advect = advect + vertical_metric[:, None, None] * (flux_z[2:] - flux_z[:-2])
    spread = jnp.roll(field, -1, 1) + jnp.roll(field, 1, 1) + jnp.roll(field, -1, 2) + jnp.roll(field, 1, 2) - 4.0 * field
    return -advect + HORIZ_DIFF * spread + source


def vertical_diffusion(field, lower_coupling, upper_coupling):
    padded = jnp.pad(field, ((1, 1), (0, 0), (0, 0)))
    return upper_coupling[:, None, None] * (padded[2:] - field) - lower_coupling[:, None, None] * (field - padded[:-2])


def sweep_solve(low_band, main_band, high_band, right_side):
    def forward(carry, row):
        ratio_prev, value_prev = carry
        low_val, main_val, high_val, rhs_row = row
        pivot_val = main_val - low_val * ratio_prev
        ratio_new = high_val / pivot_val
        value_new = (rhs_row - low_val * value_prev) / pivot_val
        return (ratio_new, value_new), (ratio_new, value_new)

    start = (jnp.zeros((), jnp.float32), jnp.zeros(right_side.shape[1:], jnp.float32))
    _, (ratios, values) = lax.scan(forward, start, (low_band, main_band, high_band, right_side))

    def backward(next_value, row):
        ratio_row, value_row = row
        solved_row = value_row - ratio_row * next_value
        return solved_row, solved_row

    _, solved = lax.scan(backward, jnp.zeros(right_side.shape[1:], jnp.float32), (ratios, values), reverse=True)
    return solved


def reference(temp, u_vel, v_vel, w_vel, temp_prev_tend, w_prev_tend, lower_coupling, upper_coupling, vertical_metric):
    temp_tend = tendency(temp, u_vel, v_vel, w_vel, vertical_metric, w_vel)
    w_tend = tendency(w_vel, u_vel, v_vel, w_vel, vertical_metric, temp)
    low_band = -lower_coupling
    main_band = 1.0 + lower_coupling + upper_coupling
    high_band = -upper_coupling
    temp_rhs = temp + vertical_diffusion(temp, lower_coupling, upper_coupling) + NEW_WEIGHT * temp_tend + OLD_WEIGHT * temp_prev_tend
    temp_next = sweep_solve(low_band, main_band, high_band, temp_rhs)
    w_rhs = w_vel + vertical_diffusion(w_vel, lower_coupling, upper_coupling) + NEW_WEIGHT * w_tend + OLD_WEIGHT * w_prev_tend
    w_next = sweep_solve(low_band, main_band, high_band, w_rhs)
    return (temp_next, w_next, temp_tend, w_tend)
```

```python
import functools

import jax
import jax.numpy as jnp
from jax import lax
from jax.experimental import pallas as pl
from jax.experimental.pallas import tpu as pltpu
from jax.sharding import PartitionSpec as P

NEW_WEIGHT = 5.0 / 12.0
HORIZ_DIFF = 0.1
FIELD_WEIGHT = 2.0 / NEW_WEIGHT
PREV_WEIGHT = (17.0 / 60.0) / NEW_WEIGHT
TILE = 8
MIB = 1024 * 1024

PIVOT_NEW, LOWER_PIVOT, UPPER_PIVOT, FIRST_GREEN, BELOW_FORWARD, PIVOT = range(6)
FIRST, CORNER, LAST, BELOW, ABOVE, METRIC_BELOW, METRIC_ABOVE = range(7)
FROM_ABOVE, FROM_BELOW = range(2)

VMEM = pltpu.VMEM
F32 = jnp.float32


def whole(space):
    return pl.BlockSpec(memory_space=space)


def held(*shape):
    return pltpu.VMEM(shape, F32)


def in_vmem(array):
    return pltpu.with_memory_space_constraint(array, pltpu.VMEM)


def in_hbm(*arrays):
    return [pltpu.with_memory_space_constraint(array, pltpu.HBM) for array in arrays]


def bit_of(axis, bit):
    return (lax.axis_index(axis) >> bit) & 1


def edges_kernel(temp, u_vel, w_vel, to_left, to_right, outer, inner, strips, layers, sems):
    levels, rows, _ = temp.shape
    copies = []
    for at, array in enumerate((temp, w_vel, u_vel)):
        for side, first in enumerate((0, rows - TILE)):
            copies.append((array.at[:, pl.ds(first, TILE), :], strips.at[at, side]))
    for at, array in enumerate((temp, w_vel)):
        for side, level in enumerate((0, levels - 1)):
            copies.append((array.at[level], layers.at[at, side]))
    copies = [pltpu.make_async_copy(src, dst, sems.at[i]) for i, (src, dst) in enumerate(copies)]
    for copy in copies:
        copy.start()
    for copy in copies:
        copy.wait()
    for field in range(2):
        at = pl.ds(field * levels, levels)
        to_left[at, :] = (HORIZ_DIFF - 0.5 * strips[2, 0, :, 0, :]) * strips[field, 0, :, 0, :]
        last = TILE - 1
        to_right[at, :] = (HORIZ_DIFF + 0.5 * strips[2, 1, :, last, :]) * strips[
            field, 1, :, last, :
        ]
    upper = bit_of("gz", 0) == 1
    for field in range(2):
        at = pl.ds(field * rows, rows)
        bottom = layers[1, 0] * layers[field, 0]
        top = layers[1, 1] * layers[field, 1]
        outer[at, :] = jnp.where(upper, top, bottom)
        inner[at, :] = jnp.where(upper, bottom, top)


def edges(temp, u_vel, w_vel):
    levels, rows, cols = temp.shape
    return pl.pallas_call(
        edges_kernel,
        out_shape=(
            held(2 * levels, cols),
            held(2 * levels, cols),
            held(2 * rows, cols),
            held(2 * rows, cols),
        ),
        in_specs=[whole(pl.ANY)] * 3,
        out_specs=[whole(VMEM)] * 4,
        scratch_shapes=[
            pltpu.VMEM((3, 2, levels, TILE, cols), F32),
            pltpu.VMEM((2, 2, rows, cols), F32),
            pltpu.SemaphoreType.DMA((10,)),
        ],
        compiler_params=pltpu.CompilerParams(vmem_limit_bytes=8 * MIB),
        name="edges",
    )(*in_hbm(temp, u_vel, w_vel))


def coefficients(lower, upper, metric, table, scalars):
    levels, _, cols = table.shape

    def row(value):
        return jnp.full((1, cols), value, F32)

    ratio = jnp.zeros((1, cols), F32)
    forward = jnp.ones((1, cols), F32)
    for level in range(levels):
        low, high = row(lower[level]), row(upper[level])
        pivot = 1.0 / (1.0 + low + high - low * ratio)
        ratio = high * pivot
        lower_pivot = low * pivot
        forward = pivot if level == 0 else lower_pivot * forward
        table[level, pl.ds(PIVOT_NEW, 1), :] = NEW_WEIGHT * pivot
        table[level, pl.ds(LOWER_PIVOT, 1), :] = lower_pivot
        table[level, pl.ds(UPPER_PIVOT, 1), :] = ratio
        table[level, pl.ds(BELOW_FORWARD, 1), :] = forward
        table[level, pl.ds(PIVOT, 1), :] = pivot
    green = forward
    table[levels - 1, pl.ds(FIRST_GREEN, 1), :] = NEW_WEIGHT * green
    for level in range(levels - 2, -1, -1):
        green = (
            table[level, pl.ds(BELOW_FORWARD, 1), :]
            + table[level, pl.ds(UPPER_PIVOT, 1), :] * green
        )
        table[level, pl.ds(FIRST_GREEN, 1), :] = NEW_WEIGHT * green
    scalars[pl.ds(FIRST, 1), :] = green
    scalars[pl.ds(CORNER, 1), :] = forward
    scalars[pl.ds(LAST, 1), :] = pivot
    scalars[pl.ds(BELOW, 1), :] = row(lower[0])
    scalars[pl.ds(ABOVE, 1), :] = row(upper[levels - 1])
    scalars[pl.ds(METRIC_BELOW, 1), :] = row(NEW_WEIGHT * metric[0])
    scalars[pl.ds(METRIC_ABOVE, 1), :] = row(NEW_WEIGHT * metric[levels - 1])
    scalars[pl.ds(7, 1), :] = row(0.0)


def bulk_kernel(
    chunks,
    lower,
    upper,
    metric,
    temp,
    u_vel,
    v_vel,
    w_vel,
    temp_prev,
    w_prev,
    temp_pad,
    w_pad,
    forward,
    tend,
    first,
    table,
    scalars,
    u_buf,
    v_buf,
    tp_buf,
    wp_buf,
    sems,
):
    levels, rows, cols = temp.shape
    depth = levels // chunks
    moves = (
        (temp, temp_pad, 1),
        (w_vel, w_pad, 1),
        (u_vel, u_buf, 0),
        (v_vel, v_buf, 0),
        (temp_prev, tp_buf, 0),
        (w_prev, wp_buf, 0),
    )

    def copies(chunk):
        return [
            pltpu.make_async_copy(
                src.at[pl.ds(chunk * depth, depth)],
                dst.at[pl.ds(chunk * depth + shift, depth)],
                sems.at[i, chunk],
            )
            for i, (src, dst, shift) in enumerate(moves)
        ]

    for chunk in range(chunks):
        for copy in copies(chunk):
            copy.start()

    zeros = jnp.zeros((rows, cols), F32)
    for pad in (temp_pad, w_pad):
        pad[0] = zeros
        pad[levels + 1] = zeros
    for field in range(2):
        forward[field, 0] = zeros
        first[field] = zeros
    coefficients(lower, upper, metric, table, scalars)

    def level_step(level, carry):
        half_u = 0.5 * u_buf[level]
        half_v = 0.5 * v_buf[level]
        u_next, u_last = HORIZ_DIFF - half_u, HORIZ_DIFF + half_u
        v_next, v_last = HORIZ_DIFF - half_v, HORIZ_DIFF + half_v
        pivot = table[level, pl.ds(PIVOT_NEW, 1), :]
        lower_pivot = table[level, pl.ds(LOWER_PIVOT, 1), :]
        green = table[level, pl.ds(FIRST_GREEN, 1), :]
        slope = metric[level]
        cells = (temp_pad[level + 1], w_pad[level + 1])
        for field, (pad, prev) in enumerate(((temp_pad, tp_buf), (w_pad, wp_buf))):
            here, other = cells[field], cells[1 - field]
            sides = (
                pltpu.roll(u_next * here, rows - 1, 0)
                + pltpu.roll(u_last * here, 1, 0)
                + pltpu.roll(v_next * here, cols - 1, 1)
                + pltpu.roll(v_last * here, 1, 1)
            )
            rise = w_pad[level + 2] * pad[level + 2] - w_pad[level] * pad[level]
            change = sides - slope * rise + (other - (4.0 * HORIZ_DIFF) * here)
            tend[field, level] = change
            right = change + (FIELD_WEIGHT * here - PREV_WEIGHT * prev[level])
            forward[field, level + 1] = pivot * right + lower_pivot * forward[field, level]
            first[field] = first[field] + green * right
        return carry

    for copy in copies(0):
        copy.wait()
    for chunk in range(chunks):
        begin, end = chunk * depth, (chunk + 1) * depth
        if chunk + 1 < chunks:
            for copy in copies(chunk + 1):
                copy.wait()
        lax.fori_loop(begin, end, level_step, 0)


def bulk(lower, upper, metric, temp, u_vel, v_vel, w_vel, temp_prev, w_prev):
    levels, rows, cols = temp.shape
    chunks = 4
    block = pltpu.VMEM((levels, rows, cols), F32)
    return pl.pallas_call(
        functools.partial(bulk_kernel, chunks),
        out_shape=(
            held(levels + 2, rows, cols),
            held(levels + 2, rows, cols),
            held(2, levels + 1, rows, cols),
            held(2, levels, rows, cols),
            held(2, rows, cols),
            held(levels, TILE, cols),
            held(TILE, cols),
        ),
        in_specs=[whole(pltpu.SMEM)] * 3 + [whole(pl.ANY)] * 6,
        out_specs=[whole(VMEM)] * 7,
        scratch_shapes=[block] * 4 + [pltpu.SemaphoreType.DMA((6, chunks))],
        compiler_params=pltpu.CompilerParams(vmem_limit_bytes=24 * MIB),
        cost_estimate=pl.CostEstimate(
            flops=70 * levels * rows * cols,
            bytes_accessed=24 * levels * rows * cols,
            transcendentals=0,
        ),
        name="bulk",
    )(lower, upper, metric, *in_hbm(temp, u_vel, v_vel, w_vel, temp_prev, w_prev))


def side_changes(to_left, to_right, from_left, from_right):
    return from_left[...] - to_right[...], from_right[...] - to_left[...]


def ends(rows, cols, head, tail):
    at = lax.broadcasted_iota(jnp.int32, (rows, cols), 0)
    return jnp.where(at == 0, head, jnp.where(at == rows - 1, tail, 0.0))


def fix_kernel(
    levels, to_left, to_right, from_left, from_right, outer, inner, forward, first, table, scalars,
    message, changes,
):
    _, rows, cols = first.shape
    diffs = side_changes(to_left, to_right, from_left, from_right)
    upper = bit_of("gz", 0) == 1

    def scalar(at):
        return scalars[pl.ds(at, 1), :]

    below, above = scalar(METRIC_BELOW), scalar(METRIC_ABOVE)
    first_gain = jnp.where(upper, -above * scalar(CORNER), below * scalar(FIRST))
    last_gain = jnp.where(upper, -above * scalar(LAST), below * scalar(CORNER))
    for field in range(2):
        firsts, lasts = [], []
        for side in range(2):
            value = jnp.zeros((1, cols), F32)
            total = jnp.zeros((1, cols), F32)
            for level in range(levels):
                right = diffs[side][field * levels + level : field * levels + level + 1, :]
                value = (
                    table[level, pl.ds(PIVOT_NEW, 1), :] * right
                    + table[level, pl.ds(LOWER_PIVOT, 1), :] * value
                )
                total = total + table[level, pl.ds(FIRST_GREEN, 1), :] * right
                changes[pl.ds((side * 2 + field) * levels + level, 1), :] = value
            firsts.append(total)
            lasts.append(value)
        flux = outer[pl.ds(field * rows, rows), :]
        message[pl.ds(field * rows, rows), :] = (
            first[field] + first_gain * flux + ends(rows, cols, *firsts)
        )
        message[pl.ds((2 + field) * rows, rows), :] = (
            forward[field, levels] + last_gain * flux + ends(rows, cols, *lasts)
        )
    message[pl.ds(4 * rows, 2 * rows), :] = inner[...]
    message[pl.ds(6 * rows, TILE), :] = scalars[...]


def fix(to_left, to_right, from_left, from_right, outer, inner, forward, first, table, scalars):
    levels = table.shape[0]
    _, rows, cols = first.shape
    return pl.pallas_call(
        functools.partial(fix_kernel, levels),
        out_shape=(held(6 * rows + TILE, cols), held(4 * levels, cols)),
        in_specs=[whole(VMEM)] * 10,
        out_specs=[whole(VMEM)] * 2,
        compiler_params=pltpu.CompilerParams(vmem_limit_bytes=8 * MIB),
        name="fix",
    )(
        to_left, to_right, from_left, from_right, outer, inner,
        in_vmem(forward), in_vmem(first), in_vmem(table), scalars,
    )


def tends_kernel(
    metric, tend, to_left, to_right, from_left, from_right, outer, other,
    temp_tend, w_tend, layers, strips, sems,
):
    _, levels, rows, cols = tend.shape
    inside = pl.ds(1, levels - 2)
    outs = (temp_tend, w_tend)
    copies = [
        pltpu.make_async_copy(
            tend.at[field, inside, pl.ds(TILE, rows - 2 * TILE), :],
            outs[field].at[inside, pl.ds(TILE, rows - 2 * TILE), :],
            sems.at[field],
        )
        for field in range(2)
    ]
    for copy in copies:
        copy.start()
    upper = bit_of("gz", 0) == 1
    diffs = side_changes(to_left, to_right, from_left, from_right)
    tile_at = lax.broadcasted_iota(jnp.int32, (TILE, cols), 0)
    for field in range(2):
        out = outs[field]
        near = other[pl.ds((4 + field) * rows, rows), :]
        far = outer[pl.ds(field * rows, rows), :]
        below = jnp.where(upper, near, far)
        above = jnp.where(upper, far, near)
        for side, level, change in (
            (0, 0, metric[0] * below),
            (1, levels - 1, -metric[levels - 1] * above),
        ):
            at = field * levels + level
            rim = ends(rows, cols, diffs[0][at : at + 1, :], diffs[1][at : at + 1, :])
            layers[field, side] = tend[field, level] + change + rim
            copies.append(
                pltpu.make_async_copy(
                    layers.at[field, side], out.at[level], sems.at[2 + 2 * field + side]
                )
            )
            copies[-1].start()
        for side, begin, row in ((0, 0, 0), (1, rows - TILE, TILE - 1)):
            for level in range(1, levels - 1):
                at = field * levels + level
                strips[field, side, level] = tend[field, level, pl.ds(begin, TILE), :] + jnp.where(
                    tile_at == row, diffs[side][at : at + 1, :], 0.0
                )
            copies.append(
                pltpu.make_async_copy(
                    strips.at[field, side, inside],
                    out.at[inside, pl.ds(begin, TILE), :],
                    sems.at[6 + 2 * field + side],
                )
            )
            copies[-1].start()
    for copy in copies:
        copy.wait()


def tends(metric, tend, to_left, to_right, from_left, from_right, outer, other):
    _, levels, rows, cols = tend.shape
    return pl.pallas_call(
        tends_kernel,
        out_shape=(jax.ShapeDtypeStruct((levels, rows, cols), F32),) * 2,
        in_specs=[whole(pltpu.SMEM)] + [whole(VMEM)] * 7,
        out_specs=[whole(pl.ANY)] * 2,
        scratch_shapes=[
            pltpu.VMEM((2, 2, rows, cols), F32),
            pltpu.VMEM((2, 2, levels, TILE, cols), F32),
            pltpu.SemaphoreType.DMA((10,)),
        ],
        compiler_params=pltpu.CompilerParams(vmem_limit_bytes=8 * MIB),
        cost_estimate=pl.CostEstimate(
            flops=levels * rows * cols,
            bytes_accessed=8 * levels * rows * cols,
            transcendentals=0,
        ),
        name="tends",
    )(metric, in_vmem(tend), to_left, to_right, from_left, from_right, outer, other)


def interface(low, high):
    coupling = low[ABOVE]
    return coupling, 1.0 / (1.0 - coupling * coupling * low[LAST] * high[FIRST])


def scalar_rows(ref, begin):
    return [ref[pl.ds(begin + at, 1), :] for at in range(7)]


def merge_kernel(bit, with_flux, halves, mine, theirs, message, base, gains):
    _, rows, cols = base.shape
    upper = bit_of("gz", bit) == 1
    parts = 6 if with_flux else 4
    own, far = scalar_rows(mine, parts * rows), scalar_rows(theirs, parts * rows)
    low = [jnp.where(upper, b, a) for a, b in zip(own, far)]
    high = [jnp.where(upper, a, b) for a, b in zip(own, far)]
    coupling, inverse = interface(low, high)
    to_high, to_low = high[FIRST] * coupling, low[LAST] * coupling
    low_out, high_out = low[CORNER] * coupling, high[CORNER] * coupling
    if halves:
        sends_last = bit_of("gz", bit + 1) == 0
    for field in range(2):

        def part(at):
            a = mine[pl.ds((at + field) * rows, rows), :]
            b = theirs[pl.ds((at + field) * rows, rows), :]
            return jnp.where(upper, b, a), jnp.where(upper, a, b)

        (low_first, high_first), (low_last, high_last) = part(0), part(2)
        if with_flux:
            low_flux, high_flux = part(4)
            low_first = low_first - (low[CORNER] * low[METRIC_ABOVE]) * high_flux
            low_last = low_last - (low[LAST] * low[METRIC_ABOVE]) * high_flux
            high_first = high_first + (high[FIRST] * high[METRIC_BELOW]) * low_flux
            high_last = high_last + (high[CORNER] * high[METRIC_BELOW]) * low_flux
        above = inverse * (high_first + to_high * low_last)
        below = inverse * (low_last + to_low * high_first)
        into = coupling * jnp.where(upper, below, above)
        if with_flux:
            into = into + jnp.where(
                upper, high[METRIC_BELOW] * low_flux, -low[METRIC_ABOVE] * high_flux
            )
        base[field] = into
        all_first = low_first + low_out * above
        all_last = high_last + high_out * below
        if halves:
            message[pl.ds(field * rows, rows), :] = jnp.where(sends_last, all_last, all_first)
        else:
            message[pl.ds(field * rows, rows), :] = all_first
            message[pl.ds((2 + field) * rows, rows), :] = all_last
    scalars = [
        low[FIRST] + low_out * inverse * to_high * low[CORNER],
        low_out * inverse * high[CORNER],
        high[LAST] + high_out * inverse * to_low * high[CORNER],
        low[BELOW],
        high[ABOVE],
        low[METRIC_BELOW],
        high[METRIC_ABOVE],
    ]
    begin = (2 if halves else 4) * rows
    for at, value in enumerate(scalars):
        message[pl.ds(begin + at, 1), :] = value
    message[pl.ds(begin + 7, 1), :] = jnp.zeros((1, cols), F32)
    scale = coupling * inverse
    gains[...] = jnp.zeros(gains.shape, F32)
    gains[pl.ds(FROM_ABOVE, 1), :] = (
        scale * high[CORNER] * jnp.where(upper, to_low, 1.0)
    )
    gains[pl.ds(FROM_BELOW, 1), :] = (
        scale * low[CORNER] * jnp.where(upper, 1.0, to_high)
    )


def merge(bit, with_flux, halves, rows, mine, theirs):
    cols = mine.shape[1]
    return pl.pallas_call(
        functools.partial(merge_kernel, bit, with_flux, halves),
        out_shape=(
            held((2 if halves else 4) * rows + TILE, cols),
            held(2, rows, cols),
            held(TILE, cols),
        ),
        in_specs=[whole(VMEM)] * 2,
        out_specs=[whole(VMEM)] * 3,
        compiler_params=pltpu.CompilerParams(vmem_limit_bytes=8 * MIB),
        name="merge",
    )(mine, theirs)


def finish_kernel(
    rounds, strips, temp_pad, w_pad, forward, table, changes, scalars, outer, mine, theirs, *rest
):
    bases, gains = rest[: rounds - 1], rest[rounds - 1 : 2 * rounds - 2]
    temp_next, w_next, result, below_in, above_in, sems = rest[2 * rounds - 2 :]
    levels = table.shape[0]
    _, _, rows, cols = forward.shape
    upper = bit_of("gz", rounds - 1) == 1
    own, far = scalar_rows(mine, 2 * rows), scalar_rows(theirs, 2 * rows)
    low = [jnp.where(upper, b, a) for a, b in zip(own, far)]
    high = [jnp.where(upper, a, b) for a, b in zip(own, far)]
    coupling, inverse = interface(low, high)
    to_other = coupling * jnp.where(upper, low[LAST], high[FIRST])
    scale = coupling * inverse
    for field in range(2):
        at = pl.ds(field * rows, rows)
        into = scale * (theirs[at, :] + to_other * mine[at, :])
        zero = jnp.zeros((rows, cols), F32)
        below, above = jnp.where(upper, into, zero), jnp.where(upper, zero, into)
        for step in range(rounds - 2, -1, -1):
            side = bit_of("gz", step) == 1
            into = (
                bases[step][field]
                + gains[step][pl.ds(FROM_ABOVE, 1), :] * above
                + gains[step][pl.ds(FROM_BELOW, 1), :] * below
            )
            below, above = jnp.where(side, into, below), jnp.where(side, above, into)
        side = bit_of("gz", 0) == 1
        flux = outer[at, :]
        gain_below = jnp.where(side, 0.0, scalars[pl.ds(METRIC_BELOW, 1), :])
        gain_above = jnp.where(side, -scalars[pl.ds(METRIC_ABOVE, 1), :], 0.0)
        below_in[field] = below + gain_below * flux
        above_in[field] = above + gain_above * flux

    size = rows // strips
    row_at = lax.broadcasted_iota(jnp.int32, (TILE, cols), 0)
    copies = []
    for field, (pad, out) in enumerate(((temp_pad, temp_next), (w_pad, w_next))):
        for strip in range(strips):
            at = pl.ds(strip * size, size)
            below = below_in[field, at, :]

            def solve(level, carry, factor, field=field, strip=strip, at=at, below=below, pad=pad):
                value = (
                    forward[field, level + 1, at, :]
                    + table[level, pl.ds(BELOW_FORWARD, 1), :] * below
                    + factor * carry
                )
                if strip == 0:
                    change = changes[pl.ds(field * levels + level, 1), :]
                    value = jnp.concatenate(
                        [value[:TILE] + jnp.where(row_at == 0, change, 0.0), value[TILE:]]
                    )
                if strip == strips - 1:
                    change = changes[pl.ds((2 + field) * levels + level, 1), :]
                    value = jnp.concatenate(
                        [value[:-TILE], value[-TILE:] + jnp.where(row_at == TILE - 1, change, 0.0)]
                    )
                result[field, level, at, :] = value - pad[level + 1, at, :]
                return value

            carry = solve(levels - 1, above_in[field, at, :], table[levels - 1, pl.ds(PIVOT, 1), :])

            def step(back, carry, solve=solve):
                level = levels - 2 - back
                return solve(level, carry, table[level, pl.ds(UPPER_PIVOT, 1), :])

            lax.fori_loop(0, levels - 1, step, carry)
            copies.append(
                pltpu.make_async_copy(
                    result.at[field, :, at, :], out.at[:, at, :], sems.at[field, strip]
                )
            )
            copies[-1].start()
    for copy in copies:
        copy.wait()


def finish(rounds, temp_pad, w_pad, forward, table, changes, scalars, outer, mine, theirs, bases, gains):
    levels = table.shape[0]
    _, _, rows, cols = forward.shape
    strips = 2
    return pl.pallas_call(
        functools.partial(finish_kernel, rounds, strips),
        out_shape=(jax.ShapeDtypeStruct((levels, rows, cols), F32),) * 2,
        in_specs=[whole(VMEM)] * (7 + 2 + 2 * (rounds - 1)),
        out_specs=[whole(pl.ANY)] * 2,
        scratch_shapes=[
            pltpu.VMEM((2, levels, rows, cols), F32),
            pltpu.VMEM((2, rows, cols), F32),
            pltpu.VMEM((2, rows, cols), F32),
            pltpu.SemaphoreType.DMA((2, strips)),
        ],
        compiler_params=pltpu.CompilerParams(vmem_limit_bytes=16 * MIB),
        name="finish",
    )(
        in_vmem(temp_pad), in_vmem(w_pad), in_vmem(forward), in_vmem(table), changes, scalars,
        outer, mine, theirs, *bases, *gains,
    )


def local(temp, u_vel, v_vel, w_vel, temp_prev, w_prev, lower, upper, metric):
    _, rows, _ = temp.shape
    across, stacked = lax.axis_size("gx"), lax.axis_size("gz")
    rounds = stacked.bit_length() - 1
    to_left, to_right, outer, inner = edges(temp, u_vel, w_vel)
    from_right = lax.ppermute(to_left, "gx", [((i + 1) % across, i) for i in range(across)])
    from_left = lax.ppermute(to_right, "gx", [(i, (i + 1) % across) for i in range(across)])
    seams = [(i, i + 1) for i in range(1, stacked - 1, 2)]
    outer = lax.ppermute(outer, "gz", seams + [(b, a) for a, b in seams])
    temp_pad, w_pad, forward, tend, first, table, scalars = bulk(
        lower, upper, metric, temp, u_vel, v_vel, w_vel, temp_prev, w_prev
    )
    mine, changes = fix(
        to_left, to_right, from_left, from_right, outer, inner, forward, first, table, scalars
    )
    bases, gains = [], []
    for step in range(rounds):
        theirs = lax.ppermute(mine, "gz", [(i, i ^ (1 << step)) for i in range(stacked)])
        if step == 0:
            temp_tend, w_tend = tends(
                metric, tend, to_left, to_right, from_left, from_right, outer, theirs
            )
        if step + 1 < rounds:
            mine, base, gain = merge(step, step == 0, step + 2 == rounds, rows, mine, theirs)
            bases.append(base)
            gains.append(gain)
    temp_next, w_next = finish(
        rounds, temp_pad, w_pad, forward, table, changes, scalars, outer, mine, theirs, bases, gains
    )
    return temp_next, w_next, temp_tend, w_tend


def solution(mesh):
    field = P("gz", "gx", None)
    return jax.shard_map(
        local,
        mesh=mesh,
        in_specs=(field,) * 6 + (P("gz"),) * 3,
        out_specs=(field,) * 4,
        check_vma=False,
    )
```

```python
import functools

import jax
import jax.numpy as jnp
from jax import lax
from jax.experimental import pallas as pl
from jax.experimental.pallas import tpu as pltpu
from jax.sharding import PartitionSpec as P

NEW_WEIGHT = 5.0 / 12.0
HORIZ_DIFF = 0.1
FIELD_WEIGHT = 2.0 / NEW_WEIGHT
PREV_WEIGHT = (17.0 / 60.0) / NEW_WEIGHT
TILE = 8
MIB = 1024 * 1024

PIVOT_NEW, LOWER_PIVOT, UPPER_PIVOT, FIRST_GREEN, BELOW_FORWARD, PIVOT = range(6)
FIRST, CORNER, LAST, BELOW, ABOVE, METRIC_BELOW, METRIC_ABOVE = range(7)
FROM_ABOVE, FROM_BELOW = range(2)

VMEM = pltpu.VMEM
F32 = jnp.float32


def whole(space):
    return pl.BlockSpec(memory_space=space)


def held(*shape):
    return pltpu.VMEM(shape, F32)


def in_vmem(array):
    return pltpu.with_memory_space_constraint(array, pltpu.VMEM)


def in_hbm(*arrays):
    return [pltpu.with_memory_space_constraint(array, pltpu.HBM) for array in arrays]


def bit_of(axis, bit):
    return (lax.axis_index(axis) >> bit) & 1


def edges_kernel(temp, u_vel, w_vel, v_vel, temp_prev, w_prev, near, far, outer, inner, strips, layers, sems):
    levels, rows, _ = temp.shape
    copies = []
    for at, array in enumerate((temp, w_vel, u_vel)):
        for side, first in enumerate((0, rows - TILE)):
            copies.append((array.at[:, pl.ds(first, TILE), :], strips.at[at, side]))
    for at, array in enumerate((temp, w_vel)):
        for side, level in enumerate((0, levels - 1)):
            copies.append((array.at[level], layers.at[at, side]))
    copies = [pltpu.make_async_copy(src, dst, sems.at[i]) for i, (src, dst) in enumerate(copies)]
    for copy in copies:
        copy.start()
    for copy in copies:
        copy.wait()
    odd = bit_of("gx", 0) == 1
    last = TILE - 1
    for field in range(2):
        at = pl.ds(field * levels, levels)
        to_left = (HORIZ_DIFF - 0.5 * strips[2, 0, :, 0, :]) * strips[field, 0, :, 0, :]
        to_right = (HORIZ_DIFF + 0.5 * strips[2, 1, :, last, :]) * strips[field, 1, :, last, :]
        near[at, :] = jnp.where(odd, to_left, to_right)
        far[at, :] = jnp.where(odd, to_right, to_left)
    upper = bit_of("gz", 0) == 1
    for field in range(2):
        at = pl.ds(field * rows, rows)
        bottom = layers[1, 0] * layers[field, 0]
        top = layers[1, 1] * layers[field, 1]
        outer[at, :] = jnp.where(upper, top, bottom)
        inner[at, :] = jnp.where(upper, bottom, top)


def edges(temp, u_vel, w_vel, *later):
    levels, rows, cols = temp.shape
    return pl.pallas_call(
        edges_kernel,
        out_shape=(
            held(2 * levels, cols),
            held(2 * levels, cols),
            held(2 * rows, cols),
            held(2 * rows, cols),
        ),
        in_specs=[whole(pl.ANY)] * 6,
        out_specs=[whole(VMEM)] * 4,
        scratch_shapes=[
            pltpu.VMEM((3, 2, levels, TILE, cols), F32),
            pltpu.VMEM((2, 2, rows, cols), F32),
            pltpu.SemaphoreType.DMA((10,)),
        ],
        compiler_params=pltpu.CompilerParams(vmem_limit_bytes=8 * MIB),
        name="edges",
    )(*in_hbm(temp, u_vel, w_vel, *later))


def coefficients(lower, upper, metric, table, scalars):
    levels, _, cols = table.shape

    def row(value):
        return jnp.full((1, cols), value, F32)

    ratio = jnp.zeros((1, cols), F32)
    forward = jnp.ones((1, cols), F32)
    for level in range(levels):
        low, high = row(lower[level]), row(upper[level])
        pivot = 1.0 / (1.0 + low + high - low * ratio)
        ratio = high * pivot
        lower_pivot = low * pivot
        forward = pivot if level == 0 else lower_pivot * forward
        table[level, pl.ds(PIVOT_NEW, 1), :] = NEW_WEIGHT * pivot
        table[level, pl.ds(LOWER_PIVOT, 1), :] = lower_pivot
        table[level, pl.ds(UPPER_PIVOT, 1), :] = ratio
        table[level, pl.ds(BELOW_FORWARD, 1), :] = forward
        table[level, pl.ds(PIVOT, 1), :] = pivot
    green = forward
    table[levels - 1, pl.ds(FIRST_GREEN, 1), :] = NEW_WEIGHT * green
    for level in range(levels - 2, -1, -1):
        green = (
            table[level, pl.ds(BELOW_FORWARD, 1), :]
            + table[level, pl.ds(UPPER_PIVOT, 1), :] * green
        )
        table[level, pl.ds(FIRST_GREEN, 1), :] = NEW_WEIGHT * green
    scalars[pl.ds(FIRST, 1), :] = green
    scalars[pl.ds(CORNER, 1), :] = forward
    scalars[pl.ds(LAST, 1), :] = pivot
    scalars[pl.ds(BELOW, 1), :] = row(lower[0])
    scalars[pl.ds(ABOVE, 1), :] = row(upper[levels - 1])
    scalars[pl.ds(METRIC_BELOW, 1), :] = row(NEW_WEIGHT * metric[0])
    scalars[pl.ds(METRIC_ABOVE, 1), :] = row(NEW_WEIGHT * metric[levels - 1])
    scalars[pl.ds(7, 1), :] = row(0.0)


def bulk_kernel(
    lower,
    upper,
    metric,
    temp,
    u_vel,
    v_vel,
    w_vel,
    temp_prev,
    w_prev,
    forward,
    tend,
    first,
    table,
    scalars,
):
    levels, rows, cols = temp.shape
    strips = rows // TILE
    fields, prevs = (temp, w_vel), (temp_prev, w_prev)
    coefficients(lower, upper, metric, table, scalars)
    for field in range(2):
        forward[field, 0] = jnp.zeros((rows, cols), F32)
        first[field] = jnp.zeros((rows, cols), F32)
    row_at = lax.broadcasted_iota(jnp.int32, (TILE, cols), 0)
    zero = jnp.zeros((TILE, cols), F32)

    def level_step(level, carry):
        pivot = jnp.broadcast_to(table[level, pl.ds(PIVOT_NEW, 1), :], (TILE, cols))
        lower_pivot = jnp.broadcast_to(table[level, pl.ds(LOWER_PIVOT, 1), :], (TILE, cols))
        green = jnp.broadcast_to(table[level, pl.ds(FIRST_GREEN, 1), :], (TILE, cols))
        slope = metric[level]
        rise = jnp.where(level < levels - 1, slope, 0.0)
        fall = jnp.where(level > 0, slope, 0.0)
        over = jnp.minimum(level + 1, levels - 1)
        under = jnp.maximum(level - 1, 0)

        def sides(strip):
            at = pl.ds(strip * TILE, TILE)
            half = 0.5 * u_vel[level, at, :]
            back, ahead = HORIZ_DIFF - half, HORIZ_DIFF + half
            here = [values[level, at, :] for values in fields]
            return (
                here,
                [pltpu.roll(back * value, TILE - 1, 0) for value in here],
                [pltpu.roll(ahead * value, 1, 0) for value in here],
            )

        before = [zero, zero]
        here, back, ahead = sides(0)
        for strip in range(strips):
            after = sides(strip + 1) if strip + 1 < strips else (None, [zero, zero], None)
            at = pl.ds(strip * TILE, TILE)
            half = 0.5 * v_vel[level, at, :]
            v_back, v_ahead = HORIZ_DIFF - half, HORIZ_DIFF + half
            w_over = rise * w_vel[over, at, :]
            w_under = fall * w_vel[under, at, :]
            for field in range(2):
                value = here[field]
                change = jnp.where(row_at == TILE - 1, after[1][field], back[field])
                change = change + jnp.where(row_at == 0, before[field], ahead[field])
                change = change + pltpu.roll(v_back * value, cols - 1, 1)
                change = change + pltpu.roll(v_ahead * value, 1, 1)
                change = change - w_over * fields[field][over, at, :]
                change = change + w_under * fields[field][under, at, :]
                change = change + (here[1 - field] - (4.0 * HORIZ_DIFF) * value)
                tend[field, level, at, :] = change
                right = change + (FIELD_WEIGHT * value - PREV_WEIGHT * prevs[field][level, at, :])
                forward[field, level + 1, at, :] = (
                    pivot * right + lower_pivot * forward[field, level, at, :]
                )
                first[field, at, :] = first[field, at, :] + green * right
            before = ahead
            here, back, ahead = after
        return carry

    lax.fori_loop(0, levels, level_step, 0)


def bulk(lower, upper, metric, *arrays):
    levels, rows, cols = arrays[0].shape
    return pl.pallas_call(
        bulk_kernel,
        out_shape=(
            held(2, levels + 1, rows, cols),
            held(2, levels, rows, cols),
            held(2, rows, cols),
            held(levels, TILE, cols),
            held(TILE, cols),
        ),
        in_specs=[whole(pltpu.SMEM)] * 3 + [whole(VMEM)] * 6,
        out_specs=[whole(VMEM)] * 5,
        compiler_params=pltpu.CompilerParams(vmem_limit_bytes=8 * MIB),
        cost_estimate=pl.CostEstimate(
            flops=70 * levels * rows * cols,
            bytes_accessed=24 * levels * rows * cols,
            transcendentals=0,
        ),
        name="bulk",
    )(lower, upper, metric, *map(in_vmem, arrays))


def side_changes(near, far):
    odd = bit_of("gx", 0) == 1
    return jnp.where(odd, near[...], far[...]), jnp.where(odd, far[...], near[...])


def ends(rows, cols, head, tail):
    at = lax.broadcasted_iota(jnp.int32, (rows, cols), 0)
    return jnp.where(at == 0, head, jnp.where(at == rows - 1, tail, 0.0))


def fix_kernel(
    levels, near, far, outer, inner, forward, first, table, scalars,
    message, changes,
):
    _, rows, cols = first.shape
    diffs = side_changes(near, far)
    upper = bit_of("gz", 0) == 1

    def scalar(at):
        return scalars[pl.ds(at, 1), :]

    below, above = scalar(METRIC_BELOW), scalar(METRIC_ABOVE)
    first_gain = jnp.where(upper, -above * scalar(CORNER), below * scalar(FIRST))
    last_gain = jnp.where(upper, -above * scalar(LAST), below * scalar(CORNER))
    for field in range(2):
        firsts, lasts = [], []
        for side in range(2):
            value = jnp.zeros((1, cols), F32)
            total = jnp.zeros((1, cols), F32)
            for level in range(levels):
                right = diffs[side][field * levels + level : field * levels + level + 1, :]
                value = (
                    table[level, pl.ds(PIVOT_NEW, 1), :] * right
                    + table[level, pl.ds(LOWER_PIVOT, 1), :] * value
                )
                total = total + table[level, pl.ds(FIRST_GREEN, 1), :] * right
                changes[pl.ds((side * 2 + field) * levels + level, 1), :] = value
            firsts.append(total)
            lasts.append(value)
        flux = outer[pl.ds(field * rows, rows), :]
        message[pl.ds(field * rows, rows), :] = (
            first[field] + first_gain * flux + ends(rows, cols, *firsts)
        )
        message[pl.ds((2 + field) * rows, rows), :] = (
            forward[field, levels] + last_gain * flux + ends(rows, cols, *lasts)
        )
    message[pl.ds(4 * rows, 2 * rows), :] = inner[...]
    message[pl.ds(6 * rows, TILE), :] = scalars[...]


def fix(near, far, outer, inner, forward, first, table, scalars):
    levels = table.shape[0]
    _, rows, cols = first.shape
    return pl.pallas_call(
        functools.partial(fix_kernel, levels),
        out_shape=(held(6 * rows + TILE, cols), held(4 * levels, cols)),
        in_specs=[whole(VMEM)] * 8,
        out_specs=[whole(VMEM)] * 2,
        compiler_params=pltpu.CompilerParams(vmem_limit_bytes=8 * MIB),
        name="fix",
    )(
        near, far, outer, inner,
        in_vmem(forward), in_vmem(first), in_vmem(table), scalars,
    )


def tends_kernel(
    metric, tend, near, far, outer, other,
    temp_tend, w_tend, layers, strips, sems,
):
    _, levels, rows, cols = tend.shape
    inside = pl.ds(1, levels - 2)
    outs = (temp_tend, w_tend)
    copies = [
        pltpu.make_async_copy(
            tend.at[field, inside, pl.ds(TILE, rows - 2 * TILE), :],
            outs[field].at[inside, pl.ds(TILE, rows - 2 * TILE), :],
            sems.at[field],
        )
        for field in range(2)
    ]
    for copy in copies:
        copy.start()
    upper = bit_of("gz", 0) == 1
    diffs = side_changes(near, far)
    tile_at = lax.broadcasted_iota(jnp.int32, (TILE, cols), 0)
    for field in range(2):
        out = outs[field]
        near = other[pl.ds((4 + field) * rows, rows), :]
        far = outer[pl.ds(field * rows, rows), :]
        below = jnp.where(upper, near, far)
        above = jnp.where(upper, far, near)
        for side, level, change in (
            (0, 0, metric[0] * below),
            (1, levels - 1, -metric[levels - 1] * above),
        ):
            at = field * levels + level
            rim = ends(rows, cols, diffs[0][at : at + 1, :], diffs[1][at : at + 1, :])
            layers[field, side] = tend[field, level] + change + rim
            copies.append(
                pltpu.make_async_copy(
                    layers.at[field, side], out.at[level], sems.at[2 + 2 * field + side]
                )
            )
            copies[-1].start()
        for side, begin, row in ((0, 0, 0), (1, rows - TILE, TILE - 1)):
            for level in range(1, levels - 1):
                at = field * levels + level
                strips[field, side, level] = tend[field, level, pl.ds(begin, TILE), :] + jnp.where(
                    tile_at == row, diffs[side][at : at + 1, :], 0.0
                )
            copies.append(
                pltpu.make_async_copy(
                    strips.at[field, side, inside],
                    out.at[inside, pl.ds(begin, TILE), :],
                    sems.at[6 + 2 * field + side],
                )
            )
            copies[-1].start()
    for copy in copies:
        copy.wait()


def tends(metric, tend, near, far, outer, other):
    _, levels, rows, cols = tend.shape
    return pl.pallas_call(
        tends_kernel,
        out_shape=(jax.ShapeDtypeStruct((levels, rows, cols), F32),) * 2,
        in_specs=[whole(pltpu.SMEM)] + [whole(VMEM)] * 5,
        out_specs=[whole(pl.ANY)] * 2,
        scratch_shapes=[
            pltpu.VMEM((2, 2, rows, cols), F32),
            pltpu.VMEM((2, 2, levels, TILE, cols), F32),
            pltpu.SemaphoreType.DMA((10,)),
        ],
        compiler_params=pltpu.CompilerParams(vmem_limit_bytes=8 * MIB),
        cost_estimate=pl.CostEstimate(
            flops=levels * rows * cols,
            bytes_accessed=8 * levels * rows * cols,
            transcendentals=0,
        ),
        name="tends",
    )(metric, in_vmem(tend), near, far, outer, other)


def interface(low, high):
    coupling = low[ABOVE]
    return coupling, 1.0 / (1.0 - coupling * coupling * low[LAST] * high[FIRST])


def scalar_rows(ref, begin):
    return [ref[pl.ds(begin + at, 1), :] for at in range(7)]


def merge_kernel(bit, with_flux, halves, mine, theirs, message, base, gains):
    _, rows, cols = base.shape
    upper = bit_of("gz", bit) == 1
    parts = 6 if with_flux else 4
    own, far = scalar_rows(mine, parts * rows), scalar_rows(theirs, parts * rows)
    low = [jnp.where(upper, b, a) for a, b in zip(own, far)]
    high = [jnp.where(upper, a, b) for a, b in zip(own, far)]
    coupling, inverse = interface(low, high)
    to_high, to_low = high[FIRST] * coupling, low[LAST] * coupling
    low_out, high_out = low[CORNER] * coupling, high[CORNER] * coupling
    if halves:
        sends_last = bit_of("gz", bit + 1) == 0
    for field in range(2):

        def part(at):
            a = mine[pl.ds((at + field) * rows, rows), :]
            b = theirs[pl.ds((at + field) * rows, rows), :]
            return jnp.where(upper, b, a), jnp.where(upper, a, b)

        (low_first, high_first), (low_last, high_last) = part(0), part(2)
        if with_flux:
            low_flux, high_flux = part(4)
            low_first = low_first - (low[CORNER] * low[METRIC_ABOVE]) * high_flux
            low_last = low_last - (low[LAST] * low[METRIC_ABOVE]) * high_flux
            high_first = high_first + (high[FIRST] * high[METRIC_BELOW]) * low_flux
            high_last = high_last + (high[CORNER] * high[METRIC_BELOW]) * low_flux
        above = inverse * (high_first + to_high * low_last)
        below = inverse * (low_last + to_low * high_first)
        into = coupling * jnp.where(upper, below, above)
        if with_flux:
            into = into + jnp.where(
                upper, high[METRIC_BELOW] * low_flux, -low[METRIC_ABOVE] * high_flux
            )
        base[field] = into
        all_first = low_first + low_out * above
        all_last = high_last + high_out * below
        if halves:
            message[pl.ds(field * rows, rows), :] = jnp.where(sends_last, all_last, all_first)
        else:
            message[pl.ds(field * rows, rows), :] = all_first
            message[pl.ds((2 + field) * rows, rows), :] = all_last
    scalars = [
        low[FIRST] + low_out * inverse * to_high * low[CORNER],
        low_out * inverse * high[CORNER],
        high[LAST] + high_out * inverse * to_low * high[CORNER],
        low[BELOW],
        high[ABOVE],
        low[METRIC_BELOW],
        high[METRIC_ABOVE],
    ]
    begin = (2 if halves else 4) * rows
    for at, value in enumerate(scalars):
        message[pl.ds(begin + at, 1), :] = value
    message[pl.ds(begin + 7, 1), :] = jnp.zeros((1, cols), F32)
    scale = coupling * inverse
    gains[...] = jnp.zeros(gains.shape, F32)
    gains[pl.ds(FROM_ABOVE, 1), :] = (
        scale * high[CORNER] * jnp.where(upper, to_low, 1.0)
    )
    gains[pl.ds(FROM_BELOW, 1), :] = (
        scale * low[CORNER] * jnp.where(upper, 1.0, to_high)
    )


def merge(bit, with_flux, halves, rows, mine, theirs):
    cols = mine.shape[1]
    return pl.pallas_call(
        functools.partial(merge_kernel, bit, with_flux, halves),
        out_shape=(
            held((2 if halves else 4) * rows + TILE, cols),
            held(2, rows, cols),
            held(TILE, cols),
        ),
        in_specs=[whole(VMEM)] * 2,
        out_specs=[whole(VMEM)] * 3,
        compiler_params=pltpu.CompilerParams(vmem_limit_bytes=8 * MIB),
        name="merge",
    )(mine, theirs)


def prepare_kernel(
    rounds, temp, w_vel, forward, table, changes, scalars, outer, *rest
):
    bases, gains = rest[: rounds - 1], rest[rounds - 1 : 2 * rounds - 2]
    known, response, below_in, above_in = rest[2 * rounds - 2 :]
    levels, rows, cols = temp.shape
    upper = bit_of("gz", rounds - 1) == 1
    one, none = jnp.ones((1, cols), F32), jnp.zeros((1, cols), F32)
    below_gain, above_gain = jnp.where(upper, one, none), jnp.where(upper, none, one)
    below = above = None
    for step in range(rounds - 2, -1, -1):
        side = bit_of("gz", step) == 1
        from_above = gains[step][pl.ds(FROM_ABOVE, 1), :]
        from_below = gains[step][pl.ds(FROM_BELOW, 1), :]
        gain = from_above * above_gain + from_below * below_gain
        below_gain = jnp.where(side, gain, below_gain)
        above_gain = jnp.where(side, above_gain, gain)
        into = [bases[step][field] for field in range(2)]
        if below is None:
            below = above = [jnp.zeros((rows, cols), F32)] * 2
        else:
            into = [
                into[field] + from_above * above[field] + from_below * below[field]
                for field in range(2)
            ]
        below = [jnp.where(side, into[field], below[field]) for field in range(2)]
        above = [jnp.where(side, above[field], into[field]) for field in range(2)]
    side = bit_of("gz", 0) == 1
    flux_below = jnp.where(side, none, scalars[pl.ds(METRIC_BELOW, 1), :])
    flux_above = jnp.where(side, -scalars[pl.ds(METRIC_ABOVE, 1), :], none)
    for field in range(2):
        flux = outer[pl.ds(field * rows, rows), :]
        below_in[field] = below[field] + flux_below * flux
        above_in[field] = above[field] + flux_above * flux

    gain = above_gain * table[levels - 1, pl.ds(PIVOT, 1), :]
    for level in range(levels - 1, -1, -1):
        if level < levels - 1:
            gain = gain * table[level, pl.ds(UPPER_PIVOT, 1), :]
        gain = gain + below_gain * table[level, pl.ds(BELOW_FORWARD, 1), :]
        response[level] = jnp.broadcast_to(gain, (TILE, cols))

    row_at = lax.broadcasted_iota(jnp.int32, (TILE, cols), 0)
    width = 2 * TILE
    for field, cells in enumerate((temp, w_vel)):
        for begin in range(0, rows, width):
            at = pl.ds(begin, width)
            below = below_in[field, at, :]

            def solve(level, carry, factor, field=field, begin=begin, at=at, below=below, cells=cells):
                value = (
                    forward[field, level + 1, at, :]
                    + table[level, pl.ds(BELOW_FORWARD, 1), :] * below
                    + factor * carry
                )
                if begin == 0:
                    change = changes[pl.ds(field * levels + level, 1), :]
                    head = value[:TILE] + jnp.where(row_at == 0, change, 0.0)
                    value = jnp.concatenate([head, value[TILE:]])
                if begin == rows - width:
                    change = changes[pl.ds((2 + field) * levels + level, 1), :]
                    tail = value[-TILE:] + jnp.where(row_at == TILE - 1, change, 0.0)
                    value = jnp.concatenate([value[:-TILE], tail])
                known[field, level, at, :] = value - cells[level, at, :]
                return value

            carry = solve(levels - 1, above_in[field, at, :], table[levels - 1, pl.ds(PIVOT, 1), :])

            def step(back, carry, solve=solve):
                level = levels - 2 - back
                return solve(level, carry, table[level, pl.ds(UPPER_PIVOT, 1), :])

            lax.fori_loop(0, levels - 1, step, carry)


def prepare(rounds, temp, w_vel, forward, table, changes, scalars, outer, bases, gains):
    levels, rows, cols = temp.shape
    return pl.pallas_call(
        functools.partial(prepare_kernel, rounds),
        out_shape=(held(2, levels, rows, cols), held(levels, TILE, cols)),
        in_specs=[whole(VMEM)] * (7 + 2 * (rounds - 1)),
        out_specs=[whole(VMEM)] * 2,
        scratch_shapes=[pltpu.VMEM((2, rows, cols), F32)] * 2,
        compiler_params=pltpu.CompilerParams(vmem_limit_bytes=8 * MIB),
        cost_estimate=pl.CostEstimate(
            flops=12 * levels * rows * cols,
            bytes_accessed=24 * levels * rows * cols,
            transcendentals=0,
        ),
        name="prepare",
    )(
        in_vmem(temp), in_vmem(w_vel), in_vmem(forward), in_vmem(table), changes, scalars,
        outer, *bases, *gains,
    )


def finish_kernel(rounds, known, response, mine, theirs, temp_next, w_next, result, sems):
    _, levels, rows, cols = known.shape
    upper = bit_of("gz", rounds - 1) == 1
    own, far = scalar_rows(mine, 2 * rows), scalar_rows(theirs, 2 * rows)
    low = [jnp.where(upper, b, a) for a, b in zip(own, far)]
    high = [jnp.where(upper, a, b) for a, b in zip(own, far)]
    coupling, inverse = interface(low, high)
    scale = coupling * inverse
    to_other = scale * coupling * jnp.where(upper, low[LAST], high[FIRST])
    width, half = 2 * TILE, rows // 2
    copies = []
    for field, out in enumerate((temp_next, w_next)):
        for part in range(2):
            for begin in range(part * half, (part + 1) * half, width):
                at = pl.ds(begin, width)
                here = pl.ds(field * rows + begin, width)
                into = scale * theirs[here, :] + to_other * mine[here, :]
                tiles = [into[i : i + TILE] for i in range(0, width, TILE)]

                def step(level, carry, field=field, begin=begin, tiles=tiles):
                    gain = response[level]
                    for i, tile in enumerate(tiles):
                        at = pl.ds(begin + i * TILE, TILE)
                        result[field, level, at, :] = known[field, level, at, :] + gain * tile
                    return carry

                lax.fori_loop(0, levels, step, 0, unroll=4)
            at = pl.ds(part * half, half)
            copies.append(
                pltpu.make_async_copy(
                    result.at[field, :, at, :], out.at[:, at, :], sems.at[field, part]
                )
            )
            copies[-1].start()
    for copy in copies:
        copy.wait()


def finish(rounds, known, response, mine, theirs):
    _, levels, rows, cols = known.shape
    return pl.pallas_call(
        functools.partial(finish_kernel, rounds),
        out_shape=(jax.ShapeDtypeStruct((levels, rows, cols), F32),) * 2,
        in_specs=[whole(VMEM)] * 4,
        out_specs=[whole(pl.ANY)] * 2,
        scratch_shapes=[
            pltpu.VMEM((2, levels, rows, cols), F32),
            pltpu.SemaphoreType.DMA((2, 2)),
        ],
        compiler_params=pltpu.CompilerParams(vmem_limit_bytes=8 * MIB),
        name="finish",
    )(in_vmem(known), response, mine, theirs)


def local(temp, u_vel, v_vel, w_vel, temp_prev, w_prev, lower, upper, metric):
    rows = temp.shape[1]
    across, stacked = lax.axis_size("gx"), lax.axis_size("gz")
    rounds = stacked.bit_length() - 1
    near, far, outer, inner = edges(temp, u_vel, w_vel, v_vel, temp_prev, w_prev)
    pairs = [(i, (i + 1) % across) for i in range(1, across, 2)]
    far = lax.ppermute(far, "gx", pairs + [(b, a) for a, b in pairs])
    pairs = [(i, i + 1) for i in range(0, across, 2)]
    near = lax.ppermute(near, "gx", pairs + [(b, a) for a, b in pairs])
    pairs = [(i, i + 1) for i in range(1, stacked - 1, 2)]
    outer = lax.ppermute(outer, "gz", pairs + [(b, a) for a, b in pairs])
    forward, tend, first, table, scalars = bulk(
        lower, upper, metric, temp, u_vel, v_vel, w_vel, temp_prev, w_prev
    )
    mine, changes = fix(near, far, outer, inner, forward, first, table, scalars)
    bases, gains = [], []
    for step in range(rounds):
        theirs = lax.ppermute(mine, "gz", [(i, i ^ (1 << step)) for i in range(stacked)])
        if step == 0:
            temp_tend, w_tend = tends(metric, tend, near, far, outer, theirs)
        if step + 1 < rounds:
            mine, base, gain = merge(step, step == 0, step + 2 == rounds, rows, mine, theirs)
            bases.append(base)
            gains.append(gain)
    known, response = prepare(
        rounds, temp, w_vel, forward, table, changes, scalars, outer, bases, gains
    )
    temp_next, w_next = finish(rounds, known, response, mine, theirs)
    return temp_next, w_next, temp_tend, w_tend


def solution(mesh):
    field = P("gz", "gx", None)
    return jax.shard_map(
        local,
        mesh=mesh,
        in_specs=(field,) * 6 + (P("gz"),) * 3,
        out_specs=(field,) * 4,
        check_vma=False,
    )
```

```python
import functools

import jax
import jax.numpy as jnp
from jax import lax
from jax.experimental import pallas as pl
from jax.experimental.pallas import tpu as pltpu
from jax.sharding import PartitionSpec as P

NEW_WEIGHT = 5.0 / 12.0
HORIZ_DIFF = 0.1
FIELD_WEIGHT = 2.0 / NEW_WEIGHT
PREV_WEIGHT = (17.0 / 60.0) / NEW_WEIGHT
TILE = 8
MIB = 1024 * 1024

PIVOT_NEW, LOWER_PIVOT, UPPER_PIVOT, FIRST_GREEN, BELOW_FORWARD, PIVOT, RISE, FALL = range(8)
FIRST, CORNER, LAST, BELOW, ABOVE, METRIC_BELOW, METRIC_ABOVE = range(7)
FROM_ABOVE, FROM_BELOW = range(2)

VMEM = pltpu.VMEM
F32 = jnp.float32


def whole(space):
    return pl.BlockSpec(memory_space=space)


def held(*shape):
    return pltpu.VMEM(shape, F32)


def in_vmem(array):
    return pltpu.with_memory_space_constraint(array, pltpu.VMEM)


def in_hbm(*arrays):
    return [pltpu.with_memory_space_constraint(array, pltpu.HBM) for array in arrays]


def bit_of(axis, bit):
    return (lax.axis_index(axis) >> bit) & 1


def edges_kernel(
    temp,
    u_vel,
    w_vel,
    v_vel,
    temp_prev,
    w_prev,
    lower,
    upper,
    metric,
    far,
    near,
    outer,
    inner,
    table,
    scalars,
    strips,
    layers,
    lower_at,
    upper_at,
    metric_at,
    sems,
):
    levels, rows, cols = temp.shape
    copies = [(lower, lower_at), (upper, upper_at), (metric, metric_at)]
    for at, array in enumerate((temp, w_vel, u_vel)):
        for side, first in enumerate((0, rows - TILE)):
            copies.append((array.at[:, pl.ds(first, TILE), :], strips.at[at, side]))
    for at, array in enumerate((temp, w_vel)):
        for side, level in enumerate((0, levels - 1)):
            copies.append((array.at[level], layers.at[at, side]))
    copies = [pltpu.make_async_copy(src, dst, sems.at[i]) for i, (src, dst) in enumerate(copies)]
    for copy in copies:
        copy.start()
    for copy in copies[:3]:
        copy.wait()
    coefficients(lower_at, upper_at, metric_at, table, scalars)
    for copy in copies[3:]:
        copy.wait()
    odd = bit_of("gx", 0) == 1
    last = TILE - 1
    for field in range(2):
        at = pl.ds(field * levels, levels)
        to_left = (HORIZ_DIFF - 0.5 * strips[2, 0, :, 0, :]) * strips[field, 0, :, 0, :]
        to_right = (HORIZ_DIFF + 0.5 * strips[2, 1, :, last, :]) * strips[field, 1, :, last, :]
        near[at, :] = jnp.where(odd, to_left, to_right)
        far[at, :] = jnp.where(odd, to_right, to_left)
    position = lax.axis_index("gz")
    upper_core = bit_of("gz", 0) == 1
    wall = (position == 0) | (position == lax.axis_size("gz") - 1)
    zero = jnp.zeros((rows, cols), F32)
    for field in range(2):
        at = pl.ds(field * rows, rows)
        bottom = layers[1, 0] * layers[field, 0]
        top = layers[1, 1] * layers[field, 1]
        outer[at, :] = jnp.where(wall, zero, jnp.where(upper_core, top, bottom))
        inner[at, :] = jnp.where(upper_core, bottom, top)


def edges(temp, u_vel, w_vel, v_vel, temp_prev, w_prev, lower, upper, metric):
    levels, rows, cols = temp.shape
    return pl.pallas_call(
        edges_kernel,
        out_shape=(
            held(2 * levels, cols),
            held(2 * levels, cols),
            held(2 * rows, cols),
            held(2 * rows, cols),
            held(levels, TILE, cols),
            held(TILE, cols),
        ),
        in_specs=[whole(pl.ANY)] * 9,
        out_specs=[whole(VMEM)] * 6,
        scratch_shapes=[
            pltpu.VMEM((3, 2, levels, TILE, cols), F32),
            pltpu.VMEM((2, 2, rows, cols), F32),
            pltpu.SMEM((levels,), F32),
            pltpu.SMEM((levels,), F32),
            pltpu.SMEM((levels,), F32),
            pltpu.SemaphoreType.DMA((13,)),
        ],
        compiler_params=pltpu.CompilerParams(vmem_limit_bytes=8 * MIB),
        name="edges",
    )(*in_hbm(temp, u_vel, w_vel, v_vel, temp_prev, w_prev, lower, upper, metric))


def coefficients(lower, upper, metric, table, scalars):
    levels, _, cols = table.shape

    def row(value):
        return jnp.full((1, cols), value, F32)

    ratio = jnp.zeros((1, cols), F32)
    forward = jnp.ones((1, cols), F32)
    for level in range(levels):
        low, high = row(lower[level]), row(upper[level])
        pivot = 1.0 / (1.0 + low + high - low * ratio)
        ratio = high * pivot
        lower_pivot = low * pivot
        forward = pivot if level == 0 else lower_pivot * forward
        table[level, pl.ds(PIVOT_NEW, 1), :] = NEW_WEIGHT * pivot
        table[level, pl.ds(LOWER_PIVOT, 1), :] = lower_pivot
        table[level, pl.ds(UPPER_PIVOT, 1), :] = ratio
        table[level, pl.ds(BELOW_FORWARD, 1), :] = forward
        table[level, pl.ds(PIVOT, 1), :] = pivot
        table[level, pl.ds(RISE, 1), :] = row(metric[level] if level < levels - 1 else 0.0)
        table[level, pl.ds(FALL, 1), :] = row(metric[level] if level > 0 else 0.0)
    green = forward
    table[levels - 1, pl.ds(FIRST_GREEN, 1), :] = NEW_WEIGHT * green
    for level in range(levels - 2, -1, -1):
        green = (
            table[level, pl.ds(BELOW_FORWARD, 1), :]
            + table[level, pl.ds(UPPER_PIVOT, 1), :] * green
        )
        table[level, pl.ds(FIRST_GREEN, 1), :] = NEW_WEIGHT * green
    scalars[pl.ds(FIRST, 1), :] = green
    scalars[pl.ds(CORNER, 1), :] = forward
    scalars[pl.ds(LAST, 1), :] = pivot
    scalars[pl.ds(BELOW, 1), :] = row(lower[0])
    scalars[pl.ds(ABOVE, 1), :] = row(upper[levels - 1])
    scalars[pl.ds(METRIC_BELOW, 1), :] = row(NEW_WEIGHT * metric[0])
    scalars[pl.ds(METRIC_ABOVE, 1), :] = row(NEW_WEIGHT * metric[levels - 1])
    scalars[pl.ds(7, 1), :] = row(0.0)


def bulk_kernel(
    table,
    temp,
    u_vel,
    v_vel,
    w_vel,
    temp_prev,
    w_prev,
    forward,
    tend,
    first,
):
    levels, rows, cols = temp.shape
    strips = rows // TILE
    fields, prevs = (temp, w_vel), (temp_prev, w_prev)
    for field in range(2):
        forward[field, 0] = jnp.zeros((rows, cols), F32)
        first[field] = jnp.zeros((rows, cols), F32)
    row_at = lax.broadcasted_iota(jnp.int32, (TILE, cols), 0)
    zero = jnp.zeros((TILE, cols), F32)

    def level_step(level, carry):
        def spread(at):
            return jnp.broadcast_to(table[level, pl.ds(at, 1), :], (TILE, cols))

        pivot, lower_pivot, green = spread(PIVOT_NEW), spread(LOWER_PIVOT), spread(FIRST_GREEN)
        rise, fall = spread(RISE), spread(FALL)
        over = jnp.minimum(level + 1, levels - 1)
        under = jnp.maximum(level - 1, 0)

        def sides(strip):
            at = pl.ds(strip * TILE, TILE)
            half = 0.5 * u_vel[level, at, :]
            back, ahead = HORIZ_DIFF - half, HORIZ_DIFF + half
            here = [values[level, at, :] for values in fields]
            return (
                here,
                [pltpu.roll(back * value, TILE - 1, 0) for value in here],
                [pltpu.roll(ahead * value, 1, 0) for value in here],
            )

        before = [zero, zero]
        here, back, ahead = sides(0)
        for strip in range(strips):
            after = sides(strip + 1) if strip + 1 < strips else (None, [zero, zero], None)
            at = pl.ds(strip * TILE, TILE)
            half = 0.5 * v_vel[level, at, :]
            v_back, v_ahead = HORIZ_DIFF - half, HORIZ_DIFF + half
            w_over = rise * w_vel[over, at, :]
            w_under = fall * w_vel[under, at, :]
            for field in range(2):
                value = here[field]
                change = jnp.where(row_at == TILE - 1, after[1][field], back[field])
                change = change + jnp.where(row_at == 0, before[field], ahead[field])
                change = change + pltpu.roll(v_back * value, cols - 1, 1)
                change = change + pltpu.roll(v_ahead * value, 1, 1)
                change = change - w_over * fields[field][over, at, :]
                change = change + w_under * fields[field][under, at, :]
                change = change + (here[1 - field] - (4.0 * HORIZ_DIFF) * value)
                tend[field, level, at, :] = change
                right = change + (FIELD_WEIGHT * value - PREV_WEIGHT * prevs[field][level, at, :])
                forward[field, level + 1, at, :] = (
                    pivot * right + lower_pivot * forward[field, level, at, :]
                )
                first[field, at, :] = first[field, at, :] + green * right
            before = ahead
            here, back, ahead = after
        return carry

    lax.fori_loop(0, levels, level_step, 0)


def bulk(table, *arrays):
    levels, rows, cols = arrays[0].shape
    return pl.pallas_call(
        bulk_kernel,
        out_shape=(
            held(2, levels + 1, rows, cols),
            held(2, levels, rows, cols),
            held(2, rows, cols),
        ),
        in_specs=[whole(VMEM)] * 7,
        out_specs=[whole(VMEM)] * 3,
        compiler_params=pltpu.CompilerParams(vmem_limit_bytes=8 * MIB),
        cost_estimate=pl.CostEstimate(
            flops=7000 * levels * rows * cols,
            bytes_accessed=24 * levels * rows * cols,
            transcendentals=0,
        ),
        name="bulk",
    )(*map(in_vmem, (table, *arrays)))


def side_changes(far, near):
    odd = bit_of("gx", 0) == 1
    return jnp.where(odd, near[...], far[...]), jnp.where(odd, far[...], near[...])


def level_fluxes(outer, inner, at):
    upper = bit_of("gz", 0) == 1
    return jnp.where(upper, inner[at, :], outer[at, :]), jnp.where(upper, outer[at, :], inner[at, :])


def ends(rows, cols, head, tail):
    at = lax.broadcasted_iota(jnp.int32, (rows, cols), 0)
    return jnp.where(at == 0, head, jnp.where(at == rows - 1, tail, 0.0))


def fix_kernel(
    levels, far, near, outer, inner, forward, first, table, scalars, message, changes
):
    _, rows, cols = first.shape
    diffs = side_changes(far, near)

    def scalar(at):
        return scalars[pl.ds(at, 1), :]

    below, above = scalar(METRIC_BELOW), -scalar(METRIC_ABOVE)
    for field in range(2):
        firsts, lasts = [], []
        for side in range(2):
            value = jnp.zeros((1, cols), F32)
            total = jnp.zeros((1, cols), F32)
            for level in range(levels):
                right = diffs[side][field * levels + level : field * levels + level + 1, :]
                value = (
                    table[level, pl.ds(PIVOT_NEW, 1), :] * right
                    + table[level, pl.ds(LOWER_PIVOT, 1), :] * value
                )
                total = total + table[level, pl.ds(FIRST_GREEN, 1), :] * right
                changes[pl.ds((side * 2 + field) * levels + level, 1), :] = value
            firsts.append(total)
            lasts.append(value)
        flux_below, flux_above = level_fluxes(outer, inner, pl.ds(field * rows, rows))
        message[pl.ds(field * rows, rows), :] = (
            first[field]
            + (below * scalar(FIRST)) * flux_below
            + (above * scalar(CORNER)) * flux_above
            + ends(rows, cols, *firsts)
        )
        message[pl.ds((2 + field) * rows, rows), :] = (
            forward[field, levels]
            + (below * scalar(CORNER)) * flux_below
            + (above * scalar(LAST)) * flux_above
            + ends(rows, cols, *lasts)
        )
    message[pl.ds(4 * rows, TILE), :] = scalars[...]


def fix(far, near, outer, inner, forward, first, table, scalars):
    levels = table.shape[0]
    _, rows, cols = first.shape
    return pl.pallas_call(
        functools.partial(fix_kernel, levels),
        out_shape=(held(4 * rows + TILE, cols), held(4 * levels, cols)),
        in_specs=[whole(VMEM)] * 8,
        out_specs=[whole(VMEM)] * 2,
        compiler_params=pltpu.CompilerParams(vmem_limit_bytes=8 * MIB),
        name="fix",
    )(far, near, outer, inner, in_vmem(forward), in_vmem(first), in_vmem(table), scalars)


def tends_kernel(field, table, tend, far, near, outer, inner, out, layers, strips, sems):
    _, levels, rows, cols = tend.shape
    inside = pl.ds(1, levels - 2)
    copies = [
        pltpu.make_async_copy(
            tend.at[field, inside, pl.ds(TILE, rows - 2 * TILE), :],
            out.at[inside, pl.ds(TILE, rows - 2 * TILE), :],
            sems.at[0],
        )
    ]
    copies[0].start()
    diffs = side_changes(far, near)
    tile_at = lax.broadcasted_iota(jnp.int32, (TILE, cols), 0)
    below, above = level_fluxes(outer, inner, pl.ds(field * rows, rows))
    for side, level, change in (
        (0, 0, table[0, pl.ds(RISE, 1), :] * below),
        (1, levels - 1, -table[levels - 1, pl.ds(FALL, 1), :] * above),
    ):
        at = field * levels + level
        rim = ends(rows, cols, diffs[0][at : at + 1, :], diffs[1][at : at + 1, :])
        layers[side] = tend[field, level] + change + rim
        copies.append(pltpu.make_async_copy(layers.at[side], out.at[level], sems.at[1 + side]))
        copies[-1].start()
    for side, begin, row in ((0, 0, 0), (1, rows - TILE, TILE - 1)):
        for level in range(1, levels - 1):
            at = field * levels + level
            strips[side, level] = tend[field, level, pl.ds(begin, TILE), :] + jnp.where(
                tile_at == row, diffs[side][at : at + 1, :], 0.0
            )
        copies.append(
            pltpu.make_async_copy(
                strips.at[side, inside], out.at[inside, pl.ds(begin, TILE), :], sems.at[3 + side]
            )
        )
        copies[-1].start()
    for copy in copies:
        copy.wait()


def tends(field, table, tend, far, near, outer, inner):
    _, levels, rows, cols = tend.shape
    return pl.pallas_call(
        functools.partial(tends_kernel, field),
        out_shape=jax.ShapeDtypeStruct((levels, rows, cols), F32),
        in_specs=[whole(VMEM)] * 6,
        out_specs=whole(pl.ANY),
        scratch_shapes=[
            pltpu.VMEM((2, rows, cols), F32),
            pltpu.VMEM((2, levels, TILE, cols), F32),
            pltpu.SemaphoreType.DMA((5,)),
        ],
        compiler_params=pltpu.CompilerParams(vmem_limit_bytes=8 * MIB),
        cost_estimate=pl.CostEstimate(
            flops=2000 * levels * rows * cols,
            bytes_accessed=4 * levels * rows * cols,
            transcendentals=0,
        ),
        name="tends",
    )(in_vmem(table), in_vmem(tend), far, near, outer, inner)


def interface(low, high):
    coupling = low[ABOVE]
    return coupling, 1.0 / (1.0 - coupling * coupling * low[LAST] * high[FIRST])


def scalar_rows(ref, begin):
    return [ref[pl.ds(begin + at, 1), :] for at in range(7)]


def merge_kernel(bit, final, beside, mine, theirs, *rest):
    base, gains, merged, *half = rest[beside:]
    _, rows, cols = base.shape
    upper = bit_of("gz", bit) == 1
    own, far = scalar_rows(mine, 4 * rows), scalar_rows(theirs, 4 * rows)
    low = [jnp.where(upper, b, a) for a, b in zip(own, far)]
    high = [jnp.where(upper, a, b) for a, b in zip(own, far)]
    coupling, inverse = interface(low, high)
    to_high, to_low = high[FIRST] * coupling, low[LAST] * coupling
    low_out, high_out = low[CORNER] * coupling, high[CORNER] * coupling
    core = bit_of("gz", 0) == 1
    sends_last = bit_of("gz", bit + 1) == 0
    for field in range(2):

        def part(at):
            a = mine[pl.ds((at + field) * rows, rows), :]
            b = theirs[pl.ds((at + field) * rows, rows), :]
            return jnp.where(upper, b, a), jnp.where(upper, a, b)

        (low_first, high_first), (low_last, high_last) = part(0), part(2)
        above = inverse * (high_first + to_high * low_last)
        below = inverse * (low_last + to_low * high_first)
        base[field] = coupling * jnp.where(upper, below, above)
        all_first = low_first + low_out * above
        all_last = high_last + high_out * below
        if final:
            entry = jnp.where(sends_last, all_last, all_first)
            merged[pl.ds(field * rows, rows), :] = entry
            size = rows // 2
            half[0][pl.ds(field * size, size), :] = jnp.where(core, entry[size:], entry[:size])
        else:
            merged[pl.ds(field * rows, rows), :] = all_first
            merged[pl.ds((2 + field) * rows, rows), :] = all_last
    scalars = [
        low[FIRST] + low_out * inverse * to_high * low[CORNER],
        low_out * inverse * high[CORNER],
        high[LAST] + high_out * inverse * to_low * high[CORNER],
        low[BELOW],
        high[ABOVE],
        low[METRIC_BELOW],
        high[METRIC_ABOVE],
        jnp.zeros((1, cols), F32),
    ]
    for at, value in enumerate(scalars):
        merged[pl.ds((2 if final else 4) * rows + at, 1), :] = value
        if final:
            half[0][pl.ds(rows + at, 1), :] = value
    scale = coupling * inverse
    gains[...] = jnp.zeros(gains.shape, F32)
    gains[pl.ds(FROM_ABOVE, 1), :] = scale * high[CORNER] * jnp.where(upper, to_low, 1.0)
    gains[pl.ds(FROM_BELOW, 1), :] = scale * low[CORNER] * jnp.where(upper, 1.0, to_high)


def merge(bit, final, rows, mine, theirs, *beside):
    cols = mine.shape[1]
    shapes = [held(2, rows, cols), held(TILE, cols), held((2 if final else 4) * rows + TILE, cols)]
    if final:
        shapes.append(held(rows + TILE, cols))
    return pl.pallas_call(
        functools.partial(merge_kernel, bit, final, len(beside)),
        out_shape=tuple(shapes),
        in_specs=[whole(VMEM)] * 2 + [whole(pl.ANY)] * len(beside),
        out_specs=[whole(VMEM)] * len(shapes),
        compiler_params=pltpu.CompilerParams(vmem_limit_bytes=8 * MIB),
        name="merge",
    )(mine, theirs, *in_hbm(*beside))


def prepare_kernel(
    rounds, temp, w_vel, forward, table, changes, scalars, outer, inner, *rest
):
    bases, gains = rest[: rounds - 1], rest[rounds - 1 : 2 * rounds - 2]
    known, response, below_in, above_in = rest[2 * rounds - 2 :]
    levels, rows, cols = temp.shape
    upper = bit_of("gz", rounds - 1) == 1
    one, none = jnp.ones((1, cols), F32), jnp.zeros((1, cols), F32)
    below_gain, above_gain = jnp.where(upper, one, none), jnp.where(upper, none, one)
    below = above = None
    for step in range(rounds - 2, -1, -1):
        side = bit_of("gz", step) == 1
        from_above = gains[step][pl.ds(FROM_ABOVE, 1), :]
        from_below = gains[step][pl.ds(FROM_BELOW, 1), :]
        gain = from_above * above_gain + from_below * below_gain
        below_gain = jnp.where(side, gain, below_gain)
        above_gain = jnp.where(side, above_gain, gain)
        into = [bases[step][field] for field in range(2)]
        if below is None:
            below = above = [jnp.zeros((rows, cols), F32)] * 2
        else:
            into = [
                into[field] + from_above * above[field] + from_below * below[field]
                for field in range(2)
            ]
        below = [jnp.where(side, into[field], below[field]) for field in range(2)]
        above = [jnp.where(side, above[field], into[field]) for field in range(2)]
    for field in range(2):
        flux_below, flux_above = level_fluxes(outer, inner, pl.ds(field * rows, rows))
        below_in[field] = below[field] + scalars[pl.ds(METRIC_BELOW, 1), :] * flux_below
        above_in[field] = above[field] - scalars[pl.ds(METRIC_ABOVE, 1), :] * flux_above

    gain = above_gain * table[levels - 1, pl.ds(PIVOT, 1), :]
    for level in range(levels - 1, -1, -1):
        if level < levels - 1:
            gain = gain * table[level, pl.ds(UPPER_PIVOT, 1), :]
        gain = gain + below_gain * table[level, pl.ds(BELOW_FORWARD, 1), :]
        response[level] = jnp.broadcast_to(gain, (TILE, cols))

    row_at = lax.broadcasted_iota(jnp.int32, (TILE, cols), 0)
    width = 2 * TILE
    for field, cells in enumerate((temp, w_vel)):
        for begin in range(0, rows, width):
            at = pl.ds(begin, width)
            below = below_in[field, at, :]

            def solve(level, carry, factor, field=field, begin=begin, at=at, below=below, cells=cells):
                value = (
                    forward[field, level + 1, at, :]
                    + table[level, pl.ds(BELOW_FORWARD, 1), :] * below
                    + factor * carry
                )
                if begin == 0:
                    change = changes[pl.ds(field * levels + level, 1), :]
                    head = value[:TILE] + jnp.where(row_at == 0, change, 0.0)
                    value = jnp.concatenate([head, value[TILE:]])
                if begin == rows - width:
                    change = changes[pl.ds((2 + field) * levels + level, 1), :]
                    tail = value[-TILE:] + jnp.where(row_at == TILE - 1, change, 0.0)
                    value = jnp.concatenate([value[:-TILE], tail])
                known[field, level, at, :] = value - cells[level, at, :]
                return value

            carry = solve(levels - 1, above_in[field, at, :], table[levels - 1, pl.ds(PIVOT, 1), :])

            def step(back, carry, solve=solve):
                level = levels - 2 - back
                return solve(level, carry, table[level, pl.ds(UPPER_PIVOT, 1), :])

            lax.fori_loop(0, levels - 1, step, carry)


def prepare(rounds, temp, w_vel, forward, table, changes, scalars, outer, inner, bases, gains):
    levels, rows, cols = temp.shape
    return pl.pallas_call(
        functools.partial(prepare_kernel, rounds),
        out_shape=(held(2, levels, rows, cols), held(levels, TILE, cols)),
        in_specs=[whole(VMEM)] * (8 + 2 * (rounds - 1)),
        out_specs=[whole(VMEM)] * 2,
        scratch_shapes=[pltpu.VMEM((2, rows, cols), F32)] * 2,
        compiler_params=pltpu.CompilerParams(vmem_limit_bytes=8 * MIB),
        cost_estimate=pl.CostEstimate(
            flops=2000 * levels * rows * cols,
            bytes_accessed=24 * levels * rows * cols,
            transcendentals=0,
        ),
        name="prepare",
    )(
        in_vmem(temp), in_vmem(w_vel), in_vmem(forward), in_vmem(table), changes, scalars,
        outer, inner, *bases, *gains,
    )


def finish_kernel(rounds, swapped, known, response, mine, theirs, *rest):
    temp_next, w_next, result, sems = rest[2 if swapped else 0 :]
    _, levels, rows, cols = known.shape
    upper = bit_of("gz", rounds - 1) == 1
    own, far = scalar_rows(mine, 2 * rows), scalar_rows(theirs, rows)
    low = [jnp.where(upper, b, a) for a, b in zip(own, far)]
    high = [jnp.where(upper, a, b) for a, b in zip(own, far)]
    coupling, inverse = interface(low, high)
    scale = coupling * inverse
    to_other = scale * coupling * jnp.where(upper, low[LAST], high[FIRST])
    width, half = 2 * TILE, rows // 2
    core = bit_of("gz", 0)
    start = pl.multiple_of((1 - core if swapped else core) * half, half)
    copies = []
    for field, out in enumerate((temp_next, w_next)):
        for begin in range(0, half, width):
            here = pl.ds(field * rows + start + begin, width)
            into = scale * theirs[pl.ds(field * half + begin, width), :] + to_other * mine[here, :]
            tiles = [into[i : i + TILE] for i in range(0, width, TILE)]

            def step(level, carry, field=field, begin=begin, tiles=tiles):
                gain = response[level]
                for i, tile in enumerate(tiles):
                    at = begin + i * TILE
                    value = known[field, level, pl.ds(start + at, TILE), :] + gain * tile
                    result[field, level, pl.ds(at, TILE), :] = value
                return carry

            lax.fori_loop(0, levels, step, 0, unroll=4)
        copies.append(
            pltpu.make_async_copy(
                result.at[field], out.at[:, pl.ds(start, half), :], sems.at[field]
            )
        )
        copies[-1].start()
    for copy in copies:
        copy.wait()


def finish(rounds, known, response, mine, theirs, written=()):
    _, levels, rows, cols = known.shape
    return pl.pallas_call(
        functools.partial(finish_kernel, rounds, bool(written)),
        out_shape=(jax.ShapeDtypeStruct((levels, rows, cols), F32),) * 2,
        in_specs=[whole(VMEM)] * 4 + [whole(pl.ANY)] * len(written),
        out_specs=[whole(pl.ANY)] * 2,
        scratch_shapes=[
            pltpu.VMEM((2, levels, rows // 2, cols), F32),
            pltpu.SemaphoreType.DMA((2,)),
        ],
        input_output_aliases={4: 0, 5: 1} if written else {},
        compiler_params=pltpu.CompilerParams(vmem_limit_bytes=8 * MIB),
        cost_estimate=pl.CostEstimate(
            flops=20000 * levels * rows * cols,
            bytes_accessed=8 * levels * rows * cols,
            transcendentals=0,
        ),
        name="finish",
    )(in_vmem(known), response, mine, theirs, *written)


def both_ways(pairs):
    return pairs + [(b, a) for a, b in pairs]


def local(temp, u_vel, v_vel, w_vel, temp_prev, w_prev, lower, upper, metric):
    rows = temp.shape[1]
    across, stacked = lax.axis_size("gx"), lax.axis_size("gz")
    rounds = stacked.bit_length() - 1
    cores = both_ways([(i, i + 1) for i in range(0, stacked, 2)])
    seams = both_ways([(i, i + 1) for i in range(1, stacked - 1, 2)])
    seams = seams + [(i, i) for i in (0, stacked - 1)]
    far, near, outer, inner, table, scalars = edges(
        temp, u_vel, w_vel, v_vel, temp_prev, w_prev, lower, upper, metric
    )
    far = lax.ppermute(far, "gx", both_ways([(i, (i + 1) % across) for i in range(1, across, 2)]))
    near = lax.ppermute(near, "gx", both_ways([(i, i + 1) for i in range(0, across, 2)]))
    outer = lax.ppermute(outer, "gz", seams)
    inner = lax.ppermute(inner, "gz", cores)
    forward, tend, first = bulk(table, temp, u_vel, v_vel, w_vel, temp_prev, w_prev)
    mine, changes = fix(far, near, outer, inner, forward, first, table, scalars)
    temp_tend = tends(0, table, tend, far, near, outer, inner)
    bases, gains = [], []
    for step in range(rounds - 1):
        theirs = lax.ppermute(mine, "gz", [(i, i ^ (1 << step)) for i in range(stacked)])
        base, gain, mine, *half = merge(step, step + 2 == rounds, rows, mine, theirs, temp_tend)
        bases.append(base)
        gains.append(gain)
    (half,) = half
    theirs = lax.ppermute(half, "gz", [(i, i ^ (stacked // 2)) for i in range(stacked)])
    swapped = lax.ppermute(theirs, "gz", cores)
    w_tend = tends(1, table, tend, far, near, outer, inner)
    known, response = prepare(
        rounds, temp, w_vel, forward, table, changes, scalars, outer, inner, bases, gains
    )
    written = finish(rounds, known, response, mine, theirs)
    temp_next, w_next = finish(rounds, known, response, mine, swapped, written)
    return temp_next, w_next, temp_tend, w_tend


def solution(mesh):
    field = P("gz", "gx", None)
    return jax.shard_map(
        local,
        mesh=mesh,
        in_specs=(field,) * 6 + (P("gz"),) * 3,
        out_specs=(field,) * 4,
        check_vma=False,
    )
```

```python
import functools

import jax
import jax.numpy as jnp
from jax import lax
from jax.experimental import pallas as pl
from jax.experimental.pallas import tpu as pltpu
from jax.sharding import PartitionSpec as P

NEW_WEIGHT = 5.0 / 12.0
HORIZ_DIFF = 0.1
FIELD_WEIGHT = 2.0 / NEW_WEIGHT
PREV_WEIGHT = (17.0 / 60.0) / NEW_WEIGHT
TILE = 8
MIB = 1024 * 1024

PIVOT_NEW, LOWER_PIVOT, UPPER_PIVOT, FIRST_GREEN, BELOW_FORWARD, PIVOT, RISE, FALL = range(8)
FIRST, CORNER, LAST, BELOW, ABOVE, METRIC_BELOW, METRIC_ABOVE = range(7)
FROM_ABOVE, FROM_BELOW = range(2)

VMEM = pltpu.VMEM
F32 = jnp.float32


def whole(space):
    return pl.BlockSpec(memory_space=space)


def held(*shape):
    return pltpu.VMEM(shape, F32)


def in_vmem(array):
    return pltpu.with_memory_space_constraint(array, pltpu.VMEM)


def in_hbm(*arrays):
    return [pltpu.with_memory_space_constraint(array, pltpu.HBM) for array in arrays]


def bit_of(axis, bit):
    return (lax.axis_index(axis) >> bit) & 1


def edges_kernel(
    temp,
    u_vel,
    w_vel,
    v_vel,
    temp_prev,
    w_prev,
    lower,
    upper,
    metric,
    near,
    far,
    fluxes,
    table,
    strips,
    layers,
    lower_at,
    upper_at,
    metric_at,
    sems,
):
    levels, rows, cols = temp.shape
    copies = [(lower, lower_at), (upper, upper_at), (metric, metric_at)]
    for at, array in enumerate((temp, w_vel, u_vel)):
        for side, first in enumerate((0, rows - TILE)):
            copies.append((array.at[:, pl.ds(first, TILE), :], strips.at[at, side]))
    for at, array in enumerate((temp, w_vel)):
        for side, level in enumerate((0, levels - 1)):
            copies.append((array.at[level], layers.at[at, side]))
    copies = [pltpu.make_async_copy(src, dst, sems.at[i]) for i, (src, dst) in enumerate(copies)]
    for copy in copies:
        copy.start()
    for copy in copies[:3]:
        copy.wait()
    coefficients(lower_at, upper_at, metric_at, table, fluxes.at[pl.ds(4 * rows, TILE)])
    for copy in copies[3:]:
        copy.wait()
    odd = bit_of("gx", 0) == 1
    last = TILE - 1
    for field in range(2):
        at = pl.ds(field * levels, levels)
        to_left = (HORIZ_DIFF - 0.5 * strips[2, 0, :, 0, :]) * strips[field, 0, :, 0, :]
        to_right = (HORIZ_DIFF + 0.5 * strips[2, 1, :, last, :]) * strips[field, 1, :, last, :]
        near[at, :] = jnp.where(odd, to_left, to_right)
        far[at, :] = jnp.where(odd, to_right, to_left)
    position = lax.axis_index("gz")
    upper_core = bit_of("gz", 0) == 1
    wall = (position == 0) | (position == lax.axis_size("gz") - 1)
    zero = jnp.zeros((rows, cols), F32)
    for field in range(2):
        bottom = layers[1, 0] * layers[field, 0]
        top = layers[1, 1] * layers[field, 1]
        fluxes[pl.ds(field * rows, rows), :] = jnp.where(upper_core, bottom, top)
        outward = jnp.where(wall, zero, jnp.where(upper_core, top, bottom))
        fluxes[pl.ds((2 + field) * rows, rows), :] = outward


def edges(temp, u_vel, w_vel, v_vel, temp_prev, w_prev, lower, upper, metric):
    levels, rows, cols = temp.shape
    return pl.pallas_call(
        edges_kernel,
        out_shape=(
            held(2 * levels, cols),
            held(2 * levels, cols),
            held(4 * rows + TILE, cols),
            held(levels, TILE, cols),
        ),
        in_specs=[whole(pl.ANY)] * 9,
        out_specs=[whole(VMEM)] * 4,
        scratch_shapes=[
            pltpu.VMEM((3, 2, levels, TILE, cols), F32),
            pltpu.VMEM((2, 2, rows, cols), F32),
            pltpu.SMEM((levels,), F32),
            pltpu.SMEM((levels,), F32),
            pltpu.SMEM((levels,), F32),
            pltpu.SemaphoreType.DMA((13,)),
        ],
        compiler_params=pltpu.CompilerParams(vmem_limit_bytes=8 * MIB),
        name="edges",
    )(*in_hbm(temp, u_vel, w_vel, v_vel, temp_prev, w_prev, lower, upper, metric))


def coefficients(lower, upper, metric, table, scalars):
    levels, _, cols = table.shape

    def row(value):
        return jnp.full((1, cols), value, F32)

    ratio = jnp.zeros((1, cols), F32)
    forward = jnp.ones((1, cols), F32)
    for level in range(levels):
        low, high = row(lower[level]), row(upper[level])
        pivot = 1.0 / (1.0 + low + high - low * ratio)
        ratio = high * pivot
        lower_pivot = low * pivot
        forward = pivot if level == 0 else lower_pivot * forward
        table[level, pl.ds(PIVOT_NEW, 1), :] = NEW_WEIGHT * pivot
        table[level, pl.ds(LOWER_PIVOT, 1), :] = lower_pivot
        table[level, pl.ds(UPPER_PIVOT, 1), :] = ratio
        table[level, pl.ds(BELOW_FORWARD, 1), :] = forward
        table[level, pl.ds(PIVOT, 1), :] = pivot
        table[level, pl.ds(RISE, 1), :] = row(metric[level] if level < levels - 1 else 0.0)
        table[level, pl.ds(FALL, 1), :] = row(metric[level] if level > 0 else 0.0)
    green = forward
    table[levels - 1, pl.ds(FIRST_GREEN, 1), :] = NEW_WEIGHT * green
    for level in range(levels - 2, -1, -1):
        green = (
            table[level, pl.ds(BELOW_FORWARD, 1), :]
            + table[level, pl.ds(UPPER_PIVOT, 1), :] * green
        )
        table[level, pl.ds(FIRST_GREEN, 1), :] = NEW_WEIGHT * green
    scalars[pl.ds(FIRST, 1), :] = green
    scalars[pl.ds(CORNER, 1), :] = forward
    scalars[pl.ds(LAST, 1), :] = pivot
    scalars[pl.ds(BELOW, 1), :] = row(lower[0])
    scalars[pl.ds(ABOVE, 1), :] = row(upper[levels - 1])
    scalars[pl.ds(METRIC_BELOW, 1), :] = row(NEW_WEIGHT * metric[0])
    scalars[pl.ds(METRIC_ABOVE, 1), :] = row(NEW_WEIGHT * metric[levels - 1])
    scalars[pl.ds(7, 1), :] = row(0.0)


def bulk_kernel(
    table,
    temp,
    u_vel,
    v_vel,
    w_vel,
    temp_prev,
    w_prev,
    forward,
    tend,
    first,
):
    levels, rows, cols = temp.shape
    strips = rows // TILE
    fields, prevs = (temp, w_vel), (temp_prev, w_prev)
    for field in range(2):
        forward[field, 0] = jnp.zeros((rows, cols), F32)
        first[field] = jnp.zeros((rows, cols), F32)
    row_at = lax.broadcasted_iota(jnp.int32, (TILE, cols), 0)
    zero = jnp.zeros((TILE, cols), F32)

    def level_step(level, carry):
        def spread(at):
            return jnp.broadcast_to(table[level, pl.ds(at, 1), :], (TILE, cols))

        pivot, lower_pivot, green = spread(PIVOT_NEW), spread(LOWER_PIVOT), spread(FIRST_GREEN)
        rise, fall = spread(RISE), spread(FALL)
        over = jnp.minimum(level + 1, levels - 1)
        under = jnp.maximum(level - 1, 0)

        def sides(strip):
            at = pl.ds(strip * TILE, TILE)
            half = 0.5 * u_vel[level, at, :]
            back, ahead = HORIZ_DIFF - half, HORIZ_DIFF + half
            here = [values[level, at, :] for values in fields]
            return (
                here,
                [pltpu.roll(back * value, TILE - 1, 0) for value in here],
                [pltpu.roll(ahead * value, 1, 0) for value in here],
            )

        before = [zero, zero]
        here, back, ahead = sides(0)
        for strip in range(strips):
            after = sides(strip + 1) if strip + 1 < strips else (None, [zero, zero], None)
            at = pl.ds(strip * TILE, TILE)
            half = 0.5 * v_vel[level, at, :]
            v_back, v_ahead = HORIZ_DIFF - half, HORIZ_DIFF + half
            w_over = rise * w_vel[over, at, :]
            w_under = fall * w_vel[under, at, :]
            for field in range(2):
                value = here[field]
                change = jnp.where(row_at == TILE - 1, after[1][field], back[field])
                change = change + jnp.where(row_at == 0, before[field], ahead[field])
                change = change + pltpu.roll(v_back * value, cols - 1, 1)
                change = change + pltpu.roll(v_ahead * value, 1, 1)
                change = change - w_over * fields[field][over, at, :]
                change = change + w_under * fields[field][under, at, :]
                change = change + (here[1 - field] - (4.0 * HORIZ_DIFF) * value)
                tend[field, level, at, :] = change
                right = change + (FIELD_WEIGHT * value - PREV_WEIGHT * prevs[field][level, at, :])
                forward[field, level + 1, at, :] = (
                    pivot * right + lower_pivot * forward[field, level, at, :]
                )
                first[field, at, :] = first[field, at, :] + green * right
            before = ahead
            here, back, ahead = after
        return carry

    lax.fori_loop(0, levels, level_step, 0)


def bulk(table, *arrays):
    levels, rows, cols = arrays[0].shape
    return pl.pallas_call(
        bulk_kernel,
        out_shape=(
            held(2, levels + 1, rows, cols),
            held(2, levels, rows, cols),
            held(2, rows, cols),
        ),
        in_specs=[whole(VMEM)] * 7,
        out_specs=[whole(VMEM)] * 3,
        compiler_params=pltpu.CompilerParams(vmem_limit_bytes=8 * MIB),
        cost_estimate=pl.CostEstimate(
            flops=100000 * levels * rows * cols,
            bytes_accessed=24 * levels * rows * cols,
            transcendentals=0,
        ),
        name="bulk",
    )(*map(in_vmem, (table, *arrays)))


def side_changes(near, far):
    odd = bit_of("gx", 0) == 1
    return jnp.where(odd, near[...], far[...]), jnp.where(odd, far[...], near[...])


def level_fluxes(inner, outer):
    upper = bit_of("gz", 0) == 1
    return jnp.where(upper, inner, outer), jnp.where(upper, outer, inner)


def beside_seam(rounds):
    return bit_of("gz", 0) != bit_of("gz", rounds - 1)


def ends(rows, cols, head, tail):
    at = lax.broadcasted_iota(jnp.int32, (rows, cols), 0)
    return jnp.where(at == 0, head, jnp.where(at == rows - 1, tail, 0.0))


def scalar_rows(ref, begin=0):
    return [ref[pl.ds(begin + at, 1), :] for at in range(7)]


def in_order(upper, own, other):
    low = [jnp.where(upper, b, a) for a, b in zip(own, other)]
    high = [jnp.where(upper, a, b) for a, b in zip(own, other)]
    return low, high


def interface(low, high):
    coupling = low[ABOVE]
    return coupling, 1.0 / (1.0 - coupling * coupling * low[LAST] * high[FIRST])


def joint_scalars(low, high):
    coupling, inverse = interface(low, high)
    low_out, high_out = low[CORNER] * coupling, high[CORNER] * coupling
    return [
        low[FIRST] + low_out * low_out * inverse * high[FIRST],
        low_out * inverse * high[CORNER],
        high[LAST] + high_out * high_out * inverse * low[LAST],
        low[BELOW],
        high[ABOVE],
        low[METRIC_BELOW],
        high[METRIC_ABOVE],
        jnp.zeros_like(coupling),
    ]


def fix_kernel(rounds, levels, near, far, fluxes, other, forward, first, table, *rest):
    outer, rest = (rest[0], rest[1:]) if rounds > 2 else (None, rest)
    message, changes, *late = rest
    _, rows, cols = first.shape
    diffs = side_changes(near, far)
    scalars = scalar_rows(fluxes, 4 * rows)
    below, above = scalars[METRIC_BELOW], -scalars[METRIC_ABOVE]
    for field in range(2):
        firsts, lasts = [], []
        for side in range(2):
            value = jnp.zeros((1, cols), F32)
            total = jnp.zeros((1, cols), F32)
            for level in range(levels):
                right = diffs[side][field * levels + level : field * levels + level + 1, :]
                value = (
                    table[level, pl.ds(PIVOT_NEW, 1), :] * right
                    + table[level, pl.ds(LOWER_PIVOT, 1), :] * value
                )
                total = total + table[level, pl.ds(FIRST_GREEN, 1), :] * right
                changes[pl.ds((side * 2 + field) * levels + level, 1), :] = value
            firsts.append(total)
            lasts.append(value)
        at = pl.ds(field * rows, rows)
        flux_below, flux_above = level_fluxes(other[at, :], 0.0 if outer is None else outer[at, :])
        message[at, :] = (
            first[field]
            + (below * scalars[FIRST]) * flux_below
            + (above * scalars[CORNER]) * flux_above
            + ends(rows, cols, *firsts)
        )
        message[pl.ds((2 + field) * rows, rows), :] = (
            forward[field, levels]
            + (below * scalars[CORNER]) * flux_below
            + (above * scalars[LAST]) * flux_above
            + ends(rows, cols, *lasts)
        )
    if not late:
        return
    seam, half = late
    core, size = bit_of("gz", 0) == 1, rows // 2
    for field in range(2):
        outward = pl.ds((2 + field) * rows, rows)
        value = jnp.where(beside_seam(rounds), fluxes[outward, :], other[outward, :])
        seam[pl.ds(field * rows, rows), :] = value
        half[pl.ds(field * size, size), :] = jnp.where(core, value[size:], value[:size])
    for at, value in enumerate(
        joint_scalars(*in_order(core, scalars, scalar_rows(other, 4 * rows)))
    ):
        half[pl.ds(rows + at, 1), :] = value


def fix(rounds, near, far, fluxes, other, forward, first, table, outer):
    levels = table.shape[0]
    _, rows, cols = first.shape
    shapes = [held(4 * rows, cols), held(4 * levels, cols)]
    if rounds == 2:
        shapes += [held(2 * rows, cols), held(rows + TILE, cols)]
    return pl.pallas_call(
        functools.partial(fix_kernel, rounds, levels),
        out_shape=tuple(shapes),
        in_specs=[whole(VMEM)] * (7 + len(outer)),
        out_specs=[whole(VMEM)] * len(shapes),
        compiler_params=pltpu.CompilerParams(vmem_limit_bytes=8 * MIB),
        name="fix",
    )(near, far, fluxes, other, in_vmem(forward), in_vmem(first), in_vmem(table), *outer)


def tends_kernel(rounds, field, table, tend, near, far, other, *rest):
    *outer, out, layers, strips, sems = rest
    _, levels, rows, cols = tend.shape
    inside = pl.ds(1, levels - 2)
    copies = [
        pltpu.make_async_copy(
            tend.at[field, inside, pl.ds(TILE, rows - 2 * TILE), :],
            out.at[inside, pl.ds(TILE, rows - 2 * TILE), :],
            sems.at[0],
        )
    ]
    copies[0].start()
    diffs = side_changes(near, far)
    tile_at = lax.broadcasted_iota(jnp.int32, (TILE, cols), 0)
    at = pl.ds(field * rows, rows)
    below, above = level_fluxes(other[at, :], outer[0][at, :] if outer else 0.0)
    for side, level, change in (
        (0, 0, table[0, pl.ds(RISE, 1), :] * below),
        (1, levels - 1, -table[levels - 1, pl.ds(FALL, 1), :] * above),
    ):
        at = field * levels + level
        rim = ends(rows, cols, diffs[0][at : at + 1, :], diffs[1][at : at + 1, :])
        layers[side] = tend[field, level] + change + rim
        copies.append(pltpu.make_async_copy(layers.at[side], out.at[level], sems.at[1 + side]))
        copies[-1].start()
    for side, begin, row in ((0, 0, 0), (1, rows - TILE, TILE - 1)):
        for level in range(1, levels - 1):
            at = field * levels + level
            strips[side, level] = tend[field, level, pl.ds(begin, TILE), :] + jnp.where(
                tile_at == row, diffs[side][at : at + 1, :], 0.0
            )
        copies.append(
            pltpu.make_async_copy(
                strips.at[side, inside], out.at[inside, pl.ds(begin, TILE), :], sems.at[3 + side]
            )
        )
        copies[-1].start()
    for copy in copies:
        copy.wait()


def tends(rounds, field, table, tend, near, far, other, outer):
    _, levels, rows, cols = tend.shape
    return pl.pallas_call(
        functools.partial(tends_kernel, rounds, field),
        out_shape=jax.ShapeDtypeStruct((levels, rows, cols), F32),
        in_specs=[whole(VMEM)] * (5 + len(outer)),
        out_specs=whole(pl.ANY),
        scratch_shapes=[
            pltpu.VMEM((2, rows, cols), F32),
            pltpu.VMEM((2, levels, TILE, cols), F32),
            pltpu.SemaphoreType.DMA((5,)),
        ],
        compiler_params=pltpu.CompilerParams(vmem_limit_bytes=8 * MIB),
        cost_estimate=pl.CostEstimate(
            flops=levels * rows * cols,
            bytes_accessed=4 * levels * rows * cols,
            transcendentals=0,
        ),
        name="tends",
    )(in_vmem(table), in_vmem(tend), near, far, other, *outer)


def merge_kernel(bit, final, own_at, other_at, mine, theirs, own, other, base, gains, scalars, merged, *half):
    _, rows, cols = base.shape
    upper = bit_of("gz", bit) == 1
    low, high = in_order(upper, scalar_rows(own, own_at), scalar_rows(other, other_at))
    coupling, inverse = interface(low, high)
    to_high, to_low = high[FIRST] * coupling, low[LAST] * coupling
    low_out, high_out = low[CORNER] * coupling, high[CORNER] * coupling
    core = bit_of("gz", 0) == 1
    sends_last = bit_of("gz", bit + 1) == 0
    for field in range(2):

        def part(at):
            a = mine[pl.ds((at + field) * rows, rows), :]
            b = theirs[pl.ds((at + field) * rows, rows), :]
            return jnp.where(upper, b, a), jnp.where(upper, a, b)

        (low_first, high_first), (low_last, high_last) = part(0), part(2)
        above = inverse * (high_first + to_high * low_last)
        below = inverse * (low_last + to_low * high_first)
        base[field] = coupling * jnp.where(upper, below, above)
        all_first = low_first + low_out * above
        all_last = high_last + high_out * below
        if final:
            entry = jnp.where(sends_last, all_last, all_first)
            merged[pl.ds(field * rows, rows), :] = entry
            size = rows // 2
            half[0][pl.ds(field * size, size), :] = jnp.where(core, entry[size:], entry[:size])
        else:
            merged[pl.ds(field * rows, rows), :] = all_first
            merged[pl.ds((2 + field) * rows, rows), :] = all_last
    for at, value in enumerate(joint_scalars(low, high)):
        scalars[pl.ds(at, 1), :] = value
    scale = coupling * inverse
    gains[...] = jnp.zeros(gains.shape, F32)
    gains[pl.ds(FROM_ABOVE, 1), :] = scale * high[CORNER] * jnp.where(upper, to_low, 1.0)
    gains[pl.ds(FROM_BELOW, 1), :] = scale * low[CORNER] * jnp.where(upper, 1.0, to_high)


def merge(bit, final, rows, mine, theirs, own, other):
    cols = mine.shape[1]
    return pl.pallas_call(
        functools.partial(
            merge_kernel, bit, final, own.shape[0] - TILE, other.shape[0] - TILE
        ),
        out_shape=(
            held(2, rows, cols),
            held(TILE, cols),
            held(TILE, cols),
            held((2 if final else 4) * rows, cols),
        )
        + (held(rows, cols),) * final,
        in_specs=[whole(VMEM)] * 4,
        out_specs=[whole(VMEM)] * (4 + final),
        compiler_params=pltpu.CompilerParams(vmem_limit_bytes=8 * MIB),
        name="merge",
    )(mine, theirs, own, other)


def prepare_kernel(
    rounds, temp, w_vel, forward, table, changes, fluxes, other, *rest
):
    outer, rest = (rest[0], rest[1:]) if rounds > 2 else (None, rest)
    bases, gains = rest[: rounds - 1], rest[rounds - 1 : 2 * rounds - 2]
    known, response, below_in, above_in = rest[2 * rounds - 2 :]
    levels, rows, cols = temp.shape
    upper = bit_of("gz", rounds - 1) == 1
    one, none = jnp.ones((1, cols), F32), jnp.zeros((1, cols), F32)
    below_gain, above_gain = jnp.where(upper, one, none), jnp.where(upper, none, one)
    below = above = None
    for step in range(rounds - 2, -1, -1):
        side = bit_of("gz", step) == 1
        from_above = gains[step][pl.ds(FROM_ABOVE, 1), :]
        from_below = gains[step][pl.ds(FROM_BELOW, 1), :]
        gain = from_above * above_gain + from_below * below_gain
        below_gain = jnp.where(side, gain, below_gain)
        above_gain = jnp.where(side, above_gain, gain)
        into = [bases[step][field] for field in range(2)]
        if below is None:
            below = above = [jnp.zeros((rows, cols), F32)] * 2
        else:
            into = [
                into[field] + from_above * above[field] + from_below * below[field]
                for field in range(2)
            ]
        below = [jnp.where(side, into[field], below[field]) for field in range(2)]
        above = [jnp.where(side, above[field], into[field]) for field in range(2)]
    scalars = scalar_rows(fluxes, 4 * rows)
    for field in range(2):
        at = pl.ds(field * rows, rows)
        flux_below, flux_above = level_fluxes(other[at, :], 0.0 if outer is None else outer[at, :])
        below_in[field] = below[field] + scalars[METRIC_BELOW] * flux_below
        above_in[field] = above[field] - scalars[METRIC_ABOVE] * flux_above

    gain = above_gain * table[levels - 1, pl.ds(PIVOT, 1), :]
    for level in range(levels - 1, -1, -1):
        if level < levels - 1:
            gain = gain * table[level, pl.ds(UPPER_PIVOT, 1), :]
        gain = gain + below_gain * table[level, pl.ds(BELOW_FORWARD, 1), :]
        response[level] = jnp.broadcast_to(gain, (TILE, cols))

    row_at = lax.broadcasted_iota(jnp.int32, (TILE, cols), 0)
    width = 2 * TILE
    for field, cells in enumerate((temp, w_vel)):
        for begin in range(0, rows, width):
            at = pl.ds(begin, width)
            below = below_in[field, at, :]

            def solve(level, carry, factor, field=field, begin=begin, at=at, below=below, cells=cells):
                value = (
                    forward[field, level + 1, at, :]
                    + table[level, pl.ds(BELOW_FORWARD, 1), :] * below
                    + factor * carry
                )
                if begin == 0:
                    change = changes[pl.ds(field * levels + level, 1), :]
                    head = value[:TILE] + jnp.where(row_at == 0, change, 0.0)
                    value = jnp.concatenate([head, value[TILE:]])
                if begin == rows - width:
                    change = changes[pl.ds((2 + field) * levels + level, 1), :]
                    tail = value[-TILE:] + jnp.where(row_at == TILE - 1, change, 0.0)
                    value = jnp.concatenate([value[:-TILE], tail])
                known[field, level, at, :] = value - cells[level, at, :]
                return value

            carry = solve(levels - 1, above_in[field, at, :], table[levels - 1, pl.ds(PIVOT, 1), :])

            def step(back, carry, solve=solve):
                level = levels - 2 - back
                return solve(level, carry, table[level, pl.ds(UPPER_PIVOT, 1), :])

            lax.fori_loop(0, levels - 1, step, carry)


def prepare(rounds, temp, w_vel, forward, table, changes, fluxes, other, outer, bases, gains):
    levels, rows, cols = temp.shape
    return pl.pallas_call(
        functools.partial(prepare_kernel, rounds),
        out_shape=(held(2, levels, rows, cols), held(levels, TILE, cols)),
        in_specs=[whole(VMEM)] * (7 + len(outer) + 2 * (rounds - 1)),
        out_specs=[whole(VMEM)] * 2,
        scratch_shapes=[pltpu.VMEM((2, rows, cols), F32)] * 2,
        compiler_params=pltpu.CompilerParams(vmem_limit_bytes=8 * MIB),
        cost_estimate=pl.CostEstimate(
            flops=levels * rows * cols,
            bytes_accessed=24 * levels * rows * cols,
            transcendentals=0,
        ),
        name="prepare",
    )(
        in_vmem(temp), in_vmem(w_vel), in_vmem(forward), in_vmem(table), changes, fluxes, other,
        *outer, *bases, *gains,
    )


def join_kernel(rounds, own_at, other_at, mine, theirs, own, other, *rest):
    *seam, joined = rest
    size = theirs.shape[0] // 2
    rows = 2 * size
    upper = bit_of("gz", rounds - 1) == 1
    low, high = in_order(upper, scalar_rows(own, own_at), scalar_rows(other, other_at))
    coupling, inverse = interface(low, high)
    scale = coupling * inverse
    to_other = scale * coupling * jnp.where(upper, low[LAST], high[FIRST])
    up, down = high[METRIC_BELOW] * inverse, -low[METRIC_ABOVE] * inverse
    own_gain = coupling * jnp.where(upper, down * low[LAST], up * high[FIRST])
    other_gain = jnp.where(upper, up, down)
    start = pl.multiple_of(bit_of("gz", 0) * size, size)
    for field in range(2):
        here, there = pl.ds(field * rows + start, size), pl.ds(field * size, size)
        into = scale * theirs[there, :] + to_other * mine[here, :]
        if seam:
            flux = other[there, :]
            into = into + (own_gain * seam[0][here, :] + other_gain * flux)
            joined[pl.ds((2 + field) * size, size), :] = flux
        joined[there, :] = into


def join(rounds, mine, theirs, own, other, seam):
    size, cols = theirs.shape
    return pl.pallas_call(
        functools.partial(join_kernel, rounds, own.shape[0] - TILE, other.shape[0] - TILE),
        out_shape=held(size * (1 + len(seam)), cols),
        in_specs=[whole(VMEM)] * (4 + len(seam)),
        out_specs=whole(VMEM),
        compiler_params=pltpu.CompilerParams(vmem_limit_bytes=8 * MIB),
        name="join",
    )(mine, theirs, own, other, *seam)


def finish_kernel(rounds, swapped, known, response, joined, *rest):
    late, results = rounds == 2, 4 if rounds == 2 else 2
    table, tend, near, far = rest[:4] if late else (None,) * 4
    rest = rest[(4 if late else 0) + (results if swapped else results - 2) :]
    outs, (result, rim, sems) = rest[:results], rest[results:]
    _, levels, rows, cols = known.shape
    width, half = 2 * TILE, rows // 2
    core = bit_of("gz", 0)
    start = pl.multiple_of((1 - core if swapped else core) * half, half)
    copies = []
    for field in range(2):
        for begin in range(0, half, width):
            into = joined[pl.ds(field * half + begin, width), :]
            tiles = [into[i : i + TILE] for i in range(0, width, TILE)]

            def step(level, carry, field=field, begin=begin, tiles=tiles):
                gain = response[level]
                for i, tile in enumerate(tiles):
                    at = begin + i * TILE
                    value = known[field, level, pl.ds(start + at, TILE), :] + gain * tile
                    result[field, level, pl.ds(at, TILE), :] = value
                return carry

            lax.fori_loop(0, levels, step, 0, unroll=4)
        copies.append(
            pltpu.make_async_copy(
                result.at[field], outs[field].at[:, pl.ds(start, half), :], sems.at[field]
            )
        )
        copies[-1].start()
    if late:
        diffs = side_changes(near, far)
        level = core * (levels - 1)
        gain = jnp.where(
            core == 1, -table[levels - 1, pl.ds(FALL, 1), :], table[0, pl.ds(RISE, 1), :]
        )
        gain = jnp.where(beside_seam(rounds), gain, 0.0)
        row_at = start + lax.broadcasted_iota(jnp.int32, (half, cols), 0)
        for field in range(2):
            head, tail = (
                jnp.where(
                    core == 1,
                    diff[(field + 1) * levels - 1 : (field + 1) * levels, :],
                    diff[field * levels : field * levels + 1, :],
                )
                for diff in diffs
            )
            edge = jnp.where(row_at == 0, head, jnp.where(row_at == rows - 1, tail, 0.0))
            flux = joined[pl.ds((2 + field) * half, half), :]
            rim[field] = tend[field, level, pl.ds(start, half), :] + gain * flux + edge
            copies.append(
                pltpu.make_async_copy(
                    rim.at[field],
                    outs[2 + field].at[level, pl.ds(start, half), :],
                    sems.at[2 + field],
                )
            )
            copies[-1].start()
    for copy in copies:
        copy.wait()


def finish(rounds, known, response, joined, late, written):
    _, levels, rows, cols = known.shape
    results = 4 if rounds == 2 else 2
    inputs = 3 + len(late)
    swapped = len(written) == results
    return pl.pallas_call(
        functools.partial(finish_kernel, rounds, swapped),
        out_shape=(jax.ShapeDtypeStruct((levels, rows, cols), F32),) * results,
        in_specs=[whole(VMEM)] * inputs + [whole(pl.ANY)] * len(written),
        out_specs=[whole(pl.ANY)] * results,
        scratch_shapes=[
            pltpu.VMEM((2, levels, rows // 2, cols), F32),
            pltpu.VMEM((2, rows // 2, cols), F32),
            pltpu.SemaphoreType.DMA((4,)),
        ],
        input_output_aliases={
            inputs + i: results - len(written) + i for i in range(len(written))
        },
        compiler_params=pltpu.CompilerParams(vmem_limit_bytes=8 * MIB),
        cost_estimate=pl.CostEstimate(
            flops=20000 * levels * rows * cols,
            bytes_accessed=8 * levels * rows * cols,
            transcendentals=0,
        ),
        name="finish",
    )(in_vmem(known), response, joined, *map(in_vmem, late), *written)


def both_ways(pairs):
    return pairs + [(b, a) for a, b in pairs]


def local(temp, u_vel, v_vel, w_vel, temp_prev, w_prev, lower, upper, metric):
    rows = temp.shape[1]
    across, stacked = lax.axis_size("gx"), lax.axis_size("gz")
    rounds = stacked.bit_length() - 1
    cores = both_ways([(i, i + 1) for i in range(0, stacked, 2)])
    near, far, fluxes, table = edges(
        temp, u_vel, w_vel, v_vel, temp_prev, w_prev, lower, upper, metric
    )
    near = lax.ppermute(near, "gx", both_ways([(i, i + 1) for i in range(0, across, 2)]))
    far = lax.ppermute(far, "gx", both_ways([(i, (i + 1) % across) for i in range(1, across, 2)]))
    other = lax.ppermute(fluxes, "gz", cores)
    outer = ()
    if rounds > 2:
        seams = both_ways([(i, i + 1) for i in range(1, stacked - 1, 2)])
        outer = (lax.ppermute(fluxes[2 * rows : 4 * rows], "gz", seams),)
    forward, tend, first = bulk(table, temp, u_vel, v_vel, w_vel, temp_prev, w_prev)
    mine, changes, *late = fix(rounds, near, far, fluxes, other, forward, first, table, outer)
    bases, gains, own, other_own = [], [], fluxes, other
    for step in range(rounds - 1):
        partners = [(i, i ^ (1 << step)) for i in range(stacked)]
        theirs = lax.ppermute(mine, "gz", partners)
        if step > 0:
            other_own = lax.ppermute(own, "gz", partners)
        base, gain, own, mine, *half = merge(
            step, step + 2 == rounds, rows, mine, theirs, own, other_own
        )
        bases.append(base)
        gains.append(gain)
    partners = [(i, i ^ (stacked // 2)) for i in range(stacked)]
    theirs = lax.ppermute(half[0], "gz", partners)
    seam = ()
    if late:
        *seam, own = late
        late = (table, tend, near, far)
    other_own = lax.ppermute(own, "gz", partners)
    known, response = prepare(
        rounds, temp, w_vel, forward, table, changes, fluxes, other, outer, bases, gains
    )
    tendencies = tuple(
        tends(rounds, field, table, tend, near, far, other, outer) for field in range(2)
    )
    joined = join(rounds, mine, theirs, own, other_own, seam)
    swapped = lax.ppermute(joined, "gz", cores)
    written = finish(rounds, known, response, joined, late, tendencies if late else ())
    written = finish(rounds, known, response, swapped, late, written)
    return tuple(written) if late else (*written, *tendencies)


def solution(mesh):
    field = P("gz", "gx", None)
    return jax.shard_map(
        local,
        mesh=mesh,
        in_specs=(field,) * 6 + (P("gz"),) * 3,
        out_specs=(field,) * 4,
        check_vma=False,
    )
```

```python
import functools

import jax
import jax.numpy as jnp
from jax import lax
from jax.experimental import pallas as pl
from jax.experimental.pallas import tpu as pltpu
from jax.sharding import PartitionSpec as P

NEW_WEIGHT = 5.0 / 12.0
HORIZ_DIFF = 0.1
FIELD_WEIGHT = 2.0 / NEW_WEIGHT
PREV_WEIGHT = (17.0 / 60.0) / NEW_WEIGHT
TILE = 8
CHUNK = 4
MIB = 1024 * 1024

PIVOT_NEW, LOWER_PIVOT, UPPER_PIVOT, FIRST_GREEN, BELOW_FORWARD, PIVOT, RISE, FALL = range(8)
FIRST, CORNER, LAST, BELOW, ABOVE, METRIC_BELOW, METRIC_ABOVE = range(7)
FROM_ABOVE, FROM_BELOW = range(2)

VMEM = pltpu.VMEM
F32 = jnp.float32


def whole(space):
    return pl.BlockSpec(memory_space=space)


def held(*shape):
    return pltpu.VMEM(shape, F32)


def in_vmem(array):
    return pltpu.with_memory_space_constraint(array, pltpu.VMEM)


def in_hbm(*arrays):
    return [pltpu.with_memory_space_constraint(array, pltpu.HBM) for array in arrays]


def bit_of(axis, bit):
    return (lax.axis_index(axis) >> bit) & 1


def edges_kernel(
    temp,
    u_vel,
    w_vel,
    v_vel,
    temp_prev,
    w_prev,
    lower,
    upper,
    metric,
    far,
    near,
    fluxes,
    outward,
    table,
    strips,
    layers,
    lower_at,
    upper_at,
    metric_at,
    sems,
):
    levels, rows, cols = temp.shape
    copies = [(lower, lower_at), (upper, upper_at), (metric, metric_at)]
    for at, array in enumerate((temp, w_vel, u_vel)):
        for side, first in enumerate((0, rows - TILE)):
            copies.append((array.at[:, pl.ds(first, TILE), :], strips.at[at, side]))
    for at, array in enumerate((temp, w_vel)):
        for side, level in enumerate((0, levels - 1)):
            copies.append((array.at[level], layers.at[at, side]))
    copies = [pltpu.make_async_copy(src, dst, sems.at[i]) for i, (src, dst) in enumerate(copies)]
    for copy in copies:
        copy.start()
    for copy in copies[:3]:
        copy.wait()
    coefficients(lower_at, upper_at, metric_at, table, fluxes.at[pl.ds(3 * rows, TILE)])
    for copy in copies[3:]:
        copy.wait()
    odd = bit_of("gx", 0) == 1
    last = TILE - 1
    for field in range(2):
        at = pl.ds(field * levels, levels)
        to_left = (HORIZ_DIFF - 0.5 * strips[2, 0, :, 0, :]) * strips[field, 0, :, 0, :]
        to_right = (HORIZ_DIFF + 0.5 * strips[2, 1, :, last, :]) * strips[field, 1, :, last, :]
        near[at, :] = jnp.where(odd, to_left, to_right)
        far[at, :] = jnp.where(odd, to_right, to_left)
    position = lax.axis_index("gz")
    upper_core = bit_of("gz", 0) == 1
    wall = (position == 0) | (position == lax.axis_size("gz") - 1)
    zero, size = jnp.zeros((rows, cols), F32), rows // 2
    for field in range(2):
        bottom = layers[1, 0] * layers[field, 0]
        top = layers[1, 1] * layers[field, 1]
        fluxes[pl.ds(field * rows, rows), :] = jnp.where(upper_core, bottom, top)
        value = jnp.where(wall, zero, jnp.where(upper_core, top, bottom))
        outward[pl.ds(field * rows, rows), :] = value
        fluxes[pl.ds(2 * rows + field * size, size), :] = jnp.where(
            upper_core, value[:size], value[size:]
        )


def edges(temp, u_vel, w_vel, v_vel, temp_prev, w_prev, lower, upper, metric):
    levels, rows, cols = temp.shape
    return pl.pallas_call(
        edges_kernel,
        out_shape=(
            held(2 * levels, cols),
            held(2 * levels, cols),
            held(3 * rows + TILE, cols),
            held(2 * rows, cols),
            held(levels, TILE, cols),
        ),
        in_specs=[whole(pl.ANY)] * 9,
        out_specs=[whole(VMEM)] * 5,
        scratch_shapes=[
            pltpu.VMEM((3, 2, levels, TILE, cols), F32),
            pltpu.VMEM((2, 2, rows, cols), F32),
            pltpu.SMEM((levels,), F32),
            pltpu.SMEM((levels,), F32),
            pltpu.SMEM((levels,), F32),
            pltpu.SemaphoreType.DMA((13,)),
        ],
        compiler_params=pltpu.CompilerParams(vmem_limit_bytes=8 * MIB),
        name="edges",
    )(*in_hbm(temp, u_vel, w_vel, v_vel, temp_prev, w_prev, lower, upper, metric))


def coefficients(lower, upper, metric, table, scalars):
    levels, _, cols = table.shape

    def row(value):
        return jnp.full((1, cols), value, F32)

    ratio = jnp.zeros((1, cols), F32)
    forward = jnp.ones((1, cols), F32)
    for level in range(levels):
        low, high = row(lower[level]), row(upper[level])
        pivot = 1.0 / (1.0 + low + high - low * ratio)
        ratio = high * pivot
        lower_pivot = low * pivot
        forward = pivot if level == 0 else lower_pivot * forward
        table[level, pl.ds(PIVOT_NEW, 1), :] = NEW_WEIGHT * pivot
        table[level, pl.ds(LOWER_PIVOT, 1), :] = lower_pivot
        table[level, pl.ds(UPPER_PIVOT, 1), :] = ratio
        table[level, pl.ds(BELOW_FORWARD, 1), :] = forward
        table[level, pl.ds(PIVOT, 1), :] = pivot
        table[level, pl.ds(RISE, 1), :] = row(metric[level] if level < levels - 1 else 0.0)
        table[level, pl.ds(FALL, 1), :] = row(metric[level] if level > 0 else 0.0)
    green = forward
    table[levels - 1, pl.ds(FIRST_GREEN, 1), :] = NEW_WEIGHT * green
    for level in range(levels - 2, -1, -1):
        green = (
            table[level, pl.ds(BELOW_FORWARD, 1), :]
            + table[level, pl.ds(UPPER_PIVOT, 1), :] * green
        )
        table[level, pl.ds(FIRST_GREEN, 1), :] = NEW_WEIGHT * green
    scalars[pl.ds(FIRST, 1), :] = green
    scalars[pl.ds(CORNER, 1), :] = forward
    scalars[pl.ds(LAST, 1), :] = pivot
    scalars[pl.ds(BELOW, 1), :] = row(lower[0])
    scalars[pl.ds(ABOVE, 1), :] = row(upper[levels - 1])
    scalars[pl.ds(METRIC_BELOW, 1), :] = row(NEW_WEIGHT * metric[0])
    scalars[pl.ds(METRIC_ABOVE, 1), :] = row(NEW_WEIGHT * metric[levels - 1])
    scalars[pl.ds(7, 1), :] = row(0.0)


def bulk_kernel(
    table,
    temp,
    u_vel,
    v_vel,
    w_vel,
    temp_prev,
    w_prev,
    forward,
    tend,
    first,
    temp_tend,
    w_tend,
    sems,
):
    levels, rows, cols = temp.shape
    strips = rows // TILE
    fields, prevs = (temp, w_vel), (temp_prev, w_prev)
    for field in range(2):
        forward[field, 0] = jnp.zeros((rows, cols), F32)
        first[field] = jnp.zeros((rows, cols), F32)
    row_at = lax.broadcasted_iota(jnp.int32, (TILE, cols), 0)
    zero = jnp.zeros((TILE, cols), F32)

    def chunk_copies(chunk):
        at = pl.ds(chunk * CHUNK, CHUNK)
        return [
            pltpu.make_async_copy(tend.at[field, at], out.at[at], sems.at[field, chunk])
            for field, out in enumerate((temp_tend, w_tend))
        ]

    def level_step(level, carry):
        def spread(at):
            return jnp.broadcast_to(table[level, pl.ds(at, 1), :], (TILE, cols))

        pivot, lower_pivot, green = spread(PIVOT_NEW), spread(LOWER_PIVOT), spread(FIRST_GREEN)
        rise, fall = spread(RISE), spread(FALL)
        over = jnp.minimum(level + 1, levels - 1)
        under = jnp.maximum(level - 1, 0)

        def sides(strip):
            at = pl.ds(strip * TILE, TILE)
            half = 0.5 * u_vel[level, at, :]
            back, ahead = HORIZ_DIFF - half, HORIZ_DIFF + half
            here = [values[level, at, :] for values in fields]
            return (
                here,
                [pltpu.roll(back * value, TILE - 1, 0) for value in here],
                [pltpu.roll(ahead * value, 1, 0) for value in here],
            )

        before = [zero, zero]
        here, back, ahead = sides(0)
        for strip in range(strips):
            after = sides(strip + 1) if strip + 1 < strips else (None, [zero, zero], None)
            at = pl.ds(strip * TILE, TILE)
            half = 0.5 * v_vel[level, at, :]
            v_back, v_ahead = HORIZ_DIFF - half, HORIZ_DIFF + half
            w_over = rise * w_vel[over, at, :]
            w_under = fall * w_vel[under, at, :]
            for field in range(2):
                value = here[field]
                change = jnp.where(row_at == TILE - 1, after[1][field], back[field])
                change = change + jnp.where(row_at == 0, before[field], ahead[field])
                change = change + pltpu.roll(v_back * value, cols - 1, 1)
                change = change + pltpu.roll(v_ahead * value, 1, 1)
                change = change - w_over * fields[field][over, at, :]
                change = change + w_under * fields[field][under, at, :]
                change = change + (here[1 - field] - (4.0 * HORIZ_DIFF) * value)
                tend[field, level, at, :] = change
                right = change + (FIELD_WEIGHT * value - PREV_WEIGHT * prevs[field][level, at, :])
                forward[field, level + 1, at, :] = (
                    pivot * right + lower_pivot * forward[field, level, at, :]
                )
                first[field, at, :] = first[field, at, :] + green * right
            before = ahead
            here, back, ahead = after

        @pl.when((level % CHUNK == CHUNK - 1) & (level < levels - CHUNK))
        def _():
            for copy in chunk_copies(level // CHUNK):
                copy.start()

        return carry

    lax.fori_loop(0, levels, level_step, 0)
    for chunk in range(levels // CHUNK - 1):
        for copy in chunk_copies(chunk):
            copy.wait()


def bulk(table, *arrays):
    levels, rows, cols = arrays[0].shape
    return pl.pallas_call(
        bulk_kernel,
        out_shape=(
            held(2, levels + 1, rows, cols),
            held(2, levels, rows, cols),
            held(2, rows, cols),
            jax.ShapeDtypeStruct((levels, rows, cols), F32),
            jax.ShapeDtypeStruct((levels, rows, cols), F32),
        ),
        in_specs=[whole(VMEM)] * 7,
        out_specs=[whole(VMEM)] * 3 + [whole(pl.ANY)] * 2,
        scratch_shapes=[pltpu.SemaphoreType.DMA((2, levels // CHUNK - 1))],
        compiler_params=pltpu.CompilerParams(vmem_limit_bytes=8 * MIB),
        cost_estimate=pl.CostEstimate(
            flops=100000 * levels * rows * cols,
            bytes_accessed=24 * levels * rows * cols,
            transcendentals=0,
        ),
        name="bulk",
    )(*map(in_vmem, (table, *arrays)))


def side_changes(far, near):
    odd = bit_of("gx", 0) == 1
    return jnp.where(odd, near[...], far[...]), jnp.where(odd, far[...], near[...])


def level_fluxes(inner, outer):
    upper = bit_of("gz", 0) == 1
    return jnp.where(upper, inner, outer), jnp.where(upper, outer, inner)


def beside_seam(rounds):
    return bit_of("gz", 0) != bit_of("gz", rounds - 1)


def ends(rows, cols, head, tail):
    at = lax.broadcasted_iota(jnp.int32, (rows, cols), 0)
    return jnp.where(at == 0, head, jnp.where(at == rows - 1, tail, 0.0))


def scalar_rows(ref, begin=0):
    return [ref[pl.ds(begin + at, 1), :] for at in range(7)]


def in_order(upper, own, other):
    low = [jnp.where(upper, b, a) for a, b in zip(own, other)]
    high = [jnp.where(upper, a, b) for a, b in zip(own, other)]
    return low, high


def interface(low, high):
    coupling = low[ABOVE]
    return coupling, 1.0 / (1.0 - coupling * coupling * low[LAST] * high[FIRST])


def joint_scalars(low, high):
    coupling, inverse = interface(low, high)
    low_out, high_out = low[CORNER] * coupling, high[CORNER] * coupling
    return [
        low[FIRST] + low_out * low_out * inverse * high[FIRST],
        low_out * inverse * high[CORNER],
        high[LAST] + high_out * high_out * inverse * low[LAST],
        low[BELOW],
        high[ABOVE],
        low[METRIC_BELOW],
        high[METRIC_ABOVE],
        jnp.zeros_like(coupling),
    ]


def fix_kernel(
    rounds, levels, far, near, fluxes, outward, other, forward, first, table, *rest
):
    outer, rest = (rest[0], rest[1:]) if rounds > 2 else (None, rest)
    entries, changes, *late = rest
    _, rows, cols = first.shape
    diffs = side_changes(far, near)
    scalars = scalar_rows(fluxes, 3 * rows)
    below, above = scalars[METRIC_BELOW], -scalars[METRIC_ABOVE]
    core, size = bit_of("gz", 0) == 1, rows // 2
    for field in range(2):
        firsts, lasts = [], []
        for side in range(2):
            value = jnp.zeros((1, cols), F32)
            total = jnp.zeros((1, cols), F32)
            for level in range(levels):
                right = diffs[side][field * levels + level : field * levels + level + 1, :]
                value = (
                    table[level, pl.ds(PIVOT_NEW, 1), :] * right
                    + table[level, pl.ds(LOWER_PIVOT, 1), :] * value
                )
                total = total + table[level, pl.ds(FIRST_GREEN, 1), :] * right
                changes[pl.ds((side * 2 + field) * levels + level, 1), :] = value
            firsts.append(total)
            lasts.append(value)
        at = pl.ds(field * rows, rows)
        flux_below, flux_above = level_fluxes(other[at, :], 0.0 if outer is None else outer[at, :])
        first_entry = (
            first[field]
            + (below * scalars[FIRST]) * flux_below
            + (above * scalars[CORNER]) * flux_above
            + ends(rows, cols, *firsts)
        )
        last_entry = (
            forward[field, levels]
            + (below * scalars[CORNER]) * flux_below
            + (above * scalars[LAST]) * flux_above
            + ends(rows, cols, *lasts)
        )
        entries[at, :] = first_entry
        entries[pl.ds((2 + field) * rows, rows), :] = last_entry
        if late:
            message, seam = late
            message[at, :] = jnp.where(core, first_entry, last_entry)
            there = pl.ds(2 * rows + field * size, size)
            message[there, :] = jnp.where(core, last_entry[:size], first_entry[size:])
            value = outward[at, :]
            value = jnp.where(core, value[size:], value[:size])
            seam[pl.ds(field * size, size), :] = jnp.where(
                beside_seam(rounds), value, other[there, :]
            )
    if late:
        far_scalars = scalar_rows(other, 3 * rows)
        for at, value in enumerate(joint_scalars(*in_order(core, scalars, far_scalars))):
            seam[pl.ds(rows + at, 1), :] = value


def fix(rounds, far, near, fluxes, outward, other, forward, first, table, outer):
    levels = table.shape[0]
    _, rows, cols = first.shape
    shapes = [held(4 * rows, cols), held(4 * levels, cols)]
    if rounds == 2:
        shapes += [held(3 * rows, cols), held(rows + TILE, cols)]
    return pl.pallas_call(
        functools.partial(fix_kernel, rounds, levels),
        out_shape=tuple(shapes),
        in_specs=[whole(VMEM)] * (8 + len(outer)),
        out_specs=[whole(VMEM)] * len(shapes),
        compiler_params=pltpu.CompilerParams(vmem_limit_bytes=8 * MIB),
        name="fix",
    )(
        far, near, fluxes, outward, other, in_vmem(forward), in_vmem(first), in_vmem(table), *outer
    )


def tends_kernel(rounds, table, tend, far, near, other, *rest):
    outer, rest = (rest[0], rest[1:]) if rounds > 2 else (None, rest)
    *outs, layers, strips, sems = rest[2:]
    _, levels, rows, cols = tend.shape
    inside, middle = pl.ds(1, levels - 2), pl.ds(TILE, rows - 2 * TILE)
    left = pl.ds(levels - CHUNK, CHUNK - 1)
    copies = []

    def send(field, at, src, dst):
        copies.append(pltpu.make_async_copy(src, dst, sems.at[field, at]))
        copies[-1].start()

    for field, out in enumerate(outs):
        send(field, 0, tend.at[field, left, middle, :], out.at[left, middle, :])
    diffs = side_changes(far, near)
    tile_at = lax.broadcasted_iota(jnp.int32, (TILE, cols), 0)
    for field, out in enumerate(outs):
        at = pl.ds(field * rows, rows)
        below, above = level_fluxes(other[at, :], 0.0 if outer is None else outer[at, :])
        for side, level, change in (
            (0, 0, table[0, pl.ds(RISE, 1), :] * below),
            (1, levels - 1, -table[levels - 1, pl.ds(FALL, 1), :] * above),
        ):
            at = field * levels + level
            rim = ends(rows, cols, diffs[0][at : at + 1, :], diffs[1][at : at + 1, :])
            layers[field, side] = tend[field, level] + change + rim
            send(field, 1 + side, layers.at[field, side], out.at[level])
        for side, begin, row in ((0, 0, 0), (1, rows - TILE, TILE - 1)):
            for level in range(1, levels - 1):
                at = field * levels + level
                edge = jnp.where(tile_at == row, diffs[side][at : at + 1, :], 0.0)
                strips[field, side, level] = tend[field, level, pl.ds(begin, TILE), :] + edge
            there = out.at[inside, pl.ds(begin, TILE), :]
            send(field, 3 + side, strips.at[field, side, inside], there)
    for copy in copies:
        copy.wait()


def tends(rounds, table, tend, far, near, other, outer, written):
    _, levels, rows, cols = tend.shape
    inputs = 5 + len(outer)
    return pl.pallas_call(
        functools.partial(tends_kernel, rounds),
        out_shape=(jax.ShapeDtypeStruct((levels, rows, cols), F32),) * 2,
        in_specs=[whole(VMEM)] * inputs + [whole(pl.ANY)] * 2,
        out_specs=[whole(pl.ANY)] * 2,
        scratch_shapes=[
            pltpu.VMEM((2, 2, rows, cols), F32),
            pltpu.VMEM((2, 2, levels, TILE, cols), F32),
            pltpu.SemaphoreType.DMA((2, 5)),
        ],
        input_output_aliases={inputs: 0, inputs + 1: 1},
        compiler_params=pltpu.CompilerParams(vmem_limit_bytes=8 * MIB),
        cost_estimate=pl.CostEstimate(
            flops=levels * rows * cols,
            bytes_accessed=8 * levels * rows * cols,
            transcendentals=0,
        ),
        name="tends",
    )(in_vmem(table), in_vmem(tend), far, near, other, *outer, *in_hbm(*written))


def merge_kernel(bit, final, late, own_at, other_at, mine, theirs, own, other, base, gains, *rest):
    _, rows, cols = base.shape
    upper = bit_of("gz", bit) == 1
    low, high = in_order(upper, scalar_rows(own, own_at), scalar_rows(other, other_at))
    coupling, inverse = interface(low, high)
    to_high, to_low = high[FIRST] * coupling, low[LAST] * coupling
    low_out, high_out = low[CORNER] * coupling, high[CORNER] * coupling
    core, size = bit_of("gz", 0) == 1, rows // 2
    sends_last = bit_of("gz", bit + 1) == 0
    for field in range(2):
        here = pl.ds(field * rows, rows)
        own_first, own_last = mine[here, :], mine[pl.ds((2 + field) * rows, rows), :]
        if late:
            low_last = jnp.where(upper, theirs[here, :], own_last)
            high_first = jnp.where(upper, own_first, theirs[here, :])
        else:
            other_first, other_last = theirs[here, :], theirs[pl.ds((2 + field) * rows, rows), :]
            low_last = jnp.where(upper, other_last, own_last)
            high_first = jnp.where(upper, own_first, other_first)
            low_first = jnp.where(upper, other_first, own_first)
            high_last = jnp.where(upper, own_last, other_last)
        above = inverse * (high_first + to_high * low_last)
        below = inverse * (low_last + to_low * high_first)
        base[field] = coupling * jnp.where(upper, below, above)
        more = jnp.where(sends_last, high_out * below, low_out * above)
        if late:
            outside = jnp.where(upper, own_last, own_first)
            outside = jnp.where(core, outside[size:], outside[:size])
            there = theirs[pl.ds(2 * rows + field * size, size), :]
            outside = jnp.where(sends_last == upper, outside, there)
        elif final:
            outside = jnp.where(sends_last, high_last, low_first)
            outside = jnp.where(core, outside[size:], outside[:size])
        if final:
            value = outside + jnp.where(core, more[size:], more[:size])
            rest[0][pl.ds(field * size, size), :] = value
        else:
            rest[0][here, :] = low_first + low_out * above
            rest[0][pl.ds((2 + field) * rows, rows), :] = high_last + high_out * below
    if not late:
        for at, value in enumerate(joint_scalars(low, high)):
            rest[1][pl.ds(at, 1), :] = value
    scale = coupling * inverse
    gains[...] = jnp.zeros(gains.shape, F32)
    gains[pl.ds(FROM_ABOVE, 1), :] = scale * high[CORNER] * jnp.where(upper, to_low, 1.0)
    gains[pl.ds(FROM_BELOW, 1), :] = scale * low[CORNER] * jnp.where(upper, 1.0, to_high)


def merge(bit, final, late, rows, mine, theirs, own, other):
    cols = mine.shape[1]
    shapes = [held(2, rows, cols), held(TILE, cols), held((1 if final else 4) * rows, cols)]
    if not late:
        shapes.append(held(TILE, cols))
    return pl.pallas_call(
        functools.partial(
            merge_kernel, bit, final, late, own.shape[0] - TILE, other.shape[0] - TILE
        ),
        out_shape=tuple(shapes),
        in_specs=[whole(VMEM)] * 4,
        out_specs=[whole(VMEM)] * len(shapes),
        compiler_params=pltpu.CompilerParams(vmem_limit_bytes=8 * MIB),
        name="merge",
    )(mine, theirs, own, other)


def prepare_kernel(
    rounds, temp, w_vel, forward, table, changes, fluxes, other, *rest
):
    outer, rest = (rest[0], rest[1:]) if rounds > 2 else (None, rest)
    bases, gains = rest[: rounds - 1], rest[rounds - 1 : 2 * rounds - 2]
    known, response, below_in, above_in = rest[2 * rounds - 2 :]
    levels, rows, cols = temp.shape
    upper = bit_of("gz", rounds - 1) == 1
    one, none = jnp.ones((1, cols), F32), jnp.zeros((1, cols), F32)
    below_gain, above_gain = jnp.where(upper, one, none), jnp.where(upper, none, one)
    below = above = None
    for step in range(rounds - 2, -1, -1):
        side = bit_of("gz", step) == 1
        from_above = gains[step][pl.ds(FROM_ABOVE, 1), :]
        from_below = gains[step][pl.ds(FROM_BELOW, 1), :]
        gain = from_above * above_gain + from_below * below_gain
        below_gain = jnp.where(side, gain, below_gain)
        above_gain = jnp.where(side, above_gain, gain)
        into = [bases[step][field] for field in range(2)]
        if below is None:
            below = above = [jnp.zeros((rows, cols), F32)] * 2
        else:
            into = [
                into[field] + from_above * above[field] + from_below * below[field]
                for field in range(2)
            ]
        below = [jnp.where(side, into[field], below[field]) for field in range(2)]
        above = [jnp.where(side, above[field], into[field]) for field in range(2)]
    scalars = scalar_rows(fluxes, 3 * rows)
    for field in range(2):
        at = pl.ds(field * rows, rows)
        flux_below, flux_above = level_fluxes(other[at, :], 0.0 if outer is None else outer[at, :])
        below_in[field] = below[field] + scalars[METRIC_BELOW] * flux_below
        above_in[field] = above[field] - scalars[METRIC_ABOVE] * flux_above

    gain = above_gain * table[levels - 1, pl.ds(PIVOT, 1), :]
    for level in range(levels - 1, -1, -1):
        if level < levels - 1:
            gain = gain * table[level, pl.ds(UPPER_PIVOT, 1), :]
        gain = gain + below_gain * table[level, pl.ds(BELOW_FORWARD, 1), :]
        response[level] = jnp.broadcast_to(gain, (TILE, cols))

    row_at = lax.broadcasted_iota(jnp.int32, (TILE, cols), 0)
    width = 2 * TILE
    for begin in range(0, rows, width):
        at = pl.ds(begin, width)

        def solve(level, carry, factor, begin=begin, at=at):
            factor = table[level, pl.ds(factor, 1), :]
            below_factor = table[level, pl.ds(BELOW_FORWARD, 1), :]
            values = []
            for field, cells in enumerate((temp, w_vel)):
                value = forward[field, level + 1, at, :] + below_factor * below_in[field, at, :]
                if begin == 0:
                    change = changes[pl.ds(field * levels + level, 1), :]
                    head = value[:TILE] + jnp.where(row_at == 0, change, 0.0)
                    value = jnp.concatenate([head, value[TILE:]])
                if begin == rows - width:
                    change = changes[pl.ds((2 + field) * levels + level, 1), :]
                    tail = value[-TILE:] + jnp.where(row_at == TILE - 1, change, 0.0)
                    value = jnp.concatenate([value[:-TILE], tail])
                value = value + factor * carry[field]
                known[field, level, at, :] = value - cells[level, at, :]
                values.append(value)
            return tuple(values)

        carry = solve(levels - 1, [above_in[field, at, :] for field in range(2)], PIVOT)

        def step(back, carry, solve=solve):
            return solve(levels - 2 - back, carry, UPPER_PIVOT)

        lax.fori_loop(0, levels - 1, step, carry, unroll=3)


def prepare(rounds, temp, w_vel, forward, table, changes, fluxes, other, outer, bases, gains):
    levels, rows, cols = temp.shape
    return pl.pallas_call(
        functools.partial(prepare_kernel, rounds),
        out_shape=(held(2, levels, rows, cols), held(levels, TILE, cols)),
        in_specs=[whole(VMEM)] * (7 + len(outer) + 2 * (rounds - 1)),
        out_specs=[whole(VMEM)] * 2,
        scratch_shapes=[pltpu.VMEM((2, rows, cols), F32)] * 2,
        compiler_params=pltpu.CompilerParams(vmem_limit_bytes=8 * MIB),
        cost_estimate=pl.CostEstimate(
            flops=levels * rows * cols,
            bytes_accessed=24 * levels * rows * cols,
            transcendentals=0,
        ),
        name="prepare",
    )(
        in_vmem(temp), in_vmem(w_vel), in_vmem(forward), in_vmem(table), changes, fluxes, other,
        *outer, *bases, *gains,
    )


def join_kernel(rounds, late, own_at, other_at, mine, theirs, own, other, joined):
    size = theirs.shape[0] // 2
    upper = bit_of("gz", rounds - 1) == 1
    low, high = in_order(upper, scalar_rows(own, own_at), scalar_rows(other, other_at))
    coupling, inverse = interface(low, high)
    scale = coupling * inverse
    to_other = scale * coupling * jnp.where(upper, low[LAST], high[FIRST])
    up, down = high[METRIC_BELOW] * inverse, -low[METRIC_ABOVE] * inverse
    own_gain = coupling * jnp.where(upper, down * low[LAST], up * high[FIRST])
    other_gain = jnp.where(upper, up, down)
    for field in range(2):
        at = pl.ds(field * size, size)
        into = scale * theirs[at, :] + to_other * mine[at, :]
        if late:
            flux = other[at, :]
            into = into + (own_gain * own[at, :] + other_gain * flux)
            joined[pl.ds((2 + field) * size, size), :] = flux
        joined[at, :] = into


def join(rounds, late, mine, theirs, own, other):
    size, cols = theirs.shape
    return pl.pallas_call(
        functools.partial(join_kernel, rounds, late, own.shape[0] - TILE, other.shape[0] - TILE),
        out_shape=held(size * (2 if late else 1), cols),
        in_specs=[whole(VMEM)] * 4,
        out_specs=whole(VMEM),
        compiler_params=pltpu.CompilerParams(vmem_limit_bytes=8 * MIB),
        name="join",
    )(mine, theirs, own, other)


def finish_kernel(rounds, swapped, known, response, joined, *rest):
    late, results = rounds == 2, 4 if rounds == 2 else 2
    table, tend, far, near = rest[:4] if late else (None,) * 4
    rest = rest[(4 if late else 0) + (results if swapped else results - 2) :]
    outs, (result, rim, sems) = rest[:results], rest[results:]
    _, levels, rows, cols = known.shape
    width, half = 2 * TILE, rows // 2
    core = bit_of("gz", 0)
    start = pl.multiple_of((1 - core if swapped else core) * half, half)
    copies = []
    if late:
        diffs = side_changes(far, near)
        level = core * (levels - 1)
        gain = jnp.where(
            core == 1, -table[levels - 1, pl.ds(FALL, 1), :], table[0, pl.ds(RISE, 1), :]
        )
        gain = jnp.where(beside_seam(rounds), gain, 0.0)
        row_at = start + lax.broadcasted_iota(jnp.int32, (half, cols), 0)
        for field in range(2):
            head, tail = (
                jnp.where(
                    core == 1,
                    diff[(field + 1) * levels - 1 : (field + 1) * levels, :],
                    diff[field * levels : field * levels + 1, :],
                )
                for diff in diffs
            )
            edge = jnp.where(row_at == 0, head, jnp.where(row_at == rows - 1, tail, 0.0))
            flux = joined[pl.ds((2 + field) * half, half), :]
            rim[field] = tend[field, level, pl.ds(start, half), :] + gain * flux + edge
            copies.append(
                pltpu.make_async_copy(
                    rim.at[field],
                    outs[2 + field].at[level, pl.ds(start, half), :],
                    sems.at[field],
                )
            )
            copies[-1].start()
    for field in range(2):
        for part, begin in enumerate(range(0, half, width)):
            into = joined[pl.ds(field * half + begin, width), :]
            tiles = [into[i : i + TILE] for i in range(0, width, TILE)]

            def step(level, carry, field=field, begin=begin, tiles=tiles):
                gain = response[level]
                for i, tile in enumerate(tiles):
                    at = begin + i * TILE
                    value = known[field, level, pl.ds(start + at, TILE), :] + gain * tile
                    result[field, level, pl.ds(at, TILE), :] = value
                return carry

            lax.fori_loop(0, levels, step, 0, unroll=4)
            copies.append(
                pltpu.make_async_copy(
                    result.at[field, :, pl.ds(begin, width), :],
                    outs[field].at[:, pl.ds(start + begin, width), :],
                    sems.at[2 + 2 * field + part],
                )
            )
            copies[-1].start()
    for copy in copies:
        copy.wait()


def finish(rounds, known, response, joined, late, written):
    _, levels, rows, cols = known.shape
    results = 4 if rounds == 2 else 2
    inputs = 3 + len(late)
    swapped = len(written) == results
    return pl.pallas_call(
        functools.partial(finish_kernel, rounds, swapped),
        out_shape=(jax.ShapeDtypeStruct((levels, rows, cols), F32),) * results,
        in_specs=[whole(VMEM)] * inputs + [whole(pl.ANY)] * len(written),
        out_specs=[whole(pl.ANY)] * results,
        scratch_shapes=[
            pltpu.VMEM((2, levels, rows // 2, cols), F32),
            pltpu.VMEM((2, rows // 2, cols), F32),
            pltpu.SemaphoreType.DMA((6,)),
        ],
        input_output_aliases={
            inputs + i: results - len(written) + i for i in range(len(written))
        },
        compiler_params=pltpu.CompilerParams(vmem_limit_bytes=8 * MIB),
        cost_estimate=pl.CostEstimate(
            flops=20000 * levels * rows * cols,
            bytes_accessed=8 * levels * rows * cols,
            transcendentals=0,
        ),
        name="finish",
    )(in_vmem(known), response, joined, *map(in_vmem, late), *written)


def both_ways(pairs):
    return pairs + [(b, a) for a, b in pairs]


def local(temp, u_vel, v_vel, w_vel, temp_prev, w_prev, lower, upper, metric):
    rows = temp.shape[1]
    across, stacked = lax.axis_size("gx"), lax.axis_size("gz")
    rounds = stacked.bit_length() - 1
    cores = both_ways([(i, i + 1) for i in range(0, stacked, 2)])
    far, near, fluxes, outward, table = edges(
        temp, u_vel, w_vel, v_vel, temp_prev, w_prev, lower, upper, metric
    )
    far = lax.ppermute(far, "gx", both_ways([(i, (i + 1) % across) for i in range(1, across, 2)]))
    near = lax.ppermute(near, "gx", both_ways([(i, i + 1) for i in range(0, across, 2)]))
    other = lax.ppermute(fluxes, "gz", cores)
    outer = ()
    if rounds > 2:
        seams = both_ways([(i, i + 1) for i in range(1, stacked - 1, 2)])
        outer = (lax.ppermute(outward, "gz", seams),)
    forward, tend, first, *written = bulk(table, temp, u_vel, v_vel, w_vel, temp_prev, w_prev)
    entries, changes, *late = fix(
        rounds, far, near, fluxes, outward, other, forward, first, table, outer
    )
    message, seam = late if late else (entries, fluxes)
    bases, gains, own, other_own = [], [], fluxes, other
    for step in range(rounds - 1):
        partners = [(i, i ^ (1 << step)) for i in range(stacked)]
        theirs = lax.ppermute(message, "gz", partners)
        if step > 0:
            other_own = lax.ppermute(own, "gz", partners)
        base, gain, message, *scalars = merge(
            step, step + 2 == rounds, bool(late), rows, entries, theirs, own, other_own
        )
        entries, own = message, scalars[0] if scalars else seam
        bases.append(base)
        gains.append(gain)
    partners = [(i, i ^ (stacked // 2)) for i in range(stacked)]
    theirs = lax.ppermute(message, "gz", partners)
    other_own = lax.ppermute(own, "gz", partners)
    known, response = prepare(
        rounds, temp, w_vel, forward, table, changes, fluxes, other, outer, bases, gains
    )
    tendencies = tends(rounds, table, tend, far, near, other, outer, written)
    joined = join(rounds, bool(late), message, theirs, own, other_own)
    swapped = lax.ppermute(joined, "gz", cores)
    late = (table, tend, far, near) if late else ()
    written = finish(rounds, known, response, joined, late, tendencies if late else ())
    written = finish(rounds, known, response, swapped, late, written)
    return tuple(written) if late else (*written, *tendencies)


def solution(mesh):
    field = P("gz", "gx", None)
    return jax.shard_map(
        local,
        mesh=mesh,
        in_specs=(field,) * 6 + (P("gz"),) * 3,
        out_specs=(field,) * 4,
        check_vma=False,
    )
```

```python
import functools

import jax
import jax.numpy as jnp
from jax import lax
from jax.experimental import pallas as pl
from jax.experimental.pallas import tpu as pltpu
from jax.sharding import PartitionSpec as P

NEW_WEIGHT = 5.0 / 12.0
HORIZ_DIFF = 0.1
FIELD_WEIGHT = 2.0 / NEW_WEIGHT
PREV_WEIGHT = (17.0 / 60.0) / NEW_WEIGHT
TILE = 8
MIB = 1024 * 1024

PIVOT_NEW, LOWER_PIVOT, UPPER_PIVOT, FIRST_GREEN, BELOW_FORWARD, PIVOT, RISE, FALL = range(8)
FIRST, CORNER, LAST, BELOW, ABOVE, METRIC_BELOW, METRIC_ABOVE = range(7)
FROM_ABOVE, FROM_BELOW = range(2)

VMEM = pltpu.VMEM
F32 = jnp.float32


def whole(space):
    return pl.BlockSpec(memory_space=space)


def held(*shape):
    return pltpu.VMEM(shape, F32)


def in_vmem(array):
    return pltpu.with_memory_space_constraint(array, pltpu.VMEM)


def in_hbm(*arrays):
    return [pltpu.with_memory_space_constraint(array, pltpu.HBM) for array in arrays]


def bit_of(axis, bit):
    return (lax.axis_index(axis) >> bit) & 1


def edges_kernel(
    temp,
    u_vel,
    w_vel,
    v_vel,
    temp_prev,
    w_prev,
    lower,
    upper,
    metric,
    far,
    near,
    fluxes,
    outward,
    table,
    strips,
    layers,
    lower_at,
    upper_at,
    metric_at,
    sems,
):
    levels, rows, cols = temp.shape
    copies = [(lower, lower_at), (upper, upper_at), (metric, metric_at)]
    for at, array in enumerate((temp, w_vel, u_vel)):
        for side, first in enumerate((0, rows - TILE)):
            copies.append((array.at[:, pl.ds(first, TILE), :], strips.at[at, side]))
    for at, array in enumerate((temp, w_vel)):
        for side, level in enumerate((0, levels - 1)):
            copies.append((array.at[level], layers.at[at, side]))
    copies = [pltpu.make_async_copy(src, dst, sems.at[i]) for i, (src, dst) in enumerate(copies)]
    for copy in copies:
        copy.start()
    for copy in copies[:3]:
        copy.wait()
    coefficients(lower_at, upper_at, metric_at, table, fluxes.at[pl.ds(3 * rows, TILE)])
    for copy in copies[3:]:
        copy.wait()
    odd = bit_of("gx", 0) == 1
    last = TILE - 1
    for field in range(2):
        at = pl.ds(field * levels, levels)
        to_left = (HORIZ_DIFF - 0.5 * strips[2, 0, :, 0, :]) * strips[field, 0, :, 0, :]
        to_right = (HORIZ_DIFF + 0.5 * strips[2, 1, :, last, :]) * strips[field, 1, :, last, :]
        near[at, :] = jnp.where(odd, to_left, to_right)
        far[at, :] = jnp.where(odd, to_right, to_left)
    position = lax.axis_index("gz")
    upper_core = bit_of("gz", 0) == 1
    wall = (position == 0) | (position == lax.axis_size("gz") - 1)
    zero, size = jnp.zeros((rows, cols), F32), rows // 2
    for field in range(2):
        bottom = layers[1, 0] * layers[field, 0]
        top = layers[1, 1] * layers[field, 1]
        fluxes[pl.ds(field * rows, rows), :] = jnp.where(upper_core, bottom, top)
        value = jnp.where(wall, zero, jnp.where(upper_core, top, bottom))
        outward[pl.ds(field * rows, rows), :] = value
        fluxes[pl.ds(2 * rows + field * size, size), :] = jnp.where(
            upper_core, value[:size], value[size:]
        )


def edges(temp, u_vel, w_vel, v_vel, temp_prev, w_prev, lower, upper, metric):
    levels, rows, cols = temp.shape
    return pl.pallas_call(
        edges_kernel,
        out_shape=(
            held(2 * levels, cols),
            held(2 * levels, cols),
            held(3 * rows + TILE, cols),
            held(2 * rows, cols),
            held(levels, TILE, cols),
        ),
        in_specs=[whole(pl.ANY)] * 9,
        out_specs=[whole(VMEM)] * 5,
        scratch_shapes=[
            pltpu.VMEM((3, 2, levels, TILE, cols), F32),
            pltpu.VMEM((2, 2, rows, cols), F32),
            pltpu.SMEM((levels,), F32),
            pltpu.SMEM((levels,), F32),
            pltpu.SMEM((levels,), F32),
            pltpu.SemaphoreType.DMA((13,)),
        ],
        compiler_params=pltpu.CompilerParams(vmem_limit_bytes=8 * MIB),
        name="edges",
    )(*in_hbm(temp, u_vel, w_vel, v_vel, temp_prev, w_prev, lower, upper, metric))


def coefficients(lower, upper, metric, table, scalars):
    levels, _, cols = table.shape

    def row(value):
        return jnp.full((1, cols), value, F32)

    ratio = jnp.zeros((1, cols), F32)
    forward = jnp.ones((1, cols), F32)
    for level in range(levels):
        low, high = row(lower[level]), row(upper[level])
        pivot = 1.0 / (1.0 + low + high - low * ratio)
        ratio = high * pivot
        lower_pivot = low * pivot
        forward = pivot if level == 0 else lower_pivot * forward
        table[level, pl.ds(PIVOT_NEW, 1), :] = NEW_WEIGHT * pivot
        table[level, pl.ds(LOWER_PIVOT, 1), :] = lower_pivot
        table[level, pl.ds(UPPER_PIVOT, 1), :] = ratio
        table[level, pl.ds(BELOW_FORWARD, 1), :] = forward
        table[level, pl.ds(PIVOT, 1), :] = pivot
        table[level, pl.ds(RISE, 1), :] = row(metric[level] if level < levels - 1 else 0.0)
        table[level, pl.ds(FALL, 1), :] = row(metric[level] if level > 0 else 0.0)
    green = forward
    table[levels - 1, pl.ds(FIRST_GREEN, 1), :] = NEW_WEIGHT * green
    for level in range(levels - 2, -1, -1):
        green = (
            table[level, pl.ds(BELOW_FORWARD, 1), :]
            + table[level, pl.ds(UPPER_PIVOT, 1), :] * green
        )
        table[level, pl.ds(FIRST_GREEN, 1), :] = NEW_WEIGHT * green
    scalars[pl.ds(FIRST, 1), :] = green
    scalars[pl.ds(CORNER, 1), :] = forward
    scalars[pl.ds(LAST, 1), :] = pivot
    scalars[pl.ds(BELOW, 1), :] = row(lower[0])
    scalars[pl.ds(ABOVE, 1), :] = row(upper[levels - 1])
    scalars[pl.ds(METRIC_BELOW, 1), :] = row(NEW_WEIGHT * metric[0])
    scalars[pl.ds(METRIC_ABOVE, 1), :] = row(NEW_WEIGHT * metric[levels - 1])
    scalars[pl.ds(7, 1), :] = row(0.0)


def bulk_kernel(
    arrived,
    table,
    temp,
    u_vel,
    v_vel,
    w_vel,
    temp_prev,
    w_prev,
    forward,
    tend,
    first,
):
    levels, rows, cols = temp.shape
    strips = rows // TILE
    fields, prevs = (temp, w_vel), (temp_prev, w_prev)
    for field in range(2):
        forward[field, 0] = jnp.zeros((rows, cols), F32)
        first[field] = jnp.zeros((rows, cols), F32)
    row_at = lax.broadcasted_iota(jnp.int32, (TILE, cols), 0)
    zero = jnp.zeros((TILE, cols), F32)

    def level_step(level, carry):
        def spread(at):
            return jnp.broadcast_to(table[level, pl.ds(at, 1), :], (TILE, cols))

        pivot, lower_pivot, green = spread(PIVOT_NEW), spread(LOWER_PIVOT), spread(FIRST_GREEN)
        rise, fall = spread(RISE), spread(FALL)
        over = jnp.minimum(level + 1, levels - 1)
        under = jnp.maximum(level - 1, 0)

        def sides(strip):
            at = pl.ds(strip * TILE, TILE)
            half = 0.5 * u_vel[level, at, :]
            back, ahead = HORIZ_DIFF - half, HORIZ_DIFF + half
            here = [values[level, at, :] for values in fields]
            return (
                here,
                [pltpu.roll(back * value, TILE - 1, 0) for value in here],
                [pltpu.roll(ahead * value, 1, 0) for value in here],
            )

        before = [zero, zero]
        here, back, ahead = sides(0)
        for strip in range(strips):
            after = sides(strip + 1) if strip + 1 < strips else (None, [zero, zero], None)
            at = pl.ds(strip * TILE, TILE)
            half = 0.5 * v_vel[level, at, :]
            v_back, v_ahead = HORIZ_DIFF - half, HORIZ_DIFF + half
            w_over = rise * w_vel[over, at, :]
            w_under = fall * w_vel[under, at, :]
            for field in range(2):
                value = here[field]
                change = jnp.where(row_at == TILE - 1, after[1][field], back[field])
                change = change + jnp.where(row_at == 0, before[field], ahead[field])
                change = change + pltpu.roll(v_back * value, cols - 1, 1)
                change = change + pltpu.roll(v_ahead * value, 1, 1)
                change = change - w_over * fields[field][over, at, :]
                change = change + w_under * fields[field][under, at, :]
                change = change + (here[1 - field] - (4.0 * HORIZ_DIFF) * value)
                tend[field, level, at, :] = change
                right = change + (FIELD_WEIGHT * value - PREV_WEIGHT * prevs[field][level, at, :])
                forward[field, level + 1, at, :] = (
                    pivot * right + lower_pivot * forward[field, level, at, :]
                )
                first[field, at, :] = first[field, at, :] + green * right
            before = ahead
            here, back, ahead = after
        return carry

    lax.fori_loop(0, levels, level_step, 0)


def bulk(arrived, table, *arrays):
    levels, rows, cols = arrays[0].shape
    return pl.pallas_call(
        bulk_kernel,
        out_shape=(
            held(2, levels + 1, rows, cols),
            held(2, levels, rows, cols),
            held(2, rows, cols),
        ),
        in_specs=[whole(pl.ANY)] + [whole(VMEM)] * 7,
        out_specs=[whole(VMEM)] * 3,
        compiler_params=pltpu.CompilerParams(vmem_limit_bytes=8 * MIB),
        cost_estimate=pl.CostEstimate(
            flops=100000 * levels * rows * cols,
            bytes_accessed=24 * levels * rows * cols,
            transcendentals=0,
        ),
        name="bulk",
    )(arrived, *map(in_vmem, (table, *arrays)))


def side_changes(far, near):
    odd = bit_of("gx", 0) == 1
    return jnp.where(odd, near[...], far[...]), jnp.where(odd, far[...], near[...])


def level_fluxes(inner, outer):
    upper = bit_of("gz", 0) == 1
    return jnp.where(upper, inner, outer), jnp.where(upper, outer, inner)


def beside_seam(rounds):
    return bit_of("gz", 0) != bit_of("gz", rounds - 1)


def ends(rows, cols, head, tail):
    at = lax.broadcasted_iota(jnp.int32, (rows, cols), 0)
    return jnp.where(at == 0, head, jnp.where(at == rows - 1, tail, 0.0))


def scalar_rows(ref, begin=0):
    return [ref[pl.ds(begin + at, 1), :] for at in range(7)]


def in_order(upper, own, other):
    low = [jnp.where(upper, b, a) for a, b in zip(own, other)]
    high = [jnp.where(upper, a, b) for a, b in zip(own, other)]
    return low, high


def interface(low, high):
    coupling = low[ABOVE]
    return coupling, 1.0 / (1.0 - coupling * coupling * low[LAST] * high[FIRST])


def joint_scalars(low, high):
    coupling, inverse = interface(low, high)
    low_out, high_out = low[CORNER] * coupling, high[CORNER] * coupling
    return [
        low[FIRST] + low_out * low_out * inverse * high[FIRST],
        low_out * inverse * high[CORNER],
        high[LAST] + high_out * high_out * inverse * low[LAST],
        low[BELOW],
        high[ABOVE],
        low[METRIC_BELOW],
        high[METRIC_ABOVE],
        jnp.zeros_like(coupling),
    ]


def fix_kernel(
    rounds, levels, other, far, near, fluxes, outward, forward, first, table, *rest
):
    outer, rest = (rest[0], rest[1:]) if rounds > 2 else (None, rest)
    entries, changes, *late = rest
    _, rows, cols = first.shape
    diffs = side_changes(far, near)
    scalars = scalar_rows(fluxes, 3 * rows)
    below, above = scalars[METRIC_BELOW], -scalars[METRIC_ABOVE]
    core, size = bit_of("gz", 0) == 1, rows // 2
    for field in range(2):
        firsts, lasts = [], []
        for side in range(2):
            value = jnp.zeros((1, cols), F32)
            total = jnp.zeros((1, cols), F32)
            for level in range(levels):
                right = diffs[side][field * levels + level : field * levels + level + 1, :]
                value = (
                    table[level, pl.ds(PIVOT_NEW, 1), :] * right
                    + table[level, pl.ds(LOWER_PIVOT, 1), :] * value
                )
                total = total + table[level, pl.ds(FIRST_GREEN, 1), :] * right
                changes[pl.ds((side * 2 + field) * levels + level, 1), :] = value
            firsts.append(total)
            lasts.append(value)
        at = pl.ds(field * rows, rows)
        flux_below, flux_above = level_fluxes(other[at, :], 0.0 if outer is None else outer[at, :])
        first_entry = (
            first[field]
            + (below * scalars[FIRST]) * flux_below
            + (above * scalars[CORNER]) * flux_above
            + ends(rows, cols, *firsts)
        )
        last_entry = (
            forward[field, levels]
            + (below * scalars[CORNER]) * flux_below
            + (above * scalars[LAST]) * flux_above
            + ends(rows, cols, *lasts)
        )
        entries[at, :] = first_entry
        entries[pl.ds((2 + field) * rows, rows), :] = last_entry
        if late:
            message, seam = late
            message[at, :] = jnp.where(core, first_entry, last_entry)
            there = pl.ds(2 * rows + field * size, size)
            message[there, :] = jnp.where(core, last_entry[:size], first_entry[size:])
            value = outward[at, :]
            value = jnp.where(core, value[size:], value[:size])
            seam[pl.ds(field * size, size), :] = jnp.where(
                beside_seam(rounds), value, other[there, :]
            )
    if late:
        far_scalars = scalar_rows(other, 3 * rows)
        for at, value in enumerate(joint_scalars(*in_order(core, scalars, far_scalars))):
            seam[pl.ds(rows + at, 1), :] = value


def fix(rounds, other, far, near, fluxes, outward, forward, first, table, outer):
    levels = table.shape[0]
    _, rows, cols = first.shape
    shapes = [held(4 * rows, cols), held(4 * levels, cols)]
    if rounds == 2:
        shapes += [held(3 * rows, cols), held(rows + TILE, cols)]
    return pl.pallas_call(
        functools.partial(fix_kernel, rounds, levels),
        out_shape=tuple(shapes),
        in_specs=[whole(VMEM)] * (8 + len(outer)),
        out_specs=[whole(VMEM)] * len(shapes),
        compiler_params=pltpu.CompilerParams(vmem_limit_bytes=8 * MIB),
        name="fix",
    )(
        other, far, near, fluxes, outward, in_vmem(forward), in_vmem(first), in_vmem(table), *outer
    )


def tends_kernel(rounds, table, tend, far, near, other, *rest):
    outer, rest = (rest[0], rest[1:]) if rounds > 2 else (None, rest)
    *outs, layers, strips, sems = rest
    _, levels, rows, cols = tend.shape
    inside, middle = pl.ds(1, levels - 2), pl.ds(TILE, rows - 2 * TILE)
    copies = []

    def send(field, at, src, dst):
        copies.append(pltpu.make_async_copy(src, dst, sems.at[field, at]))
        copies[-1].start()

    for field, out in enumerate(outs):
        send(field, 0, tend.at[field, inside, middle, :], out.at[inside, middle, :])
    diffs = side_changes(far, near)
    tile_at = lax.broadcasted_iota(jnp.int32, (TILE, cols), 0)
    for field, out in enumerate(outs):
        at = pl.ds(field * rows, rows)
        below, above = level_fluxes(other[at, :], 0.0 if outer is None else outer[at, :])
        for side, level, change in (
            (0, 0, table[0, pl.ds(RISE, 1), :] * below),
            (1, levels - 1, -table[levels - 1, pl.ds(FALL, 1), :] * above),
        ):
            at = field * levels + level
            rim = ends(rows, cols, diffs[0][at : at + 1, :], diffs[1][at : at + 1, :])
            layers[field, side] = tend[field, level] + change + rim
            send(field, 1 + side, layers.at[field, side], out.at[level])
        for side, begin, row in ((0, 0, 0), (1, rows - TILE, TILE - 1)):
            for level in range(1, levels - 1):
                at = field * levels + level
                edge = jnp.where(tile_at == row, diffs[side][at : at + 1, :], 0.0)
                strips[field, side, level] = tend[field, level, pl.ds(begin, TILE), :] + edge
            there = out.at[inside, pl.ds(begin, TILE), :]
            send(field, 3 + side, strips.at[field, side, inside], there)
    for copy in copies:
        copy.wait()


def tends(rounds, table, tend, far, near, other, outer):
    _, levels, rows, cols = tend.shape
    return pl.pallas_call(
        functools.partial(tends_kernel, rounds),
        out_shape=(jax.ShapeDtypeStruct((levels, rows, cols), F32),) * 2,
        in_specs=[whole(VMEM)] * (5 + len(outer)),
        out_specs=[whole(pl.ANY)] * 2,
        scratch_shapes=[
            pltpu.VMEM((2, 2, rows, cols), F32),
            pltpu.VMEM((2, 2, levels, TILE, cols), F32),
            pltpu.SemaphoreType.DMA((2, 5)),
        ],
        compiler_params=pltpu.CompilerParams(vmem_limit_bytes=8 * MIB),
        cost_estimate=pl.CostEstimate(
            flops=levels * rows * cols,
            bytes_accessed=8 * levels * rows * cols,
            transcendentals=0,
        ),
        name="tends",
    )(in_vmem(table), in_vmem(tend), far, near, other, *outer)


def merge_kernel(bit, final, late, own_at, other_at, mine, theirs, own, other, base, gains, *rest):
    _, rows, cols = base.shape
    upper = bit_of("gz", bit) == 1
    low, high = in_order(upper, scalar_rows(own, own_at), scalar_rows(other, other_at))
    coupling, inverse = interface(low, high)
    to_high, to_low = high[FIRST] * coupling, low[LAST] * coupling
    low_out, high_out = low[CORNER] * coupling, high[CORNER] * coupling
    core, size = bit_of("gz", 0) == 1, rows // 2
    sends_last = bit_of("gz", bit + 1) == 0
    for field in range(2):
        here = pl.ds(field * rows, rows)
        own_first, own_last = mine[here, :], mine[pl.ds((2 + field) * rows, rows), :]
        if late:
            low_last = jnp.where(upper, theirs[here, :], own_last)
            high_first = jnp.where(upper, own_first, theirs[here, :])
        else:
            other_first, other_last = theirs[here, :], theirs[pl.ds((2 + field) * rows, rows), :]
            low_last = jnp.where(upper, other_last, own_last)
            high_first = jnp.where(upper, own_first, other_first)
            low_first = jnp.where(upper, other_first, own_first)
            high_last = jnp.where(upper, own_last, other_last)
        above = inverse * (high_first + to_high * low_last)
        below = inverse * (low_last + to_low * high_first)
        base[field] = coupling * jnp.where(upper, below, above)
        more = jnp.where(sends_last, high_out * below, low_out * above)
        if late:
            outside = jnp.where(upper, own_last, own_first)
            outside = jnp.where(core, outside[size:], outside[:size])
            there = theirs[pl.ds(2 * rows + field * size, size), :]
            outside = jnp.where(sends_last == upper, outside, there)
        elif final:
            outside = jnp.where(sends_last, high_last, low_first)
            outside = jnp.where(core, outside[size:], outside[:size])
        if final:
            value = outside + jnp.where(core, more[size:], more[:size])
            rest[0][pl.ds(field * size, size), :] = value
        else:
            rest[0][here, :] = low_first + low_out * above
            rest[0][pl.ds((2 + field) * rows, rows), :] = high_last + high_out * below
    if not late:
        for at, value in enumerate(joint_scalars(low, high)):
            rest[1][pl.ds(at, 1), :] = value
    scale = coupling * inverse
    gains[...] = jnp.zeros(gains.shape, F32)
    gains[pl.ds(FROM_ABOVE, 1), :] = scale * high[CORNER] * jnp.where(upper, to_low, 1.0)
    gains[pl.ds(FROM_BELOW, 1), :] = scale * low[CORNER] * jnp.where(upper, 1.0, to_high)


def merge(bit, final, late, rows, mine, theirs, own, other):
    cols = mine.shape[1]
    shapes = [held(2, rows, cols), held(TILE, cols), held((1 if final else 4) * rows, cols)]
    if not late:
        shapes.append(held(TILE, cols))
    return pl.pallas_call(
        functools.partial(
            merge_kernel, bit, final, late, own.shape[0] - TILE, other.shape[0] - TILE
        ),
        out_shape=tuple(shapes),
        in_specs=[whole(VMEM)] * 4,
        out_specs=[whole(VMEM)] * len(shapes),
        compiler_params=pltpu.CompilerParams(vmem_limit_bytes=8 * MIB),
        name="merge",
    )(mine, theirs, own, other)


def prepare_kernel(
    rounds, temp, w_vel, forward, table, changes, fluxes, other, *rest
):
    outer, rest = (rest[0], rest[1:]) if rounds > 2 else (None, rest)
    bases, gains = rest[: rounds - 1], rest[rounds - 1 : 2 * rounds - 2]
    known, response, below_in, above_in = rest[2 * rounds - 2 :]
    levels, rows, cols = temp.shape
    upper = bit_of("gz", rounds - 1) == 1
    one, none = jnp.ones((1, cols), F32), jnp.zeros((1, cols), F32)
    below_gain, above_gain = jnp.where(upper, one, none), jnp.where(upper, none, one)
    below = above = None
    for step in range(rounds - 2, -1, -1):
        side = bit_of("gz", step) == 1
        from_above = gains[step][pl.ds(FROM_ABOVE, 1), :]
        from_below = gains[step][pl.ds(FROM_BELOW, 1), :]
        gain = from_above * above_gain + from_below * below_gain
        below_gain = jnp.where(side, gain, below_gain)
        above_gain = jnp.where(side, above_gain, gain)
        into = [bases[step][field] for field in range(2)]
        if below is None:
            below = above = [jnp.zeros((rows, cols), F32)] * 2
        else:
            into = [
                into[field] + from_above * above[field] + from_below * below[field]
                for field in range(2)
            ]
        below = [jnp.where(side, into[field], below[field]) for field in range(2)]
        above = [jnp.where(side, above[field], into[field]) for field in range(2)]
    scalars = scalar_rows(fluxes, 3 * rows)
    for field in range(2):
        at = pl.ds(field * rows, rows)
        flux_below, flux_above = level_fluxes(other[at, :], 0.0 if outer is None else outer[at, :])
        below_in[field] = below[field] + scalars[METRIC_BELOW] * flux_below
        above_in[field] = above[field] - scalars[METRIC_ABOVE] * flux_above

    gain = above_gain * table[levels - 1, pl.ds(PIVOT, 1), :]
    for level in range(levels - 1, -1, -1):
        if level < levels - 1:
            gain = gain * table[level, pl.ds(UPPER_PIVOT, 1), :]
        gain = gain + below_gain * table[level, pl.ds(BELOW_FORWARD, 1), :]
        response[level] = jnp.broadcast_to(gain, (TILE, cols))

    row_at = lax.broadcasted_iota(jnp.int32, (TILE, cols), 0)
    width = 2 * TILE
    for begin in range(0, rows, width):
        at = pl.ds(begin, width)

        def solve(level, carry, factor, begin=begin, at=at):
            factor = table[level, pl.ds(factor, 1), :]
            below_factor = table[level, pl.ds(BELOW_FORWARD, 1), :]
            values = []
            for field, cells in enumerate((temp, w_vel)):
                value = forward[field, level + 1, at, :] + below_factor * below_in[field, at, :]
                if begin == 0:
                    change = changes[pl.ds(field * levels + level, 1), :]
                    head = value[:TILE] + jnp.where(row_at == 0, change, 0.0)
                    value = jnp.concatenate([head, value[TILE:]])
                if begin == rows - width:
                    change = changes[pl.ds((2 + field) * levels + level, 1), :]
                    tail = value[-TILE:] + jnp.where(row_at == TILE - 1, change, 0.0)
                    value = jnp.concatenate([value[:-TILE], tail])
                value = value + factor * carry[field]
                known[field, level, at, :] = value - cells[level, at, :]
                values.append(value)
            return tuple(values)

        carry = solve(levels - 1, [above_in[field, at, :] for field in range(2)], PIVOT)

        def step(back, carry, solve=solve):
            return solve(levels - 2 - back, carry, UPPER_PIVOT)

        lax.fori_loop(0, levels - 1, step, carry, unroll=3)


def prepare(rounds, temp, w_vel, forward, table, changes, fluxes, other, outer, bases, gains):
    levels, rows, cols = temp.shape
    return pl.pallas_call(
        functools.partial(prepare_kernel, rounds),
        out_shape=(held(2, levels, rows, cols), held(levels, TILE, cols)),
        in_specs=[whole(VMEM)] * (7 + len(outer) + 2 * (rounds - 1)),
        out_specs=[whole(VMEM)] * 2,
        scratch_shapes=[pltpu.VMEM((2, rows, cols), F32)] * 2,
        compiler_params=pltpu.CompilerParams(vmem_limit_bytes=8 * MIB),
        cost_estimate=pl.CostEstimate(
            flops=levels * rows * cols,
            bytes_accessed=24 * levels * rows * cols,
            transcendentals=0,
        ),
        name="prepare",
    )(
        in_vmem(temp), in_vmem(w_vel), in_vmem(forward), in_vmem(table), changes, fluxes, other,
        *outer, *bases, *gains,
    )


def join_kernel(rounds, late, own_at, other_at, mine, theirs, own, other, joined):
    size = theirs.shape[0] // 2
    upper = bit_of("gz", rounds - 1) == 1
    low, high = in_order(upper, scalar_rows(own, own_at), scalar_rows(other, other_at))
    coupling, inverse = interface(low, high)
    scale = coupling * inverse
    to_other = scale * coupling * jnp.where(upper, low[LAST], high[FIRST])
    up, down = high[METRIC_BELOW] * inverse, -low[METRIC_ABOVE] * inverse
    own_gain = coupling * jnp.where(upper, down * low[LAST], up * high[FIRST])
    other_gain = jnp.where(upper, up, down)
    for field in range(2):
        at = pl.ds(field * size, size)
        into = scale * theirs[at, :] + to_other * mine[at, :]
        if late:
            flux = other[at, :]
            into = into + (own_gain * own[at, :] + other_gain * flux)
            joined[pl.ds((2 + field) * size, size), :] = flux
        joined[at, :] = into


def join(rounds, late, mine, theirs, own, other):
    size, cols = theirs.shape
    return pl.pallas_call(
        functools.partial(join_kernel, rounds, late, own.shape[0] - TILE, other.shape[0] - TILE),
        out_shape=held(size * (2 if late else 1), cols),
        in_specs=[whole(VMEM)] * 4,
        out_specs=whole(VMEM),
        compiler_params=pltpu.CompilerParams(vmem_limit_bytes=8 * MIB),
        name="join",
    )(mine, theirs, own, other)


def finish_kernel(rounds, swapped, known, response, joined, *rest):
    late, results = rounds == 2, 4 if rounds == 2 else 2
    table, tend, far, near = rest[:4] if late else (None,) * 4
    rest = rest[(4 if late else 0) + (results if swapped else results - 2) :]
    outs, (result, rim, sems) = rest[:results], rest[results:]
    _, levels, rows, cols = known.shape
    width, half = 2 * TILE, rows // 2
    core = bit_of("gz", 0)
    start = pl.multiple_of((1 - core if swapped else core) * half, half)
    copies = []
    if late:
        diffs = side_changes(far, near)
        level = core * (levels - 1)
        gain = jnp.where(
            core == 1, -table[levels - 1, pl.ds(FALL, 1), :], table[0, pl.ds(RISE, 1), :]
        )
        gain = jnp.where(beside_seam(rounds), gain, 0.0)
        row_at = start + lax.broadcasted_iota(jnp.int32, (half, cols), 0)
        for field in range(2):
            head, tail = (
                jnp.where(
                    core == 1,
                    diff[(field + 1) * levels - 1 : (field + 1) * levels, :],
                    diff[field * levels : field * levels + 1, :],
                )
                for diff in diffs
            )
            edge = jnp.where(row_at == 0, head, jnp.where(row_at == rows - 1, tail, 0.0))
            flux = joined[pl.ds((2 + field) * half, half), :]
            rim[field] = tend[field, level, pl.ds(start, half), :] + gain * flux + edge
            copies.append(
                pltpu.make_async_copy(
                    rim.at[field],
                    outs[2 + field].at[level, pl.ds(start, half), :],
                    sems.at[field],
                )
            )
            copies[-1].start()
    for field in range(2):
        for part, begin in enumerate(range(0, half, width)):
            into = joined[pl.ds(field * half + begin, width), :]
            tiles = [into[i : i + TILE] for i in range(0, width, TILE)]

            def step(level, carry, field=field, begin=begin, tiles=tiles):
                gain = response[level]
                for i, tile in enumerate(tiles):
                    at = begin + i * TILE
                    value = known[field, level, pl.ds(start + at, TILE), :] + gain * tile
                    result[field, level, pl.ds(at, TILE), :] = value
                return carry

            lax.fori_loop(0, levels, step, 0, unroll=4)
            copies.append(
                pltpu.make_async_copy(
                    result.at[field, :, pl.ds(begin, width), :],
                    outs[field].at[:, pl.ds(start + begin, width), :],
                    sems.at[2 + 2 * field + part],
                )
            )
            copies[-1].start()
    for copy in copies:
        copy.wait()


def finish(rounds, known, response, joined, late, written):
    _, levels, rows, cols = known.shape
    results = 4 if rounds == 2 else 2
    inputs = 3 + len(late)
    swapped = len(written) == results
    return pl.pallas_call(
        functools.partial(finish_kernel, rounds, swapped),
        out_shape=(jax.ShapeDtypeStruct((levels, rows, cols), F32),) * results,
        in_specs=[whole(VMEM)] * inputs + [whole(pl.ANY)] * len(written),
        out_specs=[whole(pl.ANY)] * results,
        scratch_shapes=[
            pltpu.VMEM((2, levels, rows // 2, cols), F32),
            pltpu.VMEM((2, rows // 2, cols), F32),
            pltpu.SemaphoreType.DMA((6,)),
        ],
        input_output_aliases={
            inputs + i: results - len(written) + i for i in range(len(written))
        },
        compiler_params=pltpu.CompilerParams(vmem_limit_bytes=8 * MIB),
        cost_estimate=pl.CostEstimate(
            flops=20000 * levels * rows * cols,
            bytes_accessed=8 * levels * rows * cols,
            transcendentals=0,
        ),
        name="finish",
    )(in_vmem(known), response, joined, *map(in_vmem, late), *written)


def both_ways(pairs):
    return pairs + [(b, a) for a, b in pairs]


def local(temp, u_vel, v_vel, w_vel, temp_prev, w_prev, lower, upper, metric):
    rows = temp.shape[1]
    across, stacked = lax.axis_size("gx"), lax.axis_size("gz")
    rounds = stacked.bit_length() - 1
    cores = both_ways([(i, i + 1) for i in range(0, stacked, 2)])
    far, near, fluxes, outward, table = edges(
        temp, u_vel, w_vel, v_vel, temp_prev, w_prev, lower, upper, metric
    )
    other = lax.ppermute(fluxes, "gz", cores)
    far = lax.ppermute(far, "gx", both_ways([(i, (i + 1) % across) for i in range(1, across, 2)]))
    near = lax.ppermute(near, "gx", both_ways([(i, i + 1) for i in range(0, across, 2)]))
    outer = ()
    if rounds > 2:
        seams = both_ways([(i, i + 1) for i in range(1, stacked - 1, 2)])
        outer = (lax.ppermute(outward, "gz", seams),)
    forward, tend, first = bulk(other, table, temp, u_vel, v_vel, w_vel, temp_prev, w_prev)
    entries, changes, *late = fix(
        rounds, other, far, near, fluxes, outward, forward, first, table, outer
    )
    message, seam = late if late else (entries, fluxes)
    bases, gains, own, other_own = [], [], fluxes, other
    for step in range(rounds - 1):
        partners = [(i, i ^ (1 << step)) for i in range(stacked)]
        theirs = lax.ppermute(message, "gz", partners)
        if step > 0:
            other_own = lax.ppermute(own, "gz", partners)
        base, gain, message, *scalars = merge(
            step, step + 2 == rounds, bool(late), rows, entries, theirs, own, other_own
        )
        entries, own = message, scalars[0] if scalars else seam
        bases.append(base)
        gains.append(gain)
    partners = [(i, i ^ (stacked // 2)) for i in range(stacked)]
    theirs = lax.ppermute(message, "gz", partners)
    other_own = lax.ppermute(own, "gz", partners)
    known, response = prepare(
        rounds, temp, w_vel, forward, table, changes, fluxes, other, outer, bases, gains
    )
    tendencies = tends(rounds, table, tend, far, near, other, outer)
    joined = join(rounds, bool(late), message, theirs, own, other_own)
    swapped = lax.ppermute(joined, "gz", cores)
    late = (table, tend, far, near) if late else ()
    written = finish(rounds, known, response, joined, late, tendencies if late else ())
    written = finish(rounds, known, response, swapped, late, written)
    return tuple(written) if late else (*written, *tendencies)


def solution(mesh):
    field = P("gz", "gx", None)
    return jax.shard_map(
        local,
        mesh=mesh,
        in_specs=(field,) * 6 + (P("gz"),) * 3,
        out_specs=(field,) * 4,
        check_vma=False,
    )
```

```python
import functools

import jax
import jax.numpy as jnp
from jax import lax
from jax.experimental import pallas as pl
from jax.experimental.pallas import tpu as pltpu
from jax.sharding import PartitionSpec as P

NEW_WEIGHT = 5.0 / 12.0
HORIZ_DIFF = 0.1
FIELD_WEIGHT = 2.0 / NEW_WEIGHT
PREV_WEIGHT = (17.0 / 60.0) / NEW_WEIGHT
TILE = 8
MIB = 1024 * 1024

PIVOT_NEW, LOWER_PIVOT, UPPER_PIVOT, FIRST_GREEN, BELOW_FORWARD, PIVOT, RISE, FALL = range(8)
FIRST, CORNER, LAST, BELOW, ABOVE, METRIC_BELOW, METRIC_ABOVE = range(7)
FROM_ABOVE, FROM_BELOW = range(2)

VMEM = pltpu.VMEM
F32 = jnp.float32


def whole(space):
    return pl.BlockSpec(memory_space=space)


def held(*shape):
    return pltpu.VMEM(shape, F32)


def in_vmem(array):
    return pltpu.with_memory_space_constraint(array, pltpu.VMEM)


def in_hbm(*arrays):
    return [pltpu.with_memory_space_constraint(array, pltpu.HBM) for array in arrays]


def bit_of(axis, bit):
    return (lax.axis_index(axis) >> bit) & 1


def edges_kernel(
    temp,
    u_vel,
    w_vel,
    v_vel,
    temp_prev,
    w_prev,
    lower,
    upper,
    metric,
    far,
    near,
    fluxes,
    outward,
    table,
    strips,
    layers,
    lower_at,
    upper_at,
    metric_at,
    sems,
):
    levels, rows, cols = temp.shape
    copies = [(lower, lower_at), (upper, upper_at), (metric, metric_at)]
    for at, array in enumerate((temp, w_vel, u_vel)):
        for side, first in enumerate((0, rows - TILE)):
            copies.append((array.at[:, pl.ds(first, TILE), :], strips.at[at, side]))
    for at, array in enumerate((temp, w_vel)):
        for side, level in enumerate((0, levels - 1)):
            copies.append((array.at[level], layers.at[at, side]))
    copies = [pltpu.make_async_copy(src, dst, sems.at[i]) for i, (src, dst) in enumerate(copies)]
    for copy in copies:
        copy.start()
    for copy in copies[:3]:
        copy.wait()
    coefficients(lower_at, upper_at, metric_at, table, fluxes.at[pl.ds(3 * rows, TILE)])
    for copy in copies[3:]:
        copy.wait()
    odd = bit_of("gx", 0) == 1
    last = TILE - 1
    for field in range(2):
        at = pl.ds(field * levels, levels)
        to_left = (HORIZ_DIFF - 0.5 * strips[2, 0, :, 0, :]) * strips[field, 0, :, 0, :]
        to_right = (HORIZ_DIFF + 0.5 * strips[2, 1, :, last, :]) * strips[field, 1, :, last, :]
        near[at, :] = jnp.where(odd, to_left, to_right)
        far[at, :] = jnp.where(odd, to_right, to_left)
    position = lax.axis_index("gz")
    upper_core = bit_of("gz", 0) == 1
    wall = (position == 0) | (position == lax.axis_size("gz") - 1)
    zero, size = jnp.zeros((rows, cols), F32), rows // 2
    for field in range(2):
        bottom = layers[1, 0] * layers[field, 0]
        top = layers[1, 1] * layers[field, 1]
        fluxes[pl.ds(field * rows, rows), :] = jnp.where(upper_core, bottom, top)
        value = jnp.where(wall, zero, jnp.where(upper_core, top, bottom))
        outward[pl.ds(field * rows, rows), :] = value
        fluxes[pl.ds(2 * rows + field * size, size), :] = jnp.where(
            upper_core, value[:size], value[size:]
        )


def edges(temp, u_vel, w_vel, v_vel, temp_prev, w_prev, lower, upper, metric):
    levels, rows, cols = temp.shape
    return pl.pallas_call(
        edges_kernel,
        out_shape=(
            held(2 * levels, cols),
            held(2 * levels, cols),
            held(3 * rows + TILE, cols),
            held(2 * rows, cols),
            held(levels, TILE, cols),
        ),
        in_specs=[whole(pl.ANY)] * 9,
        out_specs=[whole(VMEM)] * 5,
        scratch_shapes=[
            pltpu.VMEM((3, 2, levels, TILE, cols), F32),
            pltpu.VMEM((2, 2, rows, cols), F32),
            pltpu.SMEM((levels,), F32),
            pltpu.SMEM((levels,), F32),
            pltpu.SMEM((levels,), F32),
            pltpu.SemaphoreType.DMA((13,)),
        ],
        compiler_params=pltpu.CompilerParams(vmem_limit_bytes=8 * MIB),
        name="edges",
    )(*in_hbm(temp, u_vel, w_vel, v_vel, temp_prev, w_prev, lower, upper, metric))


def coefficients(lower, upper, metric, table, scalars):
    levels, _, cols = table.shape

    def row(value):
        return jnp.full((1, cols), value, F32)

    ratio = jnp.zeros((1, cols), F32)
    forward = jnp.ones((1, cols), F32)
    for level in range(levels):
        low, high = row(lower[level]), row(upper[level])
        pivot = 1.0 / (1.0 + low + high - low * ratio)
        ratio = high * pivot
        lower_pivot = low * pivot
        forward = pivot if level == 0 else lower_pivot * forward
        table[level, pl.ds(PIVOT_NEW, 1), :] = NEW_WEIGHT * pivot
        table[level, pl.ds(LOWER_PIVOT, 1), :] = lower_pivot
        table[level, pl.ds(UPPER_PIVOT, 1), :] = ratio
        table[level, pl.ds(BELOW_FORWARD, 1), :] = forward
        table[level, pl.ds(PIVOT, 1), :] = pivot
        table[level, pl.ds(RISE, 1), :] = row(metric[level] if level < levels - 1 else 0.0)
        table[level, pl.ds(FALL, 1), :] = row(metric[level] if level > 0 else 0.0)
    green = forward
    table[levels - 1, pl.ds(FIRST_GREEN, 1), :] = NEW_WEIGHT * green
    for level in range(levels - 2, -1, -1):
        green = (
            table[level, pl.ds(BELOW_FORWARD, 1), :]
            + table[level, pl.ds(UPPER_PIVOT, 1), :] * green
        )
        table[level, pl.ds(FIRST_GREEN, 1), :] = NEW_WEIGHT * green
    scalars[pl.ds(FIRST, 1), :] = green
    scalars[pl.ds(CORNER, 1), :] = forward
    scalars[pl.ds(LAST, 1), :] = pivot
    scalars[pl.ds(BELOW, 1), :] = row(lower[0])
    scalars[pl.ds(ABOVE, 1), :] = row(upper[levels - 1])
    scalars[pl.ds(METRIC_BELOW, 1), :] = row(NEW_WEIGHT * metric[0])
    scalars[pl.ds(METRIC_ABOVE, 1), :] = row(NEW_WEIGHT * metric[levels - 1])
    scalars[pl.ds(7, 1), :] = row(0.0)


def bulk_kernel(
    arrived,
    table,
    temp,
    u_vel,
    v_vel,
    w_vel,
    temp_prev,
    w_prev,
    forward,
    tend,
    first,
):
    levels, rows, cols = temp.shape
    strips = rows // TILE
    fields, prevs = (temp, w_vel), (temp_prev, w_prev)
    for field in range(2):
        forward[field, 0] = jnp.zeros((rows, cols), F32)
        first[field] = jnp.zeros((rows, cols), F32)
    row_at = lax.broadcasted_iota(jnp.int32, (TILE, cols), 0)
    zero = jnp.zeros((TILE, cols), F32)

    def level_step(level, carry):
        def spread(at):
            return jnp.broadcast_to(table[level, pl.ds(at, 1), :], (TILE, cols))

        pivot, lower_pivot, green = spread(PIVOT_NEW), spread(LOWER_PIVOT), spread(FIRST_GREEN)
        rise, fall = spread(RISE), spread(FALL)
        over = jnp.minimum(level + 1, levels - 1)
        under = jnp.maximum(level - 1, 0)

        def sides(strip):
            at = pl.ds(strip * TILE, TILE)
            half = 0.5 * u_vel[level, at, :]
            back, ahead = HORIZ_DIFF - half, HORIZ_DIFF + half
            here = [values[level, at, :] for values in fields]
            return (
                here,
                [pltpu.roll(back * value, TILE - 1, 0) for value in here],
                [pltpu.roll(ahead * value, 1, 0) for value in here],
            )

        before = [zero, zero]
        here, back, ahead = sides(0)
        for strip in range(strips):
            after = sides(strip + 1) if strip + 1 < strips else (None, [zero, zero], None)
            at = pl.ds(strip * TILE, TILE)
            half = 0.5 * v_vel[level, at, :]
            v_back, v_ahead = HORIZ_DIFF - half, HORIZ_DIFF + half
            w_over = rise * w_vel[over, at, :]
            w_under = fall * w_vel[under, at, :]
            for field in range(2):
                value = here[field]
                change = jnp.where(row_at == TILE - 1, after[1][field], back[field])
                change = change + jnp.where(row_at == 0, before[field], ahead[field])
                change = change + pltpu.roll(v_back * value, cols - 1, 1)
                change = change + pltpu.roll(v_ahead * value, 1, 1)
                change = change - w_over * fields[field][over, at, :]
                change = change + w_under * fields[field][under, at, :]
                change = change + (here[1 - field] - (4.0 * HORIZ_DIFF) * value)
                tend[field, level, at, :] = change
                right = change + (FIELD_WEIGHT * value - PREV_WEIGHT * prevs[field][level, at, :])
                forward[field, level + 1, at, :] = (
                    pivot * right + lower_pivot * forward[field, level, at, :]
                )
                first[field, at, :] = first[field, at, :] + green * right
            before = ahead
            here, back, ahead = after
        return carry

    lax.fori_loop(0, levels, level_step, 0)


def bulk(arrived, table, *arrays):
    levels, rows, cols = arrays[0].shape
    return pl.pallas_call(
        bulk_kernel,
        out_shape=(
            held(2, levels + 1, rows, cols),
            held(2, levels, rows, cols),
            held(2, rows, cols),
        ),
        in_specs=[whole(pl.ANY)] + [whole(VMEM)] * 7,
        out_specs=[whole(VMEM)] * 3,
        compiler_params=pltpu.CompilerParams(vmem_limit_bytes=8 * MIB),
        cost_estimate=pl.CostEstimate(
            flops=100000 * levels * rows * cols,
            bytes_accessed=24 * levels * rows * cols,
            transcendentals=0,
        ),
        name="bulk",
    )(arrived, *map(in_vmem, (table, *arrays)))


def side_changes(far, near):
    odd = bit_of("gx", 0) == 1
    return jnp.where(odd, near[...], far[...]), jnp.where(odd, far[...], near[...])


def level_fluxes(inner, outer):
    upper = bit_of("gz", 0) == 1
    return jnp.where(upper, inner, outer), jnp.where(upper, outer, inner)


def beside_seam(rounds):
    return bit_of("gz", 0) != bit_of("gz", rounds - 1)


def ends(rows, cols, head, tail):
    at = lax.broadcasted_iota(jnp.int32, (rows, cols), 0)
    return jnp.where(at == 0, head, jnp.where(at == rows - 1, tail, 0.0))


def scalar_rows(ref, begin=0):
    return [ref[pl.ds(begin + at, 1), :] for at in range(7)]


def in_order(upper, own, other):
    low = [jnp.where(upper, b, a) for a, b in zip(own, other)]
    high = [jnp.where(upper, a, b) for a, b in zip(own, other)]
    return low, high


def interface(low, high):
    coupling = low[ABOVE]
    return coupling, 1.0 / (1.0 - coupling * coupling * low[LAST] * high[FIRST])


def joint_scalars(low, high):
    coupling, inverse = interface(low, high)
    low_out, high_out = low[CORNER] * coupling, high[CORNER] * coupling
    return [
        low[FIRST] + low_out * low_out * inverse * high[FIRST],
        low_out * inverse * high[CORNER],
        high[LAST] + high_out * high_out * inverse * low[LAST],
        low[BELOW],
        high[ABOVE],
        low[METRIC_BELOW],
        high[METRIC_ABOVE],
        jnp.zeros_like(coupling),
    ]


def fix_kernel(
    rounds, levels, other, near, far, fluxes, outward, forward, first, table, *rest
):
    outer, rest = (rest[0], rest[1:]) if rounds > 2 else (None, rest)
    entries, changes, *late = rest
    _, rows, cols = first.shape
    diffs = side_changes(far, near)
    scalars = scalar_rows(fluxes, 3 * rows)
    below, above = scalars[METRIC_BELOW], -scalars[METRIC_ABOVE]
    core, size = bit_of("gz", 0) == 1, rows // 2
    for field in range(2):
        firsts, lasts = [], []
        for side in range(2):
            value = jnp.zeros((1, cols), F32)
            total = jnp.zeros((1, cols), F32)
            for level in range(levels):
                right = diffs[side][field * levels + level : field * levels + level + 1, :]
                value = (
                    table[level, pl.ds(PIVOT_NEW, 1), :] * right
                    + table[level, pl.ds(LOWER_PIVOT, 1), :] * value
                )
                total = total + table[level, pl.ds(FIRST_GREEN, 1), :] * right
                changes[pl.ds((side * 2 + field) * levels + level, 1), :] = value
            firsts.append(total)
            lasts.append(value)
        at = pl.ds(field * rows, rows)
        flux_below, flux_above = level_fluxes(other[at, :], 0.0 if outer is None else outer[at, :])
        first_entry = (
            first[field]
            + (below * scalars[FIRST]) * flux_below
            + (above * scalars[CORNER]) * flux_above
            + ends(rows, cols, *firsts)
        )
        last_entry = (
            forward[field, levels]
            + (below * scalars[CORNER]) * flux_below
            + (above * scalars[LAST]) * flux_above
            + ends(rows, cols, *lasts)
        )
        entries[at, :] = first_entry
        entries[pl.ds((2 + field) * rows, rows), :] = last_entry
        if late:
            message, seam = late
            message[at, :] = jnp.where(core, first_entry, last_entry)
            there = pl.ds(2 * rows + field * size, size)
            message[there, :] = jnp.where(core, last_entry[:size], first_entry[size:])
            value = outward[at, :]
            value = jnp.where(core, value[size:], value[:size])
            seam[pl.ds(field * size, size), :] = jnp.where(
                beside_seam(rounds), value, other[there, :]
            )
    if late:
        far_scalars = scalar_rows(other, 3 * rows)
        for at, value in enumerate(joint_scalars(*in_order(core, scalars, far_scalars))):
            seam[pl.ds(rows + at, 1), :] = value


def fix(rounds, other, near, far, fluxes, outward, forward, first, table, outer):
    levels = table.shape[0]
    _, rows, cols = first.shape
    shapes = [held(4 * rows, cols), held(4 * levels, cols)]
    if rounds == 2:
        shapes += [held(3 * rows, cols), held(rows + TILE, cols)]
    return pl.pallas_call(
        functools.partial(fix_kernel, rounds, levels),
        out_shape=tuple(shapes),
        in_specs=[whole(VMEM)] * (8 + len(outer)),
        out_specs=[whole(VMEM)] * len(shapes),
        compiler_params=pltpu.CompilerParams(vmem_limit_bytes=8 * MIB),
        name="fix",
    )(
        other, near, far, fluxes, outward, in_vmem(forward), in_vmem(first), in_vmem(table), *outer
    )


def tends_kernel(rounds, table, tend, far, near, other, *rest):
    outer, rest = (rest[0], rest[1:]) if rounds > 2 else (None, rest)
    *outs, layers, strips, sems = rest
    _, levels, rows, cols = tend.shape
    inside, middle = pl.ds(1, levels - 2), pl.ds(TILE, rows - 2 * TILE)
    copies = []

    def send(field, at, src, dst):
        copies.append(pltpu.make_async_copy(src, dst, sems.at[field, at]))
        copies[-1].start()

    for field, out in enumerate(outs):
        send(field, 0, tend.at[field, inside, middle, :], out.at[inside, middle, :])
    diffs = side_changes(far, near)
    tile_at = lax.broadcasted_iota(jnp.int32, (TILE, cols), 0)
    for field, out in enumerate(outs):
        at = pl.ds(field * rows, rows)
        below, above = level_fluxes(other[at, :], 0.0 if outer is None else outer[at, :])
        for side, level, change in (
            (0, 0, table[0, pl.ds(RISE, 1), :] * below),
            (1, levels - 1, -table[levels - 1, pl.ds(FALL, 1), :] * above),
        ):
            at = field * levels + level
            rim = ends(rows, cols, diffs[0][at : at + 1, :], diffs[1][at : at + 1, :])
            layers[field, side] = tend[field, level] + change + rim
            send(field, 1 + side, layers.at[field, side], out.at[level])
        for side, begin, row in ((0, 0, 0), (1, rows - TILE, TILE - 1)):
            for level in range(1, levels - 1):
                at = field * levels + level
                edge = jnp.where(tile_at == row, diffs[side][at : at + 1, :], 0.0)
                strips[field, side, level] = tend[field, level, pl.ds(begin, TILE), :] + edge
            there = out.at[inside, pl.ds(begin, TILE), :]
            send(field, 3 + side, strips.at[field, side, inside], there)
    for copy in copies:
        copy.wait()


def tends(rounds, table, tend, far, near, other, outer):
    _, levels, rows, cols = tend.shape
    return pl.pallas_call(
        functools.partial(tends_kernel, rounds),
        out_shape=(jax.ShapeDtypeStruct((levels, rows, cols), F32),) * 2,
        in_specs=[whole(VMEM)] * (5 + len(outer)),
        out_specs=[whole(pl.ANY)] * 2,
        scratch_shapes=[
            pltpu.VMEM((2, 2, rows, cols), F32),
            pltpu.VMEM((2, 2, levels, TILE, cols), F32),
            pltpu.SemaphoreType.DMA((2, 5)),
        ],
        compiler_params=pltpu.CompilerParams(vmem_limit_bytes=8 * MIB),
        cost_estimate=pl.CostEstimate(
            flops=levels * rows * cols,
            bytes_accessed=8 * levels * rows * cols,
            transcendentals=0,
        ),
        name="tends",
    )(in_vmem(table), in_vmem(tend), far, near, other, *outer)


def merge_kernel(bit, final, late, own_at, other_at, mine, theirs, own, other, base, gains, *rest):
    _, rows, cols = base.shape
    upper = bit_of("gz", bit) == 1
    low, high = in_order(upper, scalar_rows(own, own_at), scalar_rows(other, other_at))
    coupling, inverse = interface(low, high)
    to_high, to_low = high[FIRST] * coupling, low[LAST] * coupling
    low_out, high_out = low[CORNER] * coupling, high[CORNER] * coupling
    core, size = bit_of("gz", 0) == 1, rows // 2
    sends_last = bit_of("gz", bit + 1) == 0
    for field in range(2):
        here = pl.ds(field * rows, rows)
        own_first, own_last = mine[here, :], mine[pl.ds((2 + field) * rows, rows), :]
        if late:
            low_last = jnp.where(upper, theirs[here, :], own_last)
            high_first = jnp.where(upper, own_first, theirs[here, :])
        else:
            other_first, other_last = theirs[here, :], theirs[pl.ds((2 + field) * rows, rows), :]
            low_last = jnp.where(upper, other_last, own_last)
            high_first = jnp.where(upper, own_first, other_first)
            low_first = jnp.where(upper, other_first, own_first)
            high_last = jnp.where(upper, own_last, other_last)
        above = inverse * (high_first + to_high * low_last)
        below = inverse * (low_last + to_low * high_first)
        base[field] = coupling * jnp.where(upper, below, above)
        more = jnp.where(sends_last, high_out * below, low_out * above)
        if late:
            outside = jnp.where(upper, own_last, own_first)
            outside = jnp.where(core, outside[size:], outside[:size])
            there = theirs[pl.ds(2 * rows + field * size, size), :]
            outside = jnp.where(sends_last == upper, outside, there)
        elif final:
            outside = jnp.where(sends_last, high_last, low_first)
            outside = jnp.where(core, outside[size:], outside[:size])
        if final:
            value = outside + jnp.where(core, more[size:], more[:size])
            rest[0][pl.ds(field * size, size), :] = value
        else:
            rest[0][here, :] = low_first + low_out * above
            rest[0][pl.ds((2 + field) * rows, rows), :] = high_last + high_out * below
    if not late:
        for at, value in enumerate(joint_scalars(low, high)):
            rest[1][pl.ds(at, 1), :] = value
    scale = coupling * inverse
    gains[...] = jnp.zeros(gains.shape, F32)
    gains[pl.ds(FROM_ABOVE, 1), :] = scale * high[CORNER] * jnp.where(upper, to_low, 1.0)
    gains[pl.ds(FROM_BELOW, 1), :] = scale * low[CORNER] * jnp.where(upper, 1.0, to_high)


def merge(bit, final, late, rows, mine, theirs, own, other):
    cols = mine.shape[1]
    shapes = [held(2, rows, cols), held(TILE, cols), held((1 if final else 4) * rows, cols)]
    if not late:
        shapes.append(held(TILE, cols))
    return pl.pallas_call(
        functools.partial(
            merge_kernel, bit, final, late, own.shape[0] - TILE, other.shape[0] - TILE
        ),
        out_shape=tuple(shapes),
        in_specs=[whole(VMEM)] * 4,
        out_specs=[whole(VMEM)] * len(shapes),
        compiler_params=pltpu.CompilerParams(vmem_limit_bytes=8 * MIB),
        name="merge",
    )(mine, theirs, own, other)


def prepare_kernel(
    rounds, temp, w_vel, forward, table, changes, fluxes, other, crossing, *rest
):
    outer = crossing if rounds > 2 else None
    bases, gains = rest[: rounds - 1], rest[rounds - 1 : 2 * rounds - 2]
    known, response, *passed, below_in, above_in = rest[2 * rounds - 2 :]
    if passed:
        passed[0][...] = crossing[pl.ds(0, passed[0].shape[0]), :]
    levels, rows, cols = temp.shape
    upper = bit_of("gz", rounds - 1) == 1
    one, none = jnp.ones((1, cols), F32), jnp.zeros((1, cols), F32)
    below_gain, above_gain = jnp.where(upper, one, none), jnp.where(upper, none, one)
    below = above = None
    for step in range(rounds - 2, -1, -1):
        side = bit_of("gz", step) == 1
        from_above = gains[step][pl.ds(FROM_ABOVE, 1), :]
        from_below = gains[step][pl.ds(FROM_BELOW, 1), :]
        gain = from_above * above_gain + from_below * below_gain
        below_gain = jnp.where(side, gain, below_gain)
        above_gain = jnp.where(side, above_gain, gain)
        into = [bases[step][field] for field in range(2)]
        if below is None:
            below = above = [jnp.zeros((rows, cols), F32)] * 2
        else:
            into = [
                into[field] + from_above * above[field] + from_below * below[field]
                for field in range(2)
            ]
        below = [jnp.where(side, into[field], below[field]) for field in range(2)]
        above = [jnp.where(side, above[field], into[field]) for field in range(2)]
    scalars = scalar_rows(fluxes, 3 * rows)
    for field in range(2):
        at = pl.ds(field * rows, rows)
        flux_below, flux_above = level_fluxes(other[at, :], 0.0 if outer is None else outer[at, :])
        below_in[field] = below[field] + scalars[METRIC_BELOW] * flux_below
        above_in[field] = above[field] - scalars[METRIC_ABOVE] * flux_above

    gain = above_gain * table[levels - 1, pl.ds(PIVOT, 1), :]
    for level in range(levels - 1, -1, -1):
        if level < levels - 1:
            gain = gain * table[level, pl.ds(UPPER_PIVOT, 1), :]
        gain = gain + below_gain * table[level, pl.ds(BELOW_FORWARD, 1), :]
        response[level] = jnp.broadcast_to(gain, (TILE, cols))

    row_at = lax.broadcasted_iota(jnp.int32, (TILE, cols), 0)
    width = 2 * TILE
    for begin in range(0, rows, width):
        at = pl.ds(begin, width)

        def solve(level, carry, factor, begin=begin, at=at):
            factor = table[level, pl.ds(factor, 1), :]
            below_factor = table[level, pl.ds(BELOW_FORWARD, 1), :]
            values = []
            for field, cells in enumerate((temp, w_vel)):
                value = forward[field, level + 1, at, :] + below_factor * below_in[field, at, :]
                if begin == 0:
                    change = changes[pl.ds(field * levels + level, 1), :]
                    head = value[:TILE] + jnp.where(row_at == 0, change, 0.0)
                    value = jnp.concatenate([head, value[TILE:]])
                if begin == rows - width:
                    change = changes[pl.ds((2 + field) * levels + level, 1), :]
                    tail = value[-TILE:] + jnp.where(row_at == TILE - 1, change, 0.0)
                    value = jnp.concatenate([value[:-TILE], tail])
                value = value + factor * carry[field]
                known[field, level, at, :] = value - cells[level, at, :]
                values.append(value)
            return tuple(values)

        carry = solve(levels - 1, [above_in[field, at, :] for field in range(2)], PIVOT)

        def step(back, carry, solve=solve):
            return solve(levels - 2 - back, carry, UPPER_PIVOT)

        lax.fori_loop(0, levels - 1, step, carry, unroll=3)


def prepare(rounds, temp, w_vel, forward, table, changes, fluxes, other, crossing, bases, gains):
    levels, rows, cols = temp.shape
    shapes = (held(2, levels, rows, cols), held(levels, TILE, cols))
    shapes += (held(rows, cols),) * (rounds == 2)
    return pl.pallas_call(
        functools.partial(prepare_kernel, rounds),
        out_shape=shapes,
        in_specs=[whole(VMEM)] * (8 + 2 * (rounds - 1)),
        out_specs=[whole(VMEM)] * len(shapes),
        scratch_shapes=[pltpu.VMEM((2, rows, cols), F32)] * 2,
        compiler_params=pltpu.CompilerParams(vmem_limit_bytes=8 * MIB),
        cost_estimate=pl.CostEstimate(
            flops=levels * rows * cols,
            bytes_accessed=24 * levels * rows * cols,
            transcendentals=0,
        ),
        name="prepare",
    )(
        in_vmem(temp), in_vmem(w_vel), in_vmem(forward), in_vmem(table), changes, fluxes, other,
        crossing, *bases, *gains,
    )


def join_kernel(rounds, late, own_at, other_at, mine, theirs, own, other, joined):
    size = theirs.shape[0] // 2
    upper = bit_of("gz", rounds - 1) == 1
    low, high = in_order(upper, scalar_rows(own, own_at), scalar_rows(other, other_at))
    coupling, inverse = interface(low, high)
    scale = coupling * inverse
    to_other = scale * coupling * jnp.where(upper, low[LAST], high[FIRST])
    up, down = high[METRIC_BELOW] * inverse, -low[METRIC_ABOVE] * inverse
    own_gain = coupling * jnp.where(upper, down * low[LAST], up * high[FIRST])
    other_gain = jnp.where(upper, up, down)
    for field in range(2):
        at = pl.ds(field * size, size)
        into = scale * theirs[at, :] + to_other * mine[at, :]
        if late:
            into = into + (own_gain * own[at, :] + other_gain * other[at, :])
        joined[at, :] = into


def join(rounds, late, mine, theirs, own, other):
    size, cols = theirs.shape
    return pl.pallas_call(
        functools.partial(join_kernel, rounds, late, own.shape[0] - TILE, other.shape[0] - TILE),
        out_shape=held(size, cols),
        in_specs=[whole(VMEM)] * 4,
        out_specs=whole(VMEM),
        compiler_params=pltpu.CompilerParams(vmem_limit_bytes=8 * MIB),
        name="join",
    )(mine, theirs, own, other)


def finish_kernel(rounds, swapped, known, response, joined, *rest):
    late, results = rounds == 2, 4 if rounds == 2 else 2
    flux_in, table, tend, far, near = rest[:5] if late else (None,) * 5
    rest = rest[(5 if late else 0) + (results if swapped else results - 2) :]
    outs, (result, rim, sems) = rest[:results], rest[results:]
    _, levels, rows, cols = known.shape
    width, half = 2 * TILE, rows // 2
    core = bit_of("gz", 0)
    start = pl.multiple_of((1 - core if swapped else core) * half, half)
    copies = []
    if late:
        diffs = side_changes(far, near)
        level = core * (levels - 1)
        gain = jnp.where(
            core == 1, -table[levels - 1, pl.ds(FALL, 1), :], table[0, pl.ds(RISE, 1), :]
        )
        gain = jnp.where(beside_seam(rounds), gain, 0.0)
        row_at = start + lax.broadcasted_iota(jnp.int32, (half, cols), 0)
        for field in range(2):
            head, tail = (
                jnp.where(
                    core == 1,
                    diff[(field + 1) * levels - 1 : (field + 1) * levels, :],
                    diff[field * levels : field * levels + 1, :],
                )
                for diff in diffs
            )
            edge = jnp.where(row_at == 0, head, jnp.where(row_at == rows - 1, tail, 0.0))
            flux = flux_in[pl.ds(field * half, half), :]
            rim[field] = tend[field, level, pl.ds(start, half), :] + gain * flux + edge
            copies.append(
                pltpu.make_async_copy(
                    rim.at[field],
                    outs[2 + field].at[level, pl.ds(start, half), :],
                    sems.at[field],
                )
            )
            copies[-1].start()
    for field in range(2):
        for part, begin in enumerate(range(0, half, width)):
            into = joined[pl.ds(field * half + begin, width), :]
            tiles = [into[i : i + TILE] for i in range(0, width, TILE)]

            def step(level, carry, field=field, begin=begin, tiles=tiles):
                gain = response[level]
                for i, tile in enumerate(tiles):
                    at = begin + i * TILE
                    value = known[field, level, pl.ds(start + at, TILE), :] + gain * tile
                    result[field, level, pl.ds(at, TILE), :] = value
                return carry

            lax.fori_loop(0, levels, step, 0, unroll=4)
            copies.append(
                pltpu.make_async_copy(
                    result.at[field, :, pl.ds(begin, width), :],
                    outs[field].at[:, pl.ds(start + begin, width), :],
                    sems.at[2 + 2 * field + part],
                )
            )
            copies[-1].start()
    for copy in copies:
        copy.wait()


def finish(rounds, known, response, joined, late, written):
    _, levels, rows, cols = known.shape
    results = 4 if rounds == 2 else 2
    inputs = 3 + len(late)
    swapped = len(written) == results
    return pl.pallas_call(
        functools.partial(finish_kernel, rounds, swapped),
        out_shape=(jax.ShapeDtypeStruct((levels, rows, cols), F32),) * results,
        in_specs=[whole(VMEM)] * inputs + [whole(pl.ANY)] * len(written),
        out_specs=[whole(pl.ANY)] * results,
        scratch_shapes=[
            pltpu.VMEM((2, levels, rows // 2, cols), F32),
            pltpu.VMEM((2, rows // 2, cols), F32),
            pltpu.SemaphoreType.DMA((6,)),
        ],
        input_output_aliases={
            inputs + i: results - len(written) + i for i in range(len(written))
        },
        compiler_params=pltpu.CompilerParams(vmem_limit_bytes=8 * MIB),
        cost_estimate=pl.CostEstimate(
            flops=20000 * levels * rows * cols,
            bytes_accessed=8 * levels * rows * cols,
            transcendentals=0,
        ),
        name="finish",
    )(in_vmem(known), response, joined, *map(in_vmem, late), *written)


def both_ways(pairs):
    return pairs + [(b, a) for a, b in pairs]


def local(temp, u_vel, v_vel, w_vel, temp_prev, w_prev, lower, upper, metric):
    rows = temp.shape[1]
    across, stacked = lax.axis_size("gx"), lax.axis_size("gz")
    rounds = stacked.bit_length() - 1
    cores = both_ways([(i, i + 1) for i in range(0, stacked, 2)])
    far, near, fluxes, outward, table = edges(
        temp, u_vel, w_vel, v_vel, temp_prev, w_prev, lower, upper, metric
    )
    other = lax.ppermute(fluxes, "gz", cores)
    near = lax.ppermute(near, "gx", both_ways([(i, i + 1) for i in range(0, across, 2)]))
    far = lax.ppermute(far, "gx", both_ways([(i, (i + 1) % across) for i in range(1, across, 2)]))
    outer = ()
    if rounds > 2:
        seams = both_ways([(i, i + 1) for i in range(1, stacked - 1, 2)])
        outer = (lax.ppermute(outward, "gz", seams),)
    forward, tend, first = bulk(other, table, temp, u_vel, v_vel, w_vel, temp_prev, w_prev)
    entries, changes, *late = fix(
        rounds, other, near, far, fluxes, outward, forward, first, table, outer
    )
    message, seam = late if late else (entries, fluxes)
    bases, gains, own, other_own = [], [], fluxes, other
    for step in range(rounds - 1):
        partners = [(i, i ^ (1 << step)) for i in range(stacked)]
        theirs = lax.ppermute(message, "gz", partners)
        if step > 0:
            other_own = lax.ppermute(own, "gz", partners)
        base, gain, message, *scalars = merge(
            step, step + 2 == rounds, bool(late), rows, entries, theirs, own, other_own
        )
        entries, own = message, scalars[0] if scalars else seam
        bases.append(base)
        gains.append(gain)
    partners = [(i, i ^ (stacked // 2)) for i in range(stacked)]
    theirs = lax.ppermute(message, "gz", partners)
    other_own = lax.ppermute(own, "gz", partners)
    known, response, *passed = prepare(
        rounds, temp, w_vel, forward, table, changes, fluxes, other, *(outer or (other_own,)),
        bases, gains,
    )
    tendencies = tends(rounds, table, tend, far, near, other, outer)
    joined = join(rounds, bool(late), message, theirs, own, other_own)
    swapped = lax.ppermute(joined, "gz", cores)
    if not late:
        written = finish(rounds, known, response, joined, (), ())
        return *finish(rounds, known, response, swapped, (), written), *tendencies
    crossed = lax.ppermute(passed[0], "gz", cores)
    late = (table, tend, far, near)
    written = finish(rounds, known, response, joined, (other_own, *late), tendencies)
    return tuple(finish(rounds, known, response, swapped, (crossed, *late), written))


def solution(mesh):
    field = P("gz", "gx", None)
    return jax.shard_map(
        local,
        mesh=mesh,
        in_specs=(field,) * 6 + (P("gz"),) * 3,
        out_specs=(field,) * 4,
        check_vma=False,
    )
```

```python
import functools

import jax
import jax.numpy as jnp
from jax import lax
from jax.experimental import pallas as pl
from jax.experimental.pallas import tpu as pltpu
from jax.sharding import PartitionSpec as P

NEW_WEIGHT = 5.0 / 12.0
HORIZ_DIFF = 0.1
FIELD_WEIGHT = 2.0 / NEW_WEIGHT
PREV_WEIGHT = (17.0 / 60.0) / NEW_WEIGHT
TILE = 8
MIB = 1024 * 1024

PIVOT_NEW, LOWER_PIVOT, UPPER_PIVOT, FIRST_GREEN, BELOW_FORWARD, PIVOT, RISE, FALL = range(8)
FIRST, CORNER, LAST, BELOW, ABOVE, METRIC_BELOW, METRIC_ABOVE = range(7)
FROM_ABOVE, FROM_BELOW = range(2)

VMEM = pltpu.VMEM
F32 = jnp.float32


def whole(space):
    return pl.BlockSpec(memory_space=space)


def held(*shape):
    return pltpu.VMEM(shape, F32)


def in_vmem(array):
    return pltpu.with_memory_space_constraint(array, pltpu.VMEM)


def in_hbm(*arrays):
    return [pltpu.with_memory_space_constraint(array, pltpu.HBM) for array in arrays]


def bit_of(axis, bit):
    return (lax.axis_index(axis) >> bit) & 1


def edges_kernel(
    temp,
    u_vel,
    w_vel,
    v_vel,
    temp_prev,
    w_prev,
    lower,
    upper,
    metric,
    far,
    near,
    fluxes,
    outward,
    table,
    strips,
    layers,
    lower_at,
    upper_at,
    metric_at,
    sems,
):
    levels, rows, cols = temp.shape
    copies = [(lower, lower_at), (upper, upper_at), (metric, metric_at)]
    for at, array in enumerate((temp, w_vel, u_vel)):
        for side, row in enumerate((0, rows - 1)):
            copies.append((array.at[:, row, :], strips.at[at, side]))
    for at, array in enumerate((temp, w_vel)):
        for side, level in enumerate((0, levels - 1)):
            copies.append((array.at[level], layers.at[at, side]))
    copies = [pltpu.make_async_copy(src, dst, sems.at[i]) for i, (src, dst) in enumerate(copies)]
    for copy in copies:
        copy.start()
    for copy in copies[:3]:
        copy.wait()
    coefficients(lower_at, upper_at, metric_at, table, fluxes.at[pl.ds(3 * rows, TILE)])
    for copy in copies[3:]:
        copy.wait()
    odd = bit_of("gx", 0) == 1
    for field in range(2):
        at = pl.ds(field * levels, levels)
        to_left = (HORIZ_DIFF - 0.5 * strips[2, 0]) * strips[field, 0]
        to_right = (HORIZ_DIFF + 0.5 * strips[2, 1]) * strips[field, 1]
        near[at, :] = jnp.where(odd, to_left, to_right)
        far[at, :] = jnp.where(odd, to_right, to_left)
    position = lax.axis_index("gz")
    upper_core = bit_of("gz", 0) == 1
    wall = (position == 0) | (position == lax.axis_size("gz") - 1)
    zero, size = jnp.zeros((rows, cols), F32), rows // 2
    for field in range(2):
        bottom = layers[1, 0] * layers[field, 0]
        top = layers[1, 1] * layers[field, 1]
        fluxes[pl.ds(field * rows, rows), :] = jnp.where(upper_core, bottom, top)
        value = jnp.where(wall, zero, jnp.where(upper_core, top, bottom))
        outward[pl.ds(field * rows, rows), :] = value
        fluxes[pl.ds(2 * rows + field * size, size), :] = jnp.where(
            upper_core, value[:size], value[size:]
        )


def edges(temp, u_vel, w_vel, v_vel, temp_prev, w_prev, lower, upper, metric):
    levels, rows, cols = temp.shape
    return pl.pallas_call(
        edges_kernel,
        out_shape=(
            held(2 * levels, cols),
            held(2 * levels, cols),
            held(3 * rows + TILE, cols),
            held(2 * rows, cols),
            held(levels, TILE, cols),
        ),
        in_specs=[whole(pl.ANY)] * 9,
        out_specs=[whole(VMEM)] * 5,
        scratch_shapes=[
            pltpu.VMEM((3, 2, levels, cols), F32),
            pltpu.VMEM((2, 2, rows, cols), F32),
            pltpu.SMEM((levels,), F32),
            pltpu.SMEM((levels,), F32),
            pltpu.SMEM((levels,), F32),
            pltpu.SemaphoreType.DMA((13,)),
        ],
        compiler_params=pltpu.CompilerParams(vmem_limit_bytes=8 * MIB),
        name="edges",
    )(*in_hbm(temp, u_vel, w_vel, v_vel, temp_prev, w_prev, lower, upper, metric))


def coefficients(lower, upper, metric, table, scalars):
    levels, _, cols = table.shape

    def row(value):
        return jnp.full((1, cols), value, F32)

    ratio = jnp.zeros((1, cols), F32)
    forward = jnp.ones((1, cols), F32)
    for level in range(levels):
        low, high = row(lower[level]), row(upper[level])
        pivot = 1.0 / (1.0 + low + high - low * ratio)
        ratio = high * pivot
        lower_pivot = low * pivot
        forward = pivot if level == 0 else lower_pivot * forward
        table[level, pl.ds(PIVOT_NEW, 1), :] = NEW_WEIGHT * pivot
        table[level, pl.ds(LOWER_PIVOT, 1), :] = lower_pivot
        table[level, pl.ds(UPPER_PIVOT, 1), :] = ratio
        table[level, pl.ds(BELOW_FORWARD, 1), :] = forward
        table[level, pl.ds(PIVOT, 1), :] = pivot
        table[level, pl.ds(RISE, 1), :] = row(metric[level] if level < levels - 1 else 0.0)
        table[level, pl.ds(FALL, 1), :] = row(metric[level] if level > 0 else 0.0)
    green = forward
    table[levels - 1, pl.ds(FIRST_GREEN, 1), :] = NEW_WEIGHT * green
    for level in range(levels - 2, -1, -1):
        green = (
            table[level, pl.ds(BELOW_FORWARD, 1), :]
            + table[level, pl.ds(UPPER_PIVOT, 1), :] * green
        )
        table[level, pl.ds(FIRST_GREEN, 1), :] = NEW_WEIGHT * green
    scalars[pl.ds(FIRST, 1), :] = green
    scalars[pl.ds(CORNER, 1), :] = forward
    scalars[pl.ds(LAST, 1), :] = pivot
    scalars[pl.ds(BELOW, 1), :] = row(lower[0])
    scalars[pl.ds(ABOVE, 1), :] = row(upper[levels - 1])
    scalars[pl.ds(METRIC_BELOW, 1), :] = row(NEW_WEIGHT * metric[0])
    scalars[pl.ds(METRIC_ABOVE, 1), :] = row(NEW_WEIGHT * metric[levels - 1])
    scalars[pl.ds(7, 1), :] = row(0.0)


def bulk_kernel(
    arrived,
    table,
    temp,
    u_vel,
    v_vel,
    w_vel,
    temp_prev,
    w_prev,
    forward,
    tend,
    first,
):
    levels, rows, cols = temp.shape
    strips = rows // TILE
    fields, prevs = (temp, w_vel), (temp_prev, w_prev)
    for field in range(2):
        forward[field, 0] = jnp.zeros((rows, cols), F32)
        first[field] = jnp.zeros((rows, cols), F32)
    row_at = lax.broadcasted_iota(jnp.int32, (TILE, cols), 0)
    zero = jnp.zeros((TILE, cols), F32)

    def sides(level, strip):
        at = pl.ds(strip * TILE, TILE)
        half = 0.5 * u_vel[level, at, :]
        back, ahead = HORIZ_DIFF - half, HORIZ_DIFF + half
        here = [values[level, at, :] for values in fields]
        return (
            here,
            [pltpu.roll(back * value, TILE - 1, 0) for value in here],
            [pltpu.roll(ahead * value, 1, 0) for value in here],
        )

    def pair_step(pair, carry):
        both = (2 * pair, 2 * pair + 1)
        under, over = jnp.maximum(both[0] - 1, 0), jnp.minimum(both[1] + 1, levels - 1)

        def spread(level, at):
            return jnp.broadcast_to(table[level, pl.ds(at, 1), :], (TILE, cols))

        factors = [
            [spread(level, at) for at in (PIVOT_NEW, LOWER_PIVOT, FIRST_GREEN, RISE, FALL)]
            for level in both
        ]
        before = [[zero, zero], [zero, zero]]
        now = [sides(level, 0) for level in both]
        for strip in range(strips):
            none = (None, [zero, zero], None)
            later = [sides(level, strip + 1) if strip + 1 < strips else none for level in both]
            at = pl.ds(strip * TILE, TILE)
            beneath = [values[under, at, :] for values in fields]
            above = [values[over, at, :] for values in fields]
            solved = [forward[field, both[0], at, :] for field in range(2)]
            total = [first[field, at, :] for field in range(2)]
            for i, level in enumerate(both):
                here, back, ahead = now[i]
                pivot, lower_pivot, green, rise, fall = factors[i]
                upward = above if i else now[1][0]
                downward = now[0][0] if i else beneath
                half = 0.5 * v_vel[level, at, :]
                v_back, v_ahead = HORIZ_DIFF - half, HORIZ_DIFF + half
                w_over, w_under = rise * upward[1], fall * downward[1]
                for field in range(2):
                    value = here[field]
                    change = jnp.where(row_at == TILE - 1, later[i][1][field], back[field])
                    change = change + jnp.where(row_at == 0, before[i][field], ahead[field])
                    change = change + pltpu.roll(v_back * value, cols - 1, 1)
                    change = change + pltpu.roll(v_ahead * value, 1, 1)
                    change = change - w_over * upward[field] + w_under * downward[field]
                    change = change + (here[1 - field] - (4.0 * HORIZ_DIFF) * value)
                    tend[field, level, at, :] = change
                    old = prevs[field][level, at, :]
                    right = change + (FIELD_WEIGHT * value - PREV_WEIGHT * old)
                    solved[field] = pivot * right + lower_pivot * solved[field]
                    forward[field, level + 1, at, :] = solved[field]
                    total[field] = total[field] + green * right
            for field in range(2):
                first[field, at, :] = total[field]
            before = [now[0][2], now[1][2]]
            now = later
        return carry

    lax.fori_loop(0, levels // 2, pair_step, 0)


def bulk(arrived, table, *arrays):
    levels, rows, cols = arrays[0].shape
    return pl.pallas_call(
        bulk_kernel,
        out_shape=(
            held(2, levels + 1, rows, cols),
            held(2, levels, rows, cols),
            held(2, rows, cols),
        ),
        in_specs=[whole(pl.ANY)] + [whole(VMEM)] * 7,
        out_specs=[whole(VMEM)] * 3,
        compiler_params=pltpu.CompilerParams(vmem_limit_bytes=8 * MIB),
        cost_estimate=pl.CostEstimate(
            flops=100000 * levels * rows * cols,
            bytes_accessed=24 * levels * rows * cols,
            transcendentals=0,
        ),
        name="bulk",
    )(arrived, *map(in_vmem, (table, *arrays)))


def side_changes(far, near):
    odd = bit_of("gx", 0) == 1
    return jnp.where(odd, near[...], far[...]), jnp.where(odd, far[...], near[...])


def level_fluxes(inner, outer):
    upper = bit_of("gz", 0) == 1
    return jnp.where(upper, inner, outer), jnp.where(upper, outer, inner)


def beside_seam(rounds):
    return bit_of("gz", 0) != bit_of("gz", rounds - 1)


def ends(rows, cols, head, tail):
    at = lax.broadcasted_iota(jnp.int32, (rows, cols), 0)
    return jnp.where(at == 0, head, jnp.where(at == rows - 1, tail, 0.0))


def scalar_rows(ref, begin=0):
    return [ref[pl.ds(begin + at, 1), :] for at in range(7)]


def in_order(upper, own, other):
    low = [jnp.where(upper, b, a) for a, b in zip(own, other)]
    high = [jnp.where(upper, a, b) for a, b in zip(own, other)]
    return low, high


def interface(low, high):
    coupling = low[ABOVE]
    return coupling, 1.0 / (1.0 - coupling * coupling * low[LAST] * high[FIRST])


def joint_scalars(low, high):
    coupling, inverse = interface(low, high)
    low_out, high_out = low[CORNER] * coupling, high[CORNER] * coupling
    return [
        low[FIRST] + low_out * low_out * inverse * high[FIRST],
        low_out * inverse * high[CORNER],
        high[LAST] + high_out * high_out * inverse * low[LAST],
        low[BELOW],
        high[ABOVE],
        low[METRIC_BELOW],
        high[METRIC_ABOVE],
        jnp.zeros_like(coupling),
    ]


def fix_kernel(
    rounds, levels, other, near, far, fluxes, outward, forward, first, table, *rest
):
    outer, rest = (rest[0], rest[1:]) if rounds > 2 else (None, rest)
    entries, changes, *late = rest
    _, rows, cols = first.shape
    diffs = side_changes(far, near)
    scalars = scalar_rows(fluxes, 3 * rows)
    below, above = scalars[METRIC_BELOW], -scalars[METRIC_ABOVE]
    core, size = bit_of("gz", 0) == 1, rows // 2
    for field in range(2):
        firsts, lasts = [], []
        for side in range(2):
            value = jnp.zeros((1, cols), F32)
            total = jnp.zeros((1, cols), F32)
            for level in range(levels):
                right = diffs[side][field * levels + level : field * levels + level + 1, :]
                value = (
                    table[level, pl.ds(PIVOT_NEW, 1), :] * right
                    + table[level, pl.ds(LOWER_PIVOT, 1), :] * value
                )
                total = total + table[level, pl.ds(FIRST_GREEN, 1), :] * right
                changes[pl.ds((side * 2 + field) * levels + level, 1), :] = value
            firsts.append(total)
            lasts.append(value)
        at = pl.ds(field * rows, rows)
        flux_below, flux_above = level_fluxes(other[at, :], 0.0 if outer is None else outer[at, :])
        first_entry = (
            first[field]
            + (below * scalars[FIRST]) * flux_below
            + (above * scalars[CORNER]) * flux_above
            + ends(rows, cols, *firsts)
        )
        last_entry = (
            forward[field, levels]
            + (below * scalars[CORNER]) * flux_below
            + (above * scalars[LAST]) * flux_above
            + ends(rows, cols, *lasts)
        )
        entries[at, :] = first_entry
        entries[pl.ds((2 + field) * rows, rows), :] = last_entry
        if late:
            message, seam = late
            message[at, :] = jnp.where(core, first_entry, last_entry)
            there = pl.ds(2 * rows + field * size, size)
            message[there, :] = jnp.where(core, last_entry[:size], first_entry[size:])
            value = outward[at, :]
            value = jnp.where(core, value[size:], value[:size])
            seam[pl.ds(field * size, size), :] = jnp.where(
                beside_seam(rounds), value, other[there, :]
            )
    if late:
        far_scalars = scalar_rows(other, 3 * rows)
        for at, value in enumerate(joint_scalars(*in_order(core, scalars, far_scalars))):
            seam[pl.ds(rows + at, 1), :] = value


def fix(rounds, other, near, far, fluxes, outward, forward, first, table, outer):
    levels = table.shape[0]
    _, rows, cols = first.shape
    shapes = [held(4 * rows, cols), held(4 * levels, cols)]
    if rounds == 2:
        shapes += [held(3 * rows, cols), held(rows + TILE, cols)]
    return pl.pallas_call(
        functools.partial(fix_kernel, rounds, levels),
        out_shape=tuple(shapes),
        in_specs=[whole(VMEM)] * (8 + len(outer)),
        out_specs=[whole(VMEM)] * len(shapes),
        compiler_params=pltpu.CompilerParams(vmem_limit_bytes=8 * MIB),
        name="fix",
    )(
        other, near, far, fluxes, outward, in_vmem(forward), in_vmem(first), in_vmem(table), *outer
    )


def tends_kernel(rounds, table, tend, far, near, other, *rest):
    outer, rest = (rest[0], rest[1:]) if rounds > 2 else (None, rest)
    *outs, layers, strips, sems = rest
    _, levels, rows, cols = tend.shape
    inside, middle = pl.ds(1, levels - 2), pl.ds(TILE, rows - 2 * TILE)
    copies = []

    def send(field, at, src, dst):
        copies.append(pltpu.make_async_copy(src, dst, sems.at[field, at]))
        copies[-1].start()

    for field, out in enumerate(outs):
        send(field, 0, tend.at[field, inside, middle, :], out.at[inside, middle, :])
    diffs = side_changes(far, near)
    tile_at = lax.broadcasted_iota(jnp.int32, (TILE, cols), 0)
    for field, out in enumerate(outs):
        at = pl.ds(field * rows, rows)
        below, above = level_fluxes(other[at, :], 0.0 if outer is None else outer[at, :])
        for side, level, change in (
            (0, 0, table[0, pl.ds(RISE, 1), :] * below),
            (1, levels - 1, -table[levels - 1, pl.ds(FALL, 1), :] * above),
        ):
            at = field * levels + level
            rim = ends(rows, cols, diffs[0][at : at + 1, :], diffs[1][at : at + 1, :])
            layers[field, side] = tend[field, level] + change + rim
            send(field, 1 + side, layers.at[field, side], out.at[level])
        for side, begin, row in ((0, 0, 0), (1, rows - TILE, TILE - 1)):
            for level in range(1, levels - 1):
                at = field * levels + level
                edge = jnp.where(tile_at == row, diffs[side][at : at + 1, :], 0.0)
                strips[field, side, level] = tend[field, level, pl.ds(begin, TILE), :] + edge
            there = out.at[inside, pl.ds(begin, TILE), :]
            send(field, 3 + side, strips.at[field, side, inside], there)
    for copy in copies:
        copy.wait()


def tends(rounds, table, tend, far, near, other, outer):
    _, levels, rows, cols = tend.shape
    return pl.pallas_call(
        functools.partial(tends_kernel, rounds),
        out_shape=(jax.ShapeDtypeStruct((levels, rows, cols), F32),) * 2,
        in_specs=[whole(VMEM)] * (5 + len(outer)),
        out_specs=[whole(pl.ANY)] * 2,
        scratch_shapes=[
            pltpu.VMEM((2, 2, rows, cols), F32),
            pltpu.VMEM((2, 2, levels, TILE, cols), F32),
            pltpu.SemaphoreType.DMA((2, 5)),
        ],
        compiler_params=pltpu.CompilerParams(vmem_limit_bytes=8 * MIB),
        cost_estimate=pl.CostEstimate(
            flops=levels * rows * cols,
            bytes_accessed=8 * levels * rows * cols,
            transcendentals=0,
        ),
        name="tends",
    )(in_vmem(table), in_vmem(tend), far, near, other, *outer)


def merge_kernel(bit, final, late, own_at, other_at, mine, theirs, own, other, base, gains, *rest):
    _, rows, cols = base.shape
    upper = bit_of("gz", bit) == 1
    low, high = in_order(upper, scalar_rows(own, own_at), scalar_rows(other, other_at))
    coupling, inverse = interface(low, high)
    to_high, to_low = high[FIRST] * coupling, low[LAST] * coupling
    low_out, high_out = low[CORNER] * coupling, high[CORNER] * coupling
    core, size = bit_of("gz", 0) == 1, rows // 2
    sends_last = bit_of("gz", bit + 1) == 0
    for field in range(2):
        here = pl.ds(field * rows, rows)
        own_first, own_last = mine[here, :], mine[pl.ds((2 + field) * rows, rows), :]
        if late:
            low_last = jnp.where(upper, theirs[here, :], own_last)
            high_first = jnp.where(upper, own_first, theirs[here, :])
        else:
            other_first, other_last = theirs[here, :], theirs[pl.ds((2 + field) * rows, rows), :]
            low_last = jnp.where(upper, other_last, own_last)
            high_first = jnp.where(upper, own_first, other_first)
            low_first = jnp.where(upper, other_first, own_first)
            high_last = jnp.where(upper, own_last, other_last)
        above = inverse * (high_first + to_high * low_last)
        below = inverse * (low_last + to_low * high_first)
        base[field] = coupling * jnp.where(upper, below, above)
        more = jnp.where(sends_last, high_out * below, low_out * above)
        if late:
            outside = jnp.where(upper, own_last, own_first)
            outside = jnp.where(core, outside[size:], outside[:size])
            there = theirs[pl.ds(2 * rows + field * size, size), :]
            outside = jnp.where(sends_last == upper, outside, there)
        elif final:
            outside = jnp.where(sends_last, high_last, low_first)
            outside = jnp.where(core, outside[size:], outside[:size])
        if final:
            value = outside + jnp.where(core, more[size:], more[:size])
            rest[0][pl.ds(field * size, size), :] = value
        else:
            rest[0][here, :] = low_first + low_out * above
            rest[0][pl.ds((2 + field) * rows, rows), :] = high_last + high_out * below
    if not late:
        for at, value in enumerate(joint_scalars(low, high)):
            rest[1][pl.ds(at, 1), :] = value
    scale = coupling * inverse
    gains[...] = jnp.zeros(gains.shape, F32)
    gains[pl.ds(FROM_ABOVE, 1), :] = scale * high[CORNER] * jnp.where(upper, to_low, 1.0)
    gains[pl.ds(FROM_BELOW, 1), :] = scale * low[CORNER] * jnp.where(upper, 1.0, to_high)


def merge(bit, final, late, rows, mine, theirs, own, other):
    cols = mine.shape[1]
    shapes = [held(2, rows, cols), held(TILE, cols), held((1 if final else 4) * rows, cols)]
    if not late:
        shapes.append(held(TILE, cols))
    return pl.pallas_call(
        functools.partial(
            merge_kernel, bit, final, late, own.shape[0] - TILE, other.shape[0] - TILE
        ),
        out_shape=tuple(shapes),
        in_specs=[whole(VMEM)] * 4,
        out_specs=[whole(VMEM)] * len(shapes),
        compiler_params=pltpu.CompilerParams(vmem_limit_bytes=8 * MIB),
        name="merge",
    )(mine, theirs, own, other)


def prepare_kernel(
    rounds, temp, w_vel, forward, table, changes, fluxes, other, crossing, *rest
):
    outer = crossing if rounds > 2 else None
    bases, gains = rest[: rounds - 1], rest[rounds - 1 : 2 * rounds - 2]
    known, response, *passed, below_in, above_in = rest[2 * rounds - 2 :]
    if passed:
        passed[0][...] = crossing[pl.ds(0, passed[0].shape[0]), :]
    levels, rows, cols = temp.shape
    upper = bit_of("gz", rounds - 1) == 1
    one, none = jnp.ones((1, cols), F32), jnp.zeros((1, cols), F32)
    below_gain, above_gain = jnp.where(upper, one, none), jnp.where(upper, none, one)
    below = above = None
    for step in range(rounds - 2, -1, -1):
        side = bit_of("gz", step) == 1
        from_above = gains[step][pl.ds(FROM_ABOVE, 1), :]
        from_below = gains[step][pl.ds(FROM_BELOW, 1), :]
        gain = from_above * above_gain + from_below * below_gain
        below_gain = jnp.where(side, gain, below_gain)
        above_gain = jnp.where(side, above_gain, gain)
        into = [bases[step][field] for field in range(2)]
        if below is None:
            below = above = [jnp.zeros((rows, cols), F32)] * 2
        else:
            into = [
                into[field] + from_above * above[field] + from_below * below[field]
                for field in range(2)
            ]
        below = [jnp.where(side, into[field], below[field]) for field in range(2)]
        above = [jnp.where(side, above[field], into[field]) for field in range(2)]
    scalars = scalar_rows(fluxes, 3 * rows)
    for field in range(2):
        at = pl.ds(field * rows, rows)
        flux_below, flux_above = level_fluxes(other[at, :], 0.0 if outer is None else outer[at, :])
        below_in[field] = below[field] + scalars[METRIC_BELOW] * flux_below
        above_in[field] = above[field] - scalars[METRIC_ABOVE] * flux_above

    gain = above_gain * table[levels - 1, pl.ds(PIVOT, 1), :]
    for level in range(levels - 1, -1, -1):
        if level < levels - 1:
            gain = gain * table[level, pl.ds(UPPER_PIVOT, 1), :]
        gain = gain + below_gain * table[level, pl.ds(BELOW_FORWARD, 1), :]
        response[level] = jnp.broadcast_to(gain, (TILE, cols))

    row_at = lax.broadcasted_iota(jnp.int32, (TILE, cols), 0)
    width = 2 * TILE
    for begin in range(0, rows, width):
        at = pl.ds(begin, width)

        def solve(level, carry, factor, begin=begin, at=at):
            factor = table[level, pl.ds(factor, 1), :]
            below_factor = table[level, pl.ds(BELOW_FORWARD, 1), :]
            values = []
            for field, cells in enumerate((temp, w_vel)):
                value = forward[field, level + 1, at, :] + below_factor * below_in[field, at, :]
                if begin == 0:
                    change = changes[pl.ds(field * levels + level, 1), :]
                    head = value[:TILE] + jnp.where(row_at == 0, change, 0.0)
                    value = jnp.concatenate([head, value[TILE:]])
                if begin == rows - width:
                    change = changes[pl.ds((2 + field) * levels + level, 1), :]
                    tail = value[-TILE:] + jnp.where(row_at == TILE - 1, change, 0.0)
                    value = jnp.concatenate([value[:-TILE], tail])
                value = value + factor * carry[field]
                known[field, level, at, :] = value - cells[level, at, :]
                values.append(value)
            return tuple(values)

        carry = solve(levels - 1, [above_in[field, at, :] for field in range(2)], PIVOT)

        def step(back, carry, solve=solve):
            return solve(levels - 2 - back, carry, UPPER_PIVOT)

        lax.fori_loop(0, levels - 1, step, carry, unroll=3)


def prepare(rounds, temp, w_vel, forward, table, changes, fluxes, other, crossing, bases, gains):
    levels, rows, cols = temp.shape
    shapes = (held(2, levels, rows, cols), held(levels, TILE, cols))
    shapes += (held(rows, cols),) * (rounds == 2)
    return pl.pallas_call(
        functools.partial(prepare_kernel, rounds),
        out_shape=shapes,
        in_specs=[whole(VMEM)] * (8 + 2 * (rounds - 1)),
        out_specs=[whole(VMEM)] * len(shapes),
        scratch_shapes=[pltpu.VMEM((2, rows, cols), F32)] * 2,
        compiler_params=pltpu.CompilerParams(vmem_limit_bytes=8 * MIB),
        cost_estimate=pl.CostEstimate(
            flops=levels * rows * cols,
            bytes_accessed=24 * levels * rows * cols,
            transcendentals=0,
        ),
        name="prepare",
    )(
        in_vmem(temp), in_vmem(w_vel), in_vmem(forward), in_vmem(table), changes, fluxes, other,
        crossing, *bases, *gains,
    )


def join_kernel(rounds, late, own_at, other_at, mine, theirs, own, other, joined):
    size = theirs.shape[0] // 2
    upper = bit_of("gz", rounds - 1) == 1
    low, high = in_order(upper, scalar_rows(own, own_at), scalar_rows(other, other_at))
    coupling, inverse = interface(low, high)
    scale = coupling * inverse
    to_other = scale * coupling * jnp.where(upper, low[LAST], high[FIRST])
    up, down = high[METRIC_BELOW] * inverse, -low[METRIC_ABOVE] * inverse
    own_gain = coupling * jnp.where(upper, down * low[LAST], up * high[FIRST])
    other_gain = jnp.where(upper, up, down)
    for field in range(2):
        at = pl.ds(field * size, size)
        into = scale * theirs[at, :] + to_other * mine[at, :]
        if late:
            into = into + (own_gain * own[at, :] + other_gain * other[at, :])
        joined[at, :] = into


def join(rounds, late, mine, theirs, own, other):
    size, cols = theirs.shape
    return pl.pallas_call(
        functools.partial(join_kernel, rounds, late, own.shape[0] - TILE, other.shape[0] - TILE),
        out_shape=held(size, cols),
        in_specs=[whole(VMEM)] * 4,
        out_specs=whole(VMEM),
        compiler_params=pltpu.CompilerParams(vmem_limit_bytes=8 * MIB),
        name="join",
    )(mine, theirs, own, other)


def finish_kernel(rounds, swapped, known, response, joined, *rest):
    late, results = rounds == 2, 4 if rounds == 2 else 2
    flux_in, table, tend, far, near = rest[:5] if late else (None,) * 5
    rest = rest[(5 if late else 0) + (results if swapped else results - 2) :]
    outs, (result, rim, sems) = rest[:results], rest[results:]
    _, levels, rows, cols = known.shape
    width, half = 2 * TILE, rows // 2
    core = bit_of("gz", 0)
    start = pl.multiple_of((1 - core if swapped else core) * half, half)
    copies = []
    if late:
        diffs = side_changes(far, near)
        level = core * (levels - 1)
        gain = jnp.where(
            core == 1, -table[levels - 1, pl.ds(FALL, 1), :], table[0, pl.ds(RISE, 1), :]
        )
        gain = jnp.where(beside_seam(rounds), gain, 0.0)
        row_at = start + lax.broadcasted_iota(jnp.int32, (half, cols), 0)
        for field in range(2):
            head, tail = (
                jnp.where(
                    core == 1,
                    diff[(field + 1) * levels - 1 : (field + 1) * levels, :],
                    diff[field * levels : field * levels + 1, :],
                )
                for diff in diffs
            )
            edge = jnp.where(row_at == 0, head, jnp.where(row_at == rows - 1, tail, 0.0))
            flux = flux_in[pl.ds(field * half, half), :]
            rim[field] = tend[field, level, pl.ds(start, half), :] + gain * flux + edge
            copies.append(
                pltpu.make_async_copy(
                    rim.at[field],
                    outs[2 + field].at[level, pl.ds(start, half), :],
                    sems.at[field],
                )
            )
            copies[-1].start()
    for field in range(2):
        for part, begin in enumerate(range(0, half, width)):
            into = joined[pl.ds(field * half + begin, width), :]
            tiles = [into[i : i + TILE] for i in range(0, width, TILE)]

            def step(level, carry, field=field, begin=begin, tiles=tiles):
                gain = response[level]
                for i, tile in enumerate(tiles):
                    at = begin + i * TILE
                    value = known[field, level, pl.ds(start + at, TILE), :] + gain * tile
                    result[field, level, pl.ds(at, TILE), :] = value
                return carry

            lax.fori_loop(0, levels, step, 0, unroll=True)
            copies.append(
                pltpu.make_async_copy(
                    result.at[field, :, pl.ds(begin, width), :],
                    outs[field].at[:, pl.ds(start + begin, width), :],
                    sems.at[2 + 2 * field + part],
                )
            )
            copies[-1].start()
    for copy in copies:
        copy.wait()


def finish(rounds, known, response, joined, late, written):
    _, levels, rows, cols = known.shape
    results = 4 if rounds == 2 else 2
    inputs = 3 + len(late)
    swapped = len(written) == results
    return pl.pallas_call(
        functools.partial(finish_kernel, rounds, swapped),
        out_shape=(jax.ShapeDtypeStruct((levels, rows, cols), F32),) * results,
        in_specs=[whole(VMEM)] * inputs + [whole(pl.ANY)] * len(written),
        out_specs=[whole(pl.ANY)] * results,
        scratch_shapes=[
            pltpu.VMEM((2, levels, rows // 2, cols), F32),
            pltpu.VMEM((2, rows // 2, cols), F32),
            pltpu.SemaphoreType.DMA((6,)),
        ],
        input_output_aliases={
            inputs + i: results - len(written) + i for i in range(len(written))
        },
        compiler_params=pltpu.CompilerParams(vmem_limit_bytes=8 * MIB),
        cost_estimate=pl.CostEstimate(
            flops=20000 * levels * rows * cols,
            bytes_accessed=8 * levels * rows * cols,
            transcendentals=0,
        ),
        name="finish",
    )(in_vmem(known), response, joined, *map(in_vmem, late), *written)


def both_ways(pairs):
    return pairs + [(b, a) for a, b in pairs]


def local(temp, u_vel, v_vel, w_vel, temp_prev, w_prev, lower, upper, metric):
    rows = temp.shape[1]
    across, stacked = lax.axis_size("gx"), lax.axis_size("gz")
    rounds = stacked.bit_length() - 1
    cores = both_ways([(i, i + 1) for i in range(0, stacked, 2)])
    far, near, fluxes, outward, table = edges(
        temp, u_vel, w_vel, v_vel, temp_prev, w_prev, lower, upper, metric
    )
    other = lax.ppermute(fluxes, "gz", cores)
    near = lax.ppermute(near, "gx", both_ways([(i, i + 1) for i in range(0, across, 2)]))
    far = lax.ppermute(far, "gx", both_ways([(i, (i + 1) % across) for i in range(1, across, 2)]))
    outer = ()
    if rounds > 2:
        seams = both_ways([(i, i + 1) for i in range(1, stacked - 1, 2)])
        outer = (lax.ppermute(outward, "gz", seams),)
    forward, tend, first = bulk(other, table, temp, u_vel, v_vel, w_vel, temp_prev, w_prev)
    entries, changes, *late = fix(
        rounds, other, near, far, fluxes, outward, forward, first, table, outer
    )
    message, seam = late if late else (entries, fluxes)
    bases, gains, own, other_own = [], [], fluxes, other
    for step in range(rounds - 1):
        partners = [(i, i ^ (1 << step)) for i in range(stacked)]
        theirs = lax.ppermute(message, "gz", partners)
        if step > 0:
            other_own = lax.ppermute(own, "gz", partners)
        base, gain, message, *scalars = merge(
            step, step + 2 == rounds, bool(late), rows, entries, theirs, own, other_own
        )
        entries, own = message, scalars[0] if scalars else seam
        bases.append(base)
        gains.append(gain)
    partners = [(i, i ^ (stacked // 2)) for i in range(stacked)]
    theirs = lax.ppermute(message, "gz", partners)
    other_own = lax.ppermute(own, "gz", partners)
    known, response, *passed = prepare(
        rounds, temp, w_vel, forward, table, changes, fluxes, other, *(outer or (other_own,)),
        bases, gains,
    )
    tendencies = tends(rounds, table, tend, far, near, other, outer)
    joined = join(rounds, bool(late), message, theirs, own, other_own)
    swapped = lax.ppermute(joined, "gz", cores)
    if not late:
        written = finish(rounds, known, response, joined, (), ())
        return *finish(rounds, known, response, swapped, (), written), *tendencies
    crossed = lax.ppermute(passed[0], "gz", cores)
    late = (table, tend, far, near)
    written = finish(rounds, known, response, joined, (other_own, *late), tendencies)
    return tuple(finish(rounds, known, response, swapped, (crossed, *late), written))


def solution(mesh):
    field = P("gz", "gx", None)
    return jax.shard_map(
        local,
        mesh=mesh,
        in_specs=(field,) * 6 + (P("gz"),) * 3,
        out_specs=(field,) * 4,
        check_vma=False,
    )
```

```python
import functools

import jax
import jax.numpy as jnp
from jax import lax
from jax.experimental import pallas as pl
from jax.experimental.pallas import tpu as pltpu
from jax.sharding import PartitionSpec as P

NEW_WEIGHT = 5.0 / 12.0
HORIZ_DIFF = 0.1
FIELD_WEIGHT = 2.0 / NEW_WEIGHT
PREV_WEIGHT = (17.0 / 60.0) / NEW_WEIGHT
TILE = 8
MIB = 1024 * 1024

PIVOT_NEW, LOWER_PIVOT, UPPER_PIVOT, FIRST_GREEN, BELOW_FORWARD, PIVOT, RISE, FALL = range(8)
FIRST, CORNER, LAST, BELOW, ABOVE, METRIC_BELOW, METRIC_ABOVE = range(7)
FROM_ABOVE, FROM_BELOW = range(2)

VMEM = pltpu.VMEM
F32 = jnp.float32


def whole(space):
    return pl.BlockSpec(memory_space=space)


def held(*shape):
    return pltpu.VMEM(shape, F32)


def in_vmem(array):
    return pltpu.with_memory_space_constraint(array, pltpu.VMEM)


def in_hbm(*arrays):
    return [pltpu.with_memory_space_constraint(array, pltpu.HBM) for array in arrays]


def bit_of(axis, bit):
    return (lax.axis_index(axis) >> bit) & 1


def edges_kernel(
    temp,
    u_vel,
    w_vel,
    v_vel,
    temp_prev,
    w_prev,
    lower,
    upper,
    metric,
    far,
    near,
    fluxes,
    outward,
    table,
    strips,
    layers,
    lower_at,
    upper_at,
    metric_at,
    sems,
):
    levels, rows, cols = temp.shape
    copies = [(lower, lower_at), (upper, upper_at), (metric, metric_at)]
    for at, array in enumerate((temp, w_vel, u_vel)):
        for side, row in enumerate((0, rows - 1)):
            copies.append((array.at[:, row, :], strips.at[at, side]))
    for at, array in enumerate((temp, w_vel)):
        for side, level in enumerate((0, levels - 1)):
            copies.append((array.at[level], layers.at[at, side]))
    copies = [pltpu.make_async_copy(src, dst, sems.at[i]) for i, (src, dst) in enumerate(copies)]
    for copy in copies:
        copy.start()
    for copy in copies[:3]:
        copy.wait()
    coefficients(lower_at, upper_at, metric_at, table, fluxes.at[pl.ds(3 * rows, TILE)])
    for copy in copies[3:]:
        copy.wait()
    odd = bit_of("gx", 0) == 1
    for field in range(2):
        at = pl.ds(field * levels, levels)
        to_left = (HORIZ_DIFF - 0.5 * strips[2, 0]) * strips[field, 0]
        to_right = (HORIZ_DIFF + 0.5 * strips[2, 1]) * strips[field, 1]
        near[at, :] = jnp.where(odd, to_left, to_right)
        far[at, :] = jnp.where(odd, to_right, to_left)
    position = lax.axis_index("gz")
    upper_core = bit_of("gz", 0) == 1
    wall = (position == 0) | (position == lax.axis_size("gz") - 1)
    zero, size = jnp.zeros((rows, cols), F32), rows // 2
    for field in range(2):
        bottom = layers[1, 0] * layers[field, 0]
        top = layers[1, 1] * layers[field, 1]
        fluxes[pl.ds(field * rows, rows), :] = jnp.where(upper_core, bottom, top)
        value = jnp.where(wall, zero, jnp.where(upper_core, top, bottom))
        outward[pl.ds(field * rows, rows), :] = value
        fluxes[pl.ds(2 * rows + field * size, size), :] = jnp.where(
            upper_core, value[:size], value[size:]
        )


def edges(temp, u_vel, w_vel, v_vel, temp_prev, w_prev, lower, upper, metric):
    levels, rows, cols = temp.shape
    return pl.pallas_call(
        edges_kernel,
        out_shape=(
            held(2 * levels, cols),
            held(2 * levels, cols),
            held(3 * rows + TILE, cols),
            held(2 * rows, cols),
            held(levels, TILE, cols),
        ),
        in_specs=[whole(pl.ANY)] * 9,
        out_specs=[whole(VMEM)] * 5,
        scratch_shapes=[
            pltpu.VMEM((3, 2, levels, cols), F32),
            pltpu.VMEM((2, 2, rows, cols), F32),
            pltpu.SMEM((levels,), F32),
            pltpu.SMEM((levels,), F32),
            pltpu.SMEM((levels,), F32),
            pltpu.SemaphoreType.DMA((13,)),
        ],
        compiler_params=pltpu.CompilerParams(vmem_limit_bytes=8 * MIB),
        name="edges",
    )(*in_hbm(temp, u_vel, w_vel, v_vel, temp_prev, w_prev, lower, upper, metric))


def coefficients(lower, upper, metric, table, scalars):
    levels, _, cols = table.shape

    def row(value):
        return jnp.full((1, cols), value, F32)

    low = [row(lower[level]) for level in range(levels)]
    high = [row(upper[level]) for level in range(levels)]
    scale = [1.0 / (1.0 + a + b) for a, b in zip(low, high)]
    minors = [jnp.ones((1, cols), F32)] * 2
    for level in range(1, levels):
        product = (low[level] * scale[level]) * (high[level - 1] * scale[level - 1])
        minors.append(minors[-1] - product * minors[-2])
    pivots = [scale[level] * minors[level] * (1.0 / minors[level + 1]) for level in range(levels)]
    ratios = [a * b for a, b in zip(high, pivots)]
    forward = [pivots[0]]
    for level in range(1, levels):
        forward.append(low[level] * pivots[level] * forward[-1])
    green = [forward[-1]]
    for level in range(levels - 2, -1, -1):
        green.insert(0, forward[level] + ratios[level] * green[0])
    for level in range(levels):
        for at, value in (
            (PIVOT_NEW, NEW_WEIGHT * pivots[level]),
            (LOWER_PIVOT, low[level] * pivots[level]),
            (UPPER_PIVOT, ratios[level]),
            (FIRST_GREEN, NEW_WEIGHT * green[level]),
            (BELOW_FORWARD, forward[level]),
            (PIVOT, pivots[level]),
            (RISE, row(metric[level] if level < levels - 1 else 0.0)),
            (FALL, row(metric[level] if level > 0 else 0.0)),
        ):
            table[level, pl.ds(at, 1), :] = value
    scalars[pl.ds(FIRST, 1), :] = green[0]
    scalars[pl.ds(CORNER, 1), :] = forward[-1]
    scalars[pl.ds(LAST, 1), :] = pivots[-1]
    scalars[pl.ds(BELOW, 1), :] = row(lower[0])
    scalars[pl.ds(ABOVE, 1), :] = row(upper[levels - 1])
    scalars[pl.ds(METRIC_BELOW, 1), :] = row(NEW_WEIGHT * metric[0])
    scalars[pl.ds(METRIC_ABOVE, 1), :] = row(NEW_WEIGHT * metric[levels - 1])
    scalars[pl.ds(7, 1), :] = row(0.0)


def bulk_kernel(
    arrived,
    table,
    temp,
    u_vel,
    v_vel,
    w_vel,
    temp_prev,
    w_prev,
    forward,
    tend,
    first,
):
    levels, rows, cols = temp.shape
    strips = rows // TILE
    fields, prevs = (temp, w_vel), (temp_prev, w_prev)
    for field in range(2):
        forward[field, 0] = jnp.zeros((rows, cols), F32)
        first[field] = jnp.zeros((rows, cols), F32)
    row_at = lax.broadcasted_iota(jnp.int32, (TILE, cols), 0)
    zero = jnp.zeros((TILE, cols), F32)

    def sides(level, strip):
        at = pl.ds(strip * TILE, TILE)
        half = 0.5 * u_vel[level, at, :]
        back, ahead = HORIZ_DIFF - half, HORIZ_DIFF + half
        here = [values[level, at, :] for values in fields]
        return (
            here,
            [pltpu.roll(back * value, TILE - 1, 0) for value in here],
            [pltpu.roll(ahead * value, 1, 0) for value in here],
        )

    def pair_step(pair, carry):
        both = (2 * pair, 2 * pair + 1)
        under, over = jnp.maximum(both[0] - 1, 0), jnp.minimum(both[1] + 1, levels - 1)

        def spread(level, at):
            return jnp.broadcast_to(table[level, pl.ds(at, 1), :], (TILE, cols))

        factors = [
            [spread(level, at) for at in (PIVOT_NEW, LOWER_PIVOT, FIRST_GREEN, RISE, FALL)]
            for level in both
        ]
        before = [[zero, zero], [zero, zero]]
        now = [sides(level, 0) for level in both]
        for strip in range(strips):
            none = (None, [zero, zero], None)
            later = [sides(level, strip + 1) if strip + 1 < strips else none for level in both]
            at = pl.ds(strip * TILE, TILE)
            beneath = [values[under, at, :] for values in fields]
            above = [values[over, at, :] for values in fields]
            solved = [forward[field, both[0], at, :] for field in range(2)]
            total = [first[field, at, :] for field in range(2)]
            for i, level in enumerate(both):
                here, back, ahead = now[i]
                pivot, lower_pivot, green, rise, fall = factors[i]
                upward = above if i else now[1][0]
                downward = now[0][0] if i else beneath
                half = 0.5 * v_vel[level, at, :]
                v_back, v_ahead = HORIZ_DIFF - half, HORIZ_DIFF + half
                w_over, w_under = rise * upward[1], fall * downward[1]
                for field in range(2):
                    value = here[field]
                    change = jnp.where(row_at == TILE - 1, later[i][1][field], back[field])
                    change = change + jnp.where(row_at == 0, before[i][field], ahead[field])
                    change = change + pltpu.roll(v_back * value, cols - 1, 1)
                    change = change + pltpu.roll(v_ahead * value, 1, 1)
                    change = change - w_over * upward[field] + w_under * downward[field]
                    change = change + (here[1 - field] - (4.0 * HORIZ_DIFF) * value)
                    tend[field, level, at, :] = change
                    old = prevs[field][level, at, :]
                    right = change + (FIELD_WEIGHT * value - PREV_WEIGHT * old)
                    solved[field] = pivot * right + lower_pivot * solved[field]
                    forward[field, level + 1, at, :] = solved[field]
                    total[field] = total[field] + green * right
            for field in range(2):
                first[field, at, :] = total[field]
            before = [now[0][2], now[1][2]]
            now = later
        return carry

    lax.fori_loop(0, levels // 2, pair_step, 0)


def bulk(arrived, table, *arrays):
    levels, rows, cols = arrays[0].shape
    return pl.pallas_call(
        bulk_kernel,
        out_shape=(
            held(2, levels + 1, rows, cols),
            held(2, levels, rows, cols),
            held(2, rows, cols),
        ),
        in_specs=[whole(pl.ANY)] + [whole(VMEM)] * 7,
        out_specs=[whole(VMEM)] * 3,
        compiler_params=pltpu.CompilerParams(vmem_limit_bytes=8 * MIB),
        cost_estimate=pl.CostEstimate(
            flops=100000 * levels * rows * cols,
            bytes_accessed=24 * levels * rows * cols,
            transcendentals=0,
        ),
        name="bulk",
    )(arrived, *map(in_vmem, (table, *arrays)))


def side_changes(far, near):
    odd = bit_of("gx", 0) == 1
    return jnp.where(odd, near[...], far[...]), jnp.where(odd, far[...], near[...])


def level_fluxes(inner, outer):
    upper = bit_of("gz", 0) == 1
    return jnp.where(upper, inner, outer), jnp.where(upper, outer, inner)


def beside_seam(rounds):
    return bit_of("gz", 0) != bit_of("gz", rounds - 1)


def ends(rows, cols, head, tail):
    at = lax.broadcasted_iota(jnp.int32, (rows, cols), 0)
    return jnp.where(at == 0, head, jnp.where(at == rows - 1, tail, 0.0))


def scalar_rows(ref, begin=0):
    return [ref[pl.ds(begin + at, 1), :] for at in range(7)]


def in_order(upper, own, other):
    low = [jnp.where(upper, b, a) for a, b in zip(own, other)]
    high = [jnp.where(upper, a, b) for a, b in zip(own, other)]
    return low, high


def interface(low, high):
    coupling = low[ABOVE]
    return coupling, 1.0 / (1.0 - coupling * coupling * low[LAST] * high[FIRST])


def joint_scalars(low, high):
    coupling, inverse = interface(low, high)
    low_out, high_out = low[CORNER] * coupling, high[CORNER] * coupling
    return [
        low[FIRST] + low_out * low_out * inverse * high[FIRST],
        low_out * inverse * high[CORNER],
        high[LAST] + high_out * high_out * inverse * low[LAST],
        low[BELOW],
        high[ABOVE],
        low[METRIC_BELOW],
        high[METRIC_ABOVE],
        jnp.zeros_like(coupling),
    ]


def fix_kernel(
    rounds, levels, other, near, far, fluxes, outward, forward, first, table, *rest
):
    outer, rest = (rest[0], rest[1:]) if rounds > 2 else (None, rest)
    entries, changes, *late = rest
    _, rows, cols = first.shape
    diffs = side_changes(far, near)
    scalars = scalar_rows(fluxes, 3 * rows)
    below, above = scalars[METRIC_BELOW], -scalars[METRIC_ABOVE]
    core, size = bit_of("gz", 0) == 1, rows // 2
    for field in range(2):
        firsts, lasts = [], []
        for side in range(2):
            value = jnp.zeros((1, cols), F32)
            total = jnp.zeros((1, cols), F32)
            for level in range(levels):
                right = diffs[side][field * levels + level : field * levels + level + 1, :]
                value = (
                    table[level, pl.ds(PIVOT_NEW, 1), :] * right
                    + table[level, pl.ds(LOWER_PIVOT, 1), :] * value
                )
                total = total + table[level, pl.ds(FIRST_GREEN, 1), :] * right
                changes[pl.ds((side * 2 + field) * levels + level, 1), :] = value
            firsts.append(total)
            lasts.append(value)
        at = pl.ds(field * rows, rows)
        flux_below, flux_above = level_fluxes(other[at, :], 0.0 if outer is None else outer[at, :])
        first_entry = (
            first[field]
            + (below * scalars[FIRST]) * flux_below
            + (above * scalars[CORNER]) * flux_above
            + ends(rows, cols, *firsts)
        )
        last_entry = (
            forward[field, levels]
            + (below * scalars[CORNER]) * flux_below
            + (above * scalars[LAST]) * flux_above
            + ends(rows, cols, *lasts)
        )
        entries[at, :] = first_entry
        entries[pl.ds((2 + field) * rows, rows), :] = last_entry
        if late:
            message, seam = late
            message[at, :] = jnp.where(core, first_entry, last_entry)
            there = pl.ds(2 * rows + field * size, size)
            message[there, :] = jnp.where(core, last_entry[:size], first_entry[size:])
            value = outward[at, :]
            value = jnp.where(core, value[size:], value[:size])
            seam[pl.ds(field * size, size), :] = jnp.where(
                beside_seam(rounds), value, other[there, :]
            )
    if late:
        far_scalars = scalar_rows(other, 3 * rows)
        for at, value in enumerate(joint_scalars(*in_order(core, scalars, far_scalars))):
            seam[pl.ds(rows + at, 1), :] = value


def fix(rounds, other, near, far, fluxes, outward, forward, first, table, outer):
    levels = table.shape[0]
    _, rows, cols = first.shape
    shapes = [held(4 * rows, cols), held(4 * levels, cols)]
    if rounds == 2:
        shapes += [held(3 * rows, cols), held(rows + TILE, cols)]
    return pl.pallas_call(
        functools.partial(fix_kernel, rounds, levels),
        out_shape=tuple(shapes),
        in_specs=[whole(VMEM)] * (8 + len(outer)),
        out_specs=[whole(VMEM)] * len(shapes),
        compiler_params=pltpu.CompilerParams(vmem_limit_bytes=8 * MIB),
        name="fix",
    )(
        other, near, far, fluxes, outward, in_vmem(forward), in_vmem(first), in_vmem(table), *outer
    )


def tends_kernel(rounds, table, tend, far, near, other, *rest):
    outer, rest = (rest[0], rest[1:]) if rounds > 2 else (None, rest)
    *outs, layers, strips, sems = rest
    _, levels, rows, cols = tend.shape
    inside, middle = pl.ds(1, levels - 2), pl.ds(TILE, rows - 2 * TILE)
    copies = []

    def send(field, at, src, dst):
        copies.append(pltpu.make_async_copy(src, dst, sems.at[field, at]))
        copies[-1].start()

    for field, out in enumerate(outs):
        send(field, 0, tend.at[field, inside, middle, :], out.at[inside, middle, :])
    diffs = side_changes(far, near)
    tile_at = lax.broadcasted_iota(jnp.int32, (TILE, cols), 0)
    for field, out in enumerate(outs):
        at = pl.ds(field * rows, rows)
        below, above = level_fluxes(other[at, :], 0.0 if outer is None else outer[at, :])
        for side, level, change in (
            (0, 0, table[0, pl.ds(RISE, 1), :] * below),
            (1, levels - 1, -table[levels - 1, pl.ds(FALL, 1), :] * above),
        ):
            at = field * levels + level
            rim = ends(rows, cols, diffs[0][at : at + 1, :], diffs[1][at : at + 1, :])
            layers[field, side] = tend[field, level] + change + rim
            send(field, 1 + side, layers.at[field, side], out.at[level])
        for side, begin, row in ((0, 0, 0), (1, rows - TILE, TILE - 1)):
            for level in range(1, levels - 1):
                at = field * levels + level
                edge = jnp.where(tile_at == row, diffs[side][at : at + 1, :], 0.0)
                strips[field, side, level] = tend[field, level, pl.ds(begin, TILE), :] + edge
            there = out.at[inside, pl.ds(begin, TILE), :]
            send(field, 3 + side, strips.at[field, side, inside], there)
    for copy in copies:
        copy.wait()


def tends(rounds, table, tend, far, near, other, outer):
    _, levels, rows, cols = tend.shape
    return pl.pallas_call(
        functools.partial(tends_kernel, rounds),
        out_shape=(jax.ShapeDtypeStruct((levels, rows, cols), F32),) * 2,
        in_specs=[whole(VMEM)] * (5 + len(outer)),
        out_specs=[whole(pl.ANY)] * 2,
        scratch_shapes=[
            pltpu.VMEM((2, 2, rows, cols), F32),
            pltpu.VMEM((2, 2, levels, TILE, cols), F32),
            pltpu.SemaphoreType.DMA((2, 5)),
        ],
        compiler_params=pltpu.CompilerParams(vmem_limit_bytes=8 * MIB),
        cost_estimate=pl.CostEstimate(
            flops=levels * rows * cols,
            bytes_accessed=8 * levels * rows * cols,
            transcendentals=0,
        ),
        name="tends",
    )(in_vmem(table), in_vmem(tend), far, near, other, *outer)


def merge_kernel(bit, final, late, own_at, other_at, mine, theirs, own, other, base, gains, *rest):
    _, rows, cols = base.shape
    upper = bit_of("gz", bit) == 1
    low, high = in_order(upper, scalar_rows(own, own_at), scalar_rows(other, other_at))
    coupling, inverse = interface(low, high)
    to_high, to_low = high[FIRST] * coupling, low[LAST] * coupling
    low_out, high_out = low[CORNER] * coupling, high[CORNER] * coupling
    core, size = bit_of("gz", 0) == 1, rows // 2
    sends_last = bit_of("gz", bit + 1) == 0
    for field in range(2):
        here = pl.ds(field * rows, rows)
        own_first, own_last = mine[here, :], mine[pl.ds((2 + field) * rows, rows), :]
        if late:
            low_last = jnp.where(upper, theirs[here, :], own_last)
            high_first = jnp.where(upper, own_first, theirs[here, :])
        else:
            other_first, other_last = theirs[here, :], theirs[pl.ds((2 + field) * rows, rows), :]
            low_last = jnp.where(upper, other_last, own_last)
            high_first = jnp.where(upper, own_first, other_first)
            low_first = jnp.where(upper, other_first, own_first)
            high_last = jnp.where(upper, own_last, other_last)
        above = inverse * (high_first + to_high * low_last)
        below = inverse * (low_last + to_low * high_first)
        base[field] = coupling * jnp.where(upper, below, above)
        more = jnp.where(sends_last, high_out * below, low_out * above)
        if late:
            outside = jnp.where(upper, own_last, own_first)
            outside = jnp.where(core, outside[size:], outside[:size])
            there = theirs[pl.ds(2 * rows + field * size, size), :]
            outside = jnp.where(sends_last == upper, outside, there)
        elif final:
            outside = jnp.where(sends_last, high_last, low_first)
            outside = jnp.where(core, outside[size:], outside[:size])
        if final:
            value = outside + jnp.where(core, more[size:], more[:size])
            rest[0][pl.ds(field * size, size), :] = value
        else:
            rest[0][here, :] = low_first + low_out * above
            rest[0][pl.ds((2 + field) * rows, rows), :] = high_last + high_out * below
    if not late:
        for at, value in enumerate(joint_scalars(low, high)):
            rest[1][pl.ds(at, 1), :] = value
    scale = coupling * inverse
    gains[...] = jnp.zeros(gains.shape, F32)
    gains[pl.ds(FROM_ABOVE, 1), :] = scale * high[CORNER] * jnp.where(upper, to_low, 1.0)
    gains[pl.ds(FROM_BELOW, 1), :] = scale * low[CORNER] * jnp.where(upper, 1.0, to_high)


def merge(bit, final, late, rows, mine, theirs, own, other):
    cols = mine.shape[1]
    shapes = [held(2, rows, cols), held(TILE, cols), held((1 if final else 4) * rows, cols)]
    if not late:
        shapes.append(held(TILE, cols))
    return pl.pallas_call(
        functools.partial(
            merge_kernel, bit, final, late, own.shape[0] - TILE, other.shape[0] - TILE
        ),
        out_shape=tuple(shapes),
        in_specs=[whole(VMEM)] * 4,
        out_specs=[whole(VMEM)] * len(shapes),
        compiler_params=pltpu.CompilerParams(vmem_limit_bytes=8 * MIB),
        name="merge",
    )(mine, theirs, own, other)


def prepare_kernel(
    rounds, temp, w_vel, forward, table, changes, fluxes, other, crossing, *rest
):
    outer = crossing if rounds > 2 else None
    bases, gains = rest[: rounds - 1], rest[rounds - 1 : 2 * rounds - 2]
    known, response, *passed, below_in, above_in = rest[2 * rounds - 2 :]
    if passed:
        passed[0][...] = crossing[pl.ds(0, passed[0].shape[0]), :]
    levels, rows, cols = temp.shape
    upper = bit_of("gz", rounds - 1) == 1
    one, none = jnp.ones((1, cols), F32), jnp.zeros((1, cols), F32)
    below_gain, above_gain = jnp.where(upper, one, none), jnp.where(upper, none, one)
    below = above = None
    for step in range(rounds - 2, -1, -1):
        side = bit_of("gz", step) == 1
        from_above = gains[step][pl.ds(FROM_ABOVE, 1), :]
        from_below = gains[step][pl.ds(FROM_BELOW, 1), :]
        gain = from_above * above_gain + from_below * below_gain
        below_gain = jnp.where(side, gain, below_gain)
        above_gain = jnp.where(side, above_gain, gain)
        into = [bases[step][field] for field in range(2)]
        if below is None:
            below = above = [jnp.zeros((rows, cols), F32)] * 2
        else:
            into = [
                into[field] + from_above * above[field] + from_below * below[field]
                for field in range(2)
            ]
        below = [jnp.where(side, into[field], below[field]) for field in range(2)]
        above = [jnp.where(side, above[field], into[field]) for field in range(2)]
    scalars = scalar_rows(fluxes, 3 * rows)
    for field in range(2):
        at = pl.ds(field * rows, rows)
        flux_below, flux_above = level_fluxes(other[at, :], 0.0 if outer is None else outer[at, :])
        below_in[field] = below[field] + scalars[METRIC_BELOW] * flux_below
        above_in[field] = above[field] - scalars[METRIC_ABOVE] * flux_above

    gain = above_gain * table[levels - 1, pl.ds(PIVOT, 1), :]
    for level in range(levels - 1, -1, -1):
        if level < levels - 1:
            gain = gain * table[level, pl.ds(UPPER_PIVOT, 1), :]
        gain = gain + below_gain * table[level, pl.ds(BELOW_FORWARD, 1), :]
        response[level] = jnp.broadcast_to(gain, (TILE, cols))

    row_at = lax.broadcasted_iota(jnp.int32, (TILE, cols), 0)
    width = 2 * TILE
    for begin in range(0, rows, width):
        at = pl.ds(begin, width)

        def solve(level, carry, factor, begin=begin, at=at):
            factor = table[level, pl.ds(factor, 1), :]
            below_factor = table[level, pl.ds(BELOW_FORWARD, 1), :]
            values = []
            for field, cells in enumerate((temp, w_vel)):
                value = forward[field, level + 1, at, :] + below_factor * below_in[field, at, :]
                if begin == 0:
                    change = changes[pl.ds(field * levels + level, 1), :]
                    head = value[:TILE] + jnp.where(row_at == 0, change, 0.0)
                    value = jnp.concatenate([head, value[TILE:]])
                if begin == rows - width:
                    change = changes[pl.ds((2 + field) * levels + level, 1), :]
                    tail = value[-TILE:] + jnp.where(row_at == TILE - 1, change, 0.0)
                    value = jnp.concatenate([value[:-TILE], tail])
                value = value + factor * carry[field]
                known[field, level, at, :] = value - cells[level, at, :]
                values.append(value)
            return tuple(values)

        carry = solve(levels - 1, [above_in[field, at, :] for field in range(2)], PIVOT)

        def step(back, carry, solve=solve):
            return solve(levels - 2 - back, carry, UPPER_PIVOT)

        lax.fori_loop(0, levels - 1, step, carry, unroll=3)


def prepare(rounds, temp, w_vel, forward, table, changes, fluxes, other, crossing, bases, gains):
    levels, rows, cols = temp.shape
    shapes = (held(2, levels, rows, cols), held(levels, TILE, cols))
    shapes += (held(rows, cols),) * (rounds == 2)
    return pl.pallas_call(
        functools.partial(prepare_kernel, rounds),
        out_shape=shapes,
        in_specs=[whole(VMEM)] * (8 + 2 * (rounds - 1)),
        out_specs=[whole(VMEM)] * len(shapes),
        scratch_shapes=[pltpu.VMEM((2, rows, cols), F32)] * 2,
        compiler_params=pltpu.CompilerParams(vmem_limit_bytes=8 * MIB),
        cost_estimate=pl.CostEstimate(
            flops=levels * rows * cols,
            bytes_accessed=24 * levels * rows * cols,
            transcendentals=0,
        ),
        name="prepare",
    )(
        in_vmem(temp), in_vmem(w_vel), in_vmem(forward), in_vmem(table), changes, fluxes, other,
        crossing, *bases, *gains,
    )


def join_kernel(rounds, late, own_at, other_at, mine, theirs, own, other, joined):
    size = theirs.shape[0] // 2
    upper = bit_of("gz", rounds - 1) == 1
    low, high = in_order(upper, scalar_rows(own, own_at), scalar_rows(other, other_at))
    coupling, inverse = interface(low, high)
    scale = coupling * inverse
    to_other = scale * coupling * jnp.where(upper, low[LAST], high[FIRST])
    up, down = high[METRIC_BELOW] * inverse, -low[METRIC_ABOVE] * inverse
    own_gain = coupling * jnp.where(upper, down * low[LAST], up * high[FIRST])
    other_gain = jnp.where(upper, up, down)
    for field in range(2):
        at = pl.ds(field * size, size)
        into = scale * theirs[at, :] + to_other * mine[at, :]
        if late:
            into = into + (own_gain * own[at, :] + other_gain * other[at, :])
        joined[at, :] = into


def join(rounds, late, mine, theirs, own, other):
    size, cols = theirs.shape
    return pl.pallas_call(
        functools.partial(join_kernel, rounds, late, own.shape[0] - TILE, other.shape[0] - TILE),
        out_shape=held(size, cols),
        in_specs=[whole(VMEM)] * 4,
        out_specs=whole(VMEM),
        compiler_params=pltpu.CompilerParams(vmem_limit_bytes=8 * MIB),
        name="join",
    )(mine, theirs, own, other)


def finish_kernel(rounds, swapped, known, response, joined, *rest):
    late, results = rounds == 2, 4 if rounds == 2 else 2
    flux_in, table, tend, far, near = rest[:5] if late else (None,) * 5
    rest = rest[(5 if late else 0) + (results if swapped else results - 2) :]
    outs, (result, rim, sems) = rest[:results], rest[results:]
    _, levels, rows, cols = known.shape
    width, half = 2 * TILE, rows // 2
    core = bit_of("gz", 0)
    start = pl.multiple_of((1 - core if swapped else core) * half, half)
    copies = []
    for field in range(2):
        for part, begin in enumerate(range(0, half, width)):
            into = joined[pl.ds(field * half + begin, width), :]
            tiles = [into[i : i + TILE] for i in range(0, width, TILE)]

            def step(level, carry, field=field, begin=begin, tiles=tiles):
                gain = response[level]
                for i, tile in enumerate(tiles):
                    at = begin + i * TILE
                    value = known[field, level, pl.ds(start + at, TILE), :] + gain * tile
                    result[field, level, pl.ds(at, TILE), :] = value
                return carry

            lax.fori_loop(0, levels, step, 0, unroll=True)
            copies.append(
                pltpu.make_async_copy(
                    result.at[field, :, pl.ds(begin, width), :],
                    outs[field].at[:, pl.ds(start + begin, width), :],
                    sems.at[2 + 2 * field + part],
                )
            )
            copies[-1].start()
    if late:
        diffs = side_changes(far, near)
        level = core * (levels - 1)
        gain = jnp.where(
            core == 1, -table[levels - 1, pl.ds(FALL, 1), :], table[0, pl.ds(RISE, 1), :]
        )
        gain = jnp.where(beside_seam(rounds), gain, 0.0)
        row_at = start + lax.broadcasted_iota(jnp.int32, (half, cols), 0)
        for field in range(2):
            head, tail = (
                jnp.where(
                    core == 1,
                    diff[(field + 1) * levels - 1 : (field + 1) * levels, :],
                    diff[field * levels : field * levels + 1, :],
                )
                for diff in diffs
            )
            edge = jnp.where(row_at == 0, head, jnp.where(row_at == rows - 1, tail, 0.0))
            flux = flux_in[pl.ds(field * half, half), :]
            rim[field] = tend[field, level, pl.ds(start, half), :] + gain * flux + edge
            copies.append(
                pltpu.make_async_copy(
                    rim.at[field],
                    outs[2 + field].at[level, pl.ds(start, half), :],
                    sems.at[field],
                )
            )
            copies[-1].start()
    for copy in copies:
        copy.wait()


def finish(rounds, known, response, joined, late, written):
    _, levels, rows, cols = known.shape
    results = 4 if rounds == 2 else 2
    inputs = 3 + len(late)
    swapped = len(written) == results
    return pl.pallas_call(
        functools.partial(finish_kernel, rounds, swapped),
        out_shape=(jax.ShapeDtypeStruct((levels, rows, cols), F32),) * results,
        in_specs=[whole(VMEM)] * inputs + [whole(pl.ANY)] * len(written),
        out_specs=[whole(pl.ANY)] * results,
        scratch_shapes=[
            pltpu.VMEM((2, levels, rows // 2, cols), F32),
            pltpu.VMEM((2, rows // 2, cols), F32),
            pltpu.SemaphoreType.DMA((6,)),
        ],
        input_output_aliases={
            inputs + i: results - len(written) + i for i in range(len(written))
        },
        compiler_params=pltpu.CompilerParams(vmem_limit_bytes=8 * MIB),
        cost_estimate=pl.CostEstimate(
            flops=20000 * levels * rows * cols,
            bytes_accessed=8 * levels * rows * cols,
            transcendentals=0,
        ),
        name="finish",
    )(in_vmem(known), response, joined, *map(in_vmem, late), *written)


def both_ways(pairs):
    return pairs + [(b, a) for a, b in pairs]


def local(temp, u_vel, v_vel, w_vel, temp_prev, w_prev, lower, upper, metric):
    rows = temp.shape[1]
    across, stacked = lax.axis_size("gx"), lax.axis_size("gz")
    rounds = stacked.bit_length() - 1
    cores = both_ways([(i, i + 1) for i in range(0, stacked, 2)])
    far, near, fluxes, outward, table = edges(
        temp, u_vel, w_vel, v_vel, temp_prev, w_prev, lower, upper, metric
    )
    other = lax.ppermute(fluxes, "gz", cores)
    near = lax.ppermute(near, "gx", both_ways([(i, i + 1) for i in range(0, across, 2)]))
    far = lax.ppermute(far, "gx", both_ways([(i, (i + 1) % across) for i in range(1, across, 2)]))
    outer = ()
    if rounds > 2:
        seams = both_ways([(i, i + 1) for i in range(1, stacked - 1, 2)])
        outer = (lax.ppermute(outward, "gz", seams),)
    forward, tend, first = bulk(other, table, temp, u_vel, v_vel, w_vel, temp_prev, w_prev)
    entries, changes, *late = fix(
        rounds, other, near, far, fluxes, outward, forward, first, table, outer
    )
    message, seam = late if late else (entries, fluxes)
    bases, gains, own, other_own = [], [], fluxes, other
    for step in range(rounds - 1):
        partners = [(i, i ^ (1 << step)) for i in range(stacked)]
        theirs = lax.ppermute(message, "gz", partners)
        if step > 0:
            other_own = lax.ppermute(own, "gz", partners)
        base, gain, message, *scalars = merge(
            step, step + 2 == rounds, bool(late), rows, entries, theirs, own, other_own
        )
        entries, own = message, scalars[0] if scalars else seam
        bases.append(base)
        gains.append(gain)
    partners = [(i, i ^ (stacked // 2)) for i in range(stacked)]
    theirs = lax.ppermute(message, "gz", partners)
    other_own = lax.ppermute(own, "gz", partners)
    known, response, *passed = prepare(
        rounds, temp, w_vel, forward, table, changes, fluxes, other, *(outer or (other_own,)),
        bases, gains,
    )
    tendencies = tends(rounds, table, tend, far, near, other, outer)
    joined = join(rounds, bool(late), message, theirs, own, other_own)
    swapped = lax.ppermute(joined, "gz", cores)
    if not late:
        written = finish(rounds, known, response, joined, (), ())
        return *finish(rounds, known, response, swapped, (), written), *tendencies
    crossed = lax.ppermute(passed[0], "gz", cores)
    late = (table, tend, far, near)
    written = finish(rounds, known, response, joined, (other_own, *late), tendencies)
    return tuple(finish(rounds, known, response, swapped, (crossed, *late), written))


def solution(mesh):
    field = P("gz", "gx", None)
    return jax.shard_map(
        local,
        mesh=mesh,
        in_specs=(field,) * 6 + (P("gz"),) * 3,
        out_specs=(field,) * 4,
        check_vma=False,
    )
```

```python
import functools

import jax
import jax.numpy as jnp
from jax import lax
from jax.experimental import pallas as pl
from jax.experimental.pallas import tpu as pltpu
from jax.sharding import PartitionSpec as P

NEW_WEIGHT = 5.0 / 12.0
HORIZ_DIFF = 0.1
FIELD_WEIGHT = 2.0 / NEW_WEIGHT
PREV_WEIGHT = (17.0 / 60.0) / NEW_WEIGHT
TILE = 8
MIB = 1024 * 1024

PIVOT_NEW, LOWER_PIVOT, UPPER_PIVOT, FIRST_GREEN, BELOW_FORWARD, PIVOT, RISE, FALL = range(8)
FIRST, CORNER, LAST, BELOW, ABOVE, METRIC_BELOW, METRIC_ABOVE = range(7)
FROM_ABOVE, FROM_BELOW = range(2)

VMEM = pltpu.VMEM
F32 = jnp.float32


def whole(space):
    return pl.BlockSpec(memory_space=space)


def held(*shape):
    return pltpu.VMEM(shape, F32)


def in_vmem(array):
    return pltpu.with_memory_space_constraint(array, pltpu.VMEM)


def in_hbm(*arrays):
    return [pltpu.with_memory_space_constraint(array, pltpu.HBM) for array in arrays]


def bit_of(axis, bit):
    return (lax.axis_index(axis) >> bit) & 1


def edges_kernel(
    temp,
    u_vel,
    w_vel,
    v_vel,
    temp_prev,
    w_prev,
    lower,
    upper,
    metric,
    far,
    near,
    fluxes,
    outward,
    table,
    strips,
    layers,
    lower_at,
    upper_at,
    metric_at,
    sems,
):
    levels, rows, cols = temp.shape
    copies = [(lower, lower_at), (upper, upper_at), (metric, metric_at)]
    for at, array in enumerate((temp, w_vel, u_vel)):
        for side, row in enumerate((0, rows - 1)):
            copies.append((array.at[:, row, :], strips.at[at, side]))
    for at, array in enumerate((temp, w_vel)):
        for side, level in enumerate((0, levels - 1)):
            copies.append((array.at[level], layers.at[at, side]))
    copies = [pltpu.make_async_copy(src, dst, sems.at[i]) for i, (src, dst) in enumerate(copies)]
    for copy in copies:
        copy.start()
    for copy in copies[:3]:
        copy.wait()
    coefficients(lower_at, upper_at, metric_at, table, fluxes.at[pl.ds(3 * rows, TILE)])
    for copy in copies[3:]:
        copy.wait()
    odd = bit_of("gx", 0) == 1
    for field in range(2):
        at = pl.ds(field * levels, levels)
        to_left = (HORIZ_DIFF - 0.5 * strips[2, 0]) * strips[field, 0]
        to_right = (HORIZ_DIFF + 0.5 * strips[2, 1]) * strips[field, 1]
        near[at, :] = jnp.where(odd, to_left, to_right)
        far[at, :] = jnp.where(odd, to_right, to_left)
    position = lax.axis_index("gz")
    upper_core = bit_of("gz", 0) == 1
    wall = (position == 0) | (position == lax.axis_size("gz") - 1)
    zero, size = jnp.zeros((rows, cols), F32), rows // 2
    for field in range(2):
        bottom = layers[1, 0] * layers[field, 0]
        top = layers[1, 1] * layers[field, 1]
        fluxes[pl.ds(field * rows, rows), :] = jnp.where(upper_core, bottom, top)
        value = jnp.where(wall, zero, jnp.where(upper_core, top, bottom))
        outward[pl.ds(field * rows, rows), :] = value
        fluxes[pl.ds(2 * rows + field * size, size), :] = jnp.where(
            upper_core, value[:size], value[size:]
        )


def edges(temp, u_vel, w_vel, v_vel, temp_prev, w_prev, lower, upper, metric):
    levels, rows, cols = temp.shape
    return pl.pallas_call(
        edges_kernel,
        out_shape=(
            held(2 * levels, cols),
            held(2 * levels, cols),
            held(3 * rows + TILE, cols),
            held(2 * rows, cols),
            held(levels, TILE, cols),
        ),
        in_specs=[whole(pl.ANY)] * 9,
        out_specs=[whole(VMEM)] * 5,
        scratch_shapes=[
            pltpu.VMEM((3, 2, levels, cols), F32),
            pltpu.VMEM((2, 2, rows, cols), F32),
            pltpu.SMEM((levels,), F32),
            pltpu.SMEM((levels,), F32),
            pltpu.SMEM((levels,), F32),
            pltpu.SemaphoreType.DMA((13,)),
        ],
        compiler_params=pltpu.CompilerParams(vmem_limit_bytes=8 * MIB),
        name="edges",
    )(*in_hbm(temp, u_vel, w_vel, v_vel, temp_prev, w_prev, lower, upper, metric))


def coefficients(lower, upper, metric, table, scalars):
    levels, _, cols = table.shape

    def row(value):
        return jnp.full((1, cols), value, F32)

    ratio = jnp.zeros((1, cols), F32)
    forward = jnp.ones((1, cols), F32)
    for level in range(levels):
        low, high = row(lower[level]), row(upper[level])
        pivot = 1.0 / (1.0 + low + high - low * ratio)
        ratio = high * pivot
        lower_pivot = low * pivot
        forward = pivot if level == 0 else lower_pivot * forward
        table[level, pl.ds(PIVOT_NEW, 1), :] = NEW_WEIGHT * pivot
        table[level, pl.ds(LOWER_PIVOT, 1), :] = lower_pivot
        table[level, pl.ds(UPPER_PIVOT, 1), :] = ratio
        table[level, pl.ds(BELOW_FORWARD, 1), :] = forward
        table[level, pl.ds(PIVOT, 1), :] = pivot
        table[level, pl.ds(RISE, 1), :] = row(metric[level] if level < levels - 1 else 0.0)
        table[level, pl.ds(FALL, 1), :] = row(metric[level] if level > 0 else 0.0)
    green = forward
    table[levels - 1, pl.ds(FIRST_GREEN, 1), :] = NEW_WEIGHT * green
    for level in range(levels - 2, -1, -1):
        green = (
            table[level, pl.ds(BELOW_FORWARD, 1), :]
            + table[level, pl.ds(UPPER_PIVOT, 1), :] * green
        )
        table[level, pl.ds(FIRST_GREEN, 1), :] = NEW_WEIGHT * green
    scalars[pl.ds(FIRST, 1), :] = green
    scalars[pl.ds(CORNER, 1), :] = forward
    scalars[pl.ds(LAST, 1), :] = pivot
    scalars[pl.ds(BELOW, 1), :] = row(lower[0])
    scalars[pl.ds(ABOVE, 1), :] = row(upper[levels - 1])
    scalars[pl.ds(METRIC_BELOW, 1), :] = row(NEW_WEIGHT * metric[0])
    scalars[pl.ds(METRIC_ABOVE, 1), :] = row(NEW_WEIGHT * metric[levels - 1])
    scalars[pl.ds(7, 1), :] = row(0.0)


def bulk_kernel(
    arrived,
    table,
    temp,
    u_vel,
    v_vel,
    w_vel,
    temp_prev,
    w_prev,
    forward,
    tend,
    first,
):
    levels, rows, cols = temp.shape
    strips = rows // TILE
    fields, prevs = (temp, w_vel), (temp_prev, w_prev)
    for field in range(2):
        forward[field, 0] = jnp.zeros((rows, cols), F32)
        first[field] = jnp.zeros((rows, cols), F32)
    row_at = lax.broadcasted_iota(jnp.int32, (TILE, cols), 0)
    zero = jnp.zeros((TILE, cols), F32)

    def sides(level, strip):
        at = pl.ds(strip * TILE, TILE)
        half = 0.5 * u_vel[level, at, :]
        back, ahead = HORIZ_DIFF - half, HORIZ_DIFF + half
        here = [values[level, at, :] for values in fields]
        return (
            here,
            [pltpu.roll(back * value, TILE - 1, 0) for value in here],
            [pltpu.roll(ahead * value, 1, 0) for value in here],
        )

    def pair_step(pair, carry):
        both = (2 * pair, 2 * pair + 1)
        under, over = jnp.maximum(both[0] - 1, 0), jnp.minimum(both[1] + 1, levels - 1)

        def spread(level, at):
            return jnp.broadcast_to(table[level, pl.ds(at, 1), :], (TILE, cols))

        factors = [
            [spread(level, at) for at in (PIVOT_NEW, LOWER_PIVOT, FIRST_GREEN, RISE, FALL)]
            for level in both
        ]
        before = [[zero, zero], [zero, zero]]
        now = [sides(level, 0) for level in both]
        for strip in range(strips):
            none = (None, [zero, zero], None)
            later = [sides(level, strip + 1) if strip + 1 < strips else none for level in both]
            at = pl.ds(strip * TILE, TILE)
            beneath = [values[under, at, :] for values in fields]
            above = [values[over, at, :] for values in fields]
            solved = [forward[field, both[0], at, :] for field in range(2)]
            total = [first[field, at, :] for field in range(2)]
            for i, level in enumerate(both):
                here, back, ahead = now[i]
                pivot, lower_pivot, green, rise, fall = factors[i]
                upward = above if i else now[1][0]
                downward = now[0][0] if i else beneath
                half = 0.5 * v_vel[level, at, :]
                v_back, v_ahead = HORIZ_DIFF - half, HORIZ_DIFF + half
                w_over, w_under = rise * upward[1], fall * downward[1]
                for field in range(2):
                    value = here[field]
                    change = jnp.where(row_at == TILE - 1, later[i][1][field], back[field])
                    change = change + jnp.where(row_at == 0, before[i][field], ahead[field])
                    change = change + pltpu.roll(v_back * value, cols - 1, 1)
                    change = change + pltpu.roll(v_ahead * value, 1, 1)
                    change = change - w_over * upward[field] + w_under * downward[field]
                    change = change + (here[1 - field] - (4.0 * HORIZ_DIFF) * value)
                    tend[field, level, at, :] = change
                    old = prevs[field][level, at, :]
                    right = change + (FIELD_WEIGHT * value - PREV_WEIGHT * old)
                    solved[field] = pivot * right + lower_pivot * solved[field]
                    forward[field, level + 1, at, :] = solved[field]
                    total[field] = total[field] + green * right
            for field in range(2):
                first[field, at, :] = total[field]
            before = [now[0][2], now[1][2]]
            now = later
        return carry

    lax.fori_loop(0, levels // 2, pair_step, 0)


def bulk(arrived, table, *arrays):
    levels, rows, cols = arrays[0].shape
    return pl.pallas_call(
        bulk_kernel,
        out_shape=(
            held(2, levels + 1, rows, cols),
            held(2, levels, rows, cols),
            held(2, rows, cols),
        ),
        in_specs=[whole(pl.ANY)] + [whole(VMEM)] * 7,
        out_specs=[whole(VMEM)] * 3,
        compiler_params=pltpu.CompilerParams(vmem_limit_bytes=8 * MIB),
        cost_estimate=pl.CostEstimate(
            flops=100000 * levels * rows * cols,
            bytes_accessed=24 * levels * rows * cols,
            transcendentals=0,
        ),
        name="bulk",
    )(arrived, *map(in_vmem, (table, *arrays)))


def side_changes(far, near):
    odd = bit_of("gx", 0) == 1
    return jnp.where(odd, near[...], far[...]), jnp.where(odd, far[...], near[...])


def level_fluxes(inner, outer):
    upper = bit_of("gz", 0) == 1
    return jnp.where(upper, inner, outer), jnp.where(upper, outer, inner)


def beside_seam(rounds):
    return bit_of("gz", 0) != bit_of("gz", rounds - 1)


def ends(rows, cols, head, tail):
    at = lax.broadcasted_iota(jnp.int32, (rows, cols), 0)
    return jnp.where(at == 0, head, jnp.where(at == rows - 1, tail, 0.0))


def scalar_rows(ref, begin=0):
    return [ref[pl.ds(begin + at, 1), :] for at in range(7)]


def put_seam(ref, field, value):
    size, cols = value.shape
    for part in range(2):
        at = pl.ds((2 * part + field) * size, size)
        ref[at, :] = value[:, part * cols // 2 : (part + 1) * cols // 2]


def get_seam(ref, field, size):
    parts = [ref[pl.ds((2 * part + field) * size, size), :] for part in range(2)]
    return jnp.concatenate(parts, axis=1)


def in_order(upper, own, other):
    low = [jnp.where(upper, b, a) for a, b in zip(own, other)]
    high = [jnp.where(upper, a, b) for a, b in zip(own, other)]
    return low, high


def interface(low, high):
    coupling = low[ABOVE]
    return coupling, 1.0 / (1.0 - coupling * coupling * low[LAST] * high[FIRST])


def joint_scalars(low, high):
    coupling, inverse = interface(low, high)
    low_out, high_out = low[CORNER] * coupling, high[CORNER] * coupling
    return [
        low[FIRST] + low_out * low_out * inverse * high[FIRST],
        low_out * inverse * high[CORNER],
        high[LAST] + high_out * high_out * inverse * low[LAST],
        low[BELOW],
        high[ABOVE],
        low[METRIC_BELOW],
        high[METRIC_ABOVE],
        jnp.zeros_like(coupling),
    ]


def fix_kernel(
    rounds, levels, other, near, far, fluxes, outward, forward, first, table, *rest
):
    outer, rest = (rest[0], rest[1:]) if rounds > 2 else (None, rest)
    entries, changes, *late = rest
    _, rows, cols = first.shape
    diffs = side_changes(far, near)
    scalars = scalar_rows(fluxes, 3 * rows)
    below, above = scalars[METRIC_BELOW], -scalars[METRIC_ABOVE]
    core, size = bit_of("gz", 0) == 1, rows // 2
    for field in range(2):
        firsts, lasts = [], []
        for side in range(2):
            value = jnp.zeros((1, cols), F32)
            total = jnp.zeros((1, cols), F32)
            for level in range(levels):
                right = diffs[side][field * levels + level : field * levels + level + 1, :]
                value = (
                    table[level, pl.ds(PIVOT_NEW, 1), :] * right
                    + table[level, pl.ds(LOWER_PIVOT, 1), :] * value
                )
                total = total + table[level, pl.ds(FIRST_GREEN, 1), :] * right
                changes[pl.ds((side * 2 + field) * levels + level, 1), :] = value
            firsts.append(total)
            lasts.append(value)
        at = pl.ds(field * rows, rows)
        flux_below, flux_above = level_fluxes(other[at, :], 0.0 if outer is None else outer[at, :])
        first_entry = (
            first[field]
            + (below * scalars[FIRST]) * flux_below
            + (above * scalars[CORNER]) * flux_above
            + ends(rows, cols, *firsts)
        )
        last_entry = (
            forward[field, levels]
            + (below * scalars[CORNER]) * flux_below
            + (above * scalars[LAST]) * flux_above
            + ends(rows, cols, *lasts)
        )
        entries[at, :] = first_entry
        entries[pl.ds((2 + field) * rows, rows), :] = last_entry
        if late:
            message, seam = late
            message[at, :] = jnp.where(core, first_entry, last_entry)
            there = pl.ds(2 * rows + field * size, size)
            message[there, :] = jnp.where(core, last_entry[:size], first_entry[size:])
            value = outward[at, :]
            value = jnp.where(core, value[size:], value[:size])
            put_seam(seam, field, jnp.where(beside_seam(rounds), value, other[there, :]))
    if late:
        far_scalars = scalar_rows(other, 3 * rows)
        for at, value in enumerate(joint_scalars(*in_order(core, scalars, far_scalars))):
            seam[pl.ds(2 * rows + at, 1), :] = value[:, : cols // 2]


def fix(rounds, other, near, far, fluxes, outward, forward, first, table, outer):
    levels = table.shape[0]
    _, rows, cols = first.shape
    shapes = [held(4 * rows, cols), held(4 * levels, cols)]
    if rounds == 2:
        shapes += [held(3 * rows, cols), held(2 * rows + TILE, cols // 2)]
    return pl.pallas_call(
        functools.partial(fix_kernel, rounds, levels),
        out_shape=tuple(shapes),
        in_specs=[whole(VMEM)] * (8 + len(outer)),
        out_specs=[whole(VMEM)] * len(shapes),
        compiler_params=pltpu.CompilerParams(vmem_limit_bytes=8 * MIB),
        name="fix",
    )(
        other, near, far, fluxes, outward, in_vmem(forward), in_vmem(first), in_vmem(table), *outer
    )


def tends_kernel(rounds, table, tend, far, near, other, *rest):
    outer, rest = (rest[0], rest[1:]) if rounds > 2 else (None, rest)
    *outs, layers, strips, sems = rest
    _, levels, rows, cols = tend.shape
    inside, middle = pl.ds(1, levels - 2), pl.ds(TILE, rows - 2 * TILE)
    copies = []

    def send(field, at, src, dst):
        copies.append(pltpu.make_async_copy(src, dst, sems.at[field, at]))
        copies[-1].start()

    for field, out in enumerate(outs):
        send(field, 0, tend.at[field, inside, middle, :], out.at[inside, middle, :])
    diffs = side_changes(far, near)
    tile_at = lax.broadcasted_iota(jnp.int32, (TILE, cols), 0)
    for field, out in enumerate(outs):
        at = pl.ds(field * rows, rows)
        below, above = level_fluxes(other[at, :], 0.0 if outer is None else outer[at, :])
        for side, level, change in (
            (0, 0, table[0, pl.ds(RISE, 1), :] * below),
            (1, levels - 1, -table[levels - 1, pl.ds(FALL, 1), :] * above),
        ):
            at = field * levels + level
            rim = ends(rows, cols, diffs[0][at : at + 1, :], diffs[1][at : at + 1, :])
            layers[field, side] = tend[field, level] + change + rim
            send(field, 1 + side, layers.at[field, side], out.at[level])
        for side, begin, row in ((0, 0, 0), (1, rows - TILE, TILE - 1)):
            for level in range(1, levels - 1):
                at = field * levels + level
                edge = jnp.where(tile_at == row, diffs[side][at : at + 1, :], 0.0)
                strips[field, side, level] = tend[field, level, pl.ds(begin, TILE), :] + edge
            there = out.at[inside, pl.ds(begin, TILE), :]
            send(field, 3 + side, strips.at[field, side, inside], there)
    for copy in copies:
        copy.wait()


def tends(rounds, table, tend, far, near, other, outer):
    _, levels, rows, cols = tend.shape
    return pl.pallas_call(
        functools.partial(tends_kernel, rounds),
        out_shape=(jax.ShapeDtypeStruct((levels, rows, cols), F32),) * 2,
        in_specs=[whole(VMEM)] * (5 + len(outer)),
        out_specs=[whole(pl.ANY)] * 2,
        scratch_shapes=[
            pltpu.VMEM((2, 2, rows, cols), F32),
            pltpu.VMEM((2, 2, levels, TILE, cols), F32),
            pltpu.SemaphoreType.DMA((2, 5)),
        ],
        compiler_params=pltpu.CompilerParams(vmem_limit_bytes=8 * MIB),
        cost_estimate=pl.CostEstimate(
            flops=levels * rows * cols,
            bytes_accessed=8 * levels * rows * cols,
            transcendentals=0,
        ),
        name="tends",
    )(in_vmem(table), in_vmem(tend), far, near, other, *outer)


def merge_kernel(bit, final, late, own_at, other_at, mine, theirs, own, other, base, gains, *rest):
    _, rows, cols = base.shape
    upper = bit_of("gz", bit) == 1
    low, high = in_order(upper, scalar_rows(own, own_at), scalar_rows(other, other_at))
    coupling, inverse = interface(low, high)
    to_high, to_low = high[FIRST] * coupling, low[LAST] * coupling
    low_out, high_out = low[CORNER] * coupling, high[CORNER] * coupling
    core, size = bit_of("gz", 0) == 1, rows // 2
    sends_last = bit_of("gz", bit + 1) == 0
    for field in range(2):
        here = pl.ds(field * rows, rows)
        own_first, own_last = mine[here, :], mine[pl.ds((2 + field) * rows, rows), :]
        if late:
            low_last = jnp.where(upper, theirs[here, :], own_last)
            high_first = jnp.where(upper, own_first, theirs[here, :])
        else:
            other_first, other_last = theirs[here, :], theirs[pl.ds((2 + field) * rows, rows), :]
            low_last = jnp.where(upper, other_last, own_last)
            high_first = jnp.where(upper, own_first, other_first)
            low_first = jnp.where(upper, other_first, own_first)
            high_last = jnp.where(upper, own_last, other_last)
        above = inverse * (high_first + to_high * low_last)
        below = inverse * (low_last + to_low * high_first)
        base[field] = coupling * jnp.where(upper, below, above)
        more = jnp.where(sends_last, high_out * below, low_out * above)
        if late:
            outside = jnp.where(upper, own_last, own_first)
            outside = jnp.where(core, outside[size:], outside[:size])
            there = theirs[pl.ds(2 * rows + field * size, size), :]
            outside = jnp.where(sends_last == upper, outside, there)
        elif final:
            outside = jnp.where(sends_last, high_last, low_first)
            outside = jnp.where(core, outside[size:], outside[:size])
        if final:
            value = outside + jnp.where(core, more[size:], more[:size])
            rest[0][pl.ds(field * size, size), :] = value
        else:
            rest[0][here, :] = low_first + low_out * above
            rest[0][pl.ds((2 + field) * rows, rows), :] = high_last + high_out * below
    if not late:
        for at, value in enumerate(joint_scalars(low, high)):
            rest[1][pl.ds(at, 1), :] = value
    scale = coupling * inverse
    gains[...] = jnp.zeros(gains.shape, F32)
    gains[pl.ds(FROM_ABOVE, 1), :] = scale * high[CORNER] * jnp.where(upper, to_low, 1.0)
    gains[pl.ds(FROM_BELOW, 1), :] = scale * low[CORNER] * jnp.where(upper, 1.0, to_high)


def merge(bit, final, late, rows, mine, theirs, own, other):
    cols = mine.shape[1]
    shapes = [held(2, rows, cols), held(TILE, cols), held((1 if final else 4) * rows, cols)]
    if not late:
        shapes.append(held(TILE, cols))
    return pl.pallas_call(
        functools.partial(
            merge_kernel, bit, final, late, own.shape[0] - TILE, other.shape[0] - TILE
        ),
        out_shape=tuple(shapes),
        in_specs=[whole(VMEM)] * 4,
        out_specs=[whole(VMEM)] * len(shapes),
        compiler_params=pltpu.CompilerParams(vmem_limit_bytes=8 * MIB),
        name="merge",
    )(mine, theirs, own, other)


def prepare_kernel(
    rounds, temp, w_vel, forward, table, changes, fluxes, other, crossing, *rest
):
    outer = crossing if rounds > 2 else None
    bases, gains = rest[: rounds - 1], rest[rounds - 1 : 2 * rounds - 2]
    known, response, *passed, below_in, above_in = rest[2 * rounds - 2 :]
    if passed:
        passed[0][...] = crossing[pl.ds(0, passed[0].shape[0]), :]
    levels, rows, cols = temp.shape
    upper = bit_of("gz", rounds - 1) == 1
    one, none = jnp.ones((1, cols), F32), jnp.zeros((1, cols), F32)
    below_gain, above_gain = jnp.where(upper, one, none), jnp.where(upper, none, one)
    below = above = None
    for step in range(rounds - 2, -1, -1):
        side = bit_of("gz", step) == 1
        from_above = gains[step][pl.ds(FROM_ABOVE, 1), :]
        from_below = gains[step][pl.ds(FROM_BELOW, 1), :]
        gain = from_above * above_gain + from_below * below_gain
        below_gain = jnp.where(side, gain, below_gain)
        above_gain = jnp.where(side, above_gain, gain)
        into = [bases[step][field] for field in range(2)]
        if below is None:
            below = above = [jnp.zeros((rows, cols), F32)] * 2
        else:
            into = [
                into[field] + from_above * above[field] + from_below * below[field]
                for field in range(2)
            ]
        below = [jnp.where(side, into[field], below[field]) for field in range(2)]
        above = [jnp.where(side, above[field], into[field]) for field in range(2)]
    scalars = scalar_rows(fluxes, 3 * rows)
    for field in range(2):
        at = pl.ds(field * rows, rows)
        flux_below, flux_above = level_fluxes(other[at, :], 0.0 if outer is None else outer[at, :])
        below_in[field] = below[field] + scalars[METRIC_BELOW] * flux_below
        above_in[field] = above[field] - scalars[METRIC_ABOVE] * flux_above

    gain = above_gain * table[levels - 1, pl.ds(PIVOT, 1), :]
    for level in range(levels - 1, -1, -1):
        if level < levels - 1:
            gain = gain * table[level, pl.ds(UPPER_PIVOT, 1), :]
        gain = gain + below_gain * table[level, pl.ds(BELOW_FORWARD, 1), :]
        response[level] = jnp.broadcast_to(gain, (TILE, cols))

    row_at = lax.broadcasted_iota(jnp.int32, (TILE, cols), 0)
    width = 2 * TILE
    for begin in range(0, rows, width):
        at = pl.ds(begin, width)

        def solve(level, carry, factor, begin=begin, at=at):
            factor = table[level, pl.ds(factor, 1), :]
            below_factor = table[level, pl.ds(BELOW_FORWARD, 1), :]
            values = []
            for field, cells in enumerate((temp, w_vel)):
                value = forward[field, level + 1, at, :] + below_factor * below_in[field, at, :]
                if begin == 0:
                    change = changes[pl.ds(field * levels + level, 1), :]
                    head = value[:TILE] + jnp.where(row_at == 0, change, 0.0)
                    value = jnp.concatenate([head, value[TILE:]])
                if begin == rows - width:
                    change = changes[pl.ds((2 + field) * levels + level, 1), :]
                    tail = value[-TILE:] + jnp.where(row_at == TILE - 1, change, 0.0)
                    value = jnp.concatenate([value[:-TILE], tail])
                value = value + factor * carry[field]
                known[field, level, at, :] = value - cells[level, at, :]
                values.append(value)
            return tuple(values)

        carry = solve(levels - 1, [above_in[field, at, :] for field in range(2)], PIVOT)

        def step(back, carry, solve=solve):
            return solve(levels - 2 - back, carry, UPPER_PIVOT)

        lax.fori_loop(0, levels - 1, step, carry, unroll=3)


def prepare(rounds, temp, w_vel, forward, table, changes, fluxes, other, crossing, bases, gains):
    levels, rows, cols = temp.shape
    shapes = (held(2, levels, rows, cols), held(levels, TILE, cols))
    shapes += (held(2 * rows, cols // 2),) * (rounds == 2)
    return pl.pallas_call(
        functools.partial(prepare_kernel, rounds),
        out_shape=shapes,
        in_specs=[whole(VMEM)] * (8 + 2 * (rounds - 1)),
        out_specs=[whole(VMEM)] * len(shapes),
        scratch_shapes=[pltpu.VMEM((2, rows, cols), F32)] * 2,
        compiler_params=pltpu.CompilerParams(vmem_limit_bytes=8 * MIB),
        cost_estimate=pl.CostEstimate(
            flops=levels * rows * cols,
            bytes_accessed=24 * levels * rows * cols,
            transcendentals=0,
        ),
        name="prepare",
    )(
        in_vmem(temp), in_vmem(w_vel), in_vmem(forward), in_vmem(table), changes, fluxes, other,
        crossing, *bases, *gains,
    )


def join_kernel(rounds, late, own_at, other_at, mine, theirs, own, other, joined):
    size = theirs.shape[0] // 2
    upper = bit_of("gz", rounds - 1) == 1
    low, high = in_order(upper, scalar_rows(own, own_at), scalar_rows(other, other_at))
    if late:
        low, high = ([jnp.concatenate([a, a], axis=1) for a in rows] for rows in (low, high))
    coupling, inverse = interface(low, high)
    scale = coupling * inverse
    to_other = scale * coupling * jnp.where(upper, low[LAST], high[FIRST])
    up, down = high[METRIC_BELOW] * inverse, -low[METRIC_ABOVE] * inverse
    own_gain = coupling * jnp.where(upper, down * low[LAST], up * high[FIRST])
    other_gain = jnp.where(upper, up, down)
    for field in range(2):
        at = pl.ds(field * size, size)
        into = scale * theirs[at, :] + to_other * mine[at, :]
        if late:
            into = into + own_gain * get_seam(own, field, size)
            into = into + other_gain * get_seam(other, field, size)
        joined[at, :] = into


def join(rounds, late, mine, theirs, own, other):
    size, cols = theirs.shape
    return pl.pallas_call(
        functools.partial(join_kernel, rounds, late, own.shape[0] - TILE, other.shape[0] - TILE),
        out_shape=held(size, cols),
        in_specs=[whole(VMEM)] * 4,
        out_specs=whole(VMEM),
        compiler_params=pltpu.CompilerParams(vmem_limit_bytes=8 * MIB),
        name="join",
    )(mine, theirs, own, other)


def finish_kernel(rounds, swapped, known, response, joined, *rest):
    late, results = rounds == 2, 4 if rounds == 2 else 2
    flux_in, table, tend, far, near = rest[:5] if late else (None,) * 5
    rest = rest[(5 if late else 0) + (results if swapped else results - 2) :]
    outs, (result, rim, sems) = rest[:results], rest[results:]
    _, levels, rows, cols = known.shape
    width, half = 2 * TILE, rows // 2
    core = bit_of("gz", 0)
    start = pl.multiple_of((1 - core if swapped else core) * half, half)
    copies = []
    for field in range(2):
        for part, begin in enumerate(range(0, half, width)):
            into = joined[pl.ds(field * half + begin, width), :]
            tiles = [into[i : i + TILE] for i in range(0, width, TILE)]

            def step(level, carry, field=field, begin=begin, tiles=tiles):
                gain = response[level]
                for i, tile in enumerate(tiles):
                    at = begin + i * TILE
                    value = known[field, level, pl.ds(start + at, TILE), :] + gain * tile
                    result[field, level, pl.ds(at, TILE), :] = value
                return carry

            lax.fori_loop(0, levels, step, 0, unroll=True)
            copies.append(
                pltpu.make_async_copy(
                    result.at[field, :, pl.ds(begin, width), :],
                    outs[field].at[:, pl.ds(start + begin, width), :],
                    sems.at[2 + 2 * field + part],
                )
            )
            copies[-1].start()
    if late:
        diffs = side_changes(far, near)
        level = core * (levels - 1)
        gain = jnp.where(
            core == 1, -table[levels - 1, pl.ds(FALL, 1), :], table[0, pl.ds(RISE, 1), :]
        )
        gain = jnp.where(beside_seam(rounds), gain, 0.0)
        row_at = start + lax.broadcasted_iota(jnp.int32, (half, cols), 0)
        for field in range(2):
            head, tail = (
                jnp.where(
                    core == 1,
                    diff[(field + 1) * levels - 1 : (field + 1) * levels, :],
                    diff[field * levels : field * levels + 1, :],
                )
                for diff in diffs
            )
            edge = jnp.where(row_at == 0, head, jnp.where(row_at == rows - 1, tail, 0.0))
            flux = get_seam(flux_in, field, half)
            rim[field] = tend[field, level, pl.ds(start, half), :] + gain * flux + edge
            copies.append(
                pltpu.make_async_copy(
                    rim.at[field],
                    outs[2 + field].at[level, pl.ds(start, half), :],
                    sems.at[field],
                )
            )
            copies[-1].start()
    for copy in copies:
        copy.wait()


def finish(rounds, known, response, joined, late, written):
    _, levels, rows, cols = known.shape
    results = 4 if rounds == 2 else 2
    inputs = 3 + len(late)
    swapped = len(written) == results
    return pl.pallas_call(
        functools.partial(finish_kernel, rounds, swapped),
        out_shape=(jax.ShapeDtypeStruct((levels, rows, cols), F32),) * results,
        in_specs=[whole(VMEM)] * inputs + [whole(pl.ANY)] * len(written),
        out_specs=[whole(pl.ANY)] * results,
        scratch_shapes=[
            pltpu.VMEM((2, levels, rows // 2, cols), F32),
            pltpu.VMEM((2, rows // 2, cols), F32),
            pltpu.SemaphoreType.DMA((6,)),
        ],
        input_output_aliases={
            inputs + i: results - len(written) + i for i in range(len(written))
        },
        compiler_params=pltpu.CompilerParams(vmem_limit_bytes=8 * MIB),
        cost_estimate=pl.CostEstimate(
            flops=20000 * levels * rows * cols,
            bytes_accessed=8 * levels * rows * cols,
            transcendentals=0,
        ),
        name="finish",
    )(in_vmem(known), response, joined, *map(in_vmem, late), *written)


def both_ways(pairs):
    return pairs + [(b, a) for a, b in pairs]


def local(temp, u_vel, v_vel, w_vel, temp_prev, w_prev, lower, upper, metric):
    rows = temp.shape[1]
    across, stacked = lax.axis_size("gx"), lax.axis_size("gz")
    rounds = stacked.bit_length() - 1
    cores = both_ways([(i, i + 1) for i in range(0, stacked, 2)])
    far, near, fluxes, outward, table = edges(
        temp, u_vel, w_vel, v_vel, temp_prev, w_prev, lower, upper, metric
    )
    other = lax.ppermute(fluxes, "gz", cores)
    near = lax.ppermute(near, "gx", both_ways([(i, i + 1) for i in range(0, across, 2)]))
    far = lax.ppermute(far, "gx", both_ways([(i, (i + 1) % across) for i in range(1, across, 2)]))
    outer = ()
    if rounds > 2:
        seams = both_ways([(i, i + 1) for i in range(1, stacked - 1, 2)])
        outer = (lax.ppermute(outward, "gz", seams),)
    forward, tend, first = bulk(other, table, temp, u_vel, v_vel, w_vel, temp_prev, w_prev)
    entries, changes, *late = fix(
        rounds, other, near, far, fluxes, outward, forward, first, table, outer
    )
    message, seam = late if late else (entries, fluxes)
    bases, gains, own, other_own = [], [], fluxes, other
    for step in range(rounds - 1):
        partners = [(i, i ^ (1 << step)) for i in range(stacked)]
        theirs = lax.ppermute(message, "gz", partners)
        if step > 0:
            other_own = lax.ppermute(own, "gz", partners)
        base, gain, message, *scalars = merge(
            step, step + 2 == rounds, bool(late), rows, entries, theirs, own, other_own
        )
        entries, own = message, scalars[0] if scalars else seam
        bases.append(base)
        gains.append(gain)
    partners = [(i, i ^ (stacked // 2)) for i in range(stacked)]
    theirs = lax.ppermute(message, "gz", partners)
    other_own = lax.ppermute(own, "gz", partners)
    known, response, *passed = prepare(
        rounds, temp, w_vel, forward, table, changes, fluxes, other, *(outer or (other_own,)),
        bases, gains,
    )
    tendencies = tends(rounds, table, tend, far, near, other, outer)
    joined = join(rounds, bool(late), message, theirs, own, other_own)
    swapped = lax.ppermute(joined, "gz", cores)
    if not late:
        written = finish(rounds, known, response, joined, (), ())
        return *finish(rounds, known, response, swapped, (), written), *tendencies
    crossed = lax.ppermute(passed[0], "gz", cores)
    late = (table, tend, far, near)
    written = finish(rounds, known, response, joined, (other_own, *late), tendencies)
    return tuple(finish(rounds, known, response, swapped, (crossed, *late), written))


def solution(mesh):
    field = P("gz", "gx", None)
    return jax.shard_map(
        local,
        mesh=mesh,
        in_specs=(field,) * 6 + (P("gz"),) * 3,
        out_specs=(field,) * 4,
        check_vma=False,
    )
```

```python
import functools

import jax
import jax.numpy as jnp
from jax import lax
from jax.experimental import pallas as pl
from jax.experimental.pallas import tpu as pltpu
from jax.sharding import PartitionSpec as P

NEW_WEIGHT = 5.0 / 12.0
HORIZ_DIFF = 0.1
FIELD_WEIGHT = 2.0 / NEW_WEIGHT
PREV_WEIGHT = (17.0 / 60.0) / NEW_WEIGHT
TILE = 8
MIB = 1024 * 1024

PIVOT_NEW, LOWER_PIVOT, UPPER_PIVOT, FIRST_GREEN, BELOW_FORWARD, PIVOT, RISE, FALL = range(8)
FIRST, CORNER, LAST, BELOW, ABOVE, METRIC_BELOW, METRIC_ABOVE = range(7)
FROM_ABOVE, FROM_BELOW = range(2)

VMEM = pltpu.VMEM
F32 = jnp.float32


def whole(space):
    return pl.BlockSpec(memory_space=space)


def held(*shape):
    return pltpu.VMEM(shape, F32)


def in_vmem(array):
    return pltpu.with_memory_space_constraint(array, pltpu.VMEM)


def in_hbm(*arrays):
    return [pltpu.with_memory_space_constraint(array, pltpu.HBM) for array in arrays]


def bit_of(axis, bit):
    return (lax.axis_index(axis) >> bit) & 1


def edges_kernel(
    temp,
    u_vel,
    w_vel,
    v_vel,
    temp_prev,
    w_prev,
    lower,
    upper,
    metric,
    far,
    near,
    fluxes,
    outward,
    table,
    strips,
    layers,
    lower_at,
    upper_at,
    metric_at,
    sems,
):
    levels, rows, cols = temp.shape
    copies = [(lower, lower_at), (upper, upper_at), (metric, metric_at)]
    for at, array in enumerate((temp, w_vel, u_vel)):
        for side, row in enumerate((0, rows - 1)):
            copies.append((array.at[:, row, :], strips.at[at, side]))
    for at, array in enumerate((temp, w_vel)):
        for side, level in enumerate((0, levels - 1)):
            copies.append((array.at[level], layers.at[at, side]))
    copies = [pltpu.make_async_copy(src, dst, sems.at[i]) for i, (src, dst) in enumerate(copies)]
    for copy in copies:
        copy.start()
    for copy in copies[:3]:
        copy.wait()
    coefficients(lower_at, upper_at, metric_at, table, fluxes.at[pl.ds(3 * rows, TILE)])
    for copy in copies[3:]:
        copy.wait()
    odd = bit_of("gx", 0) == 1
    for field in range(2):
        at = pl.ds(field * levels, levels)
        to_left = (HORIZ_DIFF - 0.5 * strips[2, 0]) * strips[field, 0]
        to_right = (HORIZ_DIFF + 0.5 * strips[2, 1]) * strips[field, 1]
        near[at, :] = jnp.where(odd, to_left, to_right)
        far[at, :] = jnp.where(odd, to_right, to_left)
    position = lax.axis_index("gz")
    upper_core = bit_of("gz", 0) == 1
    wall = (position == 0) | (position == lax.axis_size("gz") - 1)
    zero, size = jnp.zeros((rows, cols), F32), rows // 2
    for field in range(2):
        bottom = layers[1, 0] * layers[field, 0]
        top = layers[1, 1] * layers[field, 1]
        fluxes[pl.ds(field * rows, rows), :] = jnp.where(upper_core, bottom, top)
        value = jnp.where(wall, zero, jnp.where(upper_core, top, bottom))
        outward[pl.ds(field * rows, rows), :] = value
        fluxes[pl.ds(2 * rows + field * size, size), :] = jnp.where(
            upper_core, value[:size], value[size:]
        )


def edges(temp, u_vel, w_vel, v_vel, temp_prev, w_prev, lower, upper, metric):
    levels, rows, cols = temp.shape
    return pl.pallas_call(
        edges_kernel,
        out_shape=(
            held(2 * levels, cols),
            held(2 * levels, cols),
            held(3 * rows + TILE, cols),
            held(2 * rows, cols),
            held(levels, TILE, cols),
        ),
        in_specs=[whole(pl.ANY)] * 9,
        out_specs=[whole(VMEM)] * 5,
        scratch_shapes=[
            pltpu.VMEM((3, 2, levels, cols), F32),
            pltpu.VMEM((2, 2, rows, cols), F32),
            pltpu.SMEM((levels,), F32),
            pltpu.SMEM((levels,), F32),
            pltpu.SMEM((levels,), F32),
            pltpu.SemaphoreType.DMA((13,)),
        ],
        compiler_params=pltpu.CompilerParams(vmem_limit_bytes=8 * MIB),
        name="edges",
    )(*in_hbm(temp, u_vel, w_vel, v_vel, temp_prev, w_prev, lower, upper, metric))


def coefficients(lower, upper, metric, table, scalars):
    levels, _, cols = table.shape

    def row(value):
        return jnp.full((1, cols), value, F32)

    ratio = jnp.zeros((1, cols), F32)
    forward = jnp.ones((1, cols), F32)
    for level in range(levels):
        low, high = row(lower[level]), row(upper[level])
        pivot = 1.0 / (1.0 + low + high - low * ratio)
        ratio = high * pivot
        lower_pivot = low * pivot
        forward = pivot if level == 0 else lower_pivot * forward
        table[level, pl.ds(PIVOT_NEW, 1), :] = NEW_WEIGHT * pivot
        table[level, pl.ds(LOWER_PIVOT, 1), :] = lower_pivot
        table[level, pl.ds(UPPER_PIVOT, 1), :] = ratio
        table[level, pl.ds(BELOW_FORWARD, 1), :] = forward
        table[level, pl.ds(PIVOT, 1), :] = pivot
        table[level, pl.ds(RISE, 1), :] = row(metric[level] if level < levels - 1 else 0.0)
        table[level, pl.ds(FALL, 1), :] = row(metric[level] if level > 0 else 0.0)
    green = forward
    table[levels - 1, pl.ds(FIRST_GREEN, 1), :] = NEW_WEIGHT * green
    for level in range(levels - 2, -1, -1):
        green = (
            table[level, pl.ds(BELOW_FORWARD, 1), :]
            + table[level, pl.ds(UPPER_PIVOT, 1), :] * green
        )
        table[level, pl.ds(FIRST_GREEN, 1), :] = NEW_WEIGHT * green
    scalars[pl.ds(FIRST, 1), :] = green
    scalars[pl.ds(CORNER, 1), :] = forward
    scalars[pl.ds(LAST, 1), :] = pivot
    scalars[pl.ds(BELOW, 1), :] = row(lower[0])
    scalars[pl.ds(ABOVE, 1), :] = row(upper[levels - 1])
    scalars[pl.ds(METRIC_BELOW, 1), :] = row(NEW_WEIGHT * metric[0])
    scalars[pl.ds(METRIC_ABOVE, 1), :] = row(NEW_WEIGHT * metric[levels - 1])
    scalars[pl.ds(7, 1), :] = row(0.0)


def bulk_kernel(
    arrived,
    table,
    temp,
    u_vel,
    v_vel,
    w_vel,
    temp_prev,
    w_prev,
    forward,
    tend,
    first,
):
    levels, rows, cols = temp.shape
    strips = rows // TILE
    fields, prevs = (temp, w_vel), (temp_prev, w_prev)
    for field in range(2):
        forward[field, 0] = jnp.zeros((rows, cols), F32)
        first[field] = jnp.zeros((rows, cols), F32)
    row_at = lax.broadcasted_iota(jnp.int32, (TILE, cols), 0)
    zero = jnp.zeros((TILE, cols), F32)

    def sides(level, strip):
        at = pl.ds(strip * TILE, TILE)
        half = 0.5 * u_vel[level, at, :]
        back, ahead = HORIZ_DIFF - half, HORIZ_DIFF + half
        here = [values[level, at, :] for values in fields]
        return (
            here,
            [pltpu.roll(back * value, TILE - 1, 0) for value in here],
            [pltpu.roll(ahead * value, 1, 0) for value in here],
        )

    def pair_step(pair, carry):
        both = (2 * pair, 2 * pair + 1)
        under, over = jnp.maximum(both[0] - 1, 0), jnp.minimum(both[1] + 1, levels - 1)

        def spread(level, at):
            tile = jnp.broadcast_to(table[level, pl.ds(at, 1), : cols // 2], (TILE, cols // 2))
            return jnp.concatenate([tile, tile], axis=1)

        factors = [
            [spread(level, at) for at in (PIVOT_NEW, LOWER_PIVOT, FIRST_GREEN, RISE, FALL)]
            for level in both
        ]
        before = [[zero, zero], [zero, zero]]
        now = [sides(level, 0) for level in both]
        for strip in range(strips):
            none = (None, [zero, zero], None)
            later = [sides(level, strip + 1) if strip + 1 < strips else none for level in both]
            at = pl.ds(strip * TILE, TILE)
            beneath = [values[under, at, :] for values in fields]
            above = [values[over, at, :] for values in fields]
            solved = [forward[field, both[0], at, :] for field in range(2)]
            total = [first[field, at, :] for field in range(2)]
            for i, level in enumerate(both):
                here, back, ahead = now[i]
                pivot, lower_pivot, green, rise, fall = factors[i]
                upward = above if i else now[1][0]
                downward = now[0][0] if i else beneath
                half = 0.5 * v_vel[level, at, :]
                v_back, v_ahead = HORIZ_DIFF - half, HORIZ_DIFF + half
                w_over, w_under = rise * upward[1], fall * downward[1]
                for field in range(2):
                    value = here[field]
                    change = jnp.where(row_at == TILE - 1, later[i][1][field], back[field])
                    change = change + jnp.where(row_at == 0, before[i][field], ahead[field])
                    change = change + pltpu.roll(v_back * value, cols - 1, 1)
                    change = change + pltpu.roll(v_ahead * value, 1, 1)
                    change = change - w_over * upward[field] + w_under * downward[field]
                    change = change + (here[1 - field] - (4.0 * HORIZ_DIFF) * value)
                    tend[field, level, at, :] = change
                    old = prevs[field][level, at, :]
                    right = change + (FIELD_WEIGHT * value - PREV_WEIGHT * old)
                    solved[field] = pivot * right + lower_pivot * solved[field]
                    forward[field, level + 1, at, :] = solved[field]
                    total[field] = total[field] + green * right
            for field in range(2):
                first[field, at, :] = total[field]
            before = [now[0][2], now[1][2]]
            now = later
        return carry

    lax.fori_loop(0, levels // 2, pair_step, 0)


def bulk(arrived, table, *arrays):
    levels, rows, cols = arrays[0].shape
    return pl.pallas_call(
        bulk_kernel,
        out_shape=(
            held(2, levels + 1, rows, cols),
            held(2, levels, rows, cols),
            held(2, rows, cols),
        ),
        in_specs=[whole(pl.ANY)] + [whole(VMEM)] * 7,
        out_specs=[whole(VMEM)] * 3,
        compiler_params=pltpu.CompilerParams(vmem_limit_bytes=8 * MIB),
        cost_estimate=pl.CostEstimate(
            flops=100000 * levels * rows * cols,
            bytes_accessed=24 * levels * rows * cols,
            transcendentals=0,
        ),
        name="bulk",
    )(arrived, *map(in_vmem, (table, *arrays)))


def side_changes(far, near):
    odd = bit_of("gx", 0) == 1
    return jnp.where(odd, near[...], far[...]), jnp.where(odd, far[...], near[...])


def level_fluxes(inner, outer):
    upper = bit_of("gz", 0) == 1
    return jnp.where(upper, inner, outer), jnp.where(upper, outer, inner)


def beside_seam(rounds):
    return bit_of("gz", 0) != bit_of("gz", rounds - 1)


def ends(rows, cols, head, tail):
    at = lax.broadcasted_iota(jnp.int32, (rows, cols), 0)
    return jnp.where(at == 0, head, jnp.where(at == rows - 1, tail, 0.0))


def scalar_rows(ref, begin=0):
    return [ref[pl.ds(begin + at, 1), :] for at in range(7)]


def put_seam(ref, field, value):
    size, cols = value.shape
    for part in range(2):
        at = pl.ds((2 * part + field) * size, size)
        ref[at, :] = value[:, part * cols // 2 : (part + 1) * cols // 2]


def get_seam(ref, field, size):
    parts = [ref[pl.ds((2 * part + field) * size, size), :] for part in range(2)]
    return jnp.concatenate(parts, axis=1)


def in_order(upper, own, other):
    low = [jnp.where(upper, b, a) for a, b in zip(own, other)]
    high = [jnp.where(upper, a, b) for a, b in zip(own, other)]
    return low, high


def interface(low, high):
    coupling = low[ABOVE]
    return coupling, 1.0 / (1.0 - coupling * coupling * low[LAST] * high[FIRST])


def joint_scalars(low, high):
    coupling, inverse = interface(low, high)
    low_out, high_out = low[CORNER] * coupling, high[CORNER] * coupling
    return [
        low[FIRST] + low_out * low_out * inverse * high[FIRST],
        low_out * inverse * high[CORNER],
        high[LAST] + high_out * high_out * inverse * low[LAST],
        low[BELOW],
        high[ABOVE],
        low[METRIC_BELOW],
        high[METRIC_ABOVE],
        jnp.zeros_like(coupling),
    ]


def fix_kernel(
    rounds, levels, other, near, far, fluxes, outward, forward, first, table, *rest
):
    outer, rest = (rest[0], rest[1:]) if rounds > 2 else (None, rest)
    entries, changes, *late = rest
    _, rows, cols = first.shape
    diffs = side_changes(far, near)
    scalars = scalar_rows(fluxes, 3 * rows)
    below, above = scalars[METRIC_BELOW], -scalars[METRIC_ABOVE]
    core, size = bit_of("gz", 0) == 1, rows // 2
    for field in range(2):
        firsts, lasts = [], []
        for side in range(2):
            value = jnp.zeros((1, cols), F32)
            total = jnp.zeros((1, cols), F32)
            for level in range(levels):
                right = diffs[side][field * levels + level : field * levels + level + 1, :]
                value = (
                    table[level, pl.ds(PIVOT_NEW, 1), :] * right
                    + table[level, pl.ds(LOWER_PIVOT, 1), :] * value
                )
                total = total + table[level, pl.ds(FIRST_GREEN, 1), :] * right
                changes[pl.ds((side * 2 + field) * levels + level, 1), :] = value
            firsts.append(total)
            lasts.append(value)
        at = pl.ds(field * rows, rows)
        flux_below, flux_above = level_fluxes(other[at, :], 0.0 if outer is None else outer[at, :])
        first_entry = (
            first[field]
            + (below * scalars[FIRST]) * flux_below
            + (above * scalars[CORNER]) * flux_above
            + ends(rows, cols, *firsts)
        )
        last_entry = (
            forward[field, levels]
            + (below * scalars[CORNER]) * flux_below
            + (above * scalars[LAST]) * flux_above
            + ends(rows, cols, *lasts)
        )
        entries[at, :] = first_entry
        entries[pl.ds((2 + field) * rows, rows), :] = last_entry
        if late:
            message, seam = late
            message[at, :] = jnp.where(core, first_entry, last_entry)
            there = pl.ds(2 * rows + field * size, size)
            message[there, :] = jnp.where(core, last_entry[:size], first_entry[size:])
            value = outward[at, :]
            value = jnp.where(core, value[size:], value[:size])
            put_seam(seam, field, jnp.where(beside_seam(rounds), value, other[there, :]))
    if late:
        far_scalars = scalar_rows(other, 3 * rows)
        for at, value in enumerate(joint_scalars(*in_order(core, scalars, far_scalars))):
            seam[pl.ds(2 * rows + at, 1), :] = value[:, : cols // 2]


def fix(rounds, other, near, far, fluxes, outward, forward, first, table, outer):
    levels = table.shape[0]
    _, rows, cols = first.shape
    shapes = [held(4 * rows, cols), held(4 * levels, cols)]
    if rounds == 2:
        shapes += [held(3 * rows, cols), held(2 * rows + TILE, cols // 2)]
    return pl.pallas_call(
        functools.partial(fix_kernel, rounds, levels),
        out_shape=tuple(shapes),
        in_specs=[whole(VMEM)] * (8 + len(outer)),
        out_specs=[whole(VMEM)] * len(shapes),
        compiler_params=pltpu.CompilerParams(vmem_limit_bytes=8 * MIB),
        name="fix",
    )(
        other, near, far, fluxes, outward, in_vmem(forward), in_vmem(first), in_vmem(table), *outer
    )


def tends_kernel(rounds, table, tend, far, near, other, *rest):
    outer, rest = (rest[0], rest[1:]) if rounds > 2 else (None, rest)
    *outs, layers, strips, sems = rest
    _, levels, rows, cols = tend.shape
    inside, middle = pl.ds(1, levels - 2), pl.ds(TILE, rows - 2 * TILE)
    copies = []

    def send(field, at, src, dst):
        copies.append(pltpu.make_async_copy(src, dst, sems.at[field, at]))
        copies[-1].start()

    for field, out in enumerate(outs):
        send(field, 0, tend.at[field, inside, middle, :], out.at[inside, middle, :])
    diffs = side_changes(far, near)
    tile_at = lax.broadcasted_iota(jnp.int32, (TILE, cols), 0)
    for field, out in enumerate(outs):
        at = pl.ds(field * rows, rows)
        below, above = level_fluxes(other[at, :], 0.0 if outer is None else outer[at, :])
        for side, level, change in (
            (0, 0, table[0, pl.ds(RISE, 1), :] * below),
            (1, levels - 1, -table[levels - 1, pl.ds(FALL, 1), :] * above),
        ):
            at = field * levels + level
            rim = ends(rows, cols, diffs[0][at : at + 1, :], diffs[1][at : at + 1, :])
            layers[field, side] = tend[field, level] + change + rim
            send(field, 1 + side, layers.at[field, side], out.at[level])
        for side, begin, row in ((0, 0, 0), (1, rows - TILE, TILE - 1)):
            for level in range(1, levels - 1):
                at = field * levels + level
                edge = jnp.where(tile_at == row, diffs[side][at : at + 1, :], 0.0)
                strips[field, side, level] = tend[field, level, pl.ds(begin, TILE), :] + edge
            there = out.at[inside, pl.ds(begin, TILE), :]
            send(field, 3 + side, strips.at[field, side, inside], there)
    for copy in copies:
        copy.wait()


def tends(rounds, table, tend, far, near, other, outer):
    _, levels, rows, cols = tend.shape
    return pl.pallas_call(
        functools.partial(tends_kernel, rounds),
        out_shape=(jax.ShapeDtypeStruct((levels, rows, cols), F32),) * 2,
        in_specs=[whole(VMEM)] * (5 + len(outer)),
        out_specs=[whole(pl.ANY)] * 2,
        scratch_shapes=[
            pltpu.VMEM((2, 2, rows, cols), F32),
            pltpu.VMEM((2, 2, levels, TILE, cols), F32),
            pltpu.SemaphoreType.DMA((2, 5)),
        ],
        compiler_params=pltpu.CompilerParams(vmem_limit_bytes=8 * MIB),
        cost_estimate=pl.CostEstimate(
            flops=levels * rows * cols,
            bytes_accessed=8 * levels * rows * cols,
            transcendentals=0,
        ),
        name="tends",
    )(in_vmem(table), in_vmem(tend), far, near, other, *outer)


def merge_kernel(bit, final, late, own_at, other_at, mine, theirs, own, other, base, gains, *rest):
    _, rows, cols = base.shape
    upper = bit_of("gz", bit) == 1
    low, high = in_order(upper, scalar_rows(own, own_at), scalar_rows(other, other_at))
    coupling, inverse = interface(low, high)
    to_high, to_low = high[FIRST] * coupling, low[LAST] * coupling
    low_out, high_out = low[CORNER] * coupling, high[CORNER] * coupling
    core, size = bit_of("gz", 0) == 1, rows // 2
    sends_last = bit_of("gz", bit + 1) == 0
    for field in range(2):
        here = pl.ds(field * rows, rows)
        own_first, own_last = mine[here, :], mine[pl.ds((2 + field) * rows, rows), :]
        if late:
            low_last = jnp.where(upper, theirs[here, :], own_last)
            high_first = jnp.where(upper, own_first, theirs[here, :])
        else:
            other_first, other_last = theirs[here, :], theirs[pl.ds((2 + field) * rows, rows), :]
            low_last = jnp.where(upper, other_last, own_last)
            high_first = jnp.where(upper, own_first, other_first)
            low_first = jnp.where(upper, other_first, own_first)
            high_last = jnp.where(upper, own_last, other_last)
        above = inverse * (high_first + to_high * low_last)
        below = inverse * (low_last + to_low * high_first)
        base[field] = coupling * jnp.where(upper, below, above)
        more = jnp.where(sends_last, high_out * below, low_out * above)
        if late:
            outside = jnp.where(upper, own_last, own_first)
            outside = jnp.where(core, outside[size:], outside[:size])
            there = theirs[pl.ds(2 * rows + field * size, size), :]
            outside = jnp.where(sends_last == upper, outside, there)
        elif final:
            outside = jnp.where(sends_last, high_last, low_first)
            outside = jnp.where(core, outside[size:], outside[:size])
        if final:
            value = outside + jnp.where(core, more[size:], more[:size])
            rest[0][pl.ds(field * size, size), :] = value
        else:
            rest[0][here, :] = low_first + low_out * above
            rest[0][pl.ds((2 + field) * rows, rows), :] = high_last + high_out * below
    if not late:
        for at, value in enumerate(joint_scalars(low, high)):
            rest[1][pl.ds(at, 1), :] = value
    scale = coupling * inverse
    gains[...] = jnp.zeros(gains.shape, F32)
    gains[pl.ds(FROM_ABOVE, 1), :] = scale * high[CORNER] * jnp.where(upper, to_low, 1.0)
    gains[pl.ds(FROM_BELOW, 1), :] = scale * low[CORNER] * jnp.where(upper, 1.0, to_high)


def merge(bit, final, late, rows, mine, theirs, own, other):
    cols = mine.shape[1]
    shapes = [held(2, rows, cols), held(TILE, cols), held((1 if final else 4) * rows, cols)]
    if not late:
        shapes.append(held(TILE, cols))
    return pl.pallas_call(
        functools.partial(
            merge_kernel, bit, final, late, own.shape[0] - TILE, other.shape[0] - TILE
        ),
        out_shape=tuple(shapes),
        in_specs=[whole(VMEM)] * 4,
        out_specs=[whole(VMEM)] * len(shapes),
        compiler_params=pltpu.CompilerParams(vmem_limit_bytes=8 * MIB),
        name="merge",
    )(mine, theirs, own, other)


def prepare_kernel(
    rounds, temp, w_vel, forward, table, changes, fluxes, other, crossing, *rest
):
    outer = crossing if rounds > 2 else None
    bases, gains = rest[: rounds - 1], rest[rounds - 1 : 2 * rounds - 2]
    known, response, *passed, below_in, above_in = rest[2 * rounds - 2 :]
    if passed:
        passed[0][...] = crossing[pl.ds(0, passed[0].shape[0]), :]
    levels, rows, cols = temp.shape
    upper = bit_of("gz", rounds - 1) == 1
    one, none = jnp.ones((1, cols), F32), jnp.zeros((1, cols), F32)
    below_gain, above_gain = jnp.where(upper, one, none), jnp.where(upper, none, one)
    below = above = None
    for step in range(rounds - 2, -1, -1):
        side = bit_of("gz", step) == 1
        from_above = gains[step][pl.ds(FROM_ABOVE, 1), :]
        from_below = gains[step][pl.ds(FROM_BELOW, 1), :]
        gain = from_above * above_gain + from_below * below_gain
        below_gain = jnp.where(side, gain, below_gain)
        above_gain = jnp.where(side, above_gain, gain)
        into = [bases[step][field] for field in range(2)]
        if below is None:
            below = above = [jnp.zeros((rows, cols), F32)] * 2
        else:
            into = [
                into[field] + from_above * above[field] + from_below * below[field]
                for field in range(2)
            ]
        below = [jnp.where(side, into[field], below[field]) for field in range(2)]
        above = [jnp.where(side, above[field], into[field]) for field in range(2)]
    scalars = scalar_rows(fluxes, 3 * rows)
    for field in range(2):
        at = pl.ds(field * rows, rows)
        flux_below, flux_above = level_fluxes(other[at, :], 0.0 if outer is None else outer[at, :])
        below_in[field] = below[field] + scalars[METRIC_BELOW] * flux_below
        above_in[field] = above[field] - scalars[METRIC_ABOVE] * flux_above

    gain = above_gain * table[levels - 1, pl.ds(PIVOT, 1), :]
    for level in range(levels - 1, -1, -1):
        if level < levels - 1:
            gain = gain * table[level, pl.ds(UPPER_PIVOT, 1), :]
        gain = gain + below_gain * table[level, pl.ds(BELOW_FORWARD, 1), :]
        response[level] = jnp.broadcast_to(gain, (TILE, cols))

    row_at = lax.broadcasted_iota(jnp.int32, (TILE, cols), 0)
    width = 2 * TILE
    for begin in range(0, rows, width):
        at = pl.ds(begin, width)

        def solve(level, carry, factor, begin=begin, at=at):
            factor = table[level, pl.ds(factor, 1), :]
            below_factor = table[level, pl.ds(BELOW_FORWARD, 1), :]
            values = []
            for field, cells in enumerate((temp, w_vel)):
                value = forward[field, level + 1, at, :] + below_factor * below_in[field, at, :]
                if begin == 0:
                    change = changes[pl.ds(field * levels + level, 1), :]
                    head = value[:TILE] + jnp.where(row_at == 0, change, 0.0)
                    value = jnp.concatenate([head, value[TILE:]])
                if begin == rows - width:
                    change = changes[pl.ds((2 + field) * levels + level, 1), :]
                    tail = value[-TILE:] + jnp.where(row_at == TILE - 1, change, 0.0)
                    value = jnp.concatenate([value[:-TILE], tail])
                value = value + factor * carry[field]
                known[field, level, at, :] = value - cells[level, at, :]
                values.append(value)
            return tuple(values)

        carry = solve(levels - 1, [above_in[field, at, :] for field in range(2)], PIVOT)

        def step(back, carry, solve=solve):
            return solve(levels - 2 - back, carry, UPPER_PIVOT)

        lax.fori_loop(0, levels - 1, step, carry, unroll=3)


def prepare(rounds, temp, w_vel, forward, table, changes, fluxes, other, crossing, bases, gains):
    levels, rows, cols = temp.shape
    shapes = (held(2, levels, rows, cols), held(levels, TILE, cols))
    shapes += (held(2 * rows, cols // 2),) * (rounds == 2)
    return pl.pallas_call(
        functools.partial(prepare_kernel, rounds),
        out_shape=shapes,
        in_specs=[whole(VMEM)] * (8 + 2 * (rounds - 1)),
        out_specs=[whole(VMEM)] * len(shapes),
        scratch_shapes=[pltpu.VMEM((2, rows, cols), F32)] * 2,
        compiler_params=pltpu.CompilerParams(vmem_limit_bytes=8 * MIB),
        cost_estimate=pl.CostEstimate(
            flops=levels * rows * cols,
            bytes_accessed=24 * levels * rows * cols,
            transcendentals=0,
        ),
        name="prepare",
    )(
        in_vmem(temp), in_vmem(w_vel), in_vmem(forward), in_vmem(table), changes, fluxes, other,
        crossing, *bases, *gains,
    )


def join_kernel(rounds, late, own_at, other_at, mine, theirs, own, other, joined):
    size = theirs.shape[0] // 2
    upper = bit_of("gz", rounds - 1) == 1
    low, high = in_order(upper, scalar_rows(own, own_at), scalar_rows(other, other_at))
    if late:
        low, high = ([jnp.concatenate([a, a], axis=1) for a in rows] for rows in (low, high))
    coupling, inverse = interface(low, high)
    scale = coupling * inverse
    to_other = scale * coupling * jnp.where(upper, low[LAST], high[FIRST])
    up, down = high[METRIC_BELOW] * inverse, -low[METRIC_ABOVE] * inverse
    own_gain = coupling * jnp.where(upper, down * low[LAST], up * high[FIRST])
    other_gain = jnp.where(upper, up, down)
    for field in range(2):
        at = pl.ds(field * size, size)
        into = scale * theirs[at, :] + to_other * mine[at, :]
        if late:
            into = into + own_gain * get_seam(own, field, size)
            into = into + other_gain * get_seam(other, field, size)
        joined[at, :] = into


def join(rounds, late, mine, theirs, own, other):
    size, cols = theirs.shape
    return pl.pallas_call(
        functools.partial(join_kernel, rounds, late, own.shape[0] - TILE, other.shape[0] - TILE),
        out_shape=held(size, cols),
        in_specs=[whole(VMEM)] * 4,
        out_specs=whole(VMEM),
        compiler_params=pltpu.CompilerParams(vmem_limit_bytes=8 * MIB),
        name="join",
    )(mine, theirs, own, other)


def finish_kernel(rounds, swapped, known, response, joined, *rest):
    late, results = rounds == 2, 4 if rounds == 2 else 2
    flux_in, table, tend, far, near = rest[:5] if late else (None,) * 5
    rest = rest[(5 if late else 0) + (results if swapped else results - 2) :]
    outs, (result, rim, sems) = rest[:results], rest[results:]
    _, levels, rows, cols = known.shape
    width, half = 2 * TILE, rows // 2
    core = bit_of("gz", 0)
    start = pl.multiple_of((1 - core if swapped else core) * half, half)
    copies = []
    for field in range(2):
        for part, begin in enumerate(range(0, half, width)):
            into = joined[pl.ds(field * half + begin, width), :]
            tiles = [into[i : i + TILE] for i in range(0, width, TILE)]

            def step(level, carry, field=field, begin=begin, tiles=tiles):
                gain = response[level]
                for i, tile in enumerate(tiles):
                    at = begin + i * TILE
                    value = known[field, level, pl.ds(start + at, TILE), :] + gain * tile
                    result[field, level, pl.ds(at, TILE), :] = value
                return carry

            lax.fori_loop(0, levels, step, 0, unroll=True)
            copies.append(
                pltpu.make_async_copy(
                    result.at[field, :, pl.ds(begin, width), :],
                    outs[field].at[:, pl.ds(start + begin, width), :],
                    sems.at[2 + 2 * field + part],
                )
            )
            copies[-1].start()
    if late:
        diffs = side_changes(far, near)
        level = core * (levels - 1)
        gain = jnp.where(
            core == 1, -table[levels - 1, pl.ds(FALL, 1), :], table[0, pl.ds(RISE, 1), :]
        )
        gain = jnp.where(beside_seam(rounds), gain, 0.0)
        row_at = start + lax.broadcasted_iota(jnp.int32, (half, cols), 0)
        for field in range(2):
            head, tail = (
                jnp.where(
                    core == 1,
                    diff[(field + 1) * levels - 1 : (field + 1) * levels, :],
                    diff[field * levels : field * levels + 1, :],
                )
                for diff in diffs
            )
            edge = jnp.where(row_at == 0, head, jnp.where(row_at == rows - 1, tail, 0.0))
            flux = get_seam(flux_in, field, half)
            rim[field] = tend[field, level, pl.ds(start, half), :] + gain * flux + edge
            copies.append(
                pltpu.make_async_copy(
                    rim.at[field],
                    outs[2 + field].at[level, pl.ds(start, half), :],
                    sems.at[field],
                )
            )
            copies[-1].start()
    for copy in copies:
        copy.wait()


def finish(rounds, known, response, joined, late, written):
    _, levels, rows, cols = known.shape
    results = 4 if rounds == 2 else 2
    inputs = 3 + len(late)
    swapped = len(written) == results
    return pl.pallas_call(
        functools.partial(finish_kernel, rounds, swapped),
        out_shape=(jax.ShapeDtypeStruct((levels, rows, cols), F32),) * results,
        in_specs=[whole(VMEM)] * inputs + [whole(pl.ANY)] * len(written),
        out_specs=[whole(pl.ANY)] * results,
        scratch_shapes=[
            pltpu.VMEM((2, levels, rows // 2, cols), F32),
            pltpu.VMEM((2, rows // 2, cols), F32),
            pltpu.SemaphoreType.DMA((6,)),
        ],
        input_output_aliases={
            inputs + i: results - len(written) + i for i in range(len(written))
        },
        compiler_params=pltpu.CompilerParams(vmem_limit_bytes=8 * MIB),
        cost_estimate=pl.CostEstimate(
            flops=20000 * levels * rows * cols,
            bytes_accessed=8 * levels * rows * cols,
            transcendentals=0,
        ),
        name="finish",
    )(in_vmem(known), response, joined, *map(in_vmem, late), *written)


def both_ways(pairs):
    return pairs + [(b, a) for a, b in pairs]


def local(temp, u_vel, v_vel, w_vel, temp_prev, w_prev, lower, upper, metric):
    rows = temp.shape[1]
    across, stacked = lax.axis_size("gx"), lax.axis_size("gz")
    rounds = stacked.bit_length() - 1
    cores = both_ways([(i, i + 1) for i in range(0, stacked, 2)])
    far, near, fluxes, outward, table = edges(
        temp, u_vel, w_vel, v_vel, temp_prev, w_prev, lower, upper, metric
    )
    other = lax.ppermute(fluxes, "gz", cores)
    near = lax.ppermute(near, "gx", both_ways([(i, i + 1) for i in range(0, across, 2)]))
    far = lax.ppermute(far, "gx", both_ways([(i, (i + 1) % across) for i in range(1, across, 2)]))
    outer = ()
    if rounds > 2:
        seams = both_ways([(i, i + 1) for i in range(1, stacked - 1, 2)])
        outer = (lax.ppermute(outward, "gz", seams),)
    forward, tend, first = bulk(other, table, temp, u_vel, v_vel, w_vel, temp_prev, w_prev)
    entries, changes, *late = fix(
        rounds, other, near, far, fluxes, outward, forward, first, table, outer
    )
    message, seam = late if late else (entries, fluxes)
    bases, gains, own, other_own = [], [], fluxes, other
    for step in range(rounds - 1):
        partners = [(i, i ^ (1 << step)) for i in range(stacked)]
        theirs = lax.ppermute(message, "gz", partners)
        if step > 0:
            other_own = lax.ppermute(own, "gz", partners)
        base, gain, message, *scalars = merge(
            step, step + 2 == rounds, bool(late), rows, entries, theirs, own, other_own
        )
        entries, own = message, scalars[0] if scalars else seam
        bases.append(base)
        gains.append(gain)
    partners = [(i, i ^ (stacked // 2)) for i in range(stacked)]
    theirs = lax.ppermute(message, "gz", partners)
    other_own = lax.ppermute(own, "gz", partners)
    known, response, *passed = prepare(
        rounds, temp, w_vel, forward, table, changes, fluxes, other, *(outer or (other_own,)),
        bases, gains,
    )
    tendencies = tends(rounds, table, tend, far, near, other, outer)
    joined = join(rounds, bool(late), message, theirs, own, other_own)
    swapped = lax.ppermute(joined, "gz", cores)
    if not late:
        written = finish(rounds, known, response, joined, (), ())
        return *finish(rounds, known, response, swapped, (), written), *tendencies
    crossed = lax.ppermute(passed[0], "gz", cores)
    late = (table, tend, far, near)
    written = finish(rounds, known, response, joined, (other_own, *late), tendencies)
    return tuple(finish(rounds, known, response, swapped, (crossed, *late), written))


def solution(mesh):
    field = P("gz", "gx", None)
    return jax.shard_map(
        local,
        mesh=mesh,
        in_specs=(field,) * 6 + (P("gz"),) * 3,
        out_specs=(field,) * 4,
        check_vma=False,
    )
```

```python
import functools

import jax
import jax.numpy as jnp
from jax import lax
from jax.experimental import pallas as pl
from jax.experimental.pallas import tpu as pltpu
from jax.sharding import PartitionSpec as P

NEW_WEIGHT = 5.0 / 12.0
HORIZ_DIFF = 0.1
FIELD_WEIGHT = 2.0 / NEW_WEIGHT
PREV_WEIGHT = (17.0 / 60.0) / NEW_WEIGHT
TILE = 8
MIB = 1024 * 1024

PIVOT_NEW, LOWER_PIVOT, UPPER_PIVOT, FIRST_GREEN, BELOW_FORWARD, PIVOT, RISE, FALL = range(8)
FIRST, CORNER, LAST, BELOW, ABOVE, METRIC_BELOW, METRIC_ABOVE = range(7)
FROM_ABOVE, FROM_BELOW = range(2)

VMEM = pltpu.VMEM
F32 = jnp.float32


def whole(space):
    return pl.BlockSpec(memory_space=space)


def held(*shape):
    return pltpu.VMEM(shape, F32)


def in_vmem(array):
    return pltpu.with_memory_space_constraint(array, pltpu.VMEM)


def in_hbm(*arrays):
    return [pltpu.with_memory_space_constraint(array, pltpu.HBM) for array in arrays]


def bit_of(axis, bit):
    return (lax.axis_index(axis) >> bit) & 1


def edges_kernel(
    temp,
    u_vel,
    w_vel,
    v_vel,
    temp_prev,
    w_prev,
    lower,
    upper,
    metric,
    far,
    near,
    fluxes,
    outward,
    table,
    strips,
    layers,
    lower_at,
    upper_at,
    metric_at,
    sems,
):
    levels, rows, cols = temp.shape
    copies = [(lower, lower_at), (upper, upper_at), (metric, metric_at)]
    for at, array in enumerate((temp, w_vel, u_vel)):
        for side, row in enumerate((0, rows - 1)):
            copies.append((array.at[:, row, :], strips.at[at, side]))
    for at, array in enumerate((temp, w_vel)):
        for side, level in enumerate((0, levels - 1)):
            copies.append((array.at[level], layers.at[at, side]))
    copies = [pltpu.make_async_copy(src, dst, sems.at[i]) for i, (src, dst) in enumerate(copies)]
    for copy in copies:
        copy.start()
    for copy in copies[:3]:
        copy.wait()
    coefficients(lower_at, upper_at, metric_at, table, fluxes.at[pl.ds(3 * rows, TILE)])
    for copy in copies[3:]:
        copy.wait()
    odd = bit_of("gx", 0) == 1
    for field in range(2):
        at = pl.ds(field * levels, levels)
        to_left = (HORIZ_DIFF - 0.5 * strips[2, 0]) * strips[field, 0]
        to_right = (HORIZ_DIFF + 0.5 * strips[2, 1]) * strips[field, 1]
        near[at, :] = jnp.where(odd, to_left, to_right)
        far[at, :] = jnp.where(odd, to_right, to_left)
    position = lax.axis_index("gz")
    upper_core = bit_of("gz", 0) == 1
    wall = (position == 0) | (position == lax.axis_size("gz") - 1)
    zero, size = jnp.zeros((rows, cols), F32), rows // 2
    for field in range(2):
        bottom = layers[1, 0] * layers[field, 0]
        top = layers[1, 1] * layers[field, 1]
        fluxes[pl.ds(field * rows, rows), :] = jnp.where(upper_core, bottom, top)
        value = jnp.where(wall, zero, jnp.where(upper_core, top, bottom))
        outward[pl.ds(field * rows, rows), :] = value
        fluxes[pl.ds(2 * rows + field * size, size), :] = jnp.where(
            upper_core, value[:size], value[size:]
        )


def edges(temp, u_vel, w_vel, v_vel, temp_prev, w_prev, lower, upper, metric):
    levels, rows, cols = temp.shape
    return pl.pallas_call(
        edges_kernel,
        out_shape=(
            held(2 * levels, cols),
            held(2 * levels, cols),
            held(3 * rows + TILE, cols),
            held(2 * rows, cols),
            held(levels, TILE, cols),
        ),
        in_specs=[whole(pl.ANY)] * 9,
        out_specs=[whole(VMEM)] * 5,
        scratch_shapes=[
            pltpu.VMEM((3, 2, levels, cols), F32),
            pltpu.VMEM((2, 2, rows, cols), F32),
            pltpu.SMEM((levels,), F32),
            pltpu.SMEM((levels,), F32),
            pltpu.SMEM((levels,), F32),
            pltpu.SemaphoreType.DMA((13,)),
        ],
        compiler_params=pltpu.CompilerParams(vmem_limit_bytes=8 * MIB),
        name="edges",
    )(*in_hbm(temp, u_vel, w_vel, v_vel, temp_prev, w_prev, lower, upper, metric))


def coefficients(lower, upper, metric, table, scalars):
    levels, _, cols = table.shape

    def row(value):
        return jnp.full((1, cols), value, F32)

    ratio = jnp.zeros((1, cols), F32)
    forward = jnp.ones((1, cols), F32)
    for level in range(levels):
        low, high = row(lower[level]), row(upper[level])
        pivot = 1.0 / (1.0 + low + high - low * ratio)
        ratio = high * pivot
        lower_pivot = low * pivot
        forward = pivot if level == 0 else lower_pivot * forward
        table[level, pl.ds(PIVOT_NEW, 1), :] = NEW_WEIGHT * pivot
        table[level, pl.ds(LOWER_PIVOT, 1), :] = lower_pivot
        table[level, pl.ds(UPPER_PIVOT, 1), :] = ratio
        table[level, pl.ds(BELOW_FORWARD, 1), :] = forward
        table[level, pl.ds(PIVOT, 1), :] = pivot
        table[level, pl.ds(RISE, 1), :] = row(metric[level] if level < levels - 1 else 0.0)
        table[level, pl.ds(FALL, 1), :] = row(metric[level] if level > 0 else 0.0)
    green = forward
    table[levels - 1, pl.ds(FIRST_GREEN, 1), :] = NEW_WEIGHT * green
    for level in range(levels - 2, -1, -1):
        green = (
            table[level, pl.ds(BELOW_FORWARD, 1), :]
            + table[level, pl.ds(UPPER_PIVOT, 1), :] * green
        )
        table[level, pl.ds(FIRST_GREEN, 1), :] = NEW_WEIGHT * green
    scalars[pl.ds(FIRST, 1), :] = green
    scalars[pl.ds(CORNER, 1), :] = forward
    scalars[pl.ds(LAST, 1), :] = pivot
    scalars[pl.ds(BELOW, 1), :] = row(lower[0])
    scalars[pl.ds(ABOVE, 1), :] = row(upper[levels - 1])
    scalars[pl.ds(METRIC_BELOW, 1), :] = row(NEW_WEIGHT * metric[0])
    scalars[pl.ds(METRIC_ABOVE, 1), :] = row(NEW_WEIGHT * metric[levels - 1])
    scalars[pl.ds(7, 1), :] = row(0.0)


def bulk_kernel(
    table,
    temp,
    u_vel,
    v_vel,
    w_vel,
    temp_prev,
    w_prev,
    forward,
    tend,
    first,
):
    levels, rows, cols = temp.shape
    strips = rows // TILE
    fields, prevs = (temp, w_vel), (temp_prev, w_prev)
    for field in range(2):
        forward[field, 0] = jnp.zeros((rows, cols), F32)
        first[field] = jnp.zeros((rows, cols), F32)
    row_at = lax.broadcasted_iota(jnp.int32, (TILE, cols), 0)
    zero = jnp.zeros((TILE, cols), F32)

    def sides(level, strip):
        at = pl.ds(strip * TILE, TILE)
        half = 0.5 * u_vel[level, at, :]
        back, ahead = HORIZ_DIFF - half, HORIZ_DIFF + half
        here = [values[level, at, :] for values in fields]
        return (
            here,
            [pltpu.roll(back * value, TILE - 1, 0) for value in here],
            [pltpu.roll(ahead * value, 1, 0) for value in here],
        )

    def pair_step(pair, carry):
        both = (2 * pair, 2 * pair + 1)
        under, over = jnp.maximum(both[0] - 1, 0), jnp.minimum(both[1] + 1, levels - 1)

        def spread(level, at):
            tile = jnp.broadcast_to(table[level, pl.ds(at, 1), : cols // 2], (TILE, cols // 2))
            return jnp.concatenate([tile, tile], axis=1)

        factors = [
            [spread(level, at) for at in (PIVOT_NEW, LOWER_PIVOT, FIRST_GREEN, RISE, FALL)]
            for level in both
        ]
        before = [[zero, zero], [zero, zero]]
        now = [sides(level, 0) for level in both]
        for strip in range(strips):
            none = (None, [zero, zero], None)
            later = [sides(level, strip + 1) if strip + 1 < strips else none for level in both]
            at = pl.ds(strip * TILE, TILE)
            beneath = [values[under, at, :] for values in fields]
            above = [values[over, at, :] for values in fields]
            solved = [forward[field, both[0], at, :] for field in range(2)]
            total = [first[field, at, :] for field in range(2)]
            for i, level in enumerate(both):
                here, back, ahead = now[i]
                pivot, lower_pivot, green, rise, fall = factors[i]
                upward = above if i else now[1][0]
                downward = now[0][0] if i else beneath
                half = 0.5 * v_vel[level, at, :]
                v_back, v_ahead = HORIZ_DIFF - half, HORIZ_DIFF + half
                w_over, w_under = rise * upward[1], fall * downward[1]
                for field in range(2):
                    value = here[field]
                    change = jnp.where(row_at == TILE - 1, later[i][1][field], back[field])
                    change = change + jnp.where(row_at == 0, before[i][field], ahead[field])
                    change = change + pltpu.roll(v_back * value, cols - 1, 1)
                    change = change + pltpu.roll(v_ahead * value, 1, 1)
                    change = change - w_over * upward[field] + w_under * downward[field]
                    change = change + (here[1 - field] - (4.0 * HORIZ_DIFF) * value)
                    tend[field, level, at, :] = change
                    old = prevs[field][level, at, :]
                    right = change + (FIELD_WEIGHT * value - PREV_WEIGHT * old)
                    solved[field] = pivot * right + lower_pivot * solved[field]
                    forward[field, level + 1, at, :] = solved[field]
                    total[field] = total[field] + green * right
            for field in range(2):
                first[field, at, :] = total[field]
            before = [now[0][2], now[1][2]]
            now = later
        return carry

    lax.fori_loop(0, levels // 2, pair_step, 0)


def bulk(table, *arrays):
    levels, rows, cols = arrays[0].shape
    return pl.pallas_call(
        bulk_kernel,
        out_shape=(
            held(2, levels + 1, rows, cols),
            held(2, levels, rows, cols),
            held(2, rows, cols),
        ),
        in_specs=[whole(VMEM)] * 7,
        out_specs=[whole(VMEM)] * 3,
        compiler_params=pltpu.CompilerParams(vmem_limit_bytes=8 * MIB),
        cost_estimate=pl.CostEstimate(
            flops=100000 * levels * rows * cols,
            bytes_accessed=24 * levels * rows * cols,
            transcendentals=0,
        ),
        name="bulk",
    )(*map(in_vmem, (table, *arrays)))


def side_changes(far, near):
    odd = bit_of("gx", 0) == 1
    return jnp.where(odd, near[...], far[...]), jnp.where(odd, far[...], near[...])


def level_fluxes(inner, outer):
    upper = bit_of("gz", 0) == 1
    return jnp.where(upper, inner, outer), jnp.where(upper, outer, inner)


def beside_seam(rounds):
    return bit_of("gz", 0) != bit_of("gz", rounds - 1)


def ends(rows, cols, head, tail):
    at = lax.broadcasted_iota(jnp.int32, (rows, cols), 0)
    return jnp.where(at == 0, head, jnp.where(at == rows - 1, tail, 0.0))


def scalar_rows(ref, begin=0):
    return [ref[pl.ds(begin + at, 1), :] for at in range(7)]


def put_seam(ref, field, value):
    size, cols = value.shape
    for part in range(2):
        at = pl.ds((2 * part + field) * size, size)
        ref[at, :] = value[:, part * cols // 2 : (part + 1) * cols // 2]


def get_seam(ref, field, size):
    parts = [ref[pl.ds((2 * part + field) * size, size), :] for part in range(2)]
    return jnp.concatenate(parts, axis=1)


def in_order(upper, own, other):
    low = [jnp.where(upper, b, a) for a, b in zip(own, other)]
    high = [jnp.where(upper, a, b) for a, b in zip(own, other)]
    return low, high


def interface(low, high):
    coupling = low[ABOVE]
    return coupling, 1.0 / (1.0 - coupling * coupling * low[LAST] * high[FIRST])


def joint_scalars(low, high):
    coupling, inverse = interface(low, high)
    low_out, high_out = low[CORNER] * coupling, high[CORNER] * coupling
    return [
        low[FIRST] + low_out * low_out * inverse * high[FIRST],
        low_out * inverse * high[CORNER],
        high[LAST] + high_out * high_out * inverse * low[LAST],
        low[BELOW],
        high[ABOVE],
        low[METRIC_BELOW],
        high[METRIC_ABOVE],
        jnp.zeros_like(coupling),
    ]


def fix_kernel(
    rounds, levels, near, far, other, fluxes, outward, forward, first, table, *rest
):
    outer, rest = (rest[0], rest[1:]) if rounds > 2 else (None, rest)
    entries, changes, *late = rest
    _, rows, cols = first.shape
    diffs = side_changes(far, near)
    scalars = scalar_rows(fluxes, 3 * rows)
    below, above = scalars[METRIC_BELOW], -scalars[METRIC_ABOVE]
    core, size = bit_of("gz", 0) == 1, rows // 2
    for field in range(2):
        firsts, lasts = [], []
        for side in range(2):
            value = jnp.zeros((1, cols), F32)
            total = jnp.zeros((1, cols), F32)
            for level in range(levels):
                right = diffs[side][field * levels + level : field * levels + level + 1, :]
                value = (
                    table[level, pl.ds(PIVOT_NEW, 1), :] * right
                    + table[level, pl.ds(LOWER_PIVOT, 1), :] * value
                )
                total = total + table[level, pl.ds(FIRST_GREEN, 1), :] * right
                changes[pl.ds((side * 2 + field) * levels + level, 1), :] = value
            firsts.append(total)
            lasts.append(value)
        at = pl.ds(field * rows, rows)
        flux_below, flux_above = level_fluxes(other[at, :], 0.0 if outer is None else outer[at, :])
        first_entry = (
            first[field]
            + (below * scalars[FIRST]) * flux_below
            + (above * scalars[CORNER]) * flux_above
            + ends(rows, cols, *firsts)
        )
        last_entry = (
            forward[field, levels]
            + (below * scalars[CORNER]) * flux_below
            + (above * scalars[LAST]) * flux_above
            + ends(rows, cols, *lasts)
        )
        entries[at, :] = first_entry
        entries[pl.ds((2 + field) * rows, rows), :] = last_entry
        if late:
            message, seam = late
            message[at, :] = jnp.where(core, first_entry, last_entry)
            there = pl.ds(2 * rows + field * size, size)
            message[there, :] = jnp.where(core, last_entry[:size], first_entry[size:])
            value = outward[at, :]
            value = jnp.where(core, value[size:], value[:size])
            put_seam(seam, field, jnp.where(beside_seam(rounds), value, other[there, :]))
    if late:
        far_scalars = scalar_rows(other, 3 * rows)
        for at, value in enumerate(joint_scalars(*in_order(core, scalars, far_scalars))):
            seam[pl.ds(2 * rows + at, 1), :] = value[:, : cols // 2]


def fix(rounds, near, far, other, fluxes, outward, forward, first, table, outer):
    levels = table.shape[0]
    _, rows, cols = first.shape
    shapes = [held(4 * rows, cols), held(4 * levels, cols)]
    if rounds == 2:
        shapes += [held(3 * rows, cols), held(2 * rows + TILE, cols // 2)]
    return pl.pallas_call(
        functools.partial(fix_kernel, rounds, levels),
        out_shape=tuple(shapes),
        in_specs=[whole(VMEM)] * (8 + len(outer)),
        out_specs=[whole(VMEM)] * len(shapes),
        compiler_params=pltpu.CompilerParams(vmem_limit_bytes=8 * MIB),
        name="fix",
    )(
        near, far, other, fluxes, outward, in_vmem(forward), in_vmem(first), in_vmem(table), *outer
    )


def tends_kernel(rounds, table, tend, far, near, other, *rest):
    outer, rest = (rest[0], rest[1:]) if rounds > 2 else (None, rest)
    *outs, layers, strips, sems = rest
    _, levels, rows, cols = tend.shape
    inside, middle = pl.ds(1, levels - 2), pl.ds(TILE, rows - 2 * TILE)
    copies = []

    def send(field, at, src, dst):
        copies.append(pltpu.make_async_copy(src, dst, sems.at[field, at]))
        copies[-1].start()

    for field, out in enumerate(outs):
        send(field, 0, tend.at[field, inside, middle, :], out.at[inside, middle, :])
    diffs = side_changes(far, near)
    tile_at = lax.broadcasted_iota(jnp.int32, (TILE, cols), 0)
    for field, out in enumerate(outs):
        at = pl.ds(field * rows, rows)
        below, above = level_fluxes(other[at, :], 0.0 if outer is None else outer[at, :])
        for side, level, change in (
            (0, 0, table[0, pl.ds(RISE, 1), :] * below),
            (1, levels - 1, -table[levels - 1, pl.ds(FALL, 1), :] * above),
        ):
            at = field * levels + level
            rim = ends(rows, cols, diffs[0][at : at + 1, :], diffs[1][at : at + 1, :])
            layers[field, side] = tend[field, level] + change + rim
            send(field, 1 + side, layers.at[field, side], out.at[level])
        for side, begin, row in ((0, 0, 0), (1, rows - TILE, TILE - 1)):
            for level in range(1, levels - 1):
                at = field * levels + level
                edge = jnp.where(tile_at == row, diffs[side][at : at + 1, :], 0.0)
                strips[field, side, level] = tend[field, level, pl.ds(begin, TILE), :] + edge
            there = out.at[inside, pl.ds(begin, TILE), :]
            send(field, 3 + side, strips.at[field, side, inside], there)
    for copy in copies:
        copy.wait()


def tends(rounds, table, tend, far, near, other, outer):
    _, levels, rows, cols = tend.shape
    return pl.pallas_call(
        functools.partial(tends_kernel, rounds),
        out_shape=(jax.ShapeDtypeStruct((levels, rows, cols), F32),) * 2,
        in_specs=[whole(VMEM)] * (5 + len(outer)),
        out_specs=[whole(pl.ANY)] * 2,
        scratch_shapes=[
            pltpu.VMEM((2, 2, rows, cols), F32),
            pltpu.VMEM((2, 2, levels, TILE, cols), F32),
            pltpu.SemaphoreType.DMA((2, 5)),
        ],
        compiler_params=pltpu.CompilerParams(vmem_limit_bytes=8 * MIB),
        cost_estimate=pl.CostEstimate(
            flops=levels * rows * cols,
            bytes_accessed=8 * levels * rows * cols,
            transcendentals=0,
        ),
        name="tends",
    )(in_vmem(table), in_vmem(tend), far, near, other, *outer)


def merge_kernel(bit, final, late, own_at, other_at, mine, theirs, own, other, base, gains, *rest):
    _, rows, cols = base.shape
    upper = bit_of("gz", bit) == 1
    low, high = in_order(upper, scalar_rows(own, own_at), scalar_rows(other, other_at))
    coupling, inverse = interface(low, high)
    to_high, to_low = high[FIRST] * coupling, low[LAST] * coupling
    low_out, high_out = low[CORNER] * coupling, high[CORNER] * coupling
    core, size = bit_of("gz", 0) == 1, rows // 2
    sends_last = bit_of("gz", bit + 1) == 0
    for field in range(2):
        here = pl.ds(field * rows, rows)
        own_first, own_last = mine[here, :], mine[pl.ds((2 + field) * rows, rows), :]
        if late:
            low_last = jnp.where(upper, theirs[here, :], own_last)
            high_first = jnp.where(upper, own_first, theirs[here, :])
        else:
            other_first, other_last = theirs[here, :], theirs[pl.ds((2 + field) * rows, rows), :]
            low_last = jnp.where(upper, other_last, own_last)
            high_first = jnp.where(upper, own_first, other_first)
            low_first = jnp.where(upper, other_first, own_first)
            high_last = jnp.where(upper, own_last, other_last)
        above = inverse * (high_first + to_high * low_last)
        below = inverse * (low_last + to_low * high_first)
        base[field] = coupling * jnp.where(upper, below, above)
        more = jnp.where(sends_last, high_out * below, low_out * above)
        if late:
            outside = jnp.where(upper, own_last, own_first)
            outside = jnp.where(core, outside[size:], outside[:size])
            there = theirs[pl.ds(2 * rows + field * size, size), :]
            outside = jnp.where(sends_last == upper, outside, there)
        elif final:
            outside = jnp.where(sends_last, high_last, low_first)
            outside = jnp.where(core, outside[size:], outside[:size])
        if final:
            value = outside + jnp.where(core, more[size:], more[:size])
            rest[0][pl.ds(field * size, size), :] = value
        else:
            rest[0][here, :] = low_first + low_out * above
            rest[0][pl.ds((2 + field) * rows, rows), :] = high_last + high_out * below
    if not late:
        for at, value in enumerate(joint_scalars(low, high)):
            rest[1][pl.ds(at, 1), :] = value
    scale = coupling * inverse
    gains[...] = jnp.zeros(gains.shape, F32)
    gains[pl.ds(FROM_ABOVE, 1), :] = scale * high[CORNER] * jnp.where(upper, to_low, 1.0)
    gains[pl.ds(FROM_BELOW, 1), :] = scale * low[CORNER] * jnp.where(upper, 1.0, to_high)


def merge(bit, final, late, rows, mine, theirs, own, other):
    cols = mine.shape[1]
    shapes = [held(2, rows, cols), held(TILE, cols), held((1 if final else 4) * rows, cols)]
    if not late:
        shapes.append(held(TILE, cols))
    return pl.pallas_call(
        functools.partial(
            merge_kernel, bit, final, late, own.shape[0] - TILE, other.shape[0] - TILE
        ),
        out_shape=tuple(shapes),
        in_specs=[whole(VMEM)] * 4,
        out_specs=[whole(VMEM)] * len(shapes),
        compiler_params=pltpu.CompilerParams(vmem_limit_bytes=8 * MIB),
        name="merge",
    )(mine, theirs, own, other)


def prepare_kernel(
    rounds, temp, w_vel, forward, table, changes, fluxes, other, crossing, *rest
):
    outer = crossing if rounds > 2 else None
    bases, gains = rest[: rounds - 1], rest[rounds - 1 : 2 * rounds - 2]
    known, response, *passed, below_in, above_in = rest[2 * rounds - 2 :]
    if passed:
        passed[0][...] = crossing[pl.ds(0, passed[0].shape[0]), :]
    levels, rows, cols = temp.shape
    upper = bit_of("gz", rounds - 1) == 1
    one, none = jnp.ones((1, cols), F32), jnp.zeros((1, cols), F32)
    below_gain, above_gain = jnp.where(upper, one, none), jnp.where(upper, none, one)
    below = above = None
    for step in range(rounds - 2, -1, -1):
        side = bit_of("gz", step) == 1
        from_above = gains[step][pl.ds(FROM_ABOVE, 1), :]
        from_below = gains[step][pl.ds(FROM_BELOW, 1), :]
        gain = from_above * above_gain + from_below * below_gain
        below_gain = jnp.where(side, gain, below_gain)
        above_gain = jnp.where(side, above_gain, gain)
        into = [bases[step][field] for field in range(2)]
        if below is None:
            below = above = [jnp.zeros((rows, cols), F32)] * 2
        else:
            into = [
                into[field] + from_above * above[field] + from_below * below[field]
                for field in range(2)
            ]
        below = [jnp.where(side, into[field], below[field]) for field in range(2)]
        above = [jnp.where(side, above[field], into[field]) for field in range(2)]
    scalars = scalar_rows(fluxes, 3 * rows)
    for field in range(2):
        at = pl.ds(field * rows, rows)
        flux_below, flux_above = level_fluxes(other[at, :], 0.0 if outer is None else outer[at, :])
        below_in[field] = below[field] + scalars[METRIC_BELOW] * flux_below
        above_in[field] = above[field] - scalars[METRIC_ABOVE] * flux_above

    gain = above_gain * table[levels - 1, pl.ds(PIVOT, 1), :]
    for level in range(levels - 1, -1, -1):
        if level < levels - 1:
            gain = gain * table[level, pl.ds(UPPER_PIVOT, 1), :]
        gain = gain + below_gain * table[level, pl.ds(BELOW_FORWARD, 1), :]
        response[level] = jnp.broadcast_to(gain, (TILE, cols))

    row_at = lax.broadcasted_iota(jnp.int32, (TILE, cols), 0)
    width = 2 * TILE
    for begin in range(0, rows, width):
        at = pl.ds(begin, width)

        def solve(level, carry, factor, begin=begin, at=at):
            factor = table[level, pl.ds(factor, 1), :]
            below_factor = table[level, pl.ds(BELOW_FORWARD, 1), :]
            values = []
            for field, cells in enumerate((temp, w_vel)):
                value = forward[field, level + 1, at, :] + below_factor * below_in[field, at, :]
                if begin == 0:
                    change = changes[pl.ds(field * levels + level, 1), :]
                    head = value[:TILE] + jnp.where(row_at == 0, change, 0.0)
                    value = jnp.concatenate([head, value[TILE:]])
                if begin == rows - width:
                    change = changes[pl.ds((2 + field) * levels + level, 1), :]
                    tail = value[-TILE:] + jnp.where(row_at == TILE - 1, change, 0.0)
                    value = jnp.concatenate([value[:-TILE], tail])
                value = value + factor * carry[field]
                known[field, level, at, :] = value - cells[level, at, :]
                values.append(value)
            return tuple(values)

        carry = solve(levels - 1, [above_in[field, at, :] for field in range(2)], PIVOT)

        def step(back, carry, solve=solve):
            return solve(levels - 2 - back, carry, UPPER_PIVOT)

        lax.fori_loop(0, levels - 1, step, carry, unroll=3)


def prepare(rounds, temp, w_vel, forward, table, changes, fluxes, other, crossing, bases, gains):
    levels, rows, cols = temp.shape
    shapes = (held(2, levels, rows, cols), held(levels, TILE, cols))
    shapes += (held(2 * rows, cols // 2),) * (rounds == 2)
    return pl.pallas_call(
        functools.partial(prepare_kernel, rounds),
        out_shape=shapes,
        in_specs=[whole(VMEM)] * (8 + 2 * (rounds - 1)),
        out_specs=[whole(VMEM)] * len(shapes),
        scratch_shapes=[pltpu.VMEM((2, rows, cols), F32)] * 2,
        compiler_params=pltpu.CompilerParams(vmem_limit_bytes=8 * MIB),
        cost_estimate=pl.CostEstimate(
            flops=levels * rows * cols,
            bytes_accessed=24 * levels * rows * cols,
            transcendentals=0,
        ),
        name="prepare",
    )(
        in_vmem(temp), in_vmem(w_vel), in_vmem(forward), in_vmem(table), changes, fluxes, other,
        crossing, *bases, *gains,
    )


def join_kernel(rounds, late, own_at, other_at, mine, theirs, own, other, joined):
    size = theirs.shape[0] // 2
    upper = bit_of("gz", rounds - 1) == 1
    low, high = in_order(upper, scalar_rows(own, own_at), scalar_rows(other, other_at))
    if late:
        low, high = ([jnp.concatenate([a, a], axis=1) for a in rows] for rows in (low, high))
    coupling, inverse = interface(low, high)
    scale = coupling * inverse
    to_other = scale * coupling * jnp.where(upper, low[LAST], high[FIRST])
    up, down = high[METRIC_BELOW] * inverse, -low[METRIC_ABOVE] * inverse
    own_gain = coupling * jnp.where(upper, down * low[LAST], up * high[FIRST])
    other_gain = jnp.where(upper, up, down)
    for field in range(2):
        at = pl.ds(field * size, size)
        into = scale * theirs[at, :] + to_other * mine[at, :]
        if late:
            into = into + own_gain * get_seam(own, field, size)
            into = into + other_gain * get_seam(other, field, size)
        joined[at, :] = into


def join(rounds, late, mine, theirs, own, other):
    size, cols = theirs.shape
    return pl.pallas_call(
        functools.partial(join_kernel, rounds, late, own.shape[0] - TILE, other.shape[0] - TILE),
        out_shape=held(size, cols),
        in_specs=[whole(VMEM)] * 4,
        out_specs=whole(VMEM),
        compiler_params=pltpu.CompilerParams(vmem_limit_bytes=8 * MIB),
        name="join",
    )(mine, theirs, own, other)


def finish_kernel(rounds, swapped, known, response, joined, *rest):
    late, results = rounds == 2, 4 if rounds == 2 else 2
    flux_in, table, tend, far, near = rest[:5] if late else (None,) * 5
    rest = rest[(5 if late else 0) + (results if swapped else results - 2) :]
    outs, (result, rim, sems) = rest[:results], rest[results:]
    _, levels, rows, cols = known.shape
    width, half = 2 * TILE, rows // 2
    core = bit_of("gz", 0)
    start = pl.multiple_of((1 - core if swapped else core) * half, half)
    copies = []
    for field in range(2):
        for part, begin in enumerate(range(0, half, width)):
            into = joined[pl.ds(field * half + begin, width), :]
            tiles = [into[i : i + TILE] for i in range(0, width, TILE)]

            def step(level, carry, field=field, begin=begin, tiles=tiles):
                gain = response[level]
                for i, tile in enumerate(tiles):
                    at = begin + i * TILE
                    value = known[field, level, pl.ds(start + at, TILE), :] + gain * tile
                    result[field, level, pl.ds(at, TILE), :] = value
                return carry

            lax.fori_loop(0, levels, step, 0, unroll=True)
            copies.append(
                pltpu.make_async_copy(
                    result.at[field, :, pl.ds(begin, width), :],
                    outs[field].at[:, pl.ds(start + begin, width), :],
                    sems.at[2 + 2 * field + part],
                )
            )
            copies[-1].start()
    if late:
        diffs = side_changes(far, near)
        level = core * (levels - 1)
        gain = jnp.where(
            core == 1, -table[levels - 1, pl.ds(FALL, 1), :], table[0, pl.ds(RISE, 1), :]
        )
        gain = jnp.where(beside_seam(rounds), gain, 0.0)
        row_at = start + lax.broadcasted_iota(jnp.int32, (half, cols), 0)
        for field in range(2):
            head, tail = (
                jnp.where(
                    core == 1,
                    diff[(field + 1) * levels - 1 : (field + 1) * levels, :],
                    diff[field * levels : field * levels + 1, :],
                )
                for diff in diffs
            )
            edge = jnp.where(row_at == 0, head, jnp.where(row_at == rows - 1, tail, 0.0))
            flux = get_seam(flux_in, field, half)
            rim[field] = tend[field, level, pl.ds(start, half), :] + gain * flux + edge
            copies.append(
                pltpu.make_async_copy(
                    rim.at[field],
                    outs[2 + field].at[level, pl.ds(start, half), :],
                    sems.at[field],
                )
            )
            copies[-1].start()
    for copy in copies:
        copy.wait()


def finish(rounds, known, response, joined, late, written):
    _, levels, rows, cols = known.shape
    results = 4 if rounds == 2 else 2
    inputs = 3 + len(late)
    swapped = len(written) == results
    return pl.pallas_call(
        functools.partial(finish_kernel, rounds, swapped),
        out_shape=(jax.ShapeDtypeStruct((levels, rows, cols), F32),) * results,
        in_specs=[whole(VMEM)] * inputs + [whole(pl.ANY)] * len(written),
        out_specs=[whole(pl.ANY)] * results,
        scratch_shapes=[
            pltpu.VMEM((2, levels, rows // 2, cols), F32),
            pltpu.VMEM((2, rows // 2, cols), F32),
            pltpu.SemaphoreType.DMA((6,)),
        ],
        input_output_aliases={
            inputs + i: results - len(written) + i for i in range(len(written))
        },
        compiler_params=pltpu.CompilerParams(vmem_limit_bytes=8 * MIB),
        cost_estimate=pl.CostEstimate(
            flops=20000 * levels * rows * cols,
            bytes_accessed=8 * levels * rows * cols,
            transcendentals=0,
        ),
        name="finish",
    )(in_vmem(known), response, joined, *map(in_vmem, late), *written)


def both_ways(pairs):
    return pairs + [(b, a) for a, b in pairs]


def local(temp, u_vel, v_vel, w_vel, temp_prev, w_prev, lower, upper, metric):
    rows = temp.shape[1]
    across, stacked = lax.axis_size("gx"), lax.axis_size("gz")
    rounds = stacked.bit_length() - 1
    cores = both_ways([(i, i + 1) for i in range(0, stacked, 2)])
    far, near, fluxes, outward, table = edges(
        temp, u_vel, w_vel, v_vel, temp_prev, w_prev, lower, upper, metric
    )
    near = lax.ppermute(near, "gx", both_ways([(i, i + 1) for i in range(0, across, 2)]))
    far = lax.ppermute(far, "gx", both_ways([(i, (i + 1) % across) for i in range(1, across, 2)]))
    other = lax.ppermute(fluxes, "gz", cores)
    outer = ()
    if rounds > 2:
        seams = both_ways([(i, i + 1) for i in range(1, stacked - 1, 2)])
        outer = (lax.ppermute(outward, "gz", seams),)
    forward, tend, first = bulk(table, temp, u_vel, v_vel, w_vel, temp_prev, w_prev)
    entries, changes, *late = fix(
        rounds, near, far, other, fluxes, outward, forward, first, table, outer
    )
    message, seam = late if late else (entries, fluxes)
    bases, gains, own, other_own = [], [], fluxes, other
    for step in range(rounds - 1):
        partners = [(i, i ^ (1 << step)) for i in range(stacked)]
        theirs = lax.ppermute(message, "gz", partners)
        if step > 0:
            other_own = lax.ppermute(own, "gz", partners)
        base, gain, message, *scalars = merge(
            step, step + 2 == rounds, bool(late), rows, entries, theirs, own, other_own
        )
        entries, own = message, scalars[0] if scalars else seam
        bases.append(base)
        gains.append(gain)
    partners = [(i, i ^ (stacked // 2)) for i in range(stacked)]
    theirs = lax.ppermute(message, "gz", partners)
    other_own = lax.ppermute(own, "gz", partners)
    known, response, *passed = prepare(
        rounds, temp, w_vel, forward, table, changes, fluxes, other, *(outer or (other_own,)),
        bases, gains,
    )
    tendencies = tends(rounds, table, tend, far, near, other, outer)
    joined = join(rounds, bool(late), message, theirs, own, other_own)
    swapped = lax.ppermute(joined, "gz", cores)
    if not late:
        written = finish(rounds, known, response, joined, (), ())
        return *finish(rounds, known, response, swapped, (), written), *tendencies
    crossed = lax.ppermute(passed[0], "gz", cores)
    late = (table, tend, far, near)
    written = finish(rounds, known, response, joined, (other_own, *late), tendencies)
    return tuple(finish(rounds, known, response, swapped, (crossed, *late), written))


def solution(mesh):
    field = P("gz", "gx", None)
    return jax.shard_map(
        local,
        mesh=mesh,
        in_specs=(field,) * 6 + (P("gz"),) * 3,
        out_specs=(field,) * 4,
        check_vma=False,
    )
```

```python
import functools

import jax
import jax.numpy as jnp
from jax import lax
from jax.experimental import pallas as pl
from jax.experimental.pallas import tpu as pltpu
from jax.sharding import PartitionSpec as P

NEW_WEIGHT = 5.0 / 12.0
HORIZ_DIFF = 0.1
FIELD_WEIGHT = 2.0 / NEW_WEIGHT
PREV_WEIGHT = (17.0 / 60.0) / NEW_WEIGHT
TILE = 8
MIB = 1024 * 1024

PIVOT_NEW, LOWER_PIVOT, UPPER_PIVOT, FIRST_GREEN, BELOW_FORWARD, PIVOT, RISE, FALL = range(8)
FIRST, CORNER, LAST, BELOW, ABOVE, METRIC_BELOW, METRIC_ABOVE = range(7)
FROM_ABOVE, FROM_BELOW = range(2)

VMEM = pltpu.VMEM
F32 = jnp.float32


def whole(space):
    return pl.BlockSpec(memory_space=space)


def held(*shape):
    return pltpu.VMEM(shape, F32)


def in_vmem(array):
    return pltpu.with_memory_space_constraint(array, pltpu.VMEM)


def in_hbm(*arrays):
    return [pltpu.with_memory_space_constraint(array, pltpu.HBM) for array in arrays]


def bit_of(axis, bit):
    return (lax.axis_index(axis) >> bit) & 1


def edges_kernel(
    temp,
    u_vel,
    w_vel,
    v_vel,
    temp_prev,
    w_prev,
    lower,
    upper,
    metric,
    far,
    near,
    fluxes,
    outward,
    table,
    strips,
    layers,
    lower_at,
    upper_at,
    metric_at,
    sems,
):
    levels, rows, cols = temp.shape
    copies = []
    for at, array in enumerate((temp, w_vel, u_vel)):
        for side, row in enumerate((0, rows - 1)):
            copies.append((array.at[:, row, :], strips.at[at, side]))
    needed = range(len(copies), len(copies) + 3)
    copies += [(lower, lower_at), (upper, upper_at), (metric, metric_at)]
    for at, array in enumerate((temp, w_vel)):
        for side, level in enumerate((0, levels - 1)):
            copies.append((array.at[level], layers.at[at, side]))
    copies = [pltpu.make_async_copy(src, dst, sems.at[i]) for i, (src, dst) in enumerate(copies)]
    for copy in copies:
        copy.start()
    for i in needed:
        copies[i].wait()
    coefficients(lower_at, upper_at, metric_at, table, fluxes.at[pl.ds(3 * rows, TILE)])
    for i, copy in enumerate(copies):
        if i not in needed:
            copy.wait()
    odd = bit_of("gx", 0) == 1
    for field in range(2):
        at = pl.ds(field * levels, levels)
        to_left = (HORIZ_DIFF - 0.5 * strips[2, 0]) * strips[field, 0]
        to_right = (HORIZ_DIFF + 0.5 * strips[2, 1]) * strips[field, 1]
        near[at, :] = jnp.where(odd, to_left, to_right)
        far[at, :] = jnp.where(odd, to_right, to_left)
    position = lax.axis_index("gz")
    upper_core = bit_of("gz", 0) == 1
    wall = (position == 0) | (position == lax.axis_size("gz") - 1)
    zero, size = jnp.zeros((rows, cols), F32), rows // 2
    for field in range(2):
        bottom = layers[1, 0] * layers[field, 0]
        top = layers[1, 1] * layers[field, 1]
        fluxes[pl.ds(field * rows, rows), :] = jnp.where(upper_core, bottom, top)
        value = jnp.where(wall, zero, jnp.where(upper_core, top, bottom))
        outward[pl.ds(field * rows, rows), :] = value
        fluxes[pl.ds(2 * rows + field * size, size), :] = jnp.where(
            upper_core, value[:size], value[size:]
        )


def edges(temp, u_vel, w_vel, v_vel, temp_prev, w_prev, lower, upper, metric):
    levels, rows, cols = temp.shape
    return pl.pallas_call(
        edges_kernel,
        out_shape=(
            held(2 * levels, cols),
            held(2 * levels, cols),
            held(3 * rows + TILE, cols),
            held(2 * rows, cols),
            held(levels, TILE, cols),
        ),
        in_specs=[whole(pl.ANY)] * 9,
        out_specs=[whole(VMEM)] * 5,
        scratch_shapes=[
            pltpu.VMEM((3, 2, levels, cols), F32),
            pltpu.VMEM((2, 2, rows, cols), F32),
            pltpu.SMEM((levels,), F32),
            pltpu.SMEM((levels,), F32),
            pltpu.SMEM((levels,), F32),
            pltpu.SemaphoreType.DMA((13,)),
        ],
        compiler_params=pltpu.CompilerParams(vmem_limit_bytes=8 * MIB),
        name="edges",
    )(*in_hbm(temp, u_vel, w_vel, v_vel, temp_prev, w_prev, lower, upper, metric))


def coefficients(lower, upper, metric, table, scalars):
    levels, _, cols = table.shape

    def row(value):
        return jnp.full((1, cols), value, F32)

    ratio = jnp.zeros((1, cols), F32)
    forward = jnp.ones((1, cols), F32)
    for level in range(levels):
        low, high = row(lower[level]), row(upper[level])
        pivot = 1.0 / (1.0 + low + high - low * ratio)
        ratio = high * pivot
        lower_pivot = low * pivot
        forward = pivot if level == 0 else lower_pivot * forward
        table[level, pl.ds(PIVOT_NEW, 1), :] = NEW_WEIGHT * pivot
        table[level, pl.ds(LOWER_PIVOT, 1), :] = lower_pivot
        table[level, pl.ds(UPPER_PIVOT, 1), :] = ratio
        table[level, pl.ds(BELOW_FORWARD, 1), :] = forward
        table[level, pl.ds(PIVOT, 1), :] = pivot
        table[level, pl.ds(RISE, 1), :] = row(metric[level] if level < levels - 1 else 0.0)
        table[level, pl.ds(FALL, 1), :] = row(metric[level] if level > 0 else 0.0)
    green = forward
    table[levels - 1, pl.ds(FIRST_GREEN, 1), :] = NEW_WEIGHT * green
    for level in range(levels - 2, -1, -1):
        green = (
            table[level, pl.ds(BELOW_FORWARD, 1), :]
            + table[level, pl.ds(UPPER_PIVOT, 1), :] * green
        )
        table[level, pl.ds(FIRST_GREEN, 1), :] = NEW_WEIGHT * green
    scalars[pl.ds(FIRST, 1), :] = green
    scalars[pl.ds(CORNER, 1), :] = forward
    scalars[pl.ds(LAST, 1), :] = pivot
    scalars[pl.ds(BELOW, 1), :] = row(lower[0])
    scalars[pl.ds(ABOVE, 1), :] = row(upper[levels - 1])
    scalars[pl.ds(METRIC_BELOW, 1), :] = row(NEW_WEIGHT * metric[0])
    scalars[pl.ds(METRIC_ABOVE, 1), :] = row(NEW_WEIGHT * metric[levels - 1])
    scalars[pl.ds(7, 1), :] = row(0.0)


def bulk_kernel(
    table,
    temp,
    u_vel,
    v_vel,
    w_vel,
    temp_prev,
    w_prev,
    forward,
    tend,
    first,
):
    levels, rows, cols = temp.shape
    strips = rows // TILE
    fields, prevs = (temp, w_vel), (temp_prev, w_prev)
    for field in range(2):
        forward[field, 0] = jnp.zeros((rows, cols), F32)
        first[field] = jnp.zeros((rows, cols), F32)
    row_at = lax.broadcasted_iota(jnp.int32, (TILE, cols), 0)
    zero = jnp.zeros((TILE, cols), F32)

    def sides(level, strip):
        at = pl.ds(strip * TILE, TILE)
        half = 0.5 * u_vel[level, at, :]
        back, ahead = HORIZ_DIFF - half, HORIZ_DIFF + half
        here = [values[level, at, :] for values in fields]
        return (
            here,
            [pltpu.roll(back * value, TILE - 1, 0) for value in here],
            [pltpu.roll(ahead * value, 1, 0) for value in here],
        )

    def pair_step(pair, carry):
        both = (2 * pair, 2 * pair + 1)
        under, over = jnp.maximum(both[0] - 1, 0), jnp.minimum(both[1] + 1, levels - 1)

        def spread(level, at):
            tile = jnp.broadcast_to(table[level, pl.ds(at, 1), : cols // 2], (TILE, cols // 2))
            return jnp.concatenate([tile, tile], axis=1)

        factors = [
            [spread(level, at) for at in (PIVOT_NEW, LOWER_PIVOT, FIRST_GREEN, RISE, FALL)]
            for level in both
        ]
        before = [[zero, zero], [zero, zero]]
        now = [sides(level, 0) for level in both]
        for strip in range(strips):
            none = (None, [zero, zero], None)
            later = [sides(level, strip + 1) if strip + 1 < strips else none for level in both]
            at = pl.ds(strip * TILE, TILE)
            beneath = [values[under, at, :] for values in fields]
            above = [values[over, at, :] for values in fields]
            solved = [forward[field, both[0], at, :] for field in range(2)]
            total = [first[field, at, :] for field in range(2)]
            for i, level in enumerate(both):
                here, back, ahead = now[i]
                pivot, lower_pivot, green, rise, fall = factors[i]
                upward = above if i else now[1][0]
                downward = now[0][0] if i else beneath
                half = 0.5 * v_vel[level, at, :]
                v_back, v_ahead = HORIZ_DIFF - half, HORIZ_DIFF + half
                w_over, w_under = rise * upward[1], fall * downward[1]
                for field in range(2):
                    value = here[field]
                    change = jnp.where(row_at == TILE - 1, later[i][1][field], back[field])
                    change = change + jnp.where(row_at == 0, before[i][field], ahead[field])
                    change = change + pltpu.roll(v_back * value, cols - 1, 1)
                    change = change + pltpu.roll(v_ahead * value, 1, 1)
                    change = change - w_over * upward[field] + w_under * downward[field]
                    change = change + (here[1 - field] - (4.0 * HORIZ_DIFF) * value)
                    tend[field, level, at, :] = change
                    old = prevs[field][level, at, :]
                    right = change + (FIELD_WEIGHT * value - PREV_WEIGHT * old)
                    solved[field] = pivot * right + lower_pivot * solved[field]
                    forward[field, level + 1, at, :] = solved[field]
                    total[field] = total[field] + green * right
            for field in range(2):
                first[field, at, :] = total[field]
            before = [now[0][2], now[1][2]]
            now = later
        return carry

    lax.fori_loop(0, levels // 2, pair_step, 0)


def bulk(table, *arrays):
    levels, rows, cols = arrays[0].shape
    return pl.pallas_call(
        bulk_kernel,
        out_shape=(
            held(2, levels + 1, rows, cols),
            held(2, levels, rows, cols),
            held(2, rows, cols),
        ),
        in_specs=[whole(VMEM)] * 7,
        out_specs=[whole(VMEM)] * 3,
        compiler_params=pltpu.CompilerParams(vmem_limit_bytes=8 * MIB),
        cost_estimate=pl.CostEstimate(
            flops=100000 * levels * rows * cols,
            bytes_accessed=24 * levels * rows * cols,
            transcendentals=0,
        ),
        name="bulk",
    )(*map(in_vmem, (table, *arrays)))


def side_changes(far, near):
    odd = bit_of("gx", 0) == 1
    return jnp.where(odd, near[...], far[...]), jnp.where(odd, far[...], near[...])


def level_fluxes(inner, outer):
    upper = bit_of("gz", 0) == 1
    return jnp.where(upper, inner, outer), jnp.where(upper, outer, inner)


def beside_seam(rounds):
    return bit_of("gz", 0) != bit_of("gz", rounds - 1)


def ends(rows, cols, head, tail):
    at = lax.broadcasted_iota(jnp.int32, (rows, cols), 0)
    return jnp.where(at == 0, head, jnp.where(at == rows - 1, tail, 0.0))


def scalar_rows(ref, begin=0):
    return [ref[pl.ds(begin + at, 1), :] for at in range(7)]


def put_seam(ref, field, value):
    size, cols = value.shape
    for part in range(2):
        at = pl.ds((2 * part + field) * size, size)
        ref[at, :] = value[:, part * cols // 2 : (part + 1) * cols // 2]


def get_seam(ref, field, size):
    parts = [ref[pl.ds((2 * part + field) * size, size), :] for part in range(2)]
    return jnp.concatenate(parts, axis=1)


def in_order(upper, own, other):
    low = [jnp.where(upper, b, a) for a, b in zip(own, other)]
    high = [jnp.where(upper, a, b) for a, b in zip(own, other)]
    return low, high


def interface(low, high):
    coupling = low[ABOVE]
    return coupling, 1.0 / (1.0 - coupling * coupling * low[LAST] * high[FIRST])


def joint_scalars(low, high):
    coupling, inverse = interface(low, high)
    low_out, high_out = low[CORNER] * coupling, high[CORNER] * coupling
    return [
        low[FIRST] + low_out * low_out * inverse * high[FIRST],
        low_out * inverse * high[CORNER],
        high[LAST] + high_out * high_out * inverse * low[LAST],
        low[BELOW],
        high[ABOVE],
        low[METRIC_BELOW],
        high[METRIC_ABOVE],
        jnp.zeros_like(coupling),
    ]


def fix_kernel(
    rounds, levels, near, far, other, fluxes, outward, forward, first, table, *rest
):
    outer, rest = (rest[0], rest[1:]) if rounds > 2 else (None, rest)
    entries, changes, *late = rest
    _, rows, cols = first.shape
    diffs = side_changes(far, near)
    scalars = scalar_rows(fluxes, 3 * rows)
    below, above = scalars[METRIC_BELOW], -scalars[METRIC_ABOVE]
    core, size = bit_of("gz", 0) == 1, rows // 2
    for field in range(2):
        firsts, lasts = [], []
        for side in range(2):
            value = jnp.zeros((1, cols), F32)
            total = jnp.zeros((1, cols), F32)
            for level in range(levels):
                right = diffs[side][field * levels + level : field * levels + level + 1, :]
                value = (
                    table[level, pl.ds(PIVOT_NEW, 1), :] * right
                    + table[level, pl.ds(LOWER_PIVOT, 1), :] * value
                )
                total = total + table[level, pl.ds(FIRST_GREEN, 1), :] * right
                changes[pl.ds((side * 2 + field) * levels + level, 1), :] = value
            firsts.append(total)
            lasts.append(value)
        at = pl.ds(field * rows, rows)
        flux_below, flux_above = level_fluxes(other[at, :], 0.0 if outer is None else outer[at, :])
        first_entry = (
            first[field]
            + (below * scalars[FIRST]) * flux_below
            + (above * scalars[CORNER]) * flux_above
            + ends(rows, cols, *firsts)
        )
        last_entry = (
            forward[field, levels]
            + (below * scalars[CORNER]) * flux_below
            + (above * scalars[LAST]) * flux_above
            + ends(rows, cols, *lasts)
        )
        entries[at, :] = first_entry
        entries[pl.ds((2 + field) * rows, rows), :] = last_entry
        if late:
            message, seam = late
            message[at, :] = jnp.where(core, first_entry, last_entry)
            there = pl.ds(2 * rows + field * size, size)
            message[there, :] = jnp.where(core, last_entry[:size], first_entry[size:])
            value = outward[at, :]
            value = jnp.where(core, value[size:], value[:size])
            put_seam(seam, field, jnp.where(beside_seam(rounds), value, other[there, :]))
    if late:
        far_scalars = scalar_rows(other, 3 * rows)
        for at, value in enumerate(joint_scalars(*in_order(core, scalars, far_scalars))):
            seam[pl.ds(2 * rows + at, 1), :] = value[:, : cols // 2]


def fix(rounds, near, far, other, fluxes, outward, forward, first, table, outer):
    levels = table.shape[0]
    _, rows, cols = first.shape
    shapes = [held(4 * rows, cols), held(4 * levels, cols)]
    if rounds == 2:
        shapes += [held(3 * rows, cols), held(2 * rows + TILE, cols // 2)]
    return pl.pallas_call(
        functools.partial(fix_kernel, rounds, levels),
        out_shape=tuple(shapes),
        in_specs=[whole(VMEM)] * (8 + len(outer)),
        out_specs=[whole(VMEM)] * len(shapes),
        compiler_params=pltpu.CompilerParams(vmem_limit_bytes=8 * MIB),
        name="fix",
    )(
        near, far, other, fluxes, outward, in_vmem(forward), in_vmem(first), in_vmem(table), *outer
    )


def tends_kernel(rounds, table, tend, far, near, other, *rest):
    outer, rest = (rest[0], rest[1:]) if rounds > 2 else (None, rest)
    *outs, layers, strips, sems = rest
    _, levels, rows, cols = tend.shape
    inside, middle = pl.ds(1, levels - 2), pl.ds(TILE, rows - 2 * TILE)
    copies = []

    def send(field, at, src, dst):
        copies.append(pltpu.make_async_copy(src, dst, sems.at[field, at]))
        copies[-1].start()

    for field, out in enumerate(outs):
        send(field, 0, tend.at[field, inside, middle, :], out.at[inside, middle, :])
    diffs = side_changes(far, near)
    tile_at = lax.broadcasted_iota(jnp.int32, (TILE, cols), 0)
    for field, out in enumerate(outs):
        at = pl.ds(field * rows, rows)
        below, above = level_fluxes(other[at, :], 0.0 if outer is None else outer[at, :])
        for side, level, change in (
            (0, 0, table[0, pl.ds(RISE, 1), :] * below),
            (1, levels - 1, -table[levels - 1, pl.ds(FALL, 1), :] * above),
        ):
            at = field * levels + level
            rim = ends(rows, cols, diffs[0][at : at + 1, :], diffs[1][at : at + 1, :])
            layers[field, side] = tend[field, level] + change + rim
            send(field, 1 + side, layers.at[field, side], out.at[level])
        for side, begin, row in ((0, 0, 0), (1, rows - TILE, TILE - 1)):
            for level in range(1, levels - 1):
                at = field * levels + level
                edge = jnp.where(tile_at == row, diffs[side][at : at + 1, :], 0.0)
                strips[field, side, level] = tend[field, level, pl.ds(begin, TILE), :] + edge
            there = out.at[inside, pl.ds(begin, TILE), :]
            send(field, 3 + side, strips.at[field, side, inside], there)
    for copy in copies:
        copy.wait()


def tends(rounds, table, tend, far, near, other, outer):
    _, levels, rows, cols = tend.shape
    return pl.pallas_call(
        functools.partial(tends_kernel, rounds),
        out_shape=(jax.ShapeDtypeStruct((levels, rows, cols), F32),) * 2,
        in_specs=[whole(VMEM)] * (5 + len(outer)),
        out_specs=[whole(pl.ANY)] * 2,
        scratch_shapes=[
            pltpu.VMEM((2, 2, rows, cols), F32),
            pltpu.VMEM((2, 2, levels, TILE, cols), F32),
            pltpu.SemaphoreType.DMA((2, 5)),
        ],
        compiler_params=pltpu.CompilerParams(vmem_limit_bytes=8 * MIB),
        cost_estimate=pl.CostEstimate(
            flops=levels * rows * cols,
            bytes_accessed=8 * levels * rows * cols,
            transcendentals=0,
        ),
        name="tends",
    )(in_vmem(table), in_vmem(tend), far, near, other, *outer)


def merge_kernel(bit, final, late, own_at, other_at, mine, theirs, own, other, base, gains, *rest):
    _, rows, cols = base.shape
    upper = bit_of("gz", bit) == 1
    low, high = in_order(upper, scalar_rows(own, own_at), scalar_rows(other, other_at))
    coupling, inverse = interface(low, high)
    to_high, to_low = high[FIRST] * coupling, low[LAST] * coupling
    low_out, high_out = low[CORNER] * coupling, high[CORNER] * coupling
    core, size = bit_of("gz", 0) == 1, rows // 2
    sends_last = bit_of("gz", bit + 1) == 0
    for field in range(2):
        here = pl.ds(field * rows, rows)
        own_first, own_last = mine[here, :], mine[pl.ds((2 + field) * rows, rows), :]
        if late:
            low_last = jnp.where(upper, theirs[here, :], own_last)
            high_first = jnp.where(upper, own_first, theirs[here, :])
        else:
            other_first, other_last = theirs[here, :], theirs[pl.ds((2 + field) * rows, rows), :]
            low_last = jnp.where(upper, other_last, own_last)
            high_first = jnp.where(upper, own_first, other_first)
            low_first = jnp.where(upper, other_first, own_first)
            high_last = jnp.where(upper, own_last, other_last)
        above = inverse * (high_first + to_high * low_last)
        below = inverse * (low_last + to_low * high_first)
        base[field] = coupling * jnp.where(upper, below, above)
        more = jnp.where(sends_last, high_out * below, low_out * above)
        if late:
            outside = jnp.where(upper, own_last, own_first)
            outside = jnp.where(core, outside[size:], outside[:size])
            there = theirs[pl.ds(2 * rows + field * size, size), :]
            outside = jnp.where(sends_last == upper, outside, there)
        elif final:
            outside = jnp.where(sends_last, high_last, low_first)
            outside = jnp.where(core, outside[size:], outside[:size])
        if final:
            value = outside + jnp.where(core, more[size:], more[:size])
            rest[0][pl.ds(field * size, size), :] = value
        else:
            rest[0][here, :] = low_first + low_out * above
            rest[0][pl.ds((2 + field) * rows, rows), :] = high_last + high_out * below
    if not late:
        for at, value in enumerate(joint_scalars(low, high)):
            rest[1][pl.ds(at, 1), :] = value
    scale = coupling * inverse
    gains[...] = jnp.zeros(gains.shape, F32)
    gains[pl.ds(FROM_ABOVE, 1), :] = scale * high[CORNER] * jnp.where(upper, to_low, 1.0)
    gains[pl.ds(FROM_BELOW, 1), :] = scale * low[CORNER] * jnp.where(upper, 1.0, to_high)


def merge(bit, final, late, rows, mine, theirs, own, other):
    cols = mine.shape[1]
    shapes = [held(2, rows, cols), held(TILE, cols), held((1 if final else 4) * rows, cols)]
    if not late:
        shapes.append(held(TILE, cols))
    return pl.pallas_call(
        functools.partial(
            merge_kernel, bit, final, late, own.shape[0] - TILE, other.shape[0] - TILE
        ),
        out_shape=tuple(shapes),
        in_specs=[whole(VMEM)] * 4,
        out_specs=[whole(VMEM)] * len(shapes),
        compiler_params=pltpu.CompilerParams(vmem_limit_bytes=8 * MIB),
        name="merge",
    )(mine, theirs, own, other)


def prepare_kernel(
    rounds, temp, w_vel, forward, table, changes, fluxes, other, crossing, *rest
):
    outer = crossing if rounds > 2 else None
    bases, gains = rest[: rounds - 1], rest[rounds - 1 : 2 * rounds - 2]
    known, response, *passed, below_in, above_in = rest[2 * rounds - 2 :]
    if passed:
        passed[0][...] = crossing[pl.ds(0, passed[0].shape[0]), :]
    levels, rows, cols = temp.shape
    upper = bit_of("gz", rounds - 1) == 1
    one, none = jnp.ones((1, cols), F32), jnp.zeros((1, cols), F32)
    below_gain, above_gain = jnp.where(upper, one, none), jnp.where(upper, none, one)
    below = above = None
    for step in range(rounds - 2, -1, -1):
        side = bit_of("gz", step) == 1
        from_above = gains[step][pl.ds(FROM_ABOVE, 1), :]
        from_below = gains[step][pl.ds(FROM_BELOW, 1), :]
        gain = from_above * above_gain + from_below * below_gain
        below_gain = jnp.where(side, gain, below_gain)
        above_gain = jnp.where(side, above_gain, gain)
        into = [bases[step][field] for field in range(2)]
        if below is None:
            below = above = [jnp.zeros((rows, cols), F32)] * 2
        else:
            into = [
                into[field] + from_above * above[field] + from_below * below[field]
                for field in range(2)
            ]
        below = [jnp.where(side, into[field], below[field]) for field in range(2)]
        above = [jnp.where(side, above[field], into[field]) for field in range(2)]
    scalars = scalar_rows(fluxes, 3 * rows)
    for field in range(2):
        at = pl.ds(field * rows, rows)
        flux_below, flux_above = level_fluxes(other[at, :], 0.0 if outer is None else outer[at, :])
        below_in[field] = below[field] + scalars[METRIC_BELOW] * flux_below
        above_in[field] = above[field] - scalars[METRIC_ABOVE] * flux_above

    gain = above_gain * table[levels - 1, pl.ds(PIVOT, 1), :]
    for level in range(levels - 1, -1, -1):
        if level < levels - 1:
            gain = gain * table[level, pl.ds(UPPER_PIVOT, 1), :]
        gain = gain + below_gain * table[level, pl.ds(BELOW_FORWARD, 1), :]
        response[level] = jnp.broadcast_to(gain, (TILE, cols))

    row_at = lax.broadcasted_iota(jnp.int32, (TILE, cols), 0)
    width = 2 * TILE
    for begin in range(0, rows, width):
        at = pl.ds(begin, width)

        def solve(level, carry, factor, begin=begin, at=at):
            factor = table[level, pl.ds(factor, 1), :]
            below_factor = table[level, pl.ds(BELOW_FORWARD, 1), :]
            values = []
            for field, cells in enumerate((temp, w_vel)):
                value = forward[field, level + 1, at, :] + below_factor * below_in[field, at, :]
                if begin == 0:
                    change = changes[pl.ds(field * levels + level, 1), :]
                    head = value[:TILE] + jnp.where(row_at == 0, change, 0.0)
                    value = jnp.concatenate([head, value[TILE:]])
                if begin == rows - width:
                    change = changes[pl.ds((2 + field) * levels + level, 1), :]
                    tail = value[-TILE:] + jnp.where(row_at == TILE - 1, change, 0.0)
                    value = jnp.concatenate([value[:-TILE], tail])
                value = value + factor * carry[field]
                known[field, level, at, :] = value - cells[level, at, :]
                values.append(value)
            return tuple(values)

        carry = solve(levels - 1, [above_in[field, at, :] for field in range(2)], PIVOT)

        def step(back, carry, solve=solve):
            return solve(levels - 2 - back, carry, UPPER_PIVOT)

        lax.fori_loop(0, levels - 1, step, carry, unroll=3)


def prepare(rounds, temp, w_vel, forward, table, changes, fluxes, other, crossing, bases, gains):
    levels, rows, cols = temp.shape
    shapes = (held(2, levels, rows, cols), held(levels, TILE, cols))
    shapes += (held(2 * rows, cols // 2),) * (rounds == 2)
    return pl.pallas_call(
        functools.partial(prepare_kernel, rounds),
        out_shape=shapes,
        in_specs=[whole(VMEM)] * (8 + 2 * (rounds - 1)),
        out_specs=[whole(VMEM)] * len(shapes),
        scratch_shapes=[pltpu.VMEM((2, rows, cols), F32)] * 2,
        compiler_params=pltpu.CompilerParams(vmem_limit_bytes=8 * MIB),
        cost_estimate=pl.CostEstimate(
            flops=levels * rows * cols,
            bytes_accessed=24 * levels * rows * cols,
            transcendentals=0,
        ),
        name="prepare",
    )(
        in_vmem(temp), in_vmem(w_vel), in_vmem(forward), in_vmem(table), changes, fluxes, other,
        crossing, *bases, *gains,
    )


def join_kernel(rounds, late, own_at, other_at, mine, theirs, own, other, joined):
    size = theirs.shape[0] // 2
    upper = bit_of("gz", rounds - 1) == 1
    low, high = in_order(upper, scalar_rows(own, own_at), scalar_rows(other, other_at))
    if late:
        low, high = ([jnp.concatenate([a, a], axis=1) for a in rows] for rows in (low, high))
    coupling, inverse = interface(low, high)
    scale = coupling * inverse
    to_other = scale * coupling * jnp.where(upper, low[LAST], high[FIRST])
    up, down = high[METRIC_BELOW] * inverse, -low[METRIC_ABOVE] * inverse
    own_gain = coupling * jnp.where(upper, down * low[LAST], up * high[FIRST])
    other_gain = jnp.where(upper, up, down)
    for field in range(2):
        at = pl.ds(field * size, size)
        into = scale * theirs[at, :] + to_other * mine[at, :]
        if late:
            into = into + own_gain * get_seam(own, field, size)
            into = into + other_gain * get_seam(other, field, size)
        joined[at, :] = into


def join(rounds, late, mine, theirs, own, other):
    size, cols = theirs.shape
    return pl.pallas_call(
        functools.partial(join_kernel, rounds, late, own.shape[0] - TILE, other.shape[0] - TILE),
        out_shape=held(size, cols),
        in_specs=[whole(VMEM)] * 4,
        out_specs=whole(VMEM),
        compiler_params=pltpu.CompilerParams(vmem_limit_bytes=8 * MIB),
        name="join",
    )(mine, theirs, own, other)


def finish_kernel(rounds, swapped, known, response, joined, *rest):
    late, results = rounds == 2, 4 if rounds == 2 else 2
    flux_in, table, tend, far, near = rest[:5] if late else (None,) * 5
    rest = rest[(5 if late else 0) + (results if swapped else results - 2) :]
    outs, (result, rim, sems) = rest[:results], rest[results:]
    _, levels, rows, cols = known.shape
    width, half = 2 * TILE, rows // 2
    core = bit_of("gz", 0)
    start = pl.multiple_of((1 - core if swapped else core) * half, half)
    copies = []
    for field in range(2):
        for part, begin in enumerate(range(0, half, width)):
            into = joined[pl.ds(field * half + begin, width), :]
            tiles = [into[i : i + TILE] for i in range(0, width, TILE)]

            def step(level, carry, field=field, begin=begin, tiles=tiles):
                gain = response[level]
                for i, tile in enumerate(tiles):
                    at = begin + i * TILE
                    value = known[field, level, pl.ds(start + at, TILE), :] + gain * tile
                    result[field, level, pl.ds(at, TILE), :] = value
                return carry

            lax.fori_loop(0, levels, step, 0, unroll=True)
            copies.append(
                pltpu.make_async_copy(
                    result.at[field, :, pl.ds(begin, width), :],
                    outs[field].at[:, pl.ds(start + begin, width), :],
                    sems.at[2 + 2 * field + part],
                )
            )
            copies[-1].start()
    if late:
        diffs = side_changes(far, near)
        level = core * (levels - 1)
        gain = jnp.where(
            core == 1, -table[levels - 1, pl.ds(FALL, 1), :], table[0, pl.ds(RISE, 1), :]
        )
        gain = jnp.where(beside_seam(rounds), gain, 0.0)
        row_at = start + lax.broadcasted_iota(jnp.int32, (half, cols), 0)
        for field in range(2):
            head, tail = (
                jnp.where(
                    core == 1,
                    diff[(field + 1) * levels - 1 : (field + 1) * levels, :],
                    diff[field * levels : field * levels + 1, :],
                )
                for diff in diffs
            )
            edge = jnp.where(row_at == 0, head, jnp.where(row_at == rows - 1, tail, 0.0))
            flux = get_seam(flux_in, field, half)
            rim[field] = tend[field, level, pl.ds(start, half), :] + gain * flux + edge
            copies.append(
                pltpu.make_async_copy(
                    rim.at[field],
                    outs[2 + field].at[level, pl.ds(start, half), :],
                    sems.at[field],
                )
            )
            copies[-1].start()
    for copy in copies:
        copy.wait()


def finish(rounds, known, response, joined, late, written):
    _, levels, rows, cols = known.shape
    results = 4 if rounds == 2 else 2
    inputs = 3 + len(late)
    swapped = len(written) == results
    return pl.pallas_call(
        functools.partial(finish_kernel, rounds, swapped),
        out_shape=(jax.ShapeDtypeStruct((levels, rows, cols), F32),) * results,
        in_specs=[whole(VMEM)] * inputs + [whole(pl.ANY)] * len(written),
        out_specs=[whole(pl.ANY)] * results,
        scratch_shapes=[
            pltpu.VMEM((2, levels, rows // 2, cols), F32),
            pltpu.VMEM((2, rows // 2, cols), F32),
            pltpu.SemaphoreType.DMA((6,)),
        ],
        input_output_aliases={
            inputs + i: results - len(written) + i for i in range(len(written))
        },
        compiler_params=pltpu.CompilerParams(vmem_limit_bytes=8 * MIB),
        cost_estimate=pl.CostEstimate(
            flops=20000 * levels * rows * cols,
            bytes_accessed=8 * levels * rows * cols,
            transcendentals=0,
        ),
        name="finish",
    )(in_vmem(known), response, joined, *map(in_vmem, late), *written)


def both_ways(pairs):
    return pairs + [(b, a) for a, b in pairs]


def local(temp, u_vel, v_vel, w_vel, temp_prev, w_prev, lower, upper, metric):
    rows = temp.shape[1]
    across, stacked = lax.axis_size("gx"), lax.axis_size("gz")
    rounds = stacked.bit_length() - 1
    cores = both_ways([(i, i + 1) for i in range(0, stacked, 2)])
    far, near, fluxes, outward, table = edges(
        temp, u_vel, w_vel, v_vel, temp_prev, w_prev, lower, upper, metric
    )
    near = lax.ppermute(near, "gx", both_ways([(i, i + 1) for i in range(0, across, 2)]))
    far = lax.ppermute(far, "gx", both_ways([(i, (i + 1) % across) for i in range(1, across, 2)]))
    other = lax.ppermute(fluxes, "gz", cores)
    outer = ()
    if rounds > 2:
        seams = both_ways([(i, i + 1) for i in range(1, stacked - 1, 2)])
        outer = (lax.ppermute(outward, "gz", seams),)
    forward, tend, first = bulk(table, temp, u_vel, v_vel, w_vel, temp_prev, w_prev)
    entries, changes, *late = fix(
        rounds, near, far, other, fluxes, outward, forward, first, table, outer
    )
    message, seam = late if late else (entries, fluxes)
    bases, gains, own, other_own = [], [], fluxes, other
    for step in range(rounds - 1):
        partners = [(i, i ^ (1 << step)) for i in range(stacked)]
        theirs = lax.ppermute(message, "gz", partners)
        if step > 0:
            other_own = lax.ppermute(own, "gz", partners)
        base, gain, message, *scalars = merge(
            step, step + 2 == rounds, bool(late), rows, entries, theirs, own, other_own
        )
        entries, own = message, scalars[0] if scalars else seam
        bases.append(base)
        gains.append(gain)
    partners = [(i, i ^ (stacked // 2)) for i in range(stacked)]
    theirs = lax.ppermute(message, "gz", partners)
    other_own = lax.ppermute(own, "gz", partners)
    known, response, *passed = prepare(
        rounds, temp, w_vel, forward, table, changes, fluxes, other, *(outer or (other_own,)),
        bases, gains,
    )
    tendencies = tends(rounds, table, tend, far, near, other, outer)
    joined = join(rounds, bool(late), message, theirs, own, other_own)
    swapped = lax.ppermute(joined, "gz", cores)
    if not late:
        written = finish(rounds, known, response, joined, (), ())
        return *finish(rounds, known, response, swapped, (), written), *tendencies
    crossed = lax.ppermute(passed[0], "gz", cores)
    late = (table, tend, far, near)
    written = finish(rounds, known, response, joined, (other_own, *late), tendencies)
    return tuple(finish(rounds, known, response, swapped, (crossed, *late), written))


def solution(mesh):
    field = P("gz", "gx", None)
    return jax.shard_map(
        local,
        mesh=mesh,
        in_specs=(field,) * 6 + (P("gz"),) * 3,
        out_specs=(field,) * 4,
        check_vma=False,
    )
```

```python
import functools

import jax
import jax.numpy as jnp
from jax import lax
from jax.experimental import pallas as pl
from jax.experimental.pallas import tpu as pltpu
from jax.sharding import PartitionSpec as P

NEW_WEIGHT = 5.0 / 12.0
HORIZ_DIFF = 0.1
FIELD_WEIGHT = 2.0 / NEW_WEIGHT
PREV_WEIGHT = (17.0 / 60.0) / NEW_WEIGHT
TILE = 8
MIB = 1024 * 1024

PIVOT_NEW, LOWER_PIVOT, UPPER_PIVOT, FIRST_GREEN, BELOW_FORWARD, PIVOT, RISE, FALL = range(8)
FIRST, CORNER, LAST, BELOW, ABOVE, METRIC_BELOW, METRIC_ABOVE = range(7)
FROM_ABOVE, FROM_BELOW = range(2)

VMEM = pltpu.VMEM
F32 = jnp.float32


def whole(space):
    return pl.BlockSpec(memory_space=space)


def held(*shape):
    return pltpu.VMEM(shape, F32)


def in_vmem(array):
    return pltpu.with_memory_space_constraint(array, pltpu.VMEM)


def in_hbm(*arrays):
    return [pltpu.with_memory_space_constraint(array, pltpu.HBM) for array in arrays]


def bit_of(axis, bit):
    return (lax.axis_index(axis) >> bit) & 1


def edges_kernel(
    temp,
    u_vel,
    w_vel,
    v_vel,
    temp_prev,
    w_prev,
    lower,
    upper,
    metric,
    far,
    near,
    fluxes,
    outward,
    table,
    strips,
    layers,
    lower_at,
    upper_at,
    metric_at,
    sems,
):
    levels, rows, cols = temp.shape
    copies = []
    for at, array in enumerate((temp, w_vel, u_vel)):
        for side, row in enumerate((0, rows - 1)):
            copies.append((array.at[:, row, :], strips.at[at, side]))
    needed = range(len(copies), len(copies) + 3)
    copies += [(lower, lower_at), (upper, upper_at), (metric, metric_at)]
    for at, array in enumerate((temp, w_vel)):
        for side, level in enumerate((0, levels - 1)):
            copies.append((array.at[level], layers.at[at, side]))
    copies = [pltpu.make_async_copy(src, dst, sems.at[i]) for i, (src, dst) in enumerate(copies)]
    for copy in copies:
        copy.start()
    for i in needed:
        copies[i].wait()
    coefficients(lower_at, upper_at, metric_at, table, fluxes.at[pl.ds(3 * rows, TILE)])
    for i, copy in enumerate(copies):
        if i not in needed:
            copy.wait()
    odd = bit_of("gx", 0) == 1
    for field in range(2):
        at = pl.ds(field * levels, levels)
        to_left = (HORIZ_DIFF - 0.5 * strips[2, 0]) * strips[field, 0]
        to_right = (HORIZ_DIFF + 0.5 * strips[2, 1]) * strips[field, 1]
        near[at, :] = jnp.where(odd, to_left, to_right)
        far[at, :] = jnp.where(odd, to_right, to_left)
    position = lax.axis_index("gz")
    upper_core = bit_of("gz", 0) == 1
    wall = (position == 0) | (position == lax.axis_size("gz") - 1)
    zero, size = jnp.zeros((rows, cols), F32), rows // 2
    for field in range(2):
        bottom = layers[1, 0] * layers[field, 0]
        top = layers[1, 1] * layers[field, 1]
        fluxes[pl.ds(field * rows, rows), :] = jnp.where(upper_core, bottom, top)
        value = jnp.where(wall, zero, jnp.where(upper_core, top, bottom))
        outward[pl.ds(field * rows, rows), :] = value
        fluxes[pl.ds(2 * rows + field * size, size), :] = jnp.where(
            upper_core, value[:size], value[size:]
        )


def edges(temp, u_vel, w_vel, v_vel, temp_prev, w_prev, lower, upper, metric):
    levels, rows, cols = temp.shape
    return pl.pallas_call(
        edges_kernel,
        out_shape=(
            held(2 * levels, cols),
            held(2 * levels, cols),
            held(3 * rows + TILE, cols),
            held(2 * rows, cols),
            held(levels, TILE, cols),
        ),
        in_specs=[whole(pl.ANY)] * 9,
        out_specs=[whole(VMEM)] * 5,
        scratch_shapes=[
            pltpu.VMEM((3, 2, levels, cols), F32),
            pltpu.VMEM((2, 2, rows, cols), F32),
            pltpu.SMEM((levels,), F32),
            pltpu.SMEM((levels,), F32),
            pltpu.SMEM((levels,), F32),
            pltpu.SemaphoreType.DMA((13,)),
        ],
        compiler_params=pltpu.CompilerParams(vmem_limit_bytes=8 * MIB),
        name="edges",
    )(*in_hbm(temp, u_vel, w_vel, v_vel, temp_prev, w_prev, lower, upper, metric))


def coefficients(lower, upper, metric, table, scalars):
    levels, _, cols = table.shape

    def row(value):
        return jnp.full((1, cols), value, F32)

    ratio = jnp.zeros((1, cols), F32)
    forward = jnp.ones((1, cols), F32)
    for level in range(levels):
        low, high = row(lower[level]), row(upper[level])
        pivot = 1.0 / (1.0 + low + high - low * ratio)
        ratio = high * pivot
        lower_pivot = low * pivot
        forward = pivot if level == 0 else lower_pivot * forward
        table[level, pl.ds(PIVOT_NEW, 1), :] = NEW_WEIGHT * pivot
        table[level, pl.ds(LOWER_PIVOT, 1), :] = lower_pivot
        table[level, pl.ds(UPPER_PIVOT, 1), :] = ratio
        table[level, pl.ds(BELOW_FORWARD, 1), :] = forward
        table[level, pl.ds(PIVOT, 1), :] = pivot
        table[level, pl.ds(RISE, 1), :] = row(metric[level] if level < levels - 1 else 0.0)
        table[level, pl.ds(FALL, 1), :] = row(metric[level] if level > 0 else 0.0)
    green = forward
    table[levels - 1, pl.ds(FIRST_GREEN, 1), :] = NEW_WEIGHT * green
    for level in range(levels - 2, -1, -1):
        green = (
            table[level, pl.ds(BELOW_FORWARD, 1), :]
            + table[level, pl.ds(UPPER_PIVOT, 1), :] * green
        )
        table[level, pl.ds(FIRST_GREEN, 1), :] = NEW_WEIGHT * green
    scalars[pl.ds(FIRST, 1), :] = green
    scalars[pl.ds(CORNER, 1), :] = forward
    scalars[pl.ds(LAST, 1), :] = pivot
    scalars[pl.ds(BELOW, 1), :] = row(lower[0])
    scalars[pl.ds(ABOVE, 1), :] = row(upper[levels - 1])
    scalars[pl.ds(METRIC_BELOW, 1), :] = row(NEW_WEIGHT * metric[0])
    scalars[pl.ds(METRIC_ABOVE, 1), :] = row(NEW_WEIGHT * metric[levels - 1])
    scalars[pl.ds(7, 1), :] = row(0.0)


def bulk_kernel(
    table,
    temp,
    u_vel,
    v_vel,
    w_vel,
    temp_prev,
    w_prev,
    forward,
    tend,
    first,
):
    levels, rows, cols = temp.shape
    strips = rows // TILE
    fields, prevs = (temp, w_vel), (temp_prev, w_prev)
    for field in range(2):
        forward[field, 0] = jnp.zeros((rows, cols), F32)
        first[field] = jnp.zeros((rows, cols), F32)
    row_at = lax.broadcasted_iota(jnp.int32, (TILE, cols), 0)
    zero = jnp.zeros((TILE, cols), F32)

    def sides(level, strip):
        at = pl.ds(strip * TILE, TILE)
        half = 0.5 * u_vel[level, at, :]
        back, ahead = HORIZ_DIFF - half, HORIZ_DIFF + half
        here = [values[level, at, :] for values in fields]
        return (
            here,
            [pltpu.roll(back * value, TILE - 1, 0) for value in here],
            [pltpu.roll(ahead * value, 1, 0) for value in here],
        )

    def pair_step(pair, carry):
        both = (2 * pair, 2 * pair + 1)
        under, over = jnp.maximum(both[0] - 1, 0), jnp.minimum(both[1] + 1, levels - 1)

        def spread(level, at):
            tile = jnp.broadcast_to(table[level, pl.ds(at, 1), : cols // 2], (TILE, cols // 2))
            return jnp.concatenate([tile, tile], axis=1)

        factors = [
            [spread(level, at) for at in (PIVOT_NEW, LOWER_PIVOT, FIRST_GREEN, RISE, FALL)]
            for level in both
        ]
        before = [[zero, zero], [zero, zero]]
        now = [sides(level, 0) for level in both]
        for strip in range(strips):
            none = (None, [zero, zero], None)
            later = [sides(level, strip + 1) if strip + 1 < strips else none for level in both]
            at = pl.ds(strip * TILE, TILE)
            beneath = [values[under, at, :] for values in fields]
            above = [values[over, at, :] for values in fields]
            solved = [forward[field, both[0], at, :] for field in range(2)]
            total = [first[field, at, :] for field in range(2)]
            for i, level in enumerate(both):
                here, back, ahead = now[i]
                pivot, lower_pivot, green, rise, fall = factors[i]
                upward = above if i else now[1][0]
                downward = now[0][0] if i else beneath
                half = 0.5 * v_vel[level, at, :]
                v_back, v_ahead = HORIZ_DIFF - half, HORIZ_DIFF + half
                w_over, w_under = rise * upward[1], fall * downward[1]
                for field in range(2):
                    value = here[field]
                    change = jnp.where(row_at == TILE - 1, later[i][1][field], back[field])
                    change = change + jnp.where(row_at == 0, before[i][field], ahead[field])
                    change = change + pltpu.roll(v_back * value, cols - 1, 1)
                    change = change + pltpu.roll(v_ahead * value, 1, 1)
                    change = change - w_over * upward[field] + w_under * downward[field]
                    change = change + (here[1 - field] - (4.0 * HORIZ_DIFF) * value)
                    tend[field, level, at, :] = change
                    old = prevs[field][level, at, :]
                    right = change + (FIELD_WEIGHT * value - PREV_WEIGHT * old)
                    solved[field] = pivot * right + lower_pivot * solved[field]
                    forward[field, level + 1, at, :] = solved[field]
                    total[field] = total[field] + green * right
            for field in range(2):
                first[field, at, :] = total[field]
            before = [now[0][2], now[1][2]]
            now = later
        return carry

    lax.fori_loop(0, levels // 2, pair_step, 0, unroll=2)


def bulk(table, *arrays):
    levels, rows, cols = arrays[0].shape
    return pl.pallas_call(
        bulk_kernel,
        out_shape=(
            held(2, levels + 1, rows, cols),
            held(2, levels, rows, cols),
            held(2, rows, cols),
        ),
        in_specs=[whole(VMEM)] * 7,
        out_specs=[whole(VMEM)] * 3,
        compiler_params=pltpu.CompilerParams(vmem_limit_bytes=8 * MIB),
        cost_estimate=pl.CostEstimate(
            flops=100000 * levels * rows * cols,
            bytes_accessed=24 * levels * rows * cols,
            transcendentals=0,
        ),
        name="bulk",
    )(*map(in_vmem, (table, *arrays)))


def side_changes(far, near):
    odd = bit_of("gx", 0) == 1
    return jnp.where(odd, near[...], far[...]), jnp.where(odd, far[...], near[...])


def level_fluxes(inner, outer):
    upper = bit_of("gz", 0) == 1
    return jnp.where(upper, inner, outer), jnp.where(upper, outer, inner)


def beside_seam(rounds):
    return bit_of("gz", 0) != bit_of("gz", rounds - 1)


def ends(rows, cols, head, tail):
    at = lax.broadcasted_iota(jnp.int32, (rows, cols), 0)
    return jnp.where(at == 0, head, jnp.where(at == rows - 1, tail, 0.0))


def scalar_rows(ref, begin=0):
    return [ref[pl.ds(begin + at, 1), :] for at in range(7)]


def put_seam(ref, field, value):
    size, cols = value.shape
    for part in range(2):
        at = pl.ds((2 * part + field) * size, size)
        ref[at, :] = value[:, part * cols // 2 : (part + 1) * cols // 2]


def get_seam(ref, field, size):
    parts = [ref[pl.ds((2 * part + field) * size, size), :] for part in range(2)]
    return jnp.concatenate(parts, axis=1)


def in_order(upper, own, other):
    low = [jnp.where(upper, b, a) for a, b in zip(own, other)]
    high = [jnp.where(upper, a, b) for a, b in zip(own, other)]
    return low, high


def interface(low, high):
    coupling = low[ABOVE]
    return coupling, 1.0 / (1.0 - coupling * coupling * low[LAST] * high[FIRST])


def joint_scalars(low, high):
    coupling, inverse = interface(low, high)
    low_out, high_out = low[CORNER] * coupling, high[CORNER] * coupling
    return [
        low[FIRST] + low_out * low_out * inverse * high[FIRST],
        low_out * inverse * high[CORNER],
        high[LAST] + high_out * high_out * inverse * low[LAST],
        low[BELOW],
        high[ABOVE],
        low[METRIC_BELOW],
        high[METRIC_ABOVE],
        jnp.zeros_like(coupling),
    ]


def fix_kernel(
    rounds, levels, near, far, other, fluxes, outward, forward, first, table, *rest
):
    outer, rest = (rest[0], rest[1:]) if rounds > 2 else (None, rest)
    entries, changes, *late = rest
    _, rows, cols = first.shape
    diffs = side_changes(far, near)
    scalars = scalar_rows(fluxes, 3 * rows)
    below, above = scalars[METRIC_BELOW], -scalars[METRIC_ABOVE]
    core, size = bit_of("gz", 0) == 1, rows // 2
    for field in range(2):
        firsts, lasts = [], []
        for side in range(2):
            value = jnp.zeros((1, cols), F32)
            total = jnp.zeros((1, cols), F32)
            for level in range(levels):
                right = diffs[side][field * levels + level : field * levels + level + 1, :]
                value = (
                    table[level, pl.ds(PIVOT_NEW, 1), :] * right
                    + table[level, pl.ds(LOWER_PIVOT, 1), :] * value
                )
                total = total + table[level, pl.ds(FIRST_GREEN, 1), :] * right
                changes[pl.ds((side * 2 + field) * levels + level, 1), :] = value
            firsts.append(total)
            lasts.append(value)
        at = pl.ds(field * rows, rows)
        flux_below, flux_above = level_fluxes(other[at, :], 0.0 if outer is None else outer[at, :])
        first_entry = (
            first[field]
            + (below * scalars[FIRST]) * flux_below
            + (above * scalars[CORNER]) * flux_above
            + ends(rows, cols, *firsts)
        )
        last_entry = (
            forward[field, levels]
            + (below * scalars[CORNER]) * flux_below
            + (above * scalars[LAST]) * flux_above
            + ends(rows, cols, *lasts)
        )
        entries[at, :] = first_entry
        entries[pl.ds((2 + field) * rows, rows), :] = last_entry
        if late:
            message, seam = late
            message[at, :] = jnp.where(core, first_entry, last_entry)
            there = pl.ds(2 * rows + field * size, size)
            message[there, :] = jnp.where(core, last_entry[:size], first_entry[size:])
            value = outward[at, :]
            value = jnp.where(core, value[size:], value[:size])
            put_seam(seam, field, jnp.where(beside_seam(rounds), value, other[there, :]))
    if late:
        far_scalars = scalar_rows(other, 3 * rows)
        for at, value in enumerate(joint_scalars(*in_order(core, scalars, far_scalars))):
            seam[pl.ds(2 * rows + at, 1), :] = value[:, : cols // 2]


def fix(rounds, near, far, other, fluxes, outward, forward, first, table, outer):
    levels = table.shape[0]
    _, rows, cols = first.shape
    shapes = [held(4 * rows, cols), held(4 * levels, cols)]
    if rounds == 2:
        shapes += [held(3 * rows, cols), held(2 * rows + TILE, cols // 2)]
    return pl.pallas_call(
        functools.partial(fix_kernel, rounds, levels),
        out_shape=tuple(shapes),
        in_specs=[whole(VMEM)] * (8 + len(outer)),
        out_specs=[whole(VMEM)] * len(shapes),
        compiler_params=pltpu.CompilerParams(vmem_limit_bytes=8 * MIB),
        name="fix",
    )(
        near, far, other, fluxes, outward, in_vmem(forward), in_vmem(first), in_vmem(table), *outer
    )


def tends_kernel(rounds, table, tend, far, near, other, *rest):
    outer, rest = (rest[0], rest[1:]) if rounds > 2 else (None, rest)
    *outs, layers, strips, sems = rest
    _, levels, rows, cols = tend.shape
    inside, middle = pl.ds(1, levels - 2), pl.ds(TILE, rows - 2 * TILE)
    copies = []

    def send(field, at, src, dst):
        copies.append(pltpu.make_async_copy(src, dst, sems.at[field, at]))
        copies[-1].start()

    for field, out in enumerate(outs):
        send(field, 0, tend.at[field, inside, middle, :], out.at[inside, middle, :])
    diffs = side_changes(far, near)
    tile_at = lax.broadcasted_iota(jnp.int32, (TILE, cols), 0)
    for field, out in enumerate(outs):
        at = pl.ds(field * rows, rows)
        below, above = level_fluxes(other[at, :], 0.0 if outer is None else outer[at, :])
        for side, level, change in (
            (0, 0, table[0, pl.ds(RISE, 1), :] * below),
            (1, levels - 1, -table[levels - 1, pl.ds(FALL, 1), :] * above),
        ):
            at = field * levels + level
            rim = ends(rows, cols, diffs[0][at : at + 1, :], diffs[1][at : at + 1, :])
            layers[field, side] = tend[field, level] + change + rim
            send(field, 1 + side, layers.at[field, side], out.at[level])
        for side, begin, row in ((0, 0, 0), (1, rows - TILE, TILE - 1)):
            for level in range(1, levels - 1):
                at = field * levels + level
                edge = jnp.where(tile_at == row, diffs[side][at : at + 1, :], 0.0)
                strips[field, side, level] = tend[field, level, pl.ds(begin, TILE), :] + edge
            there = out.at[inside, pl.ds(begin, TILE), :]
            send(field, 3 + side, strips.at[field, side, inside], there)
    for copy in copies:
        copy.wait()


def tends(rounds, table, tend, far, near, other, outer):
    _, levels, rows, cols = tend.shape
    return pl.pallas_call(
        functools.partial(tends_kernel, rounds),
        out_shape=(jax.ShapeDtypeStruct((levels, rows, cols), F32),) * 2,
        in_specs=[whole(VMEM)] * (5 + len(outer)),
        out_specs=[whole(pl.ANY)] * 2,
        scratch_shapes=[
            pltpu.VMEM((2, 2, rows, cols), F32),
            pltpu.VMEM((2, 2, levels, TILE, cols), F32),
            pltpu.SemaphoreType.DMA((2, 5)),
        ],
        compiler_params=pltpu.CompilerParams(vmem_limit_bytes=8 * MIB),
        cost_estimate=pl.CostEstimate(
            flops=levels * rows * cols,
            bytes_accessed=8 * levels * rows * cols,
            transcendentals=0,
        ),
        name="tends",
    )(in_vmem(table), in_vmem(tend), far, near, other, *outer)


def merge_kernel(bit, final, late, own_at, other_at, mine, theirs, own, other, base, gains, *rest):
    _, rows, cols = base.shape
    upper = bit_of("gz", bit) == 1
    low, high = in_order(upper, scalar_rows(own, own_at), scalar_rows(other, other_at))
    coupling, inverse = interface(low, high)
    to_high, to_low = high[FIRST] * coupling, low[LAST] * coupling
    low_out, high_out = low[CORNER] * coupling, high[CORNER] * coupling
    core, size = bit_of("gz", 0) == 1, rows // 2
    sends_last = bit_of("gz", bit + 1) == 0
    for field in range(2):
        here = pl.ds(field * rows, rows)
        own_first, own_last = mine[here, :], mine[pl.ds((2 + field) * rows, rows), :]
        if late:
            low_last = jnp.where(upper, theirs[here, :], own_last)
            high_first = jnp.where(upper, own_first, theirs[here, :])
        else:
            other_first, other_last = theirs[here, :], theirs[pl.ds((2 + field) * rows, rows), :]
            low_last = jnp.where(upper, other_last, own_last)
            high_first = jnp.where(upper, own_first, other_first)
            low_first = jnp.where(upper, other_first, own_first)
            high_last = jnp.where(upper, own_last, other_last)
        above = inverse * (high_first + to_high * low_last)
        below = inverse * (low_last + to_low * high_first)
        base[field] = coupling * jnp.where(upper, below, above)
        more = jnp.where(sends_last, high_out * below, low_out * above)
        if late:
            outside = jnp.where(upper, own_last, own_first)
            outside = jnp.where(core, outside[size:], outside[:size])
            there = theirs[pl.ds(2 * rows + field * size, size), :]
            outside = jnp.where(sends_last == upper, outside, there)
        elif final:
            outside = jnp.where(sends_last, high_last, low_first)
            outside = jnp.where(core, outside[size:], outside[:size])
        if final:
            value = outside + jnp.where(core, more[size:], more[:size])
            rest[0][pl.ds(field * size, size), :] = value
        else:
            rest[0][here, :] = low_first + low_out * above
            rest[0][pl.ds((2 + field) * rows, rows), :] = high_last + high_out * below
    if not late:
        for at, value in enumerate(joint_scalars(low, high)):
            rest[1][pl.ds(at, 1), :] = value
    scale = coupling * inverse
    gains[...] = jnp.zeros(gains.shape, F32)
    gains[pl.ds(FROM_ABOVE, 1), :] = scale * high[CORNER] * jnp.where(upper, to_low, 1.0)
    gains[pl.ds(FROM_BELOW, 1), :] = scale * low[CORNER] * jnp.where(upper, 1.0, to_high)


def merge(bit, final, late, rows, mine, theirs, own, other):
    cols = mine.shape[1]
    shapes = [held(2, rows, cols), held(TILE, cols), held((1 if final else 4) * rows, cols)]
    if not late:
        shapes.append(held(TILE, cols))
    return pl.pallas_call(
        functools.partial(
            merge_kernel, bit, final, late, own.shape[0] - TILE, other.shape[0] - TILE
        ),
        out_shape=tuple(shapes),
        in_specs=[whole(VMEM)] * 4,
        out_specs=[whole(VMEM)] * len(shapes),
        compiler_params=pltpu.CompilerParams(vmem_limit_bytes=8 * MIB),
        name="merge",
    )(mine, theirs, own, other)


def prepare_kernel(
    rounds, temp, w_vel, forward, table, changes, fluxes, other, crossing, *rest
):
    outer = crossing if rounds > 2 else None
    bases, gains = rest[: rounds - 1], rest[rounds - 1 : 2 * rounds - 2]
    known, response, *passed, below_in, above_in = rest[2 * rounds - 2 :]
    if passed:
        passed[0][...] = crossing[pl.ds(0, passed[0].shape[0]), :]
    levels, rows, cols = temp.shape
    upper = bit_of("gz", rounds - 1) == 1
    one, none = jnp.ones((1, cols), F32), jnp.zeros((1, cols), F32)
    below_gain, above_gain = jnp.where(upper, one, none), jnp.where(upper, none, one)
    below = above = None
    for step in range(rounds - 2, -1, -1):
        side = bit_of("gz", step) == 1
        from_above = gains[step][pl.ds(FROM_ABOVE, 1), :]
        from_below = gains[step][pl.ds(FROM_BELOW, 1), :]
        gain = from_above * above_gain + from_below * below_gain
        below_gain = jnp.where(side, gain, below_gain)
        above_gain = jnp.where(side, above_gain, gain)
        into = [bases[step][field] for field in range(2)]
        if below is None:
            below = above = [jnp.zeros((rows, cols), F32)] * 2
        else:
            into = [
                into[field] + from_above * above[field] + from_below * below[field]
                for field in range(2)
            ]
        below = [jnp.where(side, into[field], below[field]) for field in range(2)]
        above = [jnp.where(side, above[field], into[field]) for field in range(2)]
    scalars = scalar_rows(fluxes, 3 * rows)
    for field in range(2):
        at = pl.ds(field * rows, rows)
        flux_below, flux_above = level_fluxes(other[at, :], 0.0 if outer is None else outer[at, :])
        below_in[field] = below[field] + scalars[METRIC_BELOW] * flux_below
        above_in[field] = above[field] - scalars[METRIC_ABOVE] * flux_above

    gain = above_gain * table[levels - 1, pl.ds(PIVOT, 1), :]
    for level in range(levels - 1, -1, -1):
        if level < levels - 1:
            gain = gain * table[level, pl.ds(UPPER_PIVOT, 1), :]
        gain = gain + below_gain * table[level, pl.ds(BELOW_FORWARD, 1), :]
        response[level] = jnp.broadcast_to(gain, (TILE, cols))

    row_at = lax.broadcasted_iota(jnp.int32, (TILE, cols), 0)
    width = 2 * TILE
    for begin in range(0, rows, width):
        at = pl.ds(begin, width)

        def solve(level, carry, factor, begin=begin, at=at):
            factor = table[level, pl.ds(factor, 1), :]
            below_factor = table[level, pl.ds(BELOW_FORWARD, 1), :]
            values = []
            for field, cells in enumerate((temp, w_vel)):
                value = forward[field, level + 1, at, :] + below_factor * below_in[field, at, :]
                if begin == 0:
                    change = changes[pl.ds(field * levels + level, 1), :]
                    head = value[:TILE] + jnp.where(row_at == 0, change, 0.0)
                    value = jnp.concatenate([head, value[TILE:]])
                if begin == rows - width:
                    change = changes[pl.ds((2 + field) * levels + level, 1), :]
                    tail = value[-TILE:] + jnp.where(row_at == TILE - 1, change, 0.0)
                    value = jnp.concatenate([value[:-TILE], tail])
                value = value + factor * carry[field]
                known[field, level, at, :] = value - cells[level, at, :]
                values.append(value)
            return tuple(values)

        carry = solve(levels - 1, [above_in[field, at, :] for field in range(2)], PIVOT)

        def step(back, carry, solve=solve):
            return solve(levels - 2 - back, carry, UPPER_PIVOT)

        lax.fori_loop(0, levels - 1, step, carry, unroll=3)


def prepare(rounds, temp, w_vel, forward, table, changes, fluxes, other, crossing, bases, gains):
    levels, rows, cols = temp.shape
    shapes = (held(2, levels, rows, cols), held(levels, TILE, cols))
    shapes += (held(2 * rows, cols // 2),) * (rounds == 2)
    return pl.pallas_call(
        functools.partial(prepare_kernel, rounds),
        out_shape=shapes,
        in_specs=[whole(VMEM)] * (8 + 2 * (rounds - 1)),
        out_specs=[whole(VMEM)] * len(shapes),
        scratch_shapes=[pltpu.VMEM((2, rows, cols), F32)] * 2,
        compiler_params=pltpu.CompilerParams(vmem_limit_bytes=8 * MIB),
        cost_estimate=pl.CostEstimate(
            flops=levels * rows * cols,
            bytes_accessed=24 * levels * rows * cols,
            transcendentals=0,
        ),
        name="prepare",
    )(
        in_vmem(temp), in_vmem(w_vel), in_vmem(forward), in_vmem(table), changes, fluxes, other,
        crossing, *bases, *gains,
    )


def join_kernel(rounds, late, own_at, other_at, mine, theirs, own, other, joined):
    size = theirs.shape[0] // 2
    upper = bit_of("gz", rounds - 1) == 1
    low, high = in_order(upper, scalar_rows(own, own_at), scalar_rows(other, other_at))
    if late:
        low, high = ([jnp.concatenate([a, a], axis=1) for a in rows] for rows in (low, high))
    coupling, inverse = interface(low, high)
    scale = coupling * inverse
    to_other = scale * coupling * jnp.where(upper, low[LAST], high[FIRST])
    up, down = high[METRIC_BELOW] * inverse, -low[METRIC_ABOVE] * inverse
    own_gain = coupling * jnp.where(upper, down * low[LAST], up * high[FIRST])
    other_gain = jnp.where(upper, up, down)
    for field in range(2):
        at = pl.ds(field * size, size)
        into = scale * theirs[at, :] + to_other * mine[at, :]
        if late:
            into = into + own_gain * get_seam(own, field, size)
            into = into + other_gain * get_seam(other, field, size)
        joined[at, :] = into


def join(rounds, late, mine, theirs, own, other):
    size, cols = theirs.shape
    return pl.pallas_call(
        functools.partial(join_kernel, rounds, late, own.shape[0] - TILE, other.shape[0] - TILE),
        out_shape=held(size, cols),
        in_specs=[whole(VMEM)] * 4,
        out_specs=whole(VMEM),
        compiler_params=pltpu.CompilerParams(vmem_limit_bytes=8 * MIB),
        name="join",
    )(mine, theirs, own, other)


def finish_kernel(rounds, swapped, known, response, joined, *rest):
    late, results = rounds == 2, 4 if rounds == 2 else 2
    flux_in, table, tend, far, near = rest[:5] if late else (None,) * 5
    rest = rest[(5 if late else 0) + (results if swapped else results - 2) :]
    outs, (result, rim, sems) = rest[:results], rest[results:]
    _, levels, rows, cols = known.shape
    width, half = 2 * TILE, rows // 2
    core = bit_of("gz", 0)
    start = pl.multiple_of((1 - core if swapped else core) * half, half)
    copies = []
    for field in range(2):
        for part, begin in enumerate(range(0, half, width)):
            into = joined[pl.ds(field * half + begin, width), :]
            tiles = [into[i : i + TILE] for i in range(0, width, TILE)]

            def step(level, carry, field=field, begin=begin, tiles=tiles):
                gain = response[level]
                for i, tile in enumerate(tiles):
                    at = begin + i * TILE
                    value = known[field, level, pl.ds(start + at, TILE), :] + gain * tile
                    result[field, level, pl.ds(at, TILE), :] = value
                return carry

            lax.fori_loop(0, levels, step, 0, unroll=True)
            copies.append(
                pltpu.make_async_copy(
                    result.at[field, :, pl.ds(begin, width), :],
                    outs[field].at[:, pl.ds(start + begin, width), :],
                    sems.at[2 + 2 * field + part],
                )
            )
            copies[-1].start()
    if late:
        diffs = side_changes(far, near)
        level = core * (levels - 1)
        gain = jnp.where(
            core == 1, -table[levels - 1, pl.ds(FALL, 1), :], table[0, pl.ds(RISE, 1), :]
        )
        gain = jnp.where(beside_seam(rounds), gain, 0.0)
        row_at = start + lax.broadcasted_iota(jnp.int32, (half, cols), 0)
        for field in range(2):
            head, tail = (
                jnp.where(
                    core == 1,
                    diff[(field + 1) * levels - 1 : (field + 1) * levels, :],
                    diff[field * levels : field * levels + 1, :],
                )
                for diff in diffs
            )
            edge = jnp.where(row_at == 0, head, jnp.where(row_at == rows - 1, tail, 0.0))
            flux = get_seam(flux_in, field, half)
            rim[field] = tend[field, level, pl.ds(start, half), :] + gain * flux + edge
            copies.append(
                pltpu.make_async_copy(
                    rim.at[field],
                    outs[2 + field].at[level, pl.ds(start, half), :],
                    sems.at[field],
                )
            )
            copies[-1].start()
    for copy in copies:
        copy.wait()


def finish(rounds, known, response, joined, late, written):
    _, levels, rows, cols = known.shape
    results = 4 if rounds == 2 else 2
    inputs = 3 + len(late)
    swapped = len(written) == results
    return pl.pallas_call(
        functools.partial(finish_kernel, rounds, swapped),
        out_shape=(jax.ShapeDtypeStruct((levels, rows, cols), F32),) * results,
        in_specs=[whole(VMEM)] * inputs + [whole(pl.ANY)] * len(written),
        out_specs=[whole(pl.ANY)] * results,
        scratch_shapes=[
            pltpu.VMEM((2, levels, rows // 2, cols), F32),
            pltpu.VMEM((2, rows // 2, cols), F32),
            pltpu.SemaphoreType.DMA((6,)),
        ],
        input_output_aliases={
            inputs + i: results - len(written) + i for i in range(len(written))
        },
        compiler_params=pltpu.CompilerParams(vmem_limit_bytes=8 * MIB),
        cost_estimate=pl.CostEstimate(
            flops=20000 * levels * rows * cols,
            bytes_accessed=8 * levels * rows * cols,
            transcendentals=0,
        ),
        name="finish",
    )(in_vmem(known), response, joined, *map(in_vmem, late), *written)


def both_ways(pairs):
    return pairs + [(b, a) for a, b in pairs]


def local(temp, u_vel, v_vel, w_vel, temp_prev, w_prev, lower, upper, metric):
    rows = temp.shape[1]
    across, stacked = lax.axis_size("gx"), lax.axis_size("gz")
    rounds = stacked.bit_length() - 1
    cores = both_ways([(i, i + 1) for i in range(0, stacked, 2)])
    far, near, fluxes, outward, table = edges(
        temp, u_vel, w_vel, v_vel, temp_prev, w_prev, lower, upper, metric
    )
    near = lax.ppermute(near, "gx", both_ways([(i, i + 1) for i in range(0, across, 2)]))
    far = lax.ppermute(far, "gx", both_ways([(i, (i + 1) % across) for i in range(1, across, 2)]))
    other = lax.ppermute(fluxes, "gz", cores)
    outer = ()
    if rounds > 2:
        seams = both_ways([(i, i + 1) for i in range(1, stacked - 1, 2)])
        outer = (lax.ppermute(outward, "gz", seams),)
    forward, tend, first = bulk(table, temp, u_vel, v_vel, w_vel, temp_prev, w_prev)
    entries, changes, *late = fix(
        rounds, near, far, other, fluxes, outward, forward, first, table, outer
    )
    message, seam = late if late else (entries, fluxes)
    bases, gains, own, other_own = [], [], fluxes, other
    for step in range(rounds - 1):
        partners = [(i, i ^ (1 << step)) for i in range(stacked)]
        theirs = lax.ppermute(message, "gz", partners)
        if step > 0:
            other_own = lax.ppermute(own, "gz", partners)
        base, gain, message, *scalars = merge(
            step, step + 2 == rounds, bool(late), rows, entries, theirs, own, other_own
        )
        entries, own = message, scalars[0] if scalars else seam
        bases.append(base)
        gains.append(gain)
    partners = [(i, i ^ (stacked // 2)) for i in range(stacked)]
    theirs = lax.ppermute(message, "gz", partners)
    other_own = lax.ppermute(own, "gz", partners)
    known, response, *passed = prepare(
        rounds, temp, w_vel, forward, table, changes, fluxes, other, *(outer or (other_own,)),
        bases, gains,
    )
    tendencies = tends(rounds, table, tend, far, near, other, outer)
    joined = join(rounds, bool(late), message, theirs, own, other_own)
    swapped = lax.ppermute(joined, "gz", cores)
    if not late:
        written = finish(rounds, known, response, joined, (), ())
        return *finish(rounds, known, response, swapped, (), written), *tendencies
    crossed = lax.ppermute(passed[0], "gz", cores)
    late = (table, tend, far, near)
    written = finish(rounds, known, response, joined, (other_own, *late), tendencies)
    return tuple(finish(rounds, known, response, swapped, (crossed, *late), written))


def solution(mesh):
    field = P("gz", "gx", None)
    return jax.shard_map(
        local,
        mesh=mesh,
        in_specs=(field,) * 6 + (P("gz"),) * 3,
        out_specs=(field,) * 4,
        check_vma=False,
    )
```
